32 devices in a mesh: dp: 4 (over y, x), fsdp: 8 (over z, core).
Axes of the slice: x: 2, y: 2, z: 4, core: 2. Of those that a mesh axis runs over, the one named last changes fastest.
Arguments:
- source: bfloat16 [4096, 1024], P(('dp', 'fsdp')), may hold values from -6 to 6
- dec_in: bfloat16 [4096, 3, 1024], P(('dp', 'fsdp')), may hold values from -6 to 6
- src_lengths: int32 [32], P(('dp', 'fsdp')), may hold values from 65 to 128, as said below
- tgt_lengths: int32 [32], P(('dp', 'fsdp')), may hold values from 65 to 128, as said below
- enc_in_proj: bfloat16 [1024, 3072], P(('dp', 'fsdp')), may hold values from -0.1875 to 0.1875
- enc_out_proj: bfloat16 [1024, 1024], P(('dp', 'fsdp')), may hold values from -1.5 to 1.5
- enc_ffn_in: bfloat16 [1024, 4096], P(('dp', 'fsdp')), may hold values from -0.1875 to 0.1875
- enc_ffn_out: bfloat16 [4096, 1024], P(('dp', 'fsdp')), may hold values from -0.1875 to 0.1875
- enc_gains: bfloat16 [2048], P(('dp', 'fsdp')), may hold values from 0.5 to 1.5
- enc_biases: bfloat16 [10240], P(('dp', 'fsdp')), may hold values from -1.1953125 to 1.1953125
- dec_in_proj: bfloat16 [1024, 3072], P(('dp', 'fsdp')), may hold values from -0.1875 to 0.1875
- dec_rel_proj: bfloat16 [1024, 512], P(('dp', 'fsdp')), may hold values from -0.1875 to 0.1875
- dec_out_proj: bfloat16 [1024, 1024], P(('dp', 'fsdp')), may hold values from -1.5 to 1.5
- cross_query: bfloat16 [1024, 1024], P(('dp', 'fsdp')), may hold values from -0.1875 to 0.1875
- cross_kv: bfloat16 [1024, 2048], P(('dp', 'fsdp')), may hold values from -0.1875 to 0.1875
- cross_out: bfloat16 [1024, 1024], P(('dp', 'fsdp')), may hold values from -1.5 to 1.5
- dec_ffn_in: bfloat16 [1024, 4096], P(('dp', 'fsdp')), may hold values from -0.1875 to 0.1875
- dec_ffn_out: bfloat16 [4096, 1024], P(('dp', 'fsdp')), may hold values from -0.1875 to 0.1875
- dec_gains: bfloat16 [3072], P(('dp', 'fsdp')), may hold values from 0.5 to 1.5
- dec_biases: bfloat16 [14848], P(('dp', 'fsdp')), may hold values from -1.1953125 to 1.1953125
- enc_cot: bfloat16 [4096, 1024], P(('dp', 'fsdp')), may hold values from -6 to 6
- dec_cot: bfloat16 [4096, 3, 1024], P(('dp', 'fsdp')), may hold values from -6 to 6
Outputs:
- enc_out: bfloat16 [4096, 1024], P(('dp', 'fsdp'))
- dec_out: bfloat16 [4096, 3, 1024], P(('dp', 'fsdp'))
- source_grad: float32 [4096, 1024], P(('dp', 'fsdp'))
- dec_in_grad: float32 [4096, 3, 1024], P(('dp', 'fsdp'))
- grad_enc_in_proj: float32 [1024, 3072], P(('dp', 'fsdp'))
- grad_enc_out_proj: float32 [1024, 1024], P(('dp', 'fsdp'))
- grad_enc_ffn_in: float32 [1024, 4096], P(('dp', 'fsdp'))
- grad_enc_ffn_out: float32 [4096, 1024], P(('dp', 'fsdp'))
- grad_enc_gains: float32 [2048], P(('dp', 'fsdp'))
- grad_enc_biases: float32 [10240], P(('dp', 'fsdp'))
- grad_dec_in_proj: float32 [1024, 3072], P(('dp', 'fsdp'))
- grad_dec_rel_proj: float32 [1024, 512], P(('dp', 'fsdp'))
- grad_dec_out_proj: float32 [1024, 1024], P(('dp', 'fsdp'))
- grad_cross_query: float32 [1024, 1024], P(('dp', 'fsdp'))
- grad_cross_kv: float32 [1024, 2048], P(('dp', 'fsdp'))
- grad_cross_out: float32 [1024, 1024], P(('dp', 'fsdp'))
- grad_dec_ffn_in: float32 [1024, 4096], P(('dp', 'fsdp'))
- grad_dec_ffn_out: float32 [4096, 1024], P(('dp', 'fsdp'))
- grad_dec_gains: float32 [3072], P(('dp', 'fsdp'))
- grad_dec_biases: float32 [14848], P(('dp', 'fsdp'))
The draws below stay inside these ranges and needn't reach their ends.
Inputs may be any that keep to these rules, and one draw needn't show every extreme that they name: `src_lengths`: every draw has a source sequence of exactly 128 tokens. `tgt_lengths`: every draw has a target sequence of exactly 128 tokens.
All inputs are finite; a program needn't handle non-finite values.
Results may differ from the reference program's by a relative error of at most 0.025.
Values may be sent and summed in bfloat16 or wider, within the bound.
No kernel may reach another device: no remote copies, remote signals or barrier semaphores. Data moves between devices by JAX's collectives and lax.ppermute only.
A program may use at most 320 MiB of HBM per device.

```python
import math
import jax
import jax.numpy as jnp
from jax import lax

D = 1024
HEADS = 16
HEAD = 64
FF = 4096
NGRAM = 2
BUCKETS = 32
LEN = 128
TOKENS = 4096
DEVICES = 32


def draw_lengths(key):
    shortfall = jax.random.randint(jax.random.fold_in(key, 1), (DEVICES,), 0, LEN // 2)
    chosen = jax.random.randint(jax.random.fold_in(key, 2), (), 0, DEVICES)
    lengths = LEN - shortfall
    return jnp.where(jnp.arange(DEVICES) == chosen, LEN, lengths).astype(jnp.int32)


def draw_src_lengths(key, part):
    key = jax.random.fold_in(key, 11)
    return draw_lengths(key)


def draw_tgt_lengths(key, part):
    key = jax.random.fold_in(key, 12)
    return draw_lengths(key)


def strengthened(entries, own_key, source, target, blocks, factor):
    def block_of(position):
        return (jnp.arange(entries.shape[position]) // (entries.shape[position] // blocks)).reshape((-1,) + (1,) * (entries.ndim - 1 - position))

    one_side = jax.random.permutation(own_key, blocks)[block_of(target)]
    second = (block_of(target) + blocks // 2) % blocks
    return jnp.where((block_of(source) == one_side) | (block_of(source) == second), factor * entries, entries)


def levels(rng, extent, shards, smallest, largest):
    gain, own = 1.0, jax.random.fold_in(rng, 6)
    for position, blocks in shards:
        steps = jnp.exp(jax.random.uniform(jax.random.fold_in(own, position), (blocks,), jnp.float32, smallest / len(shards), largest / len(shards)))
        gain = gain * jnp.repeat(steps, extent[position] // blocks).reshape([-1 if axis == position else 1 for axis in range(len(extent))])
    return gain


def noise(stream_key, extent, deviation, limit, shards=(), kind=jnp.bfloat16):
    factor_of = levels(stream_key, extent, shards, -0.22, 0.18) if shards else 1.0
    values = jax.random.normal(stream_key, extent, jnp.float32) * deviation * factor_of
    return jnp.minimum(jnp.maximum(values, -limit), limit).astype(kind)


def gaussian_with(own_key, dims, width, limit, pieces, heavy, held_as=jnp.bfloat16):
    values = width * jax.random.normal(own_key, dims, jnp.float32)
    if pieces:
        values = values * levels(own_key, dims, pieces, -0.22, 0.18)
    return jnp.clip(strengthened(values, jax.random.fold_in(own_key, 3), *heavy), -limit, limit).astype(held_as)


def setup_inputs(seed: int = 0) -> dict:
    streams_of = jax.random.split(jax.random.key(seed), 23)
    source = gaussian_with(streams_of[0], (TOKENS, D), 1.0, 6.0, ((0, 32),), (0, 1, 32, 2.75))
    dec_in = gaussian_with(streams_of[1], (TOKENS, NGRAM + 1, D), 1.0, 6.0, ((0, 32),), (0, 2, 32, 2.75))
    src_lengths = draw_src_lengths(jax.random.fold_in(streams_of[22], 71), 0)
    tgt_lengths = draw_tgt_lengths(jax.random.fold_in(streams_of[22], 71), 0)
    enc_in_proj = noise(streams_of[4], (D, 3 * D), D ** -0.5, 0.1875, ((0, 32),))
    enc_out_proj = noise(streams_of[5], (D, D), (D // 64) ** -0.5, 1.5, ((0, 32),))
    enc_ffn_in = noise(streams_of[6], (D, FF), D ** -0.5, 0.1875, ((0, 32),))
    enc_ffn_out = noise(streams_of[7], (FF, D), (FF // 4) ** -0.5, 0.1875, ((0, 32),))
    enc_gains = jnp.clip(1.0 + 0.1 * jax.random.normal(streams_of[8], (2 * D,), jnp.float32), 0.5, 1.5).astype(jnp.bfloat16)
    enc_biases = noise(streams_of[9], (6 * D + FF,), 0.2, 1.1953125, ((0, 32),))
    dec_in_proj = noise(streams_of[10], (D, 3 * D), D ** -0.5, 0.1875, ((0, 32),))
    dec_rel_proj = noise(streams_of[11], (D, HEADS * BUCKETS), D ** -0.5, 0.1875, ((0, 32),))
    dec_out_proj = noise(streams_of[12], (D, D), (D // 64) ** -0.5, 1.5, ((0, 32),))
    cross_query = noise(streams_of[13], (D, D), D ** -0.5, 0.1875, ((0, 32),))
    cross_kv = noise(streams_of[14], (D, 2 * D), D ** -0.5, 0.1875, ((0, 32),))
    cross_out = noise(streams_of[15], (D, D), (D // 64) ** -0.5, 1.5, ((0, 32),))
    dec_ffn_in = noise(streams_of[16], (D, FF), D ** -0.5, 0.1875, ((0, 32),))
    dec_ffn_out = noise(streams_of[17], (FF, D), (FF // 4) ** -0.5, 0.1875, ((0, 32),))
    dec_gains = jnp.clip(1.0 + 0.1 * jax.random.normal(streams_of[18], (3 * D,), jnp.float32), 0.5, 1.5).astype(jnp.bfloat16)
    dec_biases = noise(streams_of[19], (10 * D + HEADS * BUCKETS + FF,), 0.2, 1.1953125, ((0, 32),))
    enc_cot = noise(streams_of[20], (TOKENS, D), 1.0, 6.0, ((0, 32),))
    dec_cot = noise(streams_of[21], (TOKENS, NGRAM + 1, D), 1.0, 6.0, ((0, 32),))
    return {"source": source, "dec_in": dec_in, "src_lengths": src_lengths, "tgt_lengths": tgt_lengths, "enc_in_proj": enc_in_proj, "enc_out_proj": enc_out_proj, "enc_ffn_in": enc_ffn_in, "enc_ffn_out": enc_ffn_out, "enc_gains": enc_gains, "enc_biases": enc_biases, "dec_in_proj": dec_in_proj, "dec_rel_proj": dec_rel_proj, "dec_out_proj": dec_out_proj, "cross_query": cross_query, "cross_kv": cross_kv, "cross_out": cross_out, "dec_ffn_in": dec_ffn_in, "dec_ffn_out": dec_ffn_out, "dec_gains": dec_gains, "dec_biases": dec_biases, "enc_cot": enc_cot, "dec_cot": dec_cot}


@jax.custom_vjp
def low(v):
    return lax.optimization_barrier(v.astype(jnp.bfloat16)).astype(jnp.float32)

@jax.custom_vjp
def low_back(v):
    return v

def low_keep(v):
    return (low(v), None)

def low_pass(kept, grad):
    return (grad,)

def back_keep(v):
    return (v, None)

def back_low(kept, grad):
    return (low(grad),)
low.defvjp(low_keep, low_pass)
low_back.defvjp(back_keep, back_low)
norm_epsilon = 1e-05
masked_score = -1000000000.0

def bucket_value(distance, bucket_count):
    exact_count = bucket_count // 2
    if distance < exact_count:
        return distance
    return min(bucket_count - 1, exact_count + int(math.log(distance / exact_count) / math.log(128 / exact_count) * (bucket_count - exact_count)))

def bucket_table(length, bucket_count):
    positions = jnp.arange(length, dtype=jnp.int32)
    distance = positions[:, None] - positions[None, :]
    bucket = jnp.zeros((length, length), jnp.int32)
    for target in range(1, bucket_count):
        distance_at = 1
        while bucket_value(distance_at, bucket_count) < target:
            distance_at += 1
        bucket = bucket + (distance >= distance_at).astype(jnp.int32)
    return (bucket[:, :, None] == jnp.arange(bucket_count, dtype=jnp.int32)).astype(jnp.float32)

def slices_of(vector, widths):
    starts = 0
    result = []
    for amount in widths:
        result.append(vector[starts:starts + amount])
        starts += amount
    return result

def layer_norm(values, gain_vector, shift_vector):
    average = lax.optimization_barrier(jnp.mean(values, axis=-1, keepdims=True))
    centered = values - average
    variance = lax.optimization_barrier(jnp.mean(centered * centered, axis=-1, keepdims=True))
    return centered * lax.rsqrt(variance + norm_epsilon) * gain_vector + shift_vector

def matmul_high(inputs, matrix):
    return jnp.einsum('...d,de->...e', inputs, matrix, precision=lax.Precision.HIGHEST)

def einsum_high(pattern, operand_one, operand_two):
    return jnp.einsum(pattern, operand_one, operand_two, precision=lax.Precision.HIGHEST)

def softmax_rows(scores):
    return jax.nn.softmax(scores, axis=-1)

def encoder_layer(source, src_valid, weights):
    in_proj, out_proj, ffn_in, ffn_out, gains, biases = weights
    query_bias, value_bias, out_bias, hidden_bias, ffn_bias, norm_one, norm_two = slices_of(biases, (D, D, D, FF, D, D, D))
    gain_one, gain_two = slices_of(gains, (D, D))
    score_scale = 1.0 / math.sqrt(HEAD)
    qkv_bias = jnp.concatenate([query_bias, jnp.zeros((D,), jnp.float32), value_bias])
    projected = low(low_back(matmul_high(source, in_proj) + qkv_bias)).reshape(LEN, 3, HEADS, HEAD)
    scores = low_back(einsum_high('ihe,jhe->hij', projected[:, 0], projected[:, 1]) * score_scale)
    probabilities = low(softmax_rows(jnp.where(src_valid, scores, masked_score)))
    attended = low(low_back(einsum_high('hij,jhe->ihe', probabilities, projected[:, 2]).reshape(LEN, D)))
    branch = low_back(matmul_high(attended, out_proj) + out_bias)
    first_norm = layer_norm(source + branch, gain_one, norm_one)
    hidden = low_back(matmul_high(low(first_norm), ffn_in) + hidden_bias)
    ffn_branch = low_back(matmul_high(low(jax.nn.gelu(hidden, approximate=False)), ffn_out) + ffn_bias)
    return layer_norm(first_norm + ffn_branch, gain_two, norm_two)

def stream_bias(relative, onehot):
    return einsum_high('ihk,ijk->hij', relative, onehot)

def decoder_layer(streams, memory, tgt_count, src_valid, weights, onehot):
    in_proj, rel_proj, out_proj, cross_query, cross_kv, cross_out, ffn_in, ffn_out, gains, biases = weights
    vectors = slices_of(biases, (D, D, HEADS * BUCKETS, D, D, D, D, FF, D, D, D, D))
    gain_set = slices_of(gains, (D, D, D))
    score_scale = 1.0 / math.sqrt(HEAD)
    streams_all = NGRAM + 1
    positions = jnp.arange(LEN, dtype=jnp.int32)
    inside = positions[None, :] < tgt_count
    main_valid = ((positions[None, :] <= positions[:, None]) & inside)[None]
    pred_valid = ((positions[None, :] < positions[:, None]) & inside)[None]
    own_valid = (positions >= 0)[None, :, None]
    qkv_bias = jnp.concatenate([vectors[0], jnp.zeros((D,), jnp.float32), vectors[1]])
    projected = low(low_back(matmul_high(streams, in_proj) + qkv_bias)).reshape(LEN, streams_all, 3, HEADS, HEAD)
    relative = low_back(matmul_high(streams, rel_proj) + vectors[2]).reshape(LEN, streams_all, HEADS, BUCKETS)
    key_main = projected[:, 0, 1]
    value_main = projected[:, 0, 2]
    scores = low_back(einsum_high('ihe,jhe->hij', projected[:, 0, 0], key_main) * score_scale + stream_bias(relative[:, 0], onehot))
    probabilities = low(softmax_rows(jnp.where(main_valid, scores, masked_score)))
    outputs = [einsum_high('hij,jhe->ihe', probabilities, value_main)]
    for stream in range(1, streams_all):
        queries = projected[:, stream, 0]
        main_part = einsum_high('ihe,jhe->hij', queries, key_main) * score_scale + stream_bias(relative[:, stream], onehot)
        own_part = einsum_high('ihe,ihe->hi', queries, projected[:, stream, 1]) * score_scale + jnp.transpose(relative[:, stream, :, 0])
        scores = low_back(jnp.concatenate([main_part, own_part[:, :, None]], axis=-1))
        allowed = jnp.concatenate([pred_valid, own_valid], axis=-1)
        probabilities = low(softmax_rows(jnp.where(allowed, scores, masked_score)))
        outputs.append(einsum_high('hij,jhe->ihe', probabilities[:, :, :LEN], value_main) + jnp.transpose(probabilities[:, :, LEN])[:, :, None] * projected[:, stream, 2])
    attended = low(low_back(jnp.stack(outputs, axis=1).reshape(LEN, streams_all, D)))
    branch = low_back(matmul_high(attended, out_proj) + vectors[3])
    first_norm = layer_norm(streams + branch, gain_set[0], vectors[9])
    cross_queries = low(low_back(matmul_high(low(first_norm), cross_query) + vectors[4])).reshape(LEN * streams_all, HEADS, HEAD)
    memory_pairs = low(low_back(matmul_high(memory, cross_kv) + jnp.concatenate([jnp.zeros((D,), jnp.float32), vectors[5]]))).reshape(LEN, 2, HEADS, HEAD)
    cross_scores = low_back(einsum_high('rhe,jhe->hrj', cross_queries, memory_pairs[:, 0]) * score_scale)
    cross_probabilities = low(softmax_rows(jnp.where(src_valid, cross_scores, masked_score)))
    cross_attended = low(low_back(einsum_high('hrj,jhe->rhe', cross_probabilities, memory_pairs[:, 1]).reshape(LEN, streams_all, D)))
    cross_branch = low_back(matmul_high(cross_attended, cross_out) + vectors[6])
    second_norm = layer_norm(first_norm + cross_branch, gain_set[1], vectors[10])
    hidden = low_back(matmul_high(low(second_norm), ffn_in) + vectors[7])
    ffn_branch = low_back(matmul_high(low(jax.nn.gelu(hidden, approximate=False)), ffn_out) + vectors[8])
    return layer_norm(second_norm + ffn_branch, gain_set[2], vectors[11])

def reference(source, dec_in, src_lengths, tgt_lengths, enc_in_proj, enc_out_proj, enc_ffn_in, enc_ffn_out, enc_gains, enc_biases, dec_in_proj, dec_rel_proj, dec_out_proj, cross_query, cross_kv, cross_out, dec_ffn_in, dec_ffn_out, dec_gains, dec_biases, enc_cot, dec_cot):
    enc_weights = tuple((matrix.astype(jnp.float32) for matrix in (enc_in_proj, enc_out_proj, enc_ffn_in, enc_ffn_out, enc_gains, enc_biases)))
    dec_weights = tuple((matrix.astype(jnp.float32) for matrix in (dec_in_proj, dec_rel_proj, dec_out_proj, cross_query, cross_kv, cross_out, dec_ffn_in, dec_ffn_out, dec_gains, dec_biases)))
    onehot = bucket_table(LEN, BUCKETS)
    group_size = 8
    group_count = DEVICES // group_size
    streams_all = NGRAM + 1

    def forward_one(one_source, one_streams, src_count, tgt_count, enc_params, dec_params):
        positions = jnp.arange(LEN, dtype=jnp.int32)
        src_valid = (positions < src_count)[None, None, :]
        encoded = encoder_layer(one_source, src_valid, enc_params)
        decoded = decoder_layer(one_streams, low(encoded), tgt_count, src_valid, dec_params, onehot)
        return (encoded, decoded)

    def one_group(totals, group_block):
        group_source, group_streams, group_src, group_tgt, group_enc_cot, group_dec_cot = group_block

        def run_group(sources, streams, enc_params, dec_params):
            return jax.vmap(forward_one, in_axes=(0, 0, 0, 0, None, None))(sources, streams, group_src, group_tgt, enc_params, dec_params)
        outputs, pullback = jax.vjp(run_group, group_source, group_streams, enc_weights, dec_weights)
        gradients = pullback((group_enc_cot, group_dec_cot))
        totals = jax.tree.map(jnp.add, totals, (gradients[2], gradients[3]))
        return (totals, (outputs[0], outputs[1], gradients[0], gradients[1]))
    initial = jax.tree.map(jnp.zeros_like, (enc_weights, dec_weights))
    inputs = (source.astype(jnp.float32).reshape(group_count, group_size, LEN, D), dec_in.astype(jnp.float32).reshape(group_count, group_size, LEN, streams_all, D), src_lengths.reshape(group_count, group_size), tgt_lengths.reshape(group_count, group_size), enc_cot.astype(jnp.float32).reshape(group_count, group_size, LEN, D), dec_cot.astype(jnp.float32).reshape(group_count, group_size, LEN, streams_all, D))
    totals, stacked = lax.scan(one_group, initial, inputs)
    enc_grads, dec_grads = totals
    enc_out = stacked[0].reshape(TOKENS, D).astype(jnp.bfloat16)
    dec_out = stacked[1].reshape(TOKENS, streams_all, D).astype(jnp.bfloat16)
    source_grad = stacked[2].reshape(TOKENS, D)
    dec_in_grad = stacked[3].reshape(TOKENS, streams_all, D)
    return (enc_out, dec_out, source_grad, dec_in_grad, enc_grads[0], enc_grads[1], enc_grads[2], enc_grads[3], enc_grads[4], enc_grads[5], dec_grads[0], dec_grads[1], dec_grads[2], dec_grads[3], dec_grads[4], dec_grads[5], dec_grads[6], dec_grads[7], dec_grads[8], dec_grads[9])
```

```python
import math

import jax
import jax.numpy as jnp
from jax import lax
from jax.sharding import PartitionSpec as P

D = 1024
HEADS = 16
HEAD = 64
FF = 4096
NGRAM = 2
STREAMS = NGRAM + 1
BUCKETS = 32
LEN = 128
HALF = D // 2
OWN_HEADS = HEADS // 2
REL_HALF = OWN_HEADS * BUCKETS
HIDDEN_HALF = FF // 2
WIDE = 512
EPSILON = 1e-05
MASKED = -1000000000.0
SCALE = 1.0 / math.sqrt(HEAD)
BF = jnp.bfloat16
F32 = jnp.float32
ENC_WIDTHS = (D, D, D, FF, D, D, D)
DEC_WIDTHS = (D, D, HEADS * BUCKETS, D, D, D, D, FF, D, D, D, D)


def bucket_value(distance, bucket_count):
    exact_count = bucket_count // 2
    if distance < exact_count:
        return distance
    return min(
        bucket_count - 1,
        exact_count
        + int(
            math.log(distance / exact_count)
            / math.log(128 / exact_count)
            * (bucket_count - exact_count)
        ),
    )


def bucket_table(length, bucket_count):
    positions = jnp.arange(length, dtype=jnp.int32)
    distance = positions[:, None] - positions[None, :]
    bucket = jnp.zeros((length, length), jnp.int32)
    for target in range(1, bucket_count):
        distance_at = 1
        while bucket_value(distance_at, bucket_count) < target:
            distance_at += 1
        bucket = bucket + (distance >= distance_at).astype(jnp.int32)
    return (bucket[:, :, None] == jnp.arange(bucket_count, dtype=jnp.int32)).astype(F32)


def slices_of(vector, widths):
    starts = 0
    result = []
    for amount in widths:
        result.append(vector[starts : starts + amount])
        starts += amount
    return result


def dot(a, b):
    return lax.dot_general(a, b, (((1,), (0,)), ((), ())), preferred_element_type=F32)


def dot_t(a, b):
    return lax.dot_general(a, b, (((1,), (1,)), ((), ())), preferred_element_type=F32)


def dot_g(a, b):
    return lax.dot_general(a, b, (((0,), (0,)), ((), ())), preferred_element_type=F32)


def norm_stats(values):
    average = jnp.mean(values, axis=-1, keepdims=True)
    centered = values - average
    variance = jnp.mean(centered * centered, axis=-1, keepdims=True)
    inverse = lax.rsqrt(variance + EPSILON)
    return centered * inverse, inverse


def norm(values, gain, shift):
    unit, inverse = norm_stats(values)
    return unit * gain + shift


def norm_back(values, gain, grads):
    unit, inverse = norm_stats(values)
    scaled = grads * gain
    mean_one = jnp.mean(scaled, axis=-1, keepdims=True)
    mean_two = jnp.mean(scaled * unit, axis=-1, keepdims=True)
    return (
        inverse * (scaled - mean_one - unit * mean_two),
        jnp.sum(grads * unit, axis=0),
        jnp.sum(grads, axis=0),
    )


def gelu_exact(inputs):
    return jax.nn.gelu(inputs, approximate=False)


def gelu_back(inputs, gradients):
    outputs, pullback = jax.vjp(gelu_exact, inputs)
    return pullback(gradients)[0]


def col_sum(values):
    return jnp.sum(values.astype(F32), axis=0)


class Layout:
    def __init__(self, ndp, nf):
        self.ndp = ndp
        self.nf = nf
        self.nz = nf // 2
        self.chips = ndp * self.nz
        self.devices = ndp * nf
        self.r = D // self.devices
        self.f = FF // self.devices

    def place(self):
        self.dp = lax.axis_index("dp")
        fs = lax.axis_index("fsdp")
        self.z = fs // 2
        self.core = fs % 2

    def swap(self, value):
        return lax.ppermute(value, "fsdp", [(i, i ^ 1) for i in range(self.nf)])

    def shift_z(self, value, step):
        return lax.ppermute(
            value, "fsdp", [(i, (i + 2 * step) % self.nf) for i in range(self.nf)]
        )

    def flip_dp(self, value, mask):
        return lax.ppermute(value, "dp", [(i, i ^ mask) for i in range(self.ndp)])

    def shift_dp(self, value, step):
        return lax.ppermute(value, "dp", [(i, (i + step) % self.ndp) for i in range(self.ndp)])

    def pick(self, first, second):
        return jnp.where(self.core == 0, first, second)

    def pair(self, own, other, axis):
        return self.pick(
            jnp.concatenate([own, other], axis=axis), jnp.concatenate([other, own], axis=axis)
        )


def tie(value, *others):
    return lax.optimization_barrier((value,) + others)[0]


def gather_z(lay, buf):
    out = jnp.zeros((lay.nz,) + buf.shape, buf.dtype)
    out = lax.dynamic_update_slice(out, buf[None], (lay.z, 0, 0))
    for step in range(1, lay.nz):
        got = lay.shift_z(buf, step)
        out = lax.dynamic_update_slice(out, got[None], ((lay.z - step) % lay.nz, 0, 0))
    return out


def gather_dp_first(lay, buf):
    if lay.ndp == 4:
        return [lay.flip_dp(buf, 1), lay.flip_dp(buf, 2)]
    return [lay.shift_dp(buf, step) for step in range(1, lay.ndp)]


def gather_dp_rest(lay, buf, first):
    half = lay.nz // 2
    out = jnp.zeros((lay.ndp,) + buf.shape, buf.dtype)
    if lay.ndp == 4:
        low = lay.flip_dp(first[0][:half], 2)
        high = lay.flip_dp(first[1][half:], 1)
        parts = [(0, 0, buf), (1, 0, first[0]), (2, 0, first[1]), (3, 0, low), (3, half, high)]
        for flip, at, part in parts:
            out = lax.dynamic_update_slice(out, part[None], (lay.dp ^ flip, at, 0, 0))
        return out
    out = lax.dynamic_update_slice(out, buf[None], (lay.dp, 0, 0, 0))
    for step in range(1, lay.ndp):
        out = lax.dynamic_update_slice(
            out, first[step - 1][None], ((lay.dp - step) % lay.ndp, 0, 0, 0)
        )
    return out


def gather_all(lay, bufs):
    staged = []
    results = []
    firsts = []
    for i, buf in enumerate(bufs):
        if i >= 2:
            buf = tie(buf, *firsts[i - 2])
        z = gather_z(lay, buf)
        staged.append(z)
        firsts.append(gather_dp_first(lay, z))
    for z, first in zip(staged, firsts):
        results.append(gather_dp_rest(lay, z, first))
    return results


def take(buf, index, axis=0):
    return lax.dynamic_index_in_dim(buf, index, axis, keepdims=False)


def add_low(*values):
    return sum(v.astype(F32) for v in values).astype(BF)


def scatter_dp(lay, buf):
    if lay.ndp == 4:
        half = lay.nz // 2
        far = take(buf, lay.dp ^ 3)
        to_x = take(buf, lay.dp ^ 1)
        to_y = take(buf, lay.dp ^ 2)
        own = take(buf, lay.dp)
        low = lay.flip_dp(far[:half], 2)
        high = lay.flip_dp(far[half:], 1)
        to_x = jnp.concatenate([add_low(to_x[:half], low), to_x[half:]], axis=0)
        to_y = jnp.concatenate([to_y[:half], add_low(to_y[half:], high)], axis=0)
        return add_low(own, lay.flip_dp(to_x, 1), lay.flip_dp(to_y, 2))
    parts = [take(buf, lay.dp)]
    for step in range(1, lay.ndp):
        parts.append(lay.shift_dp(take(buf, (lay.dp + step) % lay.ndp), step))
    return add_low(*parts)


def scatter_z(lay, buf):
    total = take(buf, lay.z).astype(F32)
    for step in range(1, lay.nz):
        total = total + lay.shift_z(take(buf, (lay.z + step) % lay.nz), step).astype(F32)
    return total


def attention_forward(queries, keys, values, allowed):
    scores = jnp.einsum("snihe,sjhe->snhij", queries, keys, preferred_element_type=F32) * SCALE
    probs = jax.nn.softmax(jnp.where(allowed, scores, MASKED), axis=-1)
    out = jnp.einsum("snhij,sjhe->snihe", probs.astype(BF), values, preferred_element_type=F32)
    return out.astype(BF), probs


def attention_back(queries, keys, values, probs, grad_out):
    grad_probs = jnp.einsum("snihe,sjhe->snhij", grad_out, values, preferred_element_type=F32)
    grad_values = jnp.einsum(
        "snhij,snihe->sjhe", probs.astype(BF), grad_out, preferred_element_type=F32
    )
    grad_scores = (
        probs * (grad_probs - jnp.sum(probs * grad_probs, axis=-1, keepdims=True))
    ).astype(BF)
    grad_queries = (
        jnp.einsum("snhij,sjhe->snihe", grad_scores, keys, preferred_element_type=F32) * SCALE
    )
    grad_keys = (
        jnp.einsum("snhij,snihe->sjhe", grad_scores, queries, preferred_element_type=F32) * SCALE
    )
    return grad_queries.astype(BF), grad_keys.astype(BF), grad_values.astype(BF)


def ngram_forward(dqkv, rel, tgt, onehot):
    q, k, v = dqkv[:, :, :, 0], dqkv[:, :, :, 1], dqkv[:, :, :, 2]
    positions = jnp.arange(LEN, dtype=jnp.int32)
    inside = positions[None, :] < tgt[:, None]
    main_valid = (positions[None, :] <= positions[:, None])[None] & inside[:, None]
    pred_valid = (positions[None, :] < positions[:, None])[None] & inside[:, None]
    valid = jnp.stack([main_valid] + [pred_valid] * NGRAM, axis=1)[:, :, None]
    main = jnp.einsum("snihe,sjhe->snhij", q, k[:, 0], preferred_element_type=F32) * SCALE
    main = main + jnp.einsum("snihk,ijk->snhij", rel, onehot, precision=lax.Precision.HIGHEST)
    main = jnp.where(valid, main, MASKED)
    own = jnp.einsum("snihe,snihe->snhi", q, k, preferred_element_type=F32) * SCALE
    own = own + jnp.transpose(rel[..., 0], (0, 1, 3, 2))
    stream = jnp.arange(STREAMS)[None, :, None, None]
    own = jnp.where(stream == 0, -jnp.inf, own)
    top = jnp.maximum(jnp.max(main, axis=-1), own)
    main = jnp.exp(main - top[..., None])
    own = jnp.exp(own - top)
    total = jnp.sum(main, axis=-1) + own
    main = main / total[..., None]
    own = own / total
    out = jnp.einsum("snhij,sjhe->snihe", main.astype(BF), v[:, 0], preferred_element_type=F32)
    own_low = jnp.transpose(own.astype(BF), (0, 1, 3, 2)).astype(F32)[..., None]
    out = out + own_low * v.astype(F32)
    return out.astype(BF), main, own


def ngram_back(dqkv, main, own, onehot, grad_out):
    q, k, v = dqkv[:, :, :, 0], dqkv[:, :, :, 1], dqkv[:, :, :, 2]
    grad_main = jnp.einsum("snihe,sjhe->snhij", grad_out, v[:, 0], preferred_element_type=F32)
    grad_own = jnp.einsum("snihe,snihe->snhi", grad_out, v, preferred_element_type=F32)
    inner = jnp.sum(main * grad_main, axis=-1) + own * grad_own
    ds = (main * (grad_main - inner[..., None])).astype(BF)
    ds_own = (own * (grad_own - inner)).astype(BF)
    own_rows = jnp.transpose(ds_own, (0, 1, 3, 2)).astype(F32)[..., None]
    p_rows = jnp.transpose(own.astype(BF), (0, 1, 3, 2)).astype(F32)[..., None]
    gq = (
        jnp.einsum("snhij,sjhe->snihe", ds, k[:, 0], preferred_element_type=F32)
        + own_rows * k.astype(F32)
    ) * SCALE
    gk0 = jnp.einsum("snhij,snihe->sjhe", ds, q, preferred_element_type=F32) * SCALE
    gv0 = jnp.einsum("snhij,snihe->sjhe", main.astype(BF), grad_out, preferred_element_type=F32)
    gk = own_rows * q.astype(F32) * SCALE
    gv = p_rows * grad_out.astype(F32)
    gk = jnp.concatenate([gk0[:, None], gk[:, 1:]], axis=1)
    gv = jnp.concatenate([gv0[:, None], gv[:, 1:]], axis=1)
    gqkv = jnp.stack([gq, gk, gv], axis=3).astype(BF)
    grel = jnp.einsum("snhij,ijk->snihk", ds, onehot.astype(BF), preferred_element_type=F32)
    first = (jnp.arange(BUCKETS) == 0).astype(F32)
    grel = (grel + own_rows * first).astype(BF)
    return gqkv, grel


def shards(
    ndp,
    nf,
    source,
    dec_in,
    src_lengths,
    tgt_lengths,
    enc_in_proj,
    enc_out_proj,
    enc_ffn_in,
    enc_ffn_out,
    enc_gains,
    enc_biases,
    dec_in_proj,
    dec_rel_proj,
    dec_out_proj,
    cross_query,
    cross_kv,
    cross_out,
    dec_ffn_in,
    dec_ffn_out,
    dec_gains,
    dec_biases,
    enc_cot,
    dec_cot,
):
    lay = Layout(ndp, nf)
    lay.place()
    r, f, chips = lay.r, lay.f, lay.chips
    swap, pick, pair = lay.swap, lay.pick, lay.pair
    core = lay.core

    def halves(matrix, groups, width):
        parts = matrix.reshape(r, groups, 2, width)
        return (
            pick(parts[:, :, 0], parts[:, :, 1]).reshape(r, groups * width),
            pick(parts[:, :, 1], parts[:, :, 0]).reshape(r, groups * width),
        )

    split = [
        halves(enc_in_proj, 3, HALF),
        halves(enc_ffn_in, chips, f),
        halves(dec_in_proj, 3, HALF),
        halves(cross_query, 1, HALF),
        halves(cross_kv, 2, HALF),
        halves(dec_ffn_in, chips, f),
        halves(dec_rel_proj, 1, REL_HALF),
    ]
    vec = jnp.concatenate(
        [
            enc_biases,
            enc_gains,
            dec_biases,
            dec_gains,
            src_lengths.astype(BF),
            tgt_lengths.astype(BF),
        ]
    )
    nvec = vec.shape[0]
    padded = -(-nvec // WIDE) * WIDE
    vec = jnp.pad(vec, (0, padded - nvec))
    mine = jnp.concatenate([own for own, other in split], axis=1)
    theirs = jnp.concatenate([other for own, other in split], axis=1)
    theirs_got = swap(theirs)
    vec_got = swap(vec)
    source_got = swap(source)
    dec_in_got = swap(dec_in.reshape(LEN * STREAMS, D))

    def owner_rows(start, width):
        return pair(mine[:, start : start + width], theirs_got[:, start : start + width], 0)

    def column_blocks(start, count):
        return [owner_rows(start + WIDE * i, WIDE) for i in range(count)]

    def row_blocks(matrix):
        return [matrix[:, :WIDE], matrix[:, WIDE:]]

    rel_start = mine.shape[1] - REL_HALF
    rel_own = mine[:, rel_start:]
    rel_other = theirs_got[:, rel_start:]
    vec_pair = pair(vec[None], vec_got[None], 0).reshape(-1, WIDE)
    vec_rows = -(-vec_pair.shape[0] // 16) * 16
    vec_used = vec_pair.shape[0]
    vec_pair = jnp.pad(vec_pair, ((0, vec_rows - vec_used), (0, 0)))
    wide_at = [0, 3 * WIDE, 7 * WIDE, 10 * WIDE, 11 * WIDE, 13 * WIDE]
    chunk_parts = [
        column_blocks(wide_at[0], 3) + row_blocks(enc_out_proj) + [vec_pair],
        column_blocks(wide_at[1], 4) + row_blocks(enc_ffn_out),
        column_blocks(wide_at[2], 3) + [pair(rel_own, rel_other, 1)] + row_blocks(dec_out_proj),
        column_blocks(wide_at[3], 1) + column_blocks(wide_at[4], 2) + row_blocks(cross_out),
        column_blocks(wide_at[5], 4) + row_blocks(dec_ffn_out),
    ]
    bufs = [jnp.concatenate(parts, axis=0) for parts in chunk_parts]
    full = gather_all(lay, bufs)

    def cut(index, block):
        parts = chunk_parts[index]
        at = sum(p.shape[0] for p in parts[:block])
        rows = parts[block].shape[0]
        return full[index][:, :, at : at + rows].reshape(chips * rows, WIDE)

    def columns(index, first, count):
        return jnp.concatenate([cut(index, first + i) for i in range(count)], axis=1)

    def head_rows(index, first):
        rows = columns(index, first, 2)
        low, high = rows[:HALF // 2], rows[HALF // 2 :]
        keep = pick(low, high).reshape(chips // 2, 1, r, D)
        got = swap(pick(high, low)).reshape(chips // 2, 1, r, D)
        return pair(keep, got, 1).reshape(HALF, D)

    w_enc_in = columns(0, 0, 3)
    w_enc_out = head_rows(0, 3)
    w_enc_up = columns(1, 0, 4)
    w_enc_down = columns(1, 4, 2)
    w_dec_in = columns(2, 0, 3)
    w_rel = (
        cut(2, 3)
        .reshape(chips, r, 2, REL_HALF)
        .transpose(0, 2, 1, 3)
        .reshape(D, REL_HALF)
    )
    w_dec_out = head_rows(2, 4)
    w_cross_q = columns(3, 0, 1)
    w_cross_kv = columns(3, 1, 2)
    w_cross_out = head_rows(3, 3)
    w_dec_up = columns(4, 0, 4)
    w_dec_down = columns(4, 4, 2)

    vec_all = (
        cut(0, 5).reshape(chips, vec_rows, WIDE)[:, :vec_used].reshape(lay.devices, padded).astype(F32)
    )
    widths = [enc_biases.shape[0], enc_gains.shape[0], dec_biases.shape[0], dec_gains.shape[0]]
    starts = [0]
    for width in widths:
        starts.append(starts[-1] + width)
    v_enc_b, v_enc_g, v_dec_b, v_dec_g = [
        vec_all[:, starts[i] : starts[i + 1]].reshape(-1) for i in range(4)
    ]
    ebias = slices_of(v_enc_b, ENC_WIDTHS)
    egain = slices_of(v_enc_g, (D, D))
    dbias = slices_of(v_dec_b, DEC_WIDTHS)
    dgain = slices_of(v_dec_g, (D, D, D))

    def half_of(vector):
        parts = vector.reshape(2, -1)
        return pick(parts[0], parts[1])

    def hidden_of(vector):
        parts = vector.reshape(chips, 2, f)
        return pick(parts[:, 0], parts[:, 1]).reshape(-1)

    zero_half = jnp.zeros((HALF,), F32)
    lens = jnp.stack([pair(vec[None], vec_got[None], 0)[:, nvec - 2 + i] for i in range(2)])
    lens = lens.astype(F32).astype(jnp.int32)
    src_len, tgt_len = lens[0], lens[1]
    positions = jnp.arange(LEN, dtype=jnp.int32)
    src_valid = (positions[None, :] < src_len[:, None])[:, None, None, None, :]
    onehot = bucket_table(LEN, BUCKETS)

    def both(partial):
        low = partial.astype(BF)
        return low.astype(F32) + swap(low).astype(F32)

    x = pair(source[None], source_got[None], 0).reshape(2 * LEN, D)
    qkv_bias = jnp.concatenate([half_of(ebias[0]), zero_half, half_of(ebias[1])])
    eqkv = (dot(x, w_enc_in) + qkv_bias).astype(BF).reshape(2, LEN, 3, OWN_HEADS, HEAD)
    eq, ek, ev = eqkv[:, None, :, 0], eqkv[:, :, 1], eqkv[:, :, 2]
    ea, eprobs = attention_forward(eq, ek, ev, src_valid)
    ea = ea.reshape(2 * LEN, HALF)
    ez1 = x.astype(F32) + both(dot(ea, w_enc_out)) + ebias[2]
    eh1 = norm(ez1, egain[0], ebias[5])
    eh1_low = eh1.astype(BF)
    eu = dot(eh1_low, w_enc_up) + hidden_of(ebias[3])
    eg = gelu_exact(eu).astype(BF)
    ez2 = eh1 + both(dot(eg, w_enc_down)) + ebias[4]
    enc = norm(ez2, egain[1], ebias[6])
    enc_low = enc.astype(BF)

    rows = 2 * STREAMS * LEN
    y = pair(
        dec_in.transpose(1, 0, 2)[None], dec_in_got.reshape(LEN, STREAMS, D).transpose(1, 0, 2)[None], 0
    ).reshape(rows, D)
    dqkv_bias = jnp.concatenate([half_of(dbias[0]), zero_half, half_of(dbias[1])])
    dqkv = (dot(y, w_dec_in) + dqkv_bias).astype(BF)
    dqkv = dqkv.reshape(2, STREAMS, LEN, 3, OWN_HEADS, HEAD)
    rel = (dot(y, w_rel) + half_of(dbias[2])).reshape(2, STREAMS, LEN, OWN_HEADS, BUCKETS)
    da, dmain, down = ngram_forward(dqkv, rel, tgt_len, onehot)
    da = da.reshape(rows, HALF)
    dz1 = y.astype(F32) + both(dot(da, w_dec_out)) + dbias[3]
    dh1 = norm(dz1, dgain[0], dbias[9])
    dh1_low = dh1.astype(BF)
    cq = (dot(dh1_low, w_cross_q) + half_of(dbias[4])).astype(BF)
    cq = cq.reshape(2, STREAMS, LEN, OWN_HEADS, HEAD)
    ckv = dot(enc_low, w_cross_kv) + jnp.concatenate([zero_half, half_of(dbias[5])])
    ckv = ckv.astype(BF).reshape(2, LEN, 2, OWN_HEADS, HEAD)
    ck, cv = ckv[:, :, 0], ckv[:, :, 1]
    ca, cprobs = attention_forward(cq, ck, cv, src_valid)
    ca = ca.reshape(rows, HALF)
    dz2 = dh1 + both(dot(ca, w_cross_out)) + dbias[6]
    dh2 = norm(dz2, dgain[1], dbias[10])
    dh2_low = dh2.astype(BF)
    du = dot(dh2_low, w_dec_up) + hidden_of(dbias[7])
    dg = gelu_exact(du).astype(BF)
    dz3 = dh2 + both(dot(dg, w_dec_down)) + dbias[8]
    dec = norm(dz3, dgain[2], dbias[11])

    def own_rows_of(total, count):
        blocks = total[: count * 2 * r].reshape(count, 2, r, WIDE)
        keep = pick(blocks[:, 0], blocks[:, 1])
        got = swap(pick(blocks[:, 1], blocks[:, 0]))
        return pair(keep[:, None], got[:, None], 1)

    def chip_blocks(grad):
        n = grad.shape[1] // WIDE
        shape = (lay.ndp, lay.nz, grad.shape[0] // chips, WIDE)
        low = grad.astype(BF)
        return [low[:, WIDE * i : WIDE * i + WIDE].reshape(shape) for i in range(n)]

    def head_blocks(grad):
        parts = grad.astype(BF).reshape(chips // 2, 2, r, D)
        keep = pick(parts[:, 0], parts[:, 1])
        got = swap(pick(parts[:, 1], parts[:, 0]))
        return chip_blocks(pair(keep, got, 0).reshape(chips * r, D))

    def scatter(parts, previous):
        buf = jnp.concatenate(parts, axis=2)
        if previous is not None:
            buf = tie(buf, previous)
        first = scatter_dp(lay, buf)
        return scatter_z(lay, first), first

    def split_rows(total, sizes):
        at = 0
        result = []
        for size in sizes:
            result.append(total[at : at + size])
            at += size
        return result

    dcot_got = swap(dec_cot.reshape(LEN * STREAMS, D)).reshape(LEN, STREAMS, D)
    dcot = pair(dec_cot.transpose(1, 0, 2)[None], dcot_got.transpose(1, 0, 2)[None], 0)
    dcot = dcot.reshape(rows, D).astype(F32)
    gz3, ggain3, gnorm3 = norm_back(dz3, dgain[2], dcot)
    gf = gz3.astype(BF)
    g_down = dot_g(dg, gf)
    gu = gelu_back(du, dot_t(gf, w_dec_down)).astype(BF)
    g_up = dot_g(dh2_low, gu)
    total4, first4 = scatter(chip_blocks(g_up) + chip_blocks(g_down), None)
    gz2, ggain2, gnorm2 = norm_back(dz2, dgain[1], gz3 + both(dot_t(gu, w_dec_up)))
    gx = gz2.astype(BF)
    g_cross_out = dot_g(ca, gx)
    gca = dot_t(gx, w_cross_out).astype(BF).reshape(2, STREAMS, LEN, OWN_HEADS, HEAD)
    gcq, gck, gcv = attention_back(cq, ck, cv, cprobs, gca)
    gcq = gcq.reshape(rows, HALF)
    gckv = jnp.stack([gck, gcv], axis=2).reshape(2 * LEN, D)
    g_cross_q = dot_g(dh1_low, gcq)
    g_cross_kv = dot_g(enc_low, gckv)
    total3, first3 = scatter(
        chip_blocks(g_cross_q) + chip_blocks(g_cross_kv) + head_blocks(g_cross_out), first4
    )
    ecot_got = swap(enc_cot)
    ecot = pair(enc_cot[None], ecot_got[None], 0).reshape(2 * LEN, D).astype(F32)
    genc = ecot + both(dot_t(gckv, w_cross_kv))
    gz1, ggain1, gnorm1 = norm_back(dz1, dgain[0], gz2 + both(dot_t(gcq, w_cross_q)))
    go = gz1.astype(BF)
    g_dec_out = dot_g(da, go)
    gda = dot_t(go, w_dec_out).astype(BF).reshape(2, STREAMS, LEN, OWN_HEADS, HEAD)
    gqkv, grel = ngram_back(dqkv, dmain, down, onehot, gda)
    gqkv = gqkv.reshape(rows, 3 * HALF)
    grel = grel.reshape(rows, REL_HALF)
    g_dec_in = dot_g(y, gqkv)
    g_rel = dot_g(y, grel)
    rel_block = (
        g_rel.astype(BF)
        .reshape(chips, 2, r, REL_HALF)
        .transpose(0, 2, 1, 3)
        .reshape(lay.ndp, lay.nz, r, WIDE)
    )
    total2, first2 = scatter(chip_blocks(g_dec_in) + [rel_block] + head_blocks(g_dec_out), first3)

    def own_sequence(partial, count):
        parts = partial.reshape(2, count, D)
        keep = pick(parts[0], parts[1])
        return keep + swap(pick(parts[1], parts[0]).astype(BF)).astype(F32)

    def own_part(values, count):
        parts = values.reshape(2, count, D)
        return pick(parts[0], parts[1])

    dec_rows = STREAMS * LEN
    g_dec_input = own_part(gz1, dec_rows) + own_sequence(
        dot_t(gqkv, w_dec_in) + dot_t(grel, w_rel), dec_rows
    )

    def widen(vector):
        zeros = jnp.zeros_like(vector)
        return pick(jnp.concatenate([vector, zeros]), jnp.concatenate([zeros, vector]))

    def widen_hidden(vector):
        parts = vector.reshape(chips, 1, f)
        zeros = jnp.zeros_like(parts)
        return pick(
            jnp.concatenate([parts, zeros], axis=1), jnp.concatenate([zeros, parts], axis=1)
        ).reshape(-1)

    column_sums = col_sum(gqkv)
    dec_vec = jnp.concatenate(
        [
            widen(column_sums[:HALF]),
            widen(column_sums[2 * HALF :]),
            widen(col_sum(grel)),
            0.5 * col_sum(go),
            widen(col_sum(gcq)),
            widen(col_sum(gckv)[HALF:]),
            0.5 * col_sum(gx),
            widen_hidden(col_sum(gu)),
            0.5 * col_sum(gf),
            0.5 * gnorm1,
            0.5 * gnorm2,
            0.5 * gnorm3,
            0.5 * ggain1,
            0.5 * ggain2,
            0.5 * ggain3,
        ]
    )

    gz2e, eggain2, egnorm2 = norm_back(ez2, egain[1], genc)
    gfe = gz2e.astype(BF)
    ge_down = dot_g(eg, gfe)
    gue = gelu_back(eu, dot_t(gfe, w_enc_down)).astype(BF)
    ge_up = dot_g(eh1_low, gue)
    total1, first1 = scatter(chip_blocks(ge_up) + chip_blocks(ge_down), first2)
    gz1e, eggain1, egnorm1 = norm_back(ez1, egain[0], gz2e + both(dot_t(gue, w_enc_up)))
    goe = gz1e.astype(BF)
    ge_out = dot_g(ea, goe)
    gae = dot_t(goe, w_enc_out).astype(BF).reshape(2, 1, LEN, OWN_HEADS, HEAD)
    geq, gek, gev = attention_back(eq, ek, ev, eprobs, gae)
    geqkv = jnp.stack([geq[:, 0], gek, gev], axis=2).reshape(2 * LEN, 3 * HALF)
    ge_in = dot_g(x, geqkv)
    total0, first0 = scatter(chip_blocks(ge_in) + head_blocks(ge_out), first1)
    g_source = own_part(gz1e, LEN) + own_sequence(dot_t(geqkv, w_enc_in), LEN)
    ecolumn_sums = col_sum(geqkv)
    enc_vec = jnp.concatenate(
        [
            widen(ecolumn_sums[:HALF]),
            widen(ecolumn_sums[2 * HALF :]),
            0.5 * col_sum(goe),
            widen_hidden(col_sum(gue)),
            0.5 * col_sum(gfe),
            0.5 * egnorm1,
            0.5 * egnorm2,
            0.5 * eggain1,
            0.5 * eggain2,
        ]
    )
    me = lay.dp * lay.nf + lax.axis_index("fsdp")

    def own_slice(vector):
        return take(vector.reshape(lay.devices, -1), me)

    dec_vec = lax.psum(dec_vec, ("dp", "fsdp"))
    enc_vec = lax.psum(enc_vec, ("dp", "fsdp"))
    nb = sum(ENC_WIDTHS)
    g_enc_biases, g_enc_gains = own_slice(enc_vec[:nb]), own_slice(enc_vec[nb:])
    nb = sum(DEC_WIDTHS)
    g_dec_biases, g_dec_gains = own_slice(dec_vec[:nb]), own_slice(dec_vec[nb:])

    def in_rows(blocks):
        return blocks.transpose(2, 0, 1, 3).reshape(r, -1)

    def up_rows(blocks):
        per = WIDE // f
        return blocks.reshape(4, 2, r, per, f).transpose(2, 0, 3, 1, 4).reshape(r, FF)

    def side(low, high):
        return jnp.concatenate([low, high], axis=1)

    t0 = split_rows(total0, [6 * r, r, r])
    o_enc_in, o_enc_out = in_rows(own_rows_of(t0[0], 3)), side(t0[1], t0[2])
    t1 = split_rows(total1, [8 * r, f, f])
    o_enc_up, o_enc_down = up_rows(own_rows_of(t1[0], 4)), side(t1[1], t1[2])
    t2 = split_rows(total2, [6 * r, r, r, r])
    o_dec_in, o_dec_out = in_rows(own_rows_of(t2[0], 3)), side(t2[2], t2[3])
    relp = t2[1].reshape(r, 2, REL_HALF)
    rel_keep = pick(relp[:, 0], relp[:, 1])
    o_rel = pair(rel_keep, swap(pick(relp[:, 1], relp[:, 0])), 1)
    t3 = split_rows(total3, [2 * r, 4 * r, r, r])
    o_cross_q = in_rows(own_rows_of(t3[0], 1))
    o_cross_kv = in_rows(own_rows_of(t3[1], 2))
    o_cross_out = side(t3[2], t3[3])
    t4 = split_rows(total4, [8 * r, f, f])
    o_dec_up, o_dec_down = up_rows(own_rows_of(t4[0], 4)), side(t4[1], t4[2])

    return (
        own_part(enc_low, LEN),
        own_part(dec.astype(BF), dec_rows).reshape(STREAMS, LEN, D).transpose(1, 0, 2),
        g_source,
        g_dec_input.reshape(STREAMS, LEN, D).transpose(1, 0, 2),
        o_enc_in,
        o_enc_out,
        o_enc_up,
        o_enc_down,
        g_enc_gains,
        g_enc_biases,
        o_dec_in,
        o_rel,
        o_dec_out,
        o_cross_q,
        o_cross_kv,
        o_cross_out,
        o_dec_up,
        o_dec_down,
        g_dec_gains,
        g_dec_biases,
    )


def solution(mesh):
    ndp, nf = mesh.shape["dp"], mesh.shape["fsdp"]
    whole = ("dp", "fsdp")
    one, two, three = P(whole), P(whole, None), P(whole, None, None)
    args = (two, three, one, one) + (two,) * 4 + (one,) * 2 + (two,) * 8 + (one,) * 2 + (two, three)
    outs = (two, three, two, three) + (two,) * 4 + (one,) * 2 + (two,) * 8 + (one,) * 2

    def body(*arrays):
        return shards(ndp, nf, *arrays)

    return jax.shard_map(body, mesh=mesh, in_specs=args, out_specs=outs, check_vma=False)
```

```python
import math

import jax
import jax.numpy as jnp
from jax import lax
from jax.experimental import pallas as pl
from jax.experimental.pallas import tpu as pltpu
from jax.sharding import PartitionSpec as P

D = 1024
HEADS = 16
HEAD = 64
FF = 4096
NGRAM = 2
STREAMS = NGRAM + 1
BUCKETS = 32
LEN = 128
HALF = D // 2
OWN_HEADS = HEADS // 2
REL_HALF = OWN_HEADS * BUCKETS
HIDDEN_HALF = FF // 2
WIDE = 512
EPSILON = 1e-05
MASKED = -1000000000.0
SCALE = 1.0 / math.sqrt(HEAD)
BF = jnp.bfloat16
F32 = jnp.float32
ENC_WIDTHS = (D, D, D, FF, D, D, D)
DEC_WIDTHS = (D, D, HEADS * BUCKETS, D, D, D, D, FF, D, D, D, D)


def bucket_value(distance, bucket_count):
    exact_count = bucket_count // 2
    if distance < exact_count:
        return distance
    return min(
        bucket_count - 1,
        exact_count
        + int(
            math.log(distance / exact_count)
            / math.log(128 / exact_count)
            * (bucket_count - exact_count)
        ),
    )


def bucket_table(length, bucket_count):
    positions = jnp.arange(length, dtype=jnp.int32)
    distance = positions[:, None] - positions[None, :]
    bucket = jnp.zeros((length, length), jnp.int32)
    for target in range(1, bucket_count):
        distance_at = 1
        while bucket_value(distance_at, bucket_count) < target:
            distance_at += 1
        bucket = bucket + (distance >= distance_at).astype(jnp.int32)
    return (bucket[:, :, None] == jnp.arange(bucket_count, dtype=jnp.int32)).astype(F32)


def slices_of(vector, widths):
    starts = 0
    result = []
    for amount in widths:
        result.append(vector[starts : starts + amount])
        starts += amount
    return result


def dot(a, b):
    return lax.dot_general(a, b, (((1,), (0,)), ((), ())), preferred_element_type=F32)


def dot_t(a, b):
    return lax.dot_general(a, b, (((1,), (1,)), ((), ())), preferred_element_type=F32)


def dot_g(a, b):
    return lax.dot_general(a, b, (((0,), (0,)), ((), ())), preferred_element_type=F32)


def norm_stats(values):
    average = jnp.mean(values, axis=-1, keepdims=True)
    centered = values - average
    variance = jnp.mean(centered * centered, axis=-1, keepdims=True)
    inverse = lax.rsqrt(variance + EPSILON)
    return centered * inverse, inverse


def norm(values, gain, shift):
    unit, inverse = norm_stats(values)
    return unit * gain + shift


def norm_back(values, gain, grads):
    unit, inverse = norm_stats(values)
    scaled = grads * gain
    mean_one = jnp.mean(scaled, axis=-1, keepdims=True)
    mean_two = jnp.mean(scaled * unit, axis=-1, keepdims=True)
    return (
        inverse * (scaled - mean_one - unit * mean_two),
        jnp.sum(grads * unit, axis=0),
        jnp.sum(grads, axis=0),
    )


def gelu_exact(inputs):
    return jax.nn.gelu(inputs, approximate=False)


def gelu_back(inputs, gradients):
    outputs, pullback = jax.vjp(gelu_exact, inputs)
    return pullback(gradients)[0]


def col_sum(values):
    return jnp.sum(values.astype(F32), axis=0)


class Layout:
    def __init__(self, ndp, nf):
        self.ndp = ndp
        self.nf = nf
        self.nz = nf // 2
        self.chips = ndp * self.nz
        self.devices = ndp * nf
        self.r = D // self.devices
        self.f = FF // self.devices

    def place(self):
        self.dp = lax.axis_index("dp")
        fs = lax.axis_index("fsdp")
        self.z = fs // 2
        self.core = fs % 2

    def swap(self, value):
        return lax.ppermute(value, "fsdp", [(i, i ^ 1) for i in range(self.nf)])

    def shift_z(self, value, step):
        return lax.ppermute(
            value, "fsdp", [(i, (i + 2 * step) % self.nf) for i in range(self.nf)]
        )

    def flip_dp(self, value, mask):
        return lax.ppermute(value, "dp", [(i, i ^ mask) for i in range(self.ndp)])

    def shift_dp(self, value, step):
        return lax.ppermute(value, "dp", [(i, (i + step) % self.ndp) for i in range(self.ndp)])

    def pick(self, first, second):
        return jnp.where(self.core == 0, first, second)

    def pair(self, own, other, axis):
        return self.pick(
            jnp.concatenate([own, other], axis=axis), jnp.concatenate([other, own], axis=axis)
        )


def tie(value, *others):
    return lax.optimization_barrier((value,) + others)[0]


def gather_z(lay, buf):
    out = jnp.zeros((lay.nz,) + buf.shape, buf.dtype)
    out = lax.dynamic_update_slice(out, buf[None], (lay.z, 0, 0))
    for step in range(1, lay.nz):
        got = lay.shift_z(buf, step)
        out = lax.dynamic_update_slice(out, got[None], ((lay.z - step) % lay.nz, 0, 0))
    return out


def gather_dp_first(lay, buf):
    if lay.ndp == 4:
        return [lay.flip_dp(buf, 1), lay.flip_dp(buf, 2)]
    return [lay.shift_dp(buf, step) for step in range(1, lay.ndp)]


def gather_dp_rest(lay, buf, first):
    half = lay.nz // 2
    out = jnp.zeros((lay.ndp,) + buf.shape, buf.dtype)
    if lay.ndp == 4:
        low = lay.flip_dp(first[0][:half], 2)
        high = lay.flip_dp(first[1][half:], 1)
        parts = [(0, 0, buf), (1, 0, first[0]), (2, 0, first[1]), (3, 0, low), (3, half, high)]
        for flip, at, part in parts:
            out = lax.dynamic_update_slice(out, part[None], (lay.dp ^ flip, at, 0, 0))
        return out
    out = lax.dynamic_update_slice(out, buf[None], (lay.dp, 0, 0, 0))
    for step in range(1, lay.ndp):
        out = lax.dynamic_update_slice(
            out, first[step - 1][None], ((lay.dp - step) % lay.ndp, 0, 0, 0)
        )
    return out


def gather_all(lay, bufs):
    staged = []
    results = []
    firsts = []
    for i, buf in enumerate(bufs):
        if i >= 2:
            buf = tie(buf, *firsts[i - 2])
        z = gather_z(lay, buf)
        staged.append(z)
        firsts.append(gather_dp_first(lay, z))
    for z, first in zip(staged, firsts):
        results.append(gather_dp_rest(lay, z, first))
    return results


def take(buf, index, axis=0):
    return lax.dynamic_index_in_dim(buf, index, axis, keepdims=False)


def add_low(*values):
    return sum(v.astype(F32) for v in values).astype(BF)


def scatter_dp(lay, buf):
    if lay.ndp == 4:
        half = lay.nz // 2
        far = take(buf, lay.dp ^ 3)
        to_x = take(buf, lay.dp ^ 1)
        to_y = take(buf, lay.dp ^ 2)
        own = take(buf, lay.dp)
        low = lay.flip_dp(far[:half], 2)
        high = lay.flip_dp(far[half:], 1)
        to_x = jnp.concatenate([add_low(to_x[:half], low), to_x[half:]], axis=0)
        to_y = jnp.concatenate([to_y[:half], add_low(to_y[half:], high)], axis=0)
        return add_low(own, lay.flip_dp(to_x, 1), lay.flip_dp(to_y, 2))
    parts = [take(buf, lay.dp)]
    for step in range(1, lay.ndp):
        parts.append(lay.shift_dp(take(buf, (lay.dp + step) % lay.ndp), step))
    return add_low(*parts)


def scatter_z(lay, buf):
    total = take(buf, lay.z).astype(F32)
    for step in range(1, lay.nz):
        total = total + lay.shift_z(take(buf, (lay.z + step) % lay.nz), step).astype(F32)
    return total


def attention_forward(queries, keys, values, allowed):
    scores = jnp.einsum("snihe,sjhe->snhij", queries, keys, preferred_element_type=F32) * SCALE
    probs = jax.nn.softmax(jnp.where(allowed, scores, MASKED), axis=-1)
    out = jnp.einsum("snhij,sjhe->snihe", probs.astype(BF), values, preferred_element_type=F32)
    return out.astype(BF), probs


def attention_back(queries, keys, values, probs, grad_out):
    grad_probs = jnp.einsum("snihe,sjhe->snhij", grad_out, values, preferred_element_type=F32)
    grad_values = jnp.einsum(
        "snhij,snihe->sjhe", probs.astype(BF), grad_out, preferred_element_type=F32
    )
    grad_scores = (
        probs * (grad_probs - jnp.sum(probs * grad_probs, axis=-1, keepdims=True))
    ).astype(BF)
    grad_queries = (
        jnp.einsum("snhij,sjhe->snihe", grad_scores, keys, preferred_element_type=F32) * SCALE
    )
    grad_keys = (
        jnp.einsum("snhij,snihe->sjhe", grad_scores, queries, preferred_element_type=F32) * SCALE
    )
    return grad_queries.astype(BF), grad_keys.astype(BF), grad_values.astype(BF)


def ngram_forward(dqkv, rel, tgt, onehot):
    q, k, v = dqkv[:, :, :, 0], dqkv[:, :, :, 1], dqkv[:, :, :, 2]
    positions = jnp.arange(LEN, dtype=jnp.int32)
    inside = positions[None, :] < tgt[:, None]
    main_valid = (positions[None, :] <= positions[:, None])[None] & inside[:, None]
    pred_valid = (positions[None, :] < positions[:, None])[None] & inside[:, None]
    valid = jnp.stack([main_valid] + [pred_valid] * NGRAM, axis=1)[:, :, None]
    main = jnp.einsum("snihe,sjhe->snhij", q, k[:, 0], preferred_element_type=F32) * SCALE
    main = main + jnp.einsum("snihk,ijk->snhij", rel, onehot, precision=lax.Precision.HIGHEST)
    main = jnp.where(valid, main, MASKED)
    own = jnp.einsum("snihe,snihe->snhi", q, k, preferred_element_type=F32) * SCALE
    own = own + jnp.transpose(rel[..., 0], (0, 1, 3, 2))
    stream = jnp.arange(STREAMS)[None, :, None, None]
    own = jnp.where(stream == 0, -jnp.inf, own)
    top = jnp.maximum(jnp.max(main, axis=-1), own)
    main = jnp.exp(main - top[..., None])
    own = jnp.exp(own - top)
    total = jnp.sum(main, axis=-1) + own
    main = main / total[..., None]
    own = own / total
    out = jnp.einsum("snhij,sjhe->snihe", main.astype(BF), v[:, 0], preferred_element_type=F32)
    own_low = jnp.transpose(own.astype(BF), (0, 1, 3, 2)).astype(F32)[..., None]
    out = out + own_low * v.astype(F32)
    return out.astype(BF), main, own


def ngram_back(dqkv, main, own, onehot, grad_out):
    q, k, v = dqkv[:, :, :, 0], dqkv[:, :, :, 1], dqkv[:, :, :, 2]
    grad_main = jnp.einsum("snihe,sjhe->snhij", grad_out, v[:, 0], preferred_element_type=F32)
    grad_own = jnp.einsum("snihe,snihe->snhi", grad_out, v, preferred_element_type=F32)
    inner = jnp.sum(main * grad_main, axis=-1) + own * grad_own
    ds = (main * (grad_main - inner[..., None])).astype(BF)
    ds_own = (own * (grad_own - inner)).astype(BF)
    own_rows = jnp.transpose(ds_own, (0, 1, 3, 2)).astype(F32)[..., None]
    p_rows = jnp.transpose(own.astype(BF), (0, 1, 3, 2)).astype(F32)[..., None]
    gq = (
        jnp.einsum("snhij,sjhe->snihe", ds, k[:, 0], preferred_element_type=F32)
        + own_rows * k.astype(F32)
    ) * SCALE
    gk0 = jnp.einsum("snhij,snihe->sjhe", ds, q, preferred_element_type=F32) * SCALE
    gv0 = jnp.einsum("snhij,snihe->sjhe", main.astype(BF), grad_out, preferred_element_type=F32)
    gk = own_rows * q.astype(F32) * SCALE
    gv = p_rows * grad_out.astype(F32)
    gk = jnp.concatenate([gk0[:, None], gk[:, 1:]], axis=1)
    gv = jnp.concatenate([gv0[:, None], gv[:, 1:]], axis=1)
    gqkv = jnp.stack([gq, gk, gv], axis=3).astype(BF)
    grel = jnp.einsum("snhij,ijk->snihk", ds, onehot.astype(BF), preferred_element_type=F32)
    first = (jnp.arange(BUCKETS) == 0).astype(F32)
    grel = (grel + own_rows * first).astype(BF)
    return gqkv, grel


def shards(
    ndp,
    nf,
    source,
    dec_in,
    src_lengths,
    tgt_lengths,
    enc_in_proj,
    enc_out_proj,
    enc_ffn_in,
    enc_ffn_out,
    enc_gains,
    enc_biases,
    dec_in_proj,
    dec_rel_proj,
    dec_out_proj,
    cross_query,
    cross_kv,
    cross_out,
    dec_ffn_in,
    dec_ffn_out,
    dec_gains,
    dec_biases,
    enc_cot,
    dec_cot,
):
    lay = Layout(ndp, nf)
    lay.place()
    r, f, chips = lay.r, lay.f, lay.chips
    swap, pick, pair = lay.swap, lay.pick, lay.pair
    core = lay.core

    def halves(matrix, groups, width):
        parts = matrix.reshape(r, groups, 2, width)
        return (
            pick(parts[:, :, 0], parts[:, :, 1]).reshape(r, groups * width),
            pick(parts[:, :, 1], parts[:, :, 0]).reshape(r, groups * width),
        )

    split = [
        halves(enc_in_proj, 3, HALF),
        halves(enc_ffn_in, chips, f),
        halves(dec_in_proj, 3, HALF),
        halves(cross_query, 1, HALF),
        halves(cross_kv, 2, HALF),
        halves(dec_ffn_in, chips, f),
        halves(dec_rel_proj, 1, REL_HALF),
    ]
    vec = jnp.concatenate(
        [
            enc_biases,
            enc_gains,
            dec_biases,
            dec_gains,
            src_lengths.astype(BF),
            tgt_lengths.astype(BF),
        ]
    )
    nvec = vec.shape[0]
    padded = -(-nvec // WIDE) * WIDE
    vec = jnp.pad(vec, (0, padded - nvec))
    mine = jnp.concatenate([own for own, other in split], axis=1)
    theirs = jnp.concatenate([other for own, other in split], axis=1)
    theirs_got = swap(theirs)
    vec_got = swap(vec)
    source_got = swap(source)
    dec_in_got = swap(dec_in.reshape(LEN * STREAMS, D))

    def owner_rows(start, width):
        return pair(mine[:, start : start + width], theirs_got[:, start : start + width], 0)

    def column_blocks(start, count):
        return [owner_rows(start + WIDE * i, WIDE) for i in range(count)]

    def row_blocks(matrix):
        return [matrix[:, :WIDE], matrix[:, WIDE:]]

    rel_start = mine.shape[1] - REL_HALF
    rel_own = mine[:, rel_start:]
    rel_other = theirs_got[:, rel_start:]
    vec_pair = pair(vec[None], vec_got[None], 0).reshape(-1, WIDE)
    vec_rows = -(-vec_pair.shape[0] // 16) * 16
    vec_used = vec_pair.shape[0]
    vec_pair = jnp.pad(vec_pair, ((0, vec_rows - vec_used), (0, 0)))
    wide_at = [0, 3 * WIDE, 7 * WIDE, 10 * WIDE, 11 * WIDE, 13 * WIDE]
    chunk_parts = [
        column_blocks(wide_at[0], 3) + row_blocks(enc_out_proj) + [vec_pair],
        column_blocks(wide_at[1], 4) + row_blocks(enc_ffn_out),
        column_blocks(wide_at[2], 3) + [pair(rel_own, rel_other, 1)] + row_blocks(dec_out_proj),
        column_blocks(wide_at[3], 1) + column_blocks(wide_at[4], 2) + row_blocks(cross_out),
        column_blocks(wide_at[5], 4) + row_blocks(dec_ffn_out),
    ]
    bufs = [jnp.concatenate(parts, axis=0) for parts in chunk_parts]
    full = gather_all(lay, bufs)

    def cut(index, block):
        parts = chunk_parts[index]
        at = sum(p.shape[0] for p in parts[:block])
        rows = parts[block].shape[0]
        return full[index][:, :, at : at + rows].reshape(chips * rows, WIDE)

    def columns(index, first, count):
        return jnp.concatenate([cut(index, first + i) for i in range(count)], axis=1)

    def head_rows(index, first):
        rows = columns(index, first, 2)
        low, high = rows[:HALF // 2], rows[HALF // 2 :]
        keep = pick(low, high).reshape(chips // 2, 1, r, D)
        got = swap(pick(high, low)).reshape(chips // 2, 1, r, D)
        return pair(keep, got, 1).reshape(HALF, D)

    w_enc_in = columns(0, 0, 3)
    w_enc_out = head_rows(0, 3)
    w_enc_up = columns(1, 0, 4)
    w_enc_down = columns(1, 4, 2)
    w_dec_in = columns(2, 0, 3)
    w_rel = (
        cut(2, 3)
        .reshape(chips, r, 2, REL_HALF)
        .transpose(0, 2, 1, 3)
        .reshape(D, REL_HALF)
    )
    w_dec_out = head_rows(2, 4)
    w_cross_q = columns(3, 0, 1)
    w_cross_kv = columns(3, 1, 2)
    w_cross_out = head_rows(3, 3)
    w_dec_up = columns(4, 0, 4)
    w_dec_down = columns(4, 4, 2)

    vec_all = (
        cut(0, 5).reshape(chips, vec_rows, WIDE)[:, :vec_used].reshape(lay.devices, padded).astype(F32)
    )
    widths = [enc_biases.shape[0], enc_gains.shape[0], dec_biases.shape[0], dec_gains.shape[0]]
    starts = [0]
    for width in widths:
        starts.append(starts[-1] + width)
    v_enc_b, v_enc_g, v_dec_b, v_dec_g = [
        vec_all[:, starts[i] : starts[i + 1]].reshape(-1) for i in range(4)
    ]
    ebias = slices_of(v_enc_b, ENC_WIDTHS)
    egain = slices_of(v_enc_g, (D, D))
    dbias = slices_of(v_dec_b, DEC_WIDTHS)
    dgain = slices_of(v_dec_g, (D, D, D))

    def half_of(vector):
        parts = vector.reshape(2, -1)
        return pick(parts[0], parts[1])

    def hidden_of(vector):
        parts = vector.reshape(chips, 2, f)
        return pick(parts[:, 0], parts[:, 1]).reshape(-1)

    zero_half = jnp.zeros((HALF,), F32)
    lens = jnp.stack([pair(vec[None], vec_got[None], 0)[:, nvec - 2 + i] for i in range(2)])
    lens = lens.astype(F32).astype(jnp.int32)
    src_len, tgt_len = lens[0], lens[1]
    positions = jnp.arange(LEN, dtype=jnp.int32)
    src_valid = (positions[None, :] < src_len[:, None])[:, None, None, None, :]
    onehot = bucket_table(LEN, BUCKETS)

    def both(partial):
        low = partial.astype(BF)
        return low.astype(F32) + swap(low).astype(F32)

    x = pair(source[None], source_got[None], 0).reshape(2 * LEN, D)
    qkv_bias = jnp.concatenate([half_of(ebias[0]), zero_half, half_of(ebias[1])])
    eqkv = (dot(x, w_enc_in) + qkv_bias).astype(BF).reshape(2, LEN, 3, OWN_HEADS, HEAD)
    eq, ek, ev = eqkv[:, None, :, 0], eqkv[:, :, 1], eqkv[:, :, 2]
    ea, eprobs = attention_forward(eq, ek, ev, src_valid)
    ea = ea.reshape(2 * LEN, HALF)
    ez1 = x.astype(F32) + both(dot(ea, w_enc_out)) + ebias[2]
    eh1 = norm(ez1, egain[0], ebias[5])
    eh1_low = eh1.astype(BF)
    eu = dot(eh1_low, w_enc_up) + hidden_of(ebias[3])
    eg = gelu_exact(eu).astype(BF)
    ez2 = eh1 + both(dot(eg, w_enc_down)) + ebias[4]
    enc = norm(ez2, egain[1], ebias[6])
    enc_low = enc.astype(BF)

    rows = 2 * STREAMS * LEN
    y = pair(
        dec_in.transpose(1, 0, 2)[None], dec_in_got.reshape(LEN, STREAMS, D).transpose(1, 0, 2)[None], 0
    ).reshape(rows, D)
    dqkv_bias = jnp.concatenate([half_of(dbias[0]), zero_half, half_of(dbias[1])])
    dqkv = (dot(y, w_dec_in) + dqkv_bias).astype(BF)
    dqkv = dqkv.reshape(2, STREAMS, LEN, 3, OWN_HEADS, HEAD)
    rel = (dot(y, w_rel) + half_of(dbias[2])).reshape(2, STREAMS, LEN, OWN_HEADS, BUCKETS)
    da, dmain, down = ngram_forward(dqkv, rel, tgt_len, onehot)
    da = da.reshape(rows, HALF)
    dz1 = y.astype(F32) + both(dot(da, w_dec_out)) + dbias[3]
    dh1 = norm(dz1, dgain[0], dbias[9])
    dh1_low = dh1.astype(BF)
    cq = (dot(dh1_low, w_cross_q) + half_of(dbias[4])).astype(BF)
    cq = cq.reshape(2, STREAMS, LEN, OWN_HEADS, HEAD)
    ckv = dot(enc_low, w_cross_kv) + jnp.concatenate([zero_half, half_of(dbias[5])])
    ckv = ckv.astype(BF).reshape(2, LEN, 2, OWN_HEADS, HEAD)
    ck, cv = ckv[:, :, 0], ckv[:, :, 1]
    ca, cprobs = attention_forward(cq, ck, cv, src_valid)
    ca = ca.reshape(rows, HALF)
    dz2 = dh1 + both(dot(ca, w_cross_out)) + dbias[6]
    dh2 = norm(dz2, dgain[1], dbias[10])
    dh2_low = dh2.astype(BF)
    du = dot(dh2_low, w_dec_up) + hidden_of(dbias[7])
    dg = gelu_exact(du).astype(BF)
    dz3 = dh2 + both(dot(dg, w_dec_down)) + dbias[8]
    dec = norm(dz3, dgain[2], dbias[11])

    def own_rows_of(total, count):
        blocks = total[: count * 2 * r].reshape(count, 2, r, WIDE)
        keep = pick(blocks[:, 0], blocks[:, 1])
        got = swap(pick(blocks[:, 1], blocks[:, 0]))
        return pair(keep[:, None], got[:, None], 1)

    def chip_blocks(grad):
        n = grad.shape[1] // WIDE
        shape = (lay.ndp, lay.nz, grad.shape[0] // chips, WIDE)
        low = grad.astype(BF)
        return [low[:, WIDE * i : WIDE * i + WIDE].reshape(shape) for i in range(n)]

    def head_blocks(grad):
        parts = grad.astype(BF).reshape(chips // 2, 2, r, D)
        keep = pick(parts[:, 0], parts[:, 1])
        got = swap(pick(parts[:, 1], parts[:, 0]))
        return chip_blocks(pair(keep, got, 0).reshape(chips * r, D))

    def scatter(parts, previous):
        buf = jnp.concatenate(parts, axis=2)
        if previous is not None:
            buf = tie(buf, previous)
        first = scatter_dp(lay, buf)
        return scatter_z(lay, first), first

    def split_rows(total, sizes):
        at = 0
        result = []
        for size in sizes:
            result.append(total[at : at + size])
            at += size
        return result

    dcot_got = swap(dec_cot.reshape(LEN * STREAMS, D)).reshape(LEN, STREAMS, D)
    dcot = pair(dec_cot.transpose(1, 0, 2)[None], dcot_got.transpose(1, 0, 2)[None], 0)
    dcot = dcot.reshape(rows, D).astype(F32)
    gz3, ggain3, gnorm3 = norm_back(dz3, dgain[2], dcot)
    gf = gz3.astype(BF)
    g_down = dot_g(dg, gf)
    gu = gelu_back(du, dot_t(gf, w_dec_down)).astype(BF)
    g_up = dot_g(dh2_low, gu)
    total4, first4 = scatter(chip_blocks(g_up) + chip_blocks(g_down), None)
    gz2, ggain2, gnorm2 = norm_back(dz2, dgain[1], gz3 + both(dot_t(gu, w_dec_up)))
    gx = gz2.astype(BF)
    g_cross_out = dot_g(ca, gx)
    gca = dot_t(gx, w_cross_out).astype(BF).reshape(2, STREAMS, LEN, OWN_HEADS, HEAD)
    gcq, gck, gcv = attention_back(cq, ck, cv, cprobs, gca)
    gcq = gcq.reshape(rows, HALF)
    gckv = jnp.stack([gck, gcv], axis=2).reshape(2 * LEN, D)
    g_cross_q = dot_g(dh1_low, gcq)
    g_cross_kv = dot_g(enc_low, gckv)
    total3, first3 = scatter(
        chip_blocks(g_cross_q) + chip_blocks(g_cross_kv) + head_blocks(g_cross_out), first4
    )
    ecot_got = swap(enc_cot)
    ecot = pair(enc_cot[None], ecot_got[None], 0).reshape(2 * LEN, D).astype(F32)
    genc = ecot + both(dot_t(gckv, w_cross_kv))
    gz1, ggain1, gnorm1 = norm_back(dz1, dgain[0], gz2 + both(dot_t(gcq, w_cross_q)))
    go = gz1.astype(BF)
    g_dec_out = dot_g(da, go)
    gda = dot_t(go, w_dec_out).astype(BF).reshape(2, STREAMS, LEN, OWN_HEADS, HEAD)
    gqkv, grel = ngram_back(dqkv, dmain, down, onehot, gda)
    gqkv = gqkv.reshape(rows, 3 * HALF)
    grel = grel.reshape(rows, REL_HALF)
    g_dec_in = dot_g(y, gqkv)
    g_rel = dot_g(y, grel)
    rel_block = (
        g_rel.astype(BF)
        .reshape(chips, 2, r, REL_HALF)
        .transpose(0, 2, 1, 3)
        .reshape(lay.ndp, lay.nz, r, WIDE)
    )
    total2, first2 = scatter(chip_blocks(g_dec_in) + [rel_block] + head_blocks(g_dec_out), first3)

    def own_sequence(partial, count):
        parts = partial.reshape(2, count, D)
        keep = pick(parts[0], parts[1])
        return keep + swap(pick(parts[1], parts[0]).astype(BF)).astype(F32)

    def own_part(values, count):
        parts = values.reshape(2, count, D)
        return pick(parts[0], parts[1])

    dec_rows = STREAMS * LEN
    g_dec_input = own_part(gz1, dec_rows) + own_sequence(
        dot_t(gqkv, w_dec_in) + dot_t(grel, w_rel), dec_rows
    )

    def widen(vector):
        zeros = jnp.zeros_like(vector)
        return pick(jnp.concatenate([vector, zeros]), jnp.concatenate([zeros, vector]))

    def widen_hidden(vector):
        parts = vector.reshape(chips, 1, f)
        zeros = jnp.zeros_like(parts)
        return pick(
            jnp.concatenate([parts, zeros], axis=1), jnp.concatenate([zeros, parts], axis=1)
        ).reshape(-1)

    column_sums = col_sum(gqkv)
    dec_vec = jnp.concatenate(
        [
            widen(column_sums[:HALF]),
            widen(column_sums[2 * HALF :]),
            widen(col_sum(grel)),
            0.5 * col_sum(go),
            widen(col_sum(gcq)),
            widen(col_sum(gckv)[HALF:]),
            0.5 * col_sum(gx),
            widen_hidden(col_sum(gu)),
            0.5 * col_sum(gf),
            0.5 * gnorm1,
            0.5 * gnorm2,
            0.5 * gnorm3,
            0.5 * ggain1,
            0.5 * ggain2,
            0.5 * ggain3,
        ]
    )

    gz2e, eggain2, egnorm2 = norm_back(ez2, egain[1], genc)
    gfe = gz2e.astype(BF)
    ge_down = dot_g(eg, gfe)
    gue = gelu_back(eu, dot_t(gfe, w_enc_down)).astype(BF)
    ge_up = dot_g(eh1_low, gue)
    total1, first1 = scatter(chip_blocks(ge_up) + chip_blocks(ge_down), first2)
    gz1e, eggain1, egnorm1 = norm_back(ez1, egain[0], gz2e + both(dot_t(gue, w_enc_up)))
    goe = gz1e.astype(BF)
    ge_out = dot_g(ea, goe)
    gae = dot_t(goe, w_enc_out).astype(BF).reshape(2, 1, LEN, OWN_HEADS, HEAD)
    geq, gek, gev = attention_back(eq, ek, ev, eprobs, gae)
    geqkv = jnp.stack([geq[:, 0], gek, gev], axis=2).reshape(2 * LEN, 3 * HALF)
    ge_in = dot_g(x, geqkv)
    total0, first0 = scatter(chip_blocks(ge_in) + head_blocks(ge_out), first1)
    g_source = own_part(gz1e, LEN) + own_sequence(dot_t(geqkv, w_enc_in), LEN)
    ecolumn_sums = col_sum(geqkv)
    enc_vec = jnp.concatenate(
        [
            widen(ecolumn_sums[:HALF]),
            widen(ecolumn_sums[2 * HALF :]),
            0.5 * col_sum(goe),
            widen_hidden(col_sum(gue)),
            0.5 * col_sum(gfe),
            0.5 * egnorm1,
            0.5 * egnorm2,
            0.5 * eggain1,
            0.5 * eggain2,
        ]
    )
    me = lay.dp * lay.nf + lax.axis_index("fsdp")

    def own_slice(vector):
        return take(vector.reshape(lay.devices, -1), me)

    dec_vec = lax.psum(dec_vec, ("dp", "fsdp"))
    enc_vec = lax.psum(enc_vec, ("dp", "fsdp"))
    nb = sum(ENC_WIDTHS)
    g_enc_biases, g_enc_gains = own_slice(enc_vec[:nb]), own_slice(enc_vec[nb:])
    nb = sum(DEC_WIDTHS)
    g_dec_biases, g_dec_gains = own_slice(dec_vec[:nb]), own_slice(dec_vec[nb:])

    def in_rows(blocks):
        return blocks.transpose(2, 0, 1, 3).reshape(r, -1)

    def up_rows(blocks):
        per = WIDE // f
        return blocks.reshape(4, 2, r, per, f).transpose(2, 0, 3, 1, 4).reshape(r, FF)

    def side(low, high):
        return jnp.concatenate([low, high], axis=1)

    t0 = split_rows(total0, [6 * r, r, r])
    o_enc_in, o_enc_out = in_rows(own_rows_of(t0[0], 3)), side(t0[1], t0[2])
    t1 = split_rows(total1, [8 * r, f, f])
    o_enc_up, o_enc_down = up_rows(own_rows_of(t1[0], 4)), side(t1[1], t1[2])
    t2 = split_rows(total2, [6 * r, r, r, r])
    o_dec_in, o_dec_out = in_rows(own_rows_of(t2[0], 3)), side(t2[2], t2[3])
    relp = t2[1].reshape(r, 2, REL_HALF)
    rel_keep = pick(relp[:, 0], relp[:, 1])
    o_rel = pair(rel_keep, swap(pick(relp[:, 1], relp[:, 0])), 1)
    t3 = split_rows(total3, [2 * r, 4 * r, r, r])
    o_cross_q = in_rows(own_rows_of(t3[0], 1))
    o_cross_kv = in_rows(own_rows_of(t3[1], 2))
    o_cross_out = side(t3[2], t3[3])
    t4 = split_rows(total4, [8 * r, f, f])
    o_dec_up, o_dec_down = up_rows(own_rows_of(t4[0], 4)), side(t4[1], t4[2])

    return (
        own_part(enc_low, LEN),
        own_part(dec.astype(BF), dec_rows).reshape(STREAMS, LEN, D).transpose(1, 0, 2),
        g_source,
        g_dec_input.reshape(STREAMS, LEN, D).transpose(1, 0, 2),
        o_enc_in,
        o_enc_out,
        o_enc_up,
        o_enc_down,
        g_enc_gains,
        g_enc_biases,
        o_dec_in,
        o_rel,
        o_dec_out,
        o_cross_q,
        o_cross_kv,
        o_cross_out,
        o_dec_up,
        o_dec_down,
        g_dec_gains,
        g_dec_biases,
    )


BUDGET = 58 * 1024 * 1024
PIECES = 8


def run(body, grid, ins, outs, scratch=()):
    arrays = [a for a, s in ins]
    return pl.pallas_call(
        body,
        grid=(grid,),
        in_specs=[s for a, s in ins],
        out_specs=[s for a, s in outs],
        out_shape=[a for a, s in outs],
        scratch_shapes=list(scratch),
        compiler_params=pltpu.CompilerParams(vmem_limit_bytes=BUDGET),
    )(*arrays)


def full(array):
    zeros = (0,) * array.ndim
    return array, pl.BlockSpec(array.shape, lambda t: zeros, pipeline_mode=pl.Buffered(1))


def small(array):
    return array, pl.BlockSpec(memory_space=pltpu.SMEM)


def out_full(shape, dtype):
    zeros = (0,) * len(shape)
    return jax.ShapeDtypeStruct(shape, dtype), pl.BlockSpec(shape, lambda t: zeros)


def out_cols(rows, cols, dtype, index):
    return (
        jax.ShapeDtypeStruct((rows, cols), dtype),
        pl.BlockSpec((rows, WIDE), lambda t: (0, index(t))),
    )


def in_cols(array, index, width=WIDE):
    return array, pl.BlockSpec((array.shape[0], width), lambda t: (0, index(t)))


def blocks(pieces, rows, index):
    return [
        (p, pl.BlockSpec((2, rows, WIDE), lambda t: (0, index(t), 0))) for p in pieces
    ]


def assemble(refs, scr, place):
    dp, z = place[0], place[1]
    for i in range(4):
        for half in range(2):
            for j in range(2):
                step = 2 * half + j
                scr[jnp.bitwise_xor(dp, i), jnp.bitwise_and(z - step, 3)] = refs[2 * i + half][j]


def weight_scratch(rows, width=WIDE):
    return pltpu.VMEM((4, 4, rows, width), BF)


def matrix_of(scr):
    a, b, c, d = scr.shape
    return scr[...].reshape(a * b * c, d)


def pick_matrix(parity):
    i = lax.broadcasted_iota(jnp.int32, (HALF, HALF // 2), 0)
    j = lax.broadcasted_iota(jnp.int32, (HALF, HALF // 2), 1)
    from_row = ((j >> 5) << 6) + (parity << 5) + (j & 31)
    return jnp.where(i == from_row, 1.0, 0.0).astype(BF)


def head_masks():
    lane = lax.broadcasted_iota(jnp.int32, (1, 128), 1)
    first = jnp.where(lane < HEAD, 1.0, 0.0)
    return first.astype(BF), (1.0 - first).astype(BF)


def first_lanes(rows):
    return lax.broadcasted_iota(jnp.int32, (rows, 128), 1) < HEAD


def soft_rows(scores):
    top = jnp.max(scores, axis=-1, keepdims=True)
    raised = jnp.exp(scores - top)
    return raised * (1.0 / jnp.sum(raised, axis=-1, keepdims=True))


def masked_probs(queries, keys, count):
    scores = dot_t(queries, keys) * SCALE
    column = lax.broadcasted_iota(jnp.int32, scores.shape, 1)
    return soft_rows(jnp.where(column < count, scores, MASKED))


def attend(q, k, v, count):
    rows = q.shape[0]
    out = []
    for mask in head_masks():
        probs = masked_probs(q * mask, k, count).astype(BF)
        out.append(dot(probs, v))
    return jnp.where(first_lanes(rows), out[0], out[1]).astype(BF)


def attend_back(q, k, v, g, count):
    gq, gk, gv = [], 0.0, 0.0
    for mask in head_masks():
        qm, gm = q * mask, g * mask
        probs = masked_probs(qm, k, count)
        gp = dot_t(gm, v)
        ds = (probs * (gp - jnp.sum(probs * gp, axis=-1, keepdims=True))).astype(BF)
        gq.append(dot(ds, k))
        gk = gk + dot_g(ds, qm)
        gv = gv + dot_g(probs.astype(BF), gm)
    gq = jnp.where(first_lanes(q.shape[0]), gq[0], gq[1]) * SCALE
    return gq.astype(BF), (gk * SCALE).astype(BF), gv.astype(BF)


def split_parity(heads, place, keep, send):
    core = place[2]
    keep[...] = dot(heads[...], pick_matrix(core)).astype(BF)
    send[...] = dot(heads[...], pick_matrix(1 - core)).astype(BF)


def join_parity(keep, got, place, heads):
    core = place[2]
    heads[...] = (
        dot_t(keep[...], pick_matrix(core)) + dot_t(got[...], pick_matrix(1 - core))
    ).astype(BF)


def enc_attention(place, x, bias, pieces):
    rows = x.shape[0]

    def body(place, x, bias, *refs):
        w, (qkv, keep, send, scr, heads) = refs[:PIECES], refs[PIECES:]
        t = pl.program_id(0)
        assemble(w, scr, place)
        qkv[:, pl.ds(t * WIDE, WIDE)] = (dot(x[...], matrix_of(scr)) + bias[...]).astype(BF)

        @pl.when(t == 2)
        def _():
            for s in range(2):
                r = slice(s * LEN, s * LEN + LEN)
                for j in range(4):
                    c = [slice(HALF * i + 128 * j, HALF * i + 128 * j + 128) for i in range(3)]
                    heads[r, c[0]] = attend(qkv[r, c[0]], qkv[r, c[1]], qkv[r, c[2]], place[3 + s])
            split_parity(heads, place, keep, send)

    return run(
        body,
        3,
        [small(place), full(x), in_cols(bias, lambda t: t)] + blocks(pieces, 64, lambda t: t),
        [
            out_full((rows, 3 * HALF), BF),
            out_full((rows, HALF // 2), BF),
            out_full((rows, HALF // 2), BF),
        ],
        [weight_scratch(64), pltpu.VMEM((rows, HALF), BF)],
    )


def out_projection(place, keep, got, pieces):
    rows = keep.shape[0]

    def body(place, keep, got, *refs):
        w, (out, scr) = refs[:PIECES], refs[PIECES:]
        assemble(w, scr, place)
        core = place[2]
        mine = scr[pl.ds(2 * core, 2)].reshape(HALF // 2, WIDE)
        theirs = scr[pl.ds(2 - 2 * core, 2)].reshape(HALF // 2, WIDE)
        out[...] = (dot(keep[...], mine) + dot(got[...], theirs)).astype(BF)

    return run(
        body,
        2,
        [small(place), full(keep), full(got)] + blocks(pieces, 32, lambda t: 6 + t),
        [out_cols(rows, D, BF, lambda t: t)],
        [weight_scratch(32)],
    )[0]


def stats(v):
    centered = v - jnp.mean(v, axis=-1, keepdims=True)
    inverse = lax.rsqrt(jnp.mean(centered * centered, axis=-1, keepdims=True) + EPSILON)
    return centered * inverse, inverse


def each_tile(rows, tile, step):
    def loop(m, carry):
        step(pl.multiple_of(m * tile, tile))
        return carry

    lax.fori_loop(0, rows // tile, loop, 0)


def norm_tiles(rows, base, affine, own, other, bias, gain, shift, unit_out, inv_out, low_out, at=0):
    def step(r):
        here = pl.ds(r, LEN)
        v = base[here].astype(F32)
        if affine is not None:
            v = v * affine[0] + affine[1]
        there = pl.ds(r + at, LEN)
        v = v + (own[there].astype(F32) + other[there].astype(F32)) + bias
        unit, inverse = stats(v)
        unit_out[here] = unit
        inv_out[here] = jnp.broadcast_to(inverse, (LEN, 128))
        low_out[here] = (unit * gain + shift).astype(BF)

    each_tile(rows, LEN, step)


ROOT_HALF = math.sqrt(0.5)
ROOT_TWO_PI = math.sqrt(0.5 / math.pi)


def gelu_pair(u):
    phi = 0.5 + 0.5 * lax.erf(u * ROOT_HALF)
    return u * phi, phi + u * (jnp.exp(-0.5 * u * u) * ROOT_TWO_PI)


def ffn_forward(place, base, affine, own, other, vecs, hidden_bias, pieces):
    rows = base.shape[0]
    hidden = hidden_bias.shape[1]
    ups = hidden // WIDE
    tile = 256

    def body(place, base, own, other, vecs, hb, *refs):
        wu, wd = refs[:PIECES], refs[PIECES : 2 * PIECES]
        unit, inv, low, g, gp, part, scr_u, scr_d, acts = refs[2 * PIECES :]
        t = pl.program_id(0)

        @pl.when(t == 0)
        def _():
            aff = (vecs[0:1], vecs[1:2]) if affine else None
            norm_tiles(
                rows, base, aff, own, other, vecs[2:3], vecs[3:4], vecs[4:5], unit, inv, low
            )

        @pl.when(t < ups)
        def _():
            assemble(wu, scr_u, place)
            w = matrix_of(scr_u)

            def step(r):
                here = pl.ds(r, tile)
                a, b = gelu_pair(dot(low[here], w) + hb[...])
                a = a.astype(BF)
                g[here] = a
                acts[here, pl.ds(t * WIDE, WIDE)] = a
                gp[here] = b.astype(BF)

            each_tile(rows, tile, step)

        @pl.when(t >= ups)
        def _():
            assemble(wd, scr_d, place)
            part[...] = dot(acts[...], matrix_of(scr_d)).astype(BF)

    up = lambda t: jnp.minimum(t, ups - 1)
    down = lambda t: jnp.maximum(t - ups, 0)
    return run(
        body,
        ups + 2,
        [small(place), full(base), full(own), full(other), full(vecs), in_cols(hidden_bias, up)]
        + blocks(pieces, 64, up)
        + blocks(pieces, 128, lambda t: 2 + down(t)),
        [
            out_full((rows, D), F32),
            out_full((rows, 128), F32),
            out_full((rows, D), BF),
            out_cols(rows, hidden, BF, up),
            out_cols(rows, hidden, BF, up),
            out_cols(rows, D, BF, down),
        ],
        [weight_scratch(64), weight_scratch(128), pltpu.VMEM((rows, hidden), BF)],
    )


def distance_buckets(reverse):
    row = lax.broadcasted_iota(jnp.int32, (128, 128), 0) & (BUCKETS - 1)
    lane = lax.broadcasted_iota(jnp.int32, (128, 128), 1)
    distance = ((lane + 1) if reverse else (128 - lane)) & 127
    bucket = jnp.zeros((128, 128), jnp.int32)
    for target in range(1, BUCKETS):
        at = 1
        while bucket_value(at, BUCKETS) < target:
            at += 1
        bucket = bucket + jnp.where(distance >= at, 1, 0)
    return jnp.where(bucket == row, 1.0, 0.0).astype(BF)


def skew(values):
    parts = [values[128 * n : 128 * n + 128] for n in range(values.shape[0] // 128)]
    return jnp.concatenate(
        [pltpu.roll(part, 0, 1, stride=1, stride_axis=0) for part in parts], axis=0
    )


def mirror():
    row = lax.broadcasted_iota(jnp.int32, (128, 128), 0)
    lane = lax.broadcasted_iota(jnp.int32, (128, 128), 1)
    return jnp.where(row + lane == 127, 1.0, 0.0).astype(BF)


def quarter_mask(h):
    lane = lax.broadcasted_iota(jnp.int32, (1, 128), 1)
    return jnp.where((lane >> 5) == h, 1.0, 0.0).astype(BF)


def ngram_probs(qm, prod, k0, rel_high, rel_low, table, count, h, first):
    mask = quarter_mask(h % 4)
    turned = dot(rel_high * mask, table) + dot(rel_low * mask, table)
    scores = dot_t(qm, k0) * SCALE + skew(turned)
    row = lax.broadcasted_iota(jnp.int32, scores.shape, 0)
    column = lax.broadcasted_iota(jnp.int32, scores.shape, 1)
    token = row & (LEN - 1)
    reach = jnp.where(row < LEN, token, token - 1)
    scores = jnp.where((column <= reach) & (column < count), scores, MASKED)
    own = jnp.sum(prod * first, axis=-1, keepdims=True) * SCALE + turned[:, 0:1]
    main = lax.broadcasted_iota(jnp.int32, own.shape, 0) < LEN
    own = jnp.where(main, 2.0 * MASKED, own)
    top = jnp.maximum(jnp.max(scores, axis=-1, keepdims=True), own)
    raised = jnp.exp(scores - top)
    own = jnp.exp(own - top)
    scale = 1.0 / (jnp.sum(raised, axis=-1, keepdims=True) + own)
    return raised * scale, own * scale


def split_high(values):
    high = values.astype(BF)
    return high, (values - high.astype(F32)).astype(BF)


def half_rows(rows):
    first = jnp.where(lax.broadcasted_iota(jnp.int32, (rows, 128), 1) < HEAD, 1.0, 0.0)
    return first, 1.0 - first


def ngram_attention(place, y, bias, rel_bias, pieces):
    rows = y.shape[0]
    span = STREAMS * LEN

    def body(place, y, bias, rbias, *refs):
        w, wr = refs[:PIECES], refs[PIECES : 2 * PIECES]
        qkv, rel, keep, send, scr, scr_r, heads, table = refs[2 * PIECES :]
        t = pl.program_id(0)

        @pl.when(t < 3)
        def _():
            assemble(w, scr, place)
            qkv[:, pl.ds(pl.multiple_of(t * WIDE, WIDE), WIDE)] = (
                dot(y[...], matrix_of(scr)) + bias[...]
            ).astype(BF)

        @pl.when(t == 3)
        def _():
            assemble_rel(wr, scr_r, place)
            rel[...] = dot(y[...], scr_r[...].reshape(D, REL_HALF)) + rbias[...]
            table[...] = distance_buckets(False)
            lanes = half_rows(span)

            def step(s, carry):
                r = pl.ds(pl.multiple_of(s * span, span), span)
                r0 = pl.ds(pl.multiple_of(s * span, span), LEN)
                count = place[5 + s]
                for j in range(4):
                    c = [slice(HALF * i + 128 * j, HALF * i + 128 * j + 128) for i in range(3)]
                    q, k, v = qkv[r, c[0]], qkv[r, c[1]], qkv[r, c[2]]
                    k0, v0 = qkv[r0, c[1]], qkv[r0, c[2]]
                    high, low = split_high(rel[r, 128 * (j // 2) : 128 * (j // 2) + 128])
                    prod = q.astype(F32) * k.astype(F32)
                    out = []
                    for i, mask in enumerate(head_masks()):
                        probs, own = ngram_probs(
                            q * mask, prod, k0, high, low, table[...], count, 2 * j + i, lanes[i]
                        )
                        own = own.astype(BF).astype(F32)
                        out.append(dot(probs.astype(BF), v0) + own * v.astype(F32))
                    heads[r, c[0]] = jnp.where(first_lanes(span), out[0], out[1]).astype(BF)
                return carry

            lax.fori_loop(0, 2, step, 0)
            split_parity(heads, place, keep, send)

    third = lambda t: jnp.minimum(t, 2)
    return run(
        body,
        4,
        [small(place), full(y), in_cols(bias, third), full(rel_bias)]
        + blocks(pieces, 64, third)
        + blocks(pieces, 32, lambda t: 8),
        [
            out_full((rows, 3 * HALF), BF),
            out_full((rows, REL_HALF), F32),
            out_full((rows, HALF // 2), BF),
            out_full((rows, HALF // 2), BF),
        ],
        [
            weight_scratch(64),
            pltpu.VMEM((4, 4, 2, 32, REL_HALF), BF),
            pltpu.VMEM((rows, HALF), BF),
            pltpu.VMEM((128, 128), BF),
        ],
    )


def assemble_rel(refs, scr, place):
    dp, z = place[0], place[1]
    for i in range(4):
        for half in range(2):
            for j in range(2):
                block = refs[2 * i + half][j]
                a, b = jnp.bitwise_xor(dp, i), jnp.bitwise_and(z - (2 * half + j), 3)
                scr[a, b, 0] = block[:, :REL_HALF]
                scr[a, b, 1] = block[:, REL_HALF:]


def cross_forward(place, y, own, other, vecs, eunit, evecs, eown, eother, q_bias, kv_bias, pieces):
    rows, mem = y.shape[0], eunit.shape[0]
    span = STREAMS * LEN

    def body(place, y, own, other, vecs, eunit, evecs, eown, eother, qb, kvb, *refs):
        w = refs[:PIECES]
        unit, inv, low, eunit2, einv2, elow, q, kv, keep, send, scr, heads = refs[PIECES:]
        t = pl.program_id(0)
        assemble(w, scr, place)

        @pl.when(t == 0)
        def _():
            norm_tiles(
                rows, y, None, own, other, vecs[0:1], vecs[1:2], vecs[2:3], unit, inv, low
            )
            norm_tiles(
                mem,
                eunit,
                (evecs[0:1], evecs[1:2]),
                eown,
                eother,
                evecs[2:3],
                evecs[3:4],
                evecs[4:5],
                eunit2,
                einv2,
                elow,
            )
            q[...] = (dot(low[...], matrix_of(scr)) + qb[...]).astype(BF)

        @pl.when(t > 0)
        def _():
            at = pl.multiple_of((t - 1) * WIDE, WIDE)
            kv[:, pl.ds(at, WIDE)] = (dot(elow[...], matrix_of(scr)) + kvb[...]).astype(BF)

        @pl.when(t == 2)
        def _():
            for s in range(2):
                r = slice(s * span, s * span + span)
                m = slice(s * LEN, s * LEN + LEN)
                for j in range(4):
                    c = slice(128 * j, 128 * j + 128)
                    c2 = slice(HALF + 128 * j, HALF + 128 * j + 128)
                    heads[r, c] = attend(q[r, c], kv[m, c], kv[m, c2], place[3 + s])
            split_parity(heads, place, keep, send)

    return run(
        body,
        3,
        [small(place)]
        + [full(a) for a in (y, own, other, vecs, eunit, evecs, eown, eother, q_bias)]
        + [in_cols(kv_bias, lambda t: jnp.maximum(t - 1, 0))]
        + blocks(pieces, 64, lambda t: t),
        [
            out_full((rows, D), F32),
            out_full((rows, 128), F32),
            out_full((rows, D), BF),
            out_full((mem, D), F32),
            out_full((mem, 128), F32),
            out_full((mem, D), BF),
            out_full((rows, HALF), BF),
            out_full((mem, D), BF),
            out_full((rows, HALF // 2), BF),
            out_full((rows, HALF // 2), BF),
        ],
        [weight_scratch(64), pltpu.VMEM((rows, HALF), BF)],
    )


def fold(values):
    return jnp.sum(values.reshape(values.shape[0] // 8, 8, values.shape[1]), axis=0)


def norm_back_tile(total, unit, inverse, gain):
    scaled = total * gain
    one = jnp.mean(scaled, axis=-1, keepdims=True)
    two = jnp.mean(scaled * unit, axis=-1, keepdims=True)
    return inverse * (scaled - one - unit * two)


def ffn_back(place, final, total_ins, unit_ins, vecs, gp, pieces):
    rows, hidden = gp.shape
    ups = hidden // WIDE
    n_total, n_unit = len(total_ins), len(unit_ins)
    mine = rows // 2

    def body(place, vecs, gp, *refs):
        at = 0

        def take_refs(n):
            nonlocal at
            at += n
            return refs[at - n : at]

        tot, uni = take_refs(n_total), take_refs(n_unit)
        wu, wd = take_refs(PIECES), take_refs(PIECES)
        outs = take_refs(1) if final else ()
        gz, gf, gu, part, s_gain, s_shift, s_gf, s_gu = take_refs(8)
        scr_u, scr_d, all_u, scr_all_u, acc = refs[at:]
        t = pl.program_id(0)

        @pl.when(t == 0)
        def _():
            acc[...] = jnp.zeros_like(acc)

            def step(r):
                here = pl.ds(r, LEN)
                if final:
                    v = uni[0][here] * vecs[0:1] + vecs[1:2]
                    v = v + (uni[1][here].astype(F32) + uni[2][here].astype(F32)) + vecs[2:3]
                    unit, inverse = stats(v)

                    @pl.when((r >= mine) == (place[2] == 1))
                    def _():
                        to = pl.ds(pl.multiple_of(r - mine * place[2], LEN), LEN)
                        outs[0][to] = (unit * vecs[3:4] + vecs[4:5]).astype(BF)

                else:
                    unit, inverse = uni[0][here], uni[1][here, 0:1]
                total = tot[0][here].astype(F32)
                if n_total > 1:
                    there = pl.ds(r + tot[1].shape[0] - rows, LEN)
                    total = total + (tot[1][there].astype(F32) + tot[2][there].astype(F32))
                acc[0:8] += fold(total * unit)
                acc[8:16] += fold(total)
                back = norm_back_tile(total, unit, inverse, vecs[3:4])
                gz[here] = back
                low = back.astype(BF)
                gf[here] = low
                acc[16:24] += fold(low.astype(F32))

            each_tile(rows, LEN, step)
            s_gain[...] = jnp.sum(acc[0:8], axis=0, keepdims=True)
            s_shift[...] = jnp.sum(acc[8:16], axis=0, keepdims=True)
            s_gf[...] = jnp.sum(acc[16:24], axis=0, keepdims=True)

        @pl.when(t < 2)
        def _():
            assemble(wd, scr_d.at[t], place)

        @pl.when(t >= 2)
        def _():
            b = t - 2
            assemble(wu, scr_u, place)
            scr_all_u[:, pl.ds(pl.multiple_of(b * WIDE, WIDE), WIDE)] = matrix_of(scr_u)
            w0 = scr_d[0, b].reshape(WIDE, WIDE)
            w1 = scr_d[1, b].reshape(WIDE, WIDE)
            back = dot_t(gf[:, :WIDE], w0) + dot_t(gf[:, WIDE:], w1)
            low = (back * gp[...].astype(F32)).astype(BF)
            gu[...] = low
            all_u[:, pl.ds(pl.multiple_of(b * WIDE, WIDE), WIDE)] = low
            s_gu[...] = jnp.sum(fold(low.astype(F32)), axis=0, keepdims=True)

        @pl.when(t == ups + 1)
        def _():
            part[...] = dot_t(all_u[...], scr_all_u[...]).astype(BF)

    up = lambda t: jnp.maximum(t - 2, 0)
    down = lambda t: jnp.minimum(t, 1)
    outs = [out_full((mine, D), BF)] if final else []
    outs += [
        out_full((rows, D), F32),
        out_full((rows, D), BF),
        out_cols(rows, hidden, BF, up),
        out_full((rows, D), BF),
        out_full((1, D), F32),
        out_full((1, D), F32),
        out_full((1, D), F32),
        out_cols(1, hidden, F32, up),
    ]
    return run(
        body,
        ups + 2,
        [small(place), full(vecs), in_cols(gp, up)]
        + [full(a) for a in total_ins]
        + [full(a) for a in unit_ins]
        + blocks(pieces, 64, up)
        + blocks(pieces, 128, lambda t: 2 + down(t)),
        outs,
        [
            weight_scratch(64),
            pltpu.VMEM((2, 4, 4, 128, WIDE), BF),
            pltpu.VMEM((rows, hidden), BF),
            pltpu.VMEM((D, hidden), BF),
            pltpu.VMEM((24, D), F32),
        ],
    )


def branch_back(place, resid, own, other, unit, inv, gain, pieces):
    rows = resid.shape[0]

    def body(place, resid, own, other, unit, inv, gain, *refs):
        w = refs[:PIECES]
        gz, gx, keep, send, s_gain, s_shift, s_gx, scr, total_out, acc = refs[PIECES:]
        t = pl.program_id(0)
        assemble(w, scr, place)

        @pl.when(t == 0)
        def _():
            acc[...] = jnp.zeros_like(acc)

            def step(r):
                here = pl.ds(r, LEN)
                total = resid[here] + (own[here].astype(F32) + other[here].astype(F32))
                acc[0:8] += fold(total * unit[here])
                acc[8:16] += fold(total)
                back = norm_back_tile(total, unit[here], inv[here, 0:1], gain[...])
                gz[here] = back
                low = back.astype(BF)
                gx[here] = low
                acc[16:24] += fold(low.astype(F32))

            each_tile(rows, LEN, step)
            s_gain[...] = jnp.sum(acc[0:8], axis=0, keepdims=True)
            s_shift[...] = jnp.sum(acc[8:16], axis=0, keepdims=True)
            s_gx[...] = jnp.sum(acc[16:24], axis=0, keepdims=True)
            total_out[...] = dot_t(gx[:, :WIDE], matrix_of(scr))

        @pl.when(t == 1)
        def _():
            total_out[...] += dot_t(gx[:, WIDE:], matrix_of(scr))
            core = place[2]
            quarter = HALF // 2
            keep[...] = total_out[:, pl.ds(pl.multiple_of(quarter * core, 128), quarter)].astype(BF)
            send[...] = total_out[
                :, pl.ds(pl.multiple_of(quarter * (1 - core), 128), quarter)
            ].astype(BF)

    return run(
        body,
        2,
        [small(place)]
        + [full(a) for a in (resid, own, other, unit, inv, gain)]
        + blocks(pieces, 32, lambda t: 6 + t),
        [
            out_full((rows, D), F32),
            out_full((rows, D), BF),
            out_full((rows, HALF // 2), BF),
            out_full((rows, HALF // 2), BF),
            out_full((1, D), F32),
            out_full((1, D), F32),
            out_full((1, D), F32),
        ],
        [weight_scratch(32), pltpu.VMEM((rows, HALF), F32), pltpu.VMEM((24, D), F32)],
    )


def column_sums(out, values):
    out[...] = jnp.sum(fold(values.astype(F32)), axis=0, keepdims=True)


def cross_back(place, q, kv, keep, got, pieces):
    rows, mem = q.shape[0], kv.shape[0]
    span = STREAMS * LEN

    def body(place, q, kv, keep, got, *refs):
        w = refs[:PIECES]
        gq, gkv, part, s_gq, s_gkv, scr, g, acc = refs[PIECES:]
        t = pl.program_id(0)
        assemble(w, scr, place)

        @pl.when(t == 0)
        def _():
            join_parity(keep, got, place, g)
            for s in range(2):
                r = slice(s * span, s * span + span)
                m = slice(s * LEN, s * LEN + LEN)
                for j in range(4):
                    c = slice(128 * j, 128 * j + 128)
                    c2 = slice(HALF + 128 * j, HALF + 128 * j + 128)
                    gq[r, c], gkv[m, c], gkv[m, c2] = attend_back(
                        q[r, c], kv[m, c], kv[m, c2], g[r, c], place[3 + s]
                    )
            column_sums(s_gq, gq[...])
            column_sums(s_gkv, gkv[...])
            part[:rows] = dot_t(gq[...], matrix_of(scr)).astype(BF)

        @pl.when(t == 1)
        def _():
            acc[...] = dot_t(gkv[:, :HALF], matrix_of(scr))

        @pl.when(t == 2)
        def _():
            part[rows:] = (acc[...] + dot_t(gkv[:, HALF:], matrix_of(scr))).astype(BF)

    return run(
        body,
        3,
        [small(place), full(q), full(kv), full(keep), full(got)]
        + blocks(pieces, 64, lambda t: t),
        [
            out_full((rows, HALF), BF),
            out_full((mem, D), BF),
            out_full((rows + mem, D), BF),
            out_full((1, HALF), F32),
            out_full((1, D), F32),
        ],
        [weight_scratch(64), pltpu.VMEM((rows, HALF), BF), pltpu.VMEM((mem, D), F32)],
    )


def input_grads(place, gz, parts, keep, send):
    rows = gz.shape[0] // 2
    core = place[2]
    here = pl.ds(pl.multiple_of(rows * core, LEN), rows)
    there = pl.ds(pl.multiple_of(rows * (1 - core), LEN), rows)
    total = gz[here]
    for g, w in parts:
        total = total + dot_t(g[here], w)
    keep[...] = total
    total = 0.0
    for g, w in parts:
        total = total + dot_t(g[there], w)
    send[...] = total.astype(BF)


def enc_attention_back(place, qkv, keep, got, gz, pieces):
    rows = qkv.shape[0]

    def body(place, qkv, keep, got, gz, *refs):
        w = refs[:PIECES]
        gqkv, out, send, sums, scr, g, win = refs[PIECES:]
        t = pl.program_id(0)
        assemble(w, scr, place)
        win[:, pl.ds(pl.multiple_of(t * WIDE, WIDE), WIDE)] = matrix_of(scr)

        @pl.when(t == 0)
        def _():
            join_parity(keep, got, place, g)
            for s in range(2):
                r = slice(s * LEN, s * LEN + LEN)
                for j in range(4):
                    c = [slice(HALF * i + 128 * j, HALF * i + 128 * j + 128) for i in range(3)]
                    gqkv[r, c[0]], gqkv[r, c[1]], gqkv[r, c[2]] = attend_back(
                        qkv[r, c[0]], qkv[r, c[1]], qkv[r, c[2]], g[r, c[0]], place[3 + s]
                    )
            column_sums(sums, gqkv[...])

        @pl.when(t == 2)
        def _():
            input_grads(place, gz, [(gqkv, win[...])], out, send)

    return run(
        body,
        3,
        [small(place), full(qkv), full(keep), full(got), full(gz)]
        + blocks(pieces, 64, lambda t: t),
        [
            out_full((rows, 3 * HALF), BF),
            out_full((rows // 2, D), F32),
            out_full((rows // 2, D), BF),
            out_full((1, 3 * HALF), F32),
        ],
        [weight_scratch(64), pltpu.VMEM((rows, HALF), BF), pltpu.VMEM((D, 3 * HALF), BF)],
    )


def ngram_back_kernel(place, qkv, rel, keep, got, gz, pieces):
    rows = qkv.shape[0]
    span = STREAMS * LEN

    def body(place, qkv, rel, keep, got, gz, *refs):
        w, wr = refs[:PIECES], refs[PIECES : 2 * PIECES]
        gqkv, grel, out, send, sums, s_rel, scr, scr_r, g, win, *tables = refs[2 * PIECES :]
        table, table_back, flip = tables
        t = pl.program_id(0)

        @pl.when(t < 3)
        def _():
            assemble(w, scr, place)
            win[:, pl.ds(pl.multiple_of(t * WIDE, WIDE), WIDE)] = matrix_of(scr)

        @pl.when(t == 0)
        def _():
            join_parity(keep, got, place, g)
            table[...] = distance_buckets(False)
            table_back[...] = distance_buckets(True)
            flip[...] = mirror()
            lanes = half_rows(span)

            def step(s, carry):
                r = pl.ds(pl.multiple_of(s * span, span), span)
                r0 = pl.ds(pl.multiple_of(s * span, span), LEN)
                r1 = pl.ds(pl.multiple_of(s * span + LEN, LEN), span - LEN)
                count = place[5 + s]
                for j in range(4):
                    c = [slice(HALF * i + 128 * j, HALF * i + 128 * j + 128) for i in range(3)]
                    q, k, v = qkv[r, c[0]], qkv[r, c[1]], qkv[r, c[2]]
                    k0, v0 = qkv[r0, c[1]], qkv[r0, c[2]]
                    go = g[r, c[0]]
                    high, low = split_high(rel[r, 128 * (j // 2) : 128 * (j // 2) + 128])
                    prod = q.astype(F32) * k.astype(F32)
                    prod_g = go.astype(F32) * v.astype(F32)
                    gq, gk0, gv0, p_own, d_own, turned = [], 0.0, 0.0, [], [], []
                    for i, mask in enumerate(head_masks()):
                        qm, gm = q * mask, go * mask
                        h = 2 * j + i
                        probs, own = ngram_probs(
                            qm, prod, k0, high, low, table[...], count, h, lanes[i]
                        )
                        gp = dot_t(gm, v0)
                        g_own = jnp.sum(prod_g * lanes[i], axis=-1, keepdims=True)
                        inner = jnp.sum(probs * gp, axis=-1, keepdims=True) + own * g_own
                        ds = (probs * (gp - inner)).astype(BF)
                        ds_own = (own * (g_own - inner)).astype(BF).astype(F32)
                        gq.append(dot(ds, k0))
                        gk0 = gk0 + dot_g(ds, qm)
                        gv0 = gv0 + dot_g(probs.astype(BF), gm)
                        p_own.append(own.astype(BF).astype(F32))
                        d_own.append(ds_own)
                        back = skew(dot(ds, flip[...]))
                        lane = lax.broadcasted_iota(jnp.int32, back.shape, 1)
                        main = lax.broadcasted_iota(jnp.int32, back.shape, 0) < LEN
                        back = jnp.where((lane == 127) & jnp.logical_not(main), ds_own, back)
                        grads = dot_t(back.astype(BF), table_back[...])
                        turned.append(grads * quarter_mask(h % 4).astype(F32))
                    first = first_lanes(span)
                    d_own = jnp.where(first, d_own[0], d_own[1])
                    p_own = jnp.where(first, p_own[0], p_own[1])
                    gqf = jnp.where(first, gq[0], gq[1]) + d_own * k.astype(F32)
                    gqkv[r, c[0]] = (gqf * SCALE).astype(BF)
                    gkn = d_own * q.astype(F32) * SCALE
                    gvn = p_own * go.astype(F32)
                    gqkv[r0, c[1]] = (gk0 * SCALE).astype(BF)
                    gqkv[r0, c[2]] = gv0.astype(BF)
                    gqkv[r1, c[1]] = gkn[LEN:].astype(BF)
                    gqkv[r1, c[2]] = gvn[LEN:].astype(BF)
                    both = turned[0] + turned[1]
                    at = slice(128 * (j // 2), 128 * (j // 2) + 128)
                    if j % 2 == 0:
                        held = both
                    else:
                        grel[r, at] = (held + both).astype(BF)
                return carry

            lax.fori_loop(0, 2, step, 0)
            column_sums(sums, gqkv[...])
            column_sums(s_rel, grel[...])

        @pl.when(t == 3)
        def _():
            assemble_rel(wr, scr_r, place)
            wrel = scr_r[...].reshape(D, REL_HALF)
            input_grads(place, gz, [(gqkv, win[...]), (grel, wrel)], out, send)

    third = lambda t: jnp.minimum(t, 2)
    return run(
        body,
        4,
        [small(place), full(qkv), full(rel), full(keep), full(got), full(gz)]
        + blocks(pieces, 64, third)
        + blocks(pieces, 32, lambda t: 8),
        [
            out_full((rows, 3 * HALF), BF),
            out_full((rows, REL_HALF), BF),
            out_full((rows // 2, D), F32),
            out_full((rows // 2, D), BF),
            out_full((1, 3 * HALF), F32),
            out_full((1, REL_HALF), F32),
        ],
        [
            weight_scratch(64),
            pltpu.VMEM((4, 4, 2, 32, REL_HALF), BF),
            pltpu.VMEM((rows, HALF), BF),
            pltpu.VMEM((D, 3 * HALF), BF),
        ]
        + [pltpu.VMEM((128, 128), BF)] * 3,
    )


def grad_chunk(place, arrays, terms, total_rows):
    n = len(arrays)

    def body(place, *refs):
        ins, outs, scr = refs[:n], refs[n : n + 7], refs[n + 7]
        t = pl.program_id(0)
        dp, z, core = place[0], place[1], place[2]

        def spread(value, at, rows):
            v = value.astype(BF).reshape(4, 4, rows, WIDE)
            scr[:, :, :rows] = v
            for i in range(4):
                for step in range(4):
                    block = scr[jnp.bitwise_xor(dp, i), jnp.bitwise_and(z + step, 3), :rows]
                    if i == 0:
                        outs[0][step, at : at + rows] = block
                    else:
                        outs[2 * i - 1 + step // 2][step % 2, at : at + rows] = block

        for index, (kind, at, x, g, col) in enumerate(terms):

            @pl.when(t == index)
            def _(kind=kind, at=at, x=x, g=g, col=col):
                if kind == "whole":
                    spread(ins[x][...], at, ins[x].shape[0] // 16)
                    return
                if kind == "heads":
                    right = ins[g][:, col : col + WIDE]
                    mine, theirs = ins[x][...], ins[x + 1][...]
                    keep, got = dot_g(mine, right), dot_g(theirs, right)
                    quarter = (2, 4, 32, WIDE)
                    scr[pl.ds(2 * core, 2), :, :32] = keep.astype(BF).reshape(quarter)
                    scr[pl.ds(2 - 2 * core, 2), :, :32] = got.astype(BF).reshape(quarter)
                    spread(scr[:, :, :32], at, 32)
                    return
                if kind == "rel":
                    v = dot_g(ins[x][...], ins[g][...]).astype(BF).reshape(16, 2, 32, REL_HALF)
                    spread(jnp.concatenate([v[:, 0], v[:, 1]], axis=-1), at, 32)
                    return
                value = dot_g(ins[x][...], ins[g][:, col : col + WIDE])
                spread(value, at, value.shape[0] // 16)

    shape = (2, total_rows, WIDE)
    return run(
        body,
        len(terms),
        [small(place)] + [full(a) for a in arrays],
        [out_full((4, total_rows, WIDE), BF)] + [out_full(shape, BF)] * 6,
        [weight_scratch(128)],
    )


def vec_chunk(place, pieces):
    def body(place, *refs):
        assemble(refs[:PIECES], refs[PIECES], place)

    return run(
        body,
        1,
        [small(place)] + blocks(pieces, 16, lambda t: 18),
        [out_full((4, 4, 16, WIDE), BF)],
    )[0]


def gather_pieces(lay, buf):
    got = [buf] + [lay.shift_z(buf, step) for step in range(1, 4)]
    low = jnp.stack(got[:2])
    high = jnp.stack(got[2:])
    x_low, y_low = lay.flip_dp(low, 1), lay.flip_dp(low, 2)
    x_high, y_high = lay.flip_dp(high, 1), lay.flip_dp(high, 2)
    d_low = lay.flip_dp(x_low, 2)
    d_high = lay.flip_dp(y_high, 1)
    return [low, high, x_low, x_high, y_low, y_high, d_low, d_high]


def scatter_pieces(lay, parts):
    own, x_low, x_high, y_low, y_high, d_low, d_high = parts
    d_low = lay.flip_dp(d_low, 2)
    d_high = lay.flip_dp(d_high, 1)
    x_high = lay.flip_dp(x_high, 1)
    y_low = lay.flip_dp(y_low, 2)
    x_low = lay.flip_dp(add_low(x_low, d_low), 1)
    y_high = lay.flip_dp(add_low(y_high, d_high), 2)
    sides = [(x_low, y_low, 0), (x_low, y_low, 1), (x_high, y_high, 0), (x_high, y_high, 1)]
    sums = [add_low(own[s], x[i], y[i]) for s, (x, y, i) in enumerate(sides)]
    total = sums[0].astype(F32)
    for step in range(1, 4):
        total = total + lay.shift_z(sums[step], step).astype(F32)
    return total


def shards_fast(
    ndp,
    nf,
    source,
    dec_in,
    src_lengths,
    tgt_lengths,
    enc_in_proj,
    enc_out_proj,
    enc_ffn_in,
    enc_ffn_out,
    enc_gains,
    enc_biases,
    dec_in_proj,
    dec_rel_proj,
    dec_out_proj,
    cross_query,
    cross_kv,
    cross_out,
    dec_ffn_in,
    dec_ffn_out,
    dec_gains,
    dec_biases,
    enc_cot,
    dec_cot,
):
    lay = Layout(ndp, nf)
    lay.place()
    r, f, chips = lay.r, lay.f, lay.chips
    swap, pick, pair = lay.swap, lay.pick, lay.pair
    core = lay.core
    dec_rows = STREAMS * LEN

    def halves(matrix, groups, width):
        parts = matrix.reshape(r, groups, 2, width)
        return (
            pick(parts[:, :, 0], parts[:, :, 1]).reshape(r, groups * width),
            pick(parts[:, :, 1], parts[:, :, 0]).reshape(r, groups * width),
        )

    split = [
        halves(enc_in_proj, 3, HALF),
        halves(enc_ffn_in, chips, f),
        halves(dec_in_proj, 3, HALF),
        halves(cross_query, 1, HALF),
        halves(cross_kv, 2, HALF),
        halves(dec_ffn_in, chips, f),
        halves(dec_rel_proj, 1, REL_HALF),
    ]
    vec = jnp.concatenate(
        [
            enc_biases,
            enc_gains,
            dec_biases,
            dec_gains,
            src_lengths.astype(BF),
            tgt_lengths.astype(BF),
        ]
    )
    nvec = vec.shape[0]
    padded = -(-nvec // WIDE) * WIDE
    vec = jnp.pad(vec, (0, padded - nvec))
    mine = jnp.concatenate([own for own, other in split], axis=1)
    theirs = jnp.concatenate([other for own, other in split], axis=1)
    theirs_got = swap(theirs)
    vec_got = swap(vec)
    source_got = swap(source)
    dec_own = dec_in.transpose(1, 0, 2).reshape(dec_rows, D)
    dec_got = swap(dec_own)

    def column_blocks(start, count):
        return [
            pair(
                mine[:, start + WIDE * i : start + WIDE * i + WIDE],
                theirs_got[:, start + WIDE * i : start + WIDE * i + WIDE],
                0,
            )
            for i in range(count)
        ]

    def row_blocks(matrix):
        return [matrix[:, :WIDE], matrix[:, WIDE:]]

    rel_start = mine.shape[1] - REL_HALF
    rel_block = pair(mine[:, rel_start:], theirs_got[:, rel_start:], 1)
    vec_pair = pair(vec[None], vec_got[None], 0)
    vec_used = 2 * padded // WIDE
    vec_block = jnp.pad(vec_pair.reshape(vec_used, WIDE), ((0, 16 - vec_used), (0, 0)))
    at = [0, 3 * WIDE, 7 * WIDE, 10 * WIDE, 11 * WIDE, 13 * WIDE]
    chunk_parts = {
        "enc": column_blocks(at[0], 3) + row_blocks(enc_out_proj),
        "enc_ffn": column_blocks(at[1], 4) + row_blocks(enc_ffn_out),
        "dec": column_blocks(at[2], 3) + row_blocks(dec_out_proj) + [rel_block, vec_block],
        "cross": column_blocks(at[3], 1) + column_blocks(at[4], 2) + row_blocks(cross_out),
        "dec_ffn": column_blocks(at[5], 4) + row_blocks(dec_ffn_out),
    }
    w = {}
    order = ["dec", "enc", "enc_ffn", "cross", "dec_ffn"]
    for i, name in enumerate(order):
        buf = jnp.concatenate(chunk_parts[name], axis=0)
        if i >= 2:
            buf = tie(buf, *w[order[i - 2]][2:4])
        w[name] = gather_pieces(lay, buf)

    lens = vec_pair[:, nvec - 2 :].T.reshape(-1).astype(F32).astype(jnp.int32)
    place = jnp.concatenate(
        [jnp.stack([lay.dp, lay.z, core]).astype(jnp.int32), lens, jnp.zeros((1,), jnp.int32)]
    )

    vec_all = vec_chunk(place, w["dec"]).reshape(chips, 16, WIDE)[:, :vec_used]
    vec_all = vec_all.reshape(lay.devices, padded).astype(F32)
    widths = [enc_biases.shape[0], enc_gains.shape[0], dec_biases.shape[0], dec_gains.shape[0]]
    starts = [0]
    for width in widths:
        starts.append(starts[-1] + width)
    v_enc_b, v_enc_g, v_dec_b, v_dec_g = [
        vec_all[:, starts[i] : starts[i + 1]].reshape(-1) for i in range(4)
    ]
    eb, eg_rows = v_enc_b.reshape(-1, D), v_enc_g.reshape(2, D)
    dg_rows = v_dec_g.reshape(3, D)
    d_split = 2 * D + HEADS * BUCKETS
    db = v_dec_b[d_split:].reshape(-1, D)

    def half_of(vector):
        parts = vector.reshape(2, -1)
        return pick(parts[0], parts[1])

    def hidden_of(vector):
        parts = vector.reshape(chips, 2, f)
        return pick(parts[:, 0], parts[:, 1]).reshape(1, -1)

    zero_half = jnp.zeros((HALF,), F32)

    def qkv_bias(q, v):
        return jnp.concatenate([half_of(q), zero_half, half_of(v)])[None]

    def rows_of(*vectors):
        return jnp.stack(vectors)

    x = pair(source, source_got, 0)
    y = pair(dec_own, dec_got, 0)
    dqkv, rel, da_keep, da_send = ngram_attention(
        place,
        y,
        qkv_bias(v_dec_b[:D], v_dec_b[D : 2 * D]),
        half_of(v_dec_b[2 * D : d_split])[None],
        w["dec"],
    )
    da_got = swap(da_send)
    p3 = out_projection(place, da_keep, da_got, w["dec"])
    p3_got = swap(p3)
    eqkv, ea_keep, ea_send = enc_attention(place, x, qkv_bias(eb[0], eb[1]), w["enc"])
    ea_got = swap(ea_send)
    p1 = out_projection(place, ea_keep, ea_got, w["enc"])
    p1_got = swap(p1)
    eunit1, einv1, eh1_low, eg, egp, p2 = ffn_forward(
        place,
        x,
        False,
        p1,
        p1_got,
        rows_of(eb[2], eb[2], eb[2], eg_rows[0], eb[8]),
        hidden_of(eb[3:7]),
        w["enc_ffn"],
    )
    p2_got = swap(p2)
    dunit1, dinv1, dh1_low, eunit2, einv2, enc_low, cq, ckv, ca_keep, ca_send = cross_forward(
        place,
        y,
        p3,
        p3_got,
        rows_of(db[0], dg_rows[0], db[9]),
        eunit1,
        rows_of(eg_rows[0], eb[8], eb[7], eg_rows[1], eb[9]),
        p2,
        p2_got,
        half_of(db[1])[None],
        jnp.concatenate([zero_half, half_of(db[2])])[None],
        w["cross"],
    )
    ca_got = swap(ca_send)
    p4 = out_projection(place, ca_keep, ca_got, w["cross"])
    p4_got = swap(p4)
    dunit2, dinv2, dh2_low, dg, dgp, p5 = ffn_forward(
        place,
        dunit1,
        True,
        p4,
        p4_got,
        rows_of(dg_rows[0], db[9], db[3], dg_rows[1], db[10]),
        hidden_of(db[4:8]),
        w["dec_ffn"],
    )
    p5_got = swap(p5)

    dcot_own = dec_cot.transpose(1, 0, 2).reshape(dec_rows, D)
    dcot = pair(dcot_own, swap(dcot_own), 0)
    ecot = pair(enc_cot, swap(enc_cot), 0)
    dec_out, gz3, gf, gu, p6, s_gain3, s_shift3, s_gf, s_gu = ffn_back(
        place,
        True,
        [dcot],
        [dunit2, p5, p5_got],
        rows_of(dg_rows[1], db[10], db[8], dg_rows[2], db[11]),
        dgp,
        w["dec_ffn"],
    )
    p6_got = swap(p6)
    up_terms = [("plain", 64 * b, 0, 1, WIDE * b) for b in range(4)]
    down_terms = [("plain", 256 + 128 * h, 2, 3, WIDE * h) for h in range(2)]
    total4 = scatter_pieces(
        lay, grad_chunk(place, [dh2_low, gu, dg, gf], up_terms + down_terms, 512)
    )
    gz2, gx, gca_keep, gca_send, s_gain2, s_shift2, s_gx = branch_back(
        place, gz3, p6, p6_got, dunit2, dinv2, dg_rows[1:2], w["cross"]
    )
    gca_got = swap(gca_send)
    gcq, gckv, p7, s_gcq, s_gckv = cross_back(place, cq, ckv, gca_keep, gca_got, w["cross"])
    p7_got = swap(p7)
    total3 = scatter_pieces(
        lay,
        grad_chunk(
            place,
            [dh1_low, gcq, enc_low, gckv, ca_keep, ca_got, gx],
            [
                ("plain", 0, 0, 1, 0),
                ("plain", 64, 2, 3, 0),
                ("plain", 128, 2, 3, WIDE),
                ("heads", 192, 4, 6, 0),
                ("heads", 224, 4, 6, WIDE),
            ],
            256,
        ),
    )
    gz1, go, gda_keep, gda_send, s_gain1, s_shift1, s_go = branch_back(
        place, gz2, p7, p7_got, dunit1, dinv1, dg_rows[0:1], w["dec"]
    )
    gda_got = swap(gda_send)
    gqkv, grel, p8, p8_send, s_gqkv, s_grel = ngram_back_kernel(
        place, dqkv, rel, gda_keep, gda_got, gz1, w["dec"]
    )
    p8_got = swap(p8_send)
    total2 = scatter_pieces(
        lay,
        grad_chunk(
            place,
            [y, gqkv, da_keep, da_got, go, grel],
            [("plain", 64 * b, 0, 1, WIDE * b) for b in range(3)]
            + [("heads", 192, 2, 4, 0), ("heads", 224, 2, 4, WIDE), ("rel", 256, 0, 5, 0)],
            288,
        ),
    )
    gz2e, gfe, gue, p9, e_gain2, e_shift2, s_gfe, s_gue = ffn_back(
        place,
        False,
        [ecot, p7, p7_got],
        [eunit2, einv2],
        rows_of(*([eg_rows[1]] * 5)),
        egp,
        w["enc_ffn"],
    )
    p9_got = swap(p9)
    total1 = scatter_pieces(
        lay, grad_chunk(place, [eh1_low, gue, eg, gfe], up_terms + down_terms, 512)
    )
    gz1e, goe, gea_keep, gea_send, e_gain1, e_shift1, s_goe = branch_back(
        place, gz2e, p9, p9_got, eunit1, einv1, eg_rows[0:1], w["enc"]
    )
    gea_got = swap(gea_send)
    geqkv, p10, p10_send, s_geqkv = enc_attention_back(
        place, eqkv, gea_keep, gea_got, gz1e, w["enc"]
    )
    p10_got = swap(p10_send)

    def widen(vector):
        zeros = jnp.zeros_like(vector)
        return pick(jnp.concatenate([vector, zeros]), jnp.concatenate([zeros, vector]))

    def widen_hidden(vector):
        parts = vector.reshape(chips, 1, f)
        zeros = jnp.zeros_like(parts)
        return pick(
            jnp.concatenate([parts, zeros], axis=1), jnp.concatenate([zeros, parts], axis=1)
        ).reshape(-1)

    def owned(*vectors):
        return jnp.concatenate(vectors).reshape(lay.devices, -1)

    vec_grads = jnp.concatenate(
        [
            owned(
                widen(s_geqkv[0, :HALF]),
                widen(s_geqkv[0, 2 * HALF :]),
                0.5 * s_goe[0],
                widen_hidden(s_gue),
                0.5 * s_gfe[0],
                0.5 * e_shift1[0],
                0.5 * e_shift2[0],
            ),
            owned(0.5 * e_gain1[0], 0.5 * e_gain2[0]),
            owned(
                widen(s_gqkv[0, :HALF]),
                widen(s_gqkv[0, 2 * HALF :]),
                widen(s_grel[0]),
                0.5 * s_go[0],
                widen(s_gcq[0]),
                widen(s_gckv[0, HALF:]),
                0.5 * s_gx[0],
                widen_hidden(s_gu),
                0.5 * s_gf[0],
                0.5 * s_shift1[0],
                0.5 * s_shift2[0],
                0.5 * s_shift3[0],
            ),
            owned(0.5 * s_gain1[0], 0.5 * s_gain2[0], 0.5 * s_gain3[0]),
        ],
        axis=1,
    ).astype(BF)
    vec_width = vec_grads.shape[1]
    vec_grads = jnp.pad(vec_grads, ((0, 0), (0, padded - vec_width)))
    vec_grads = vec_grads.reshape(chips, vec_used, WIDE)
    vec_grads = jnp.pad(vec_grads, ((0, 0), (0, 16 - vec_used), (0, 0))).reshape(chips * 16, WIDE)
    total0 = scatter_pieces(
        lay,
        grad_chunk(
            place,
            [x, geqkv, ea_keep, ea_got, goe, vec_grads],
            [("plain", 64 * b, 0, 1, WIDE * b) for b in range(3)]
            + [("heads", 192, 2, 4, 0), ("heads", 224, 2, 4, WIDE), ("whole", 256, 5, 5, 0)],
            272,
        ),
    )

    def split_rows(total, sizes):
        at = 0
        result = []
        for size in sizes:
            result.append(total[at : at + size])
            at += size
        return result

    def own_rows_of(total, count):
        rows = total.reshape(count, 2, r, WIDE)
        keep = pick(rows[:, 0], rows[:, 1])
        got = swap(pick(rows[:, 1], rows[:, 0]))
        return pair(keep[:, None], got[:, None], 1)

    def in_rows(rows):
        return rows.transpose(2, 0, 1, 3).reshape(r, -1)

    def up_rows(rows):
        per = WIDE // f
        return rows.reshape(4, 2, r, per, f).transpose(2, 0, 3, 1, 4).reshape(r, FF)

    def side(low, high):
        return jnp.concatenate([low, high], axis=1)

    t0 = split_rows(total0, [6 * r, r, r, 16])
    o_enc_in, o_enc_out = in_rows(own_rows_of(t0[0], 3)), side(t0[1], t0[2])
    vec_sum = t0[3][:vec_used].reshape(2, padded)
    vec_sum = pick(vec_sum[0], vec_sum[1]) + swap(pick(vec_sum[1], vec_sum[0]))
    o_vec = [vec_sum[starts[i] : starts[i + 1]] for i in range(4)]
    t1 = split_rows(total1, [8 * r, f, f])
    o_enc_up, o_enc_down = up_rows(own_rows_of(t1[0], 4)), side(t1[1], t1[2])
    t2 = split_rows(total2, [6 * r, r, r, r])
    o_dec_in, o_dec_out = in_rows(own_rows_of(t2[0], 3)), side(t2[1], t2[2])
    relp = t2[3].reshape(r, 2, REL_HALF)
    o_rel = pair(pick(relp[:, 0], relp[:, 1]), swap(pick(relp[:, 1], relp[:, 0])), 1)
    t3 = split_rows(total3, [2 * r, 4 * r, r, r])
    o_cross_q = in_rows(own_rows_of(t3[0], 1))
    o_cross_kv = in_rows(own_rows_of(t3[1], 2))
    o_cross_out = side(t3[2], t3[3])
    t4 = split_rows(total4, [8 * r, f, f])
    o_dec_up, o_dec_down = up_rows(own_rows_of(t4[0], 4)), side(t4[1], t4[2])

    return (
        pick(enc_low[:LEN], enc_low[LEN:]),
        dec_out.reshape(STREAMS, LEN, D).transpose(1, 0, 2),
        p10 + p10_got.astype(F32),
        (p8 + p8_got.astype(F32)).reshape(STREAMS, LEN, D).transpose(1, 0, 2),
        o_enc_in,
        o_enc_out,
        o_enc_up,
        o_enc_down,
        o_vec[1],
        o_vec[0],
        o_dec_in,
        o_rel,
        o_dec_out,
        o_cross_q,
        o_cross_kv,
        o_cross_out,
        o_dec_up,
        o_dec_down,
        o_vec[3],
        o_vec[2],
    )


def solution(mesh):
    ndp, nf = mesh.shape["dp"], mesh.shape["fsdp"]
    whole = ("dp", "fsdp")
    one, two, three = P(whole), P(whole, None), P(whole, None, None)
    args = (two, three, one, one) + (two,) * 4 + (one,) * 2 + (two,) * 8 + (one,) * 2 + (two, three)
    outs = (two, three, two, three) + (two,) * 4 + (one,) * 2 + (two,) * 8 + (one,) * 2

    def body(*arrays):
        if (ndp, nf) == (4, 8):
            return shards_fast(ndp, nf, *arrays)
        return shards(ndp, nf, *arrays)

    return jax.shard_map(body, mesh=mesh, in_specs=args, out_specs=outs, check_vma=False)
```

```python
import math

import jax
import jax.numpy as jnp
from jax import lax
from jax.experimental import pallas as pl
from jax.experimental.pallas import tpu as pltpu
from jax.sharding import PartitionSpec as P

D = 1024
HEADS = 16
HEAD = 64
FF = 4096
NGRAM = 2
STREAMS = NGRAM + 1
BUCKETS = 32
LEN = 128
HALF = D // 2
OWN_HEADS = HEADS // 2
REL_HALF = OWN_HEADS * BUCKETS
HIDDEN_HALF = FF // 2
WIDE = 512
EPSILON = 1e-05
MASKED = -1000000000.0
SCALE = 1.0 / math.sqrt(HEAD)
BF = jnp.bfloat16
F32 = jnp.float32
ENC_WIDTHS = (D, D, D, FF, D, D, D)
DEC_WIDTHS = (D, D, HEADS * BUCKETS, D, D, D, D, FF, D, D, D, D)


def bucket_value(distance, bucket_count):
    exact_count = bucket_count // 2
    if distance < exact_count:
        return distance
    return min(
        bucket_count - 1,
        exact_count
        + int(
            math.log(distance / exact_count)
            / math.log(128 / exact_count)
            * (bucket_count - exact_count)
        ),
    )


def bucket_table(length, bucket_count):
    positions = jnp.arange(length, dtype=jnp.int32)
    distance = positions[:, None] - positions[None, :]
    bucket = jnp.zeros((length, length), jnp.int32)
    for target in range(1, bucket_count):
        distance_at = 1
        while bucket_value(distance_at, bucket_count) < target:
            distance_at += 1
        bucket = bucket + (distance >= distance_at).astype(jnp.int32)
    return (bucket[:, :, None] == jnp.arange(bucket_count, dtype=jnp.int32)).astype(F32)


def slices_of(vector, widths):
    starts = 0
    result = []
    for amount in widths:
        result.append(vector[starts : starts + amount])
        starts += amount
    return result


def dot(a, b):
    return lax.dot_general(a, b, (((1,), (0,)), ((), ())), preferred_element_type=F32)


def dot_t(a, b):
    return lax.dot_general(a, b, (((1,), (1,)), ((), ())), preferred_element_type=F32)


def dot_g(a, b):
    return lax.dot_general(a, b, (((0,), (0,)), ((), ())), preferred_element_type=F32)


def norm_stats(values):
    average = jnp.mean(values, axis=-1, keepdims=True)
    centered = values - average
    variance = jnp.mean(centered * centered, axis=-1, keepdims=True)
    inverse = lax.rsqrt(variance + EPSILON)
    return centered * inverse, inverse


def norm(values, gain, shift):
    unit, inverse = norm_stats(values)
    return unit * gain + shift


def norm_back(values, gain, grads):
    unit, inverse = norm_stats(values)
    scaled = grads * gain
    mean_one = jnp.mean(scaled, axis=-1, keepdims=True)
    mean_two = jnp.mean(scaled * unit, axis=-1, keepdims=True)
    return (
        inverse * (scaled - mean_one - unit * mean_two),
        jnp.sum(grads * unit, axis=0),
        jnp.sum(grads, axis=0),
    )


def gelu_exact(inputs):
    return jax.nn.gelu(inputs, approximate=False)


def gelu_back(inputs, gradients):
    outputs, pullback = jax.vjp(gelu_exact, inputs)
    return pullback(gradients)[0]


def col_sum(values):
    return jnp.sum(values.astype(F32), axis=0)


class Layout:
    def __init__(self, ndp, nf):
        self.ndp = ndp
        self.nf = nf
        self.nz = nf // 2
        self.chips = ndp * self.nz
        self.devices = ndp * nf
        self.r = D // self.devices
        self.f = FF // self.devices

    def place(self):
        self.dp = lax.axis_index("dp")
        fs = lax.axis_index("fsdp")
        self.z = fs // 2
        self.core = fs % 2

    def swap(self, value):
        return lax.ppermute(value, "fsdp", [(i, i ^ 1) for i in range(self.nf)])

    def shift_z(self, value, step):
        return lax.ppermute(
            value, "fsdp", [(i, (i + 2 * step) % self.nf) for i in range(self.nf)]
        )

    def flip_dp(self, value, mask):
        return lax.ppermute(value, "dp", [(i, i ^ mask) for i in range(self.ndp)])

    def shift_dp(self, value, step):
        return lax.ppermute(value, "dp", [(i, (i + step) % self.ndp) for i in range(self.ndp)])

    def pick(self, first, second):
        return jnp.where(self.core == 0, first, second)

    def pair(self, own, other, axis):
        return self.pick(
            jnp.concatenate([own, other], axis=axis), jnp.concatenate([other, own], axis=axis)
        )


def tie(value, *others):
    return lax.optimization_barrier((value,) + others)[0]


def gather_z(lay, buf):
    out = jnp.zeros((lay.nz,) + buf.shape, buf.dtype)
    out = lax.dynamic_update_slice(out, buf[None], (lay.z, 0, 0))
    for step in range(1, lay.nz):
        got = lay.shift_z(buf, step)
        out = lax.dynamic_update_slice(out, got[None], ((lay.z - step) % lay.nz, 0, 0))
    return out


def gather_dp_first(lay, buf):
    if lay.ndp == 4:
        return [lay.flip_dp(buf, 1), lay.flip_dp(buf, 2)]
    return [lay.shift_dp(buf, step) for step in range(1, lay.ndp)]


def gather_dp_rest(lay, buf, first):
    half = lay.nz // 2
    out = jnp.zeros((lay.ndp,) + buf.shape, buf.dtype)
    if lay.ndp == 4:
        low = lay.flip_dp(first[0][:half], 2)
        high = lay.flip_dp(first[1][half:], 1)
        parts = [(0, 0, buf), (1, 0, first[0]), (2, 0, first[1]), (3, 0, low), (3, half, high)]
        for flip, at, part in parts:
            out = lax.dynamic_update_slice(out, part[None], (lay.dp ^ flip, at, 0, 0))
        return out
    out = lax.dynamic_update_slice(out, buf[None], (lay.dp, 0, 0, 0))
    for step in range(1, lay.ndp):
        out = lax.dynamic_update_slice(
            out, first[step - 1][None], ((lay.dp - step) % lay.ndp, 0, 0, 0)
        )
    return out


def gather_all(lay, bufs):
    staged = []
    results = []
    firsts = []
    for i, buf in enumerate(bufs):
        if i >= 2:
            buf = tie(buf, *firsts[i - 2])
        z = gather_z(lay, buf)
        staged.append(z)
        firsts.append(gather_dp_first(lay, z))
    for z, first in zip(staged, firsts):
        results.append(gather_dp_rest(lay, z, first))
    return results


def take(buf, index, axis=0):
    return lax.dynamic_index_in_dim(buf, index, axis, keepdims=False)


def add_low(*values):
    return sum(v.astype(F32) for v in values).astype(BF)


def scatter_dp(lay, buf):
    if lay.ndp == 4:
        half = lay.nz // 2
        far = take(buf, lay.dp ^ 3)
        to_x = take(buf, lay.dp ^ 1)
        to_y = take(buf, lay.dp ^ 2)
        own = take(buf, lay.dp)
        low = lay.flip_dp(far[:half], 2)
        high = lay.flip_dp(far[half:], 1)
        to_x = jnp.concatenate([add_low(to_x[:half], low), to_x[half:]], axis=0)
        to_y = jnp.concatenate([to_y[:half], add_low(to_y[half:], high)], axis=0)
        return add_low(own, lay.flip_dp(to_x, 1), lay.flip_dp(to_y, 2))
    parts = [take(buf, lay.dp)]
    for step in range(1, lay.ndp):
        parts.append(lay.shift_dp(take(buf, (lay.dp + step) % lay.ndp), step))
    return add_low(*parts)


def scatter_z(lay, buf):
    total = take(buf, lay.z).astype(F32)
    for step in range(1, lay.nz):
        total = total + lay.shift_z(take(buf, (lay.z + step) % lay.nz), step).astype(F32)
    return total


def attention_forward(queries, keys, values, allowed):
    scores = jnp.einsum("snihe,sjhe->snhij", queries, keys, preferred_element_type=F32) * SCALE
    probs = jax.nn.softmax(jnp.where(allowed, scores, MASKED), axis=-1)
    out = jnp.einsum("snhij,sjhe->snihe", probs.astype(BF), values, preferred_element_type=F32)
    return out.astype(BF), probs


def attention_back(queries, keys, values, probs, grad_out):
    grad_probs = jnp.einsum("snihe,sjhe->snhij", grad_out, values, preferred_element_type=F32)
    grad_values = jnp.einsum(
        "snhij,snihe->sjhe", probs.astype(BF), grad_out, preferred_element_type=F32
    )
    grad_scores = (
        probs * (grad_probs - jnp.sum(probs * grad_probs, axis=-1, keepdims=True))
    ).astype(BF)
    grad_queries = (
        jnp.einsum("snhij,sjhe->snihe", grad_scores, keys, preferred_element_type=F32) * SCALE
    )
    grad_keys = (
        jnp.einsum("snhij,snihe->sjhe", grad_scores, queries, preferred_element_type=F32) * SCALE
    )
    return grad_queries.astype(BF), grad_keys.astype(BF), grad_values.astype(BF)


def ngram_forward(dqkv, rel, tgt, onehot):
    q, k, v = dqkv[:, :, :, 0], dqkv[:, :, :, 1], dqkv[:, :, :, 2]
    positions = jnp.arange(LEN, dtype=jnp.int32)
    inside = positions[None, :] < tgt[:, None]
    main_valid = (positions[None, :] <= positions[:, None])[None] & inside[:, None]
    pred_valid = (positions[None, :] < positions[:, None])[None] & inside[:, None]
    valid = jnp.stack([main_valid] + [pred_valid] * NGRAM, axis=1)[:, :, None]
    main = jnp.einsum("snihe,sjhe->snhij", q, k[:, 0], preferred_element_type=F32) * SCALE
    main = main + jnp.einsum("snihk,ijk->snhij", rel, onehot, precision=lax.Precision.HIGHEST)
    main = jnp.where(valid, main, MASKED)
    own = jnp.einsum("snihe,snihe->snhi", q, k, preferred_element_type=F32) * SCALE
    own = own + jnp.transpose(rel[..., 0], (0, 1, 3, 2))
    stream = jnp.arange(STREAMS)[None, :, None, None]
    own = jnp.where(stream == 0, -jnp.inf, own)
    top = jnp.maximum(jnp.max(main, axis=-1), own)
    main = jnp.exp(main - top[..., None])
    own = jnp.exp(own - top)
    total = jnp.sum(main, axis=-1) + own
    main = main / total[..., None]
    own = own / total
    out = jnp.einsum("snhij,sjhe->snihe", main.astype(BF), v[:, 0], preferred_element_type=F32)
    own_low = jnp.transpose(own.astype(BF), (0, 1, 3, 2)).astype(F32)[..., None]
    out = out + own_low * v.astype(F32)
    return out.astype(BF), main, own


def ngram_back(dqkv, main, own, onehot, grad_out):
    q, k, v = dqkv[:, :, :, 0], dqkv[:, :, :, 1], dqkv[:, :, :, 2]
    grad_main = jnp.einsum("snihe,sjhe->snhij", grad_out, v[:, 0], preferred_element_type=F32)
    grad_own = jnp.einsum("snihe,snihe->snhi", grad_out, v, preferred_element_type=F32)
    inner = jnp.sum(main * grad_main, axis=-1) + own * grad_own
    ds = (main * (grad_main - inner[..., None])).astype(BF)
    ds_own = (own * (grad_own - inner)).astype(BF)
    own_rows = jnp.transpose(ds_own, (0, 1, 3, 2)).astype(F32)[..., None]
    p_rows = jnp.transpose(own.astype(BF), (0, 1, 3, 2)).astype(F32)[..., None]
    gq = (
        jnp.einsum("snhij,sjhe->snihe", ds, k[:, 0], preferred_element_type=F32)
        + own_rows * k.astype(F32)
    ) * SCALE
    gk0 = jnp.einsum("snhij,snihe->sjhe", ds, q, preferred_element_type=F32) * SCALE
    gv0 = jnp.einsum("snhij,snihe->sjhe", main.astype(BF), grad_out, preferred_element_type=F32)
    gk = own_rows * q.astype(F32) * SCALE
    gv = p_rows * grad_out.astype(F32)
    gk = jnp.concatenate([gk0[:, None], gk[:, 1:]], axis=1)
    gv = jnp.concatenate([gv0[:, None], gv[:, 1:]], axis=1)
    gqkv = jnp.stack([gq, gk, gv], axis=3).astype(BF)
    grel = jnp.einsum("snhij,ijk->snihk", ds, onehot.astype(BF), preferred_element_type=F32)
    first = (jnp.arange(BUCKETS) == 0).astype(F32)
    grel = (grel + own_rows * first).astype(BF)
    return gqkv, grel


def shards(
    ndp,
    nf,
    source,
    dec_in,
    src_lengths,
    tgt_lengths,
    enc_in_proj,
    enc_out_proj,
    enc_ffn_in,
    enc_ffn_out,
    enc_gains,
    enc_biases,
    dec_in_proj,
    dec_rel_proj,
    dec_out_proj,
    cross_query,
    cross_kv,
    cross_out,
    dec_ffn_in,
    dec_ffn_out,
    dec_gains,
    dec_biases,
    enc_cot,
    dec_cot,
):
    lay = Layout(ndp, nf)
    lay.place()
    r, f, chips = lay.r, lay.f, lay.chips
    swap, pick, pair = lay.swap, lay.pick, lay.pair
    core = lay.core

    def halves(matrix, groups, width):
        parts = matrix.reshape(r, groups, 2, width)
        return (
            pick(parts[:, :, 0], parts[:, :, 1]).reshape(r, groups * width),
            pick(parts[:, :, 1], parts[:, :, 0]).reshape(r, groups * width),
        )

    split = [
        halves(enc_in_proj, 3, HALF),
        halves(enc_ffn_in, chips, f),
        halves(dec_in_proj, 3, HALF),
        halves(cross_query, 1, HALF),
        halves(cross_kv, 2, HALF),
        halves(dec_ffn_in, chips, f),
        halves(dec_rel_proj, 1, REL_HALF),
    ]
    vec = jnp.concatenate(
        [
            enc_biases,
            enc_gains,
            dec_biases,
            dec_gains,
            src_lengths.astype(BF),
            tgt_lengths.astype(BF),
        ]
    )
    nvec = vec.shape[0]
    padded = -(-nvec // WIDE) * WIDE
    vec = jnp.pad(vec, (0, padded - nvec))
    mine = jnp.concatenate([own for own, other in split], axis=1)
    theirs = jnp.concatenate([other for own, other in split], axis=1)
    theirs_got = swap(theirs)
    vec_got = swap(vec)
    source_got = swap(source)
    dec_in_got = swap(dec_in.reshape(LEN * STREAMS, D))

    def owner_rows(start, width):
        return pair(mine[:, start : start + width], theirs_got[:, start : start + width], 0)

    def column_blocks(start, count):
        return [owner_rows(start + WIDE * i, WIDE) for i in range(count)]

    def row_blocks(matrix):
        return [matrix[:, :WIDE], matrix[:, WIDE:]]

    rel_start = mine.shape[1] - REL_HALF
    rel_own = mine[:, rel_start:]
    rel_other = theirs_got[:, rel_start:]
    vec_pair = pair(vec[None], vec_got[None], 0).reshape(-1, WIDE)
    vec_rows = -(-vec_pair.shape[0] // 16) * 16
    vec_used = vec_pair.shape[0]
    vec_pair = jnp.pad(vec_pair, ((0, vec_rows - vec_used), (0, 0)))
    wide_at = [0, 3 * WIDE, 7 * WIDE, 10 * WIDE, 11 * WIDE, 13 * WIDE]
    chunk_parts = [
        column_blocks(wide_at[0], 3) + row_blocks(enc_out_proj) + [vec_pair],
        column_blocks(wide_at[1], 4) + row_blocks(enc_ffn_out),
        column_blocks(wide_at[2], 3) + [pair(rel_own, rel_other, 1)] + row_blocks(dec_out_proj),
        column_blocks(wide_at[3], 1) + column_blocks(wide_at[4], 2) + row_blocks(cross_out),
        column_blocks(wide_at[5], 4) + row_blocks(dec_ffn_out),
    ]
    bufs = [jnp.concatenate(parts, axis=0) for parts in chunk_parts]
    full = gather_all(lay, bufs)

    def cut(index, block):
        parts = chunk_parts[index]
        at = sum(p.shape[0] for p in parts[:block])
        rows = parts[block].shape[0]
        return full[index][:, :, at : at + rows].reshape(chips * rows, WIDE)

    def columns(index, first, count):
        return jnp.concatenate([cut(index, first + i) for i in range(count)], axis=1)

    def head_rows(index, first):
        rows = columns(index, first, 2)
        low, high = rows[:HALF // 2], rows[HALF // 2 :]
        keep = pick(low, high).reshape(chips // 2, 1, r, D)
        got = swap(pick(high, low)).reshape(chips // 2, 1, r, D)
        return pair(keep, got, 1).reshape(HALF, D)

    w_enc_in = columns(0, 0, 3)
    w_enc_out = head_rows(0, 3)
    w_enc_up = columns(1, 0, 4)
    w_enc_down = columns(1, 4, 2)
    w_dec_in = columns(2, 0, 3)
    w_rel = (
        cut(2, 3)
        .reshape(chips, r, 2, REL_HALF)
        .transpose(0, 2, 1, 3)
        .reshape(D, REL_HALF)
    )
    w_dec_out = head_rows(2, 4)
    w_cross_q = columns(3, 0, 1)
    w_cross_kv = columns(3, 1, 2)
    w_cross_out = head_rows(3, 3)
    w_dec_up = columns(4, 0, 4)
    w_dec_down = columns(4, 4, 2)

    vec_all = (
        cut(0, 5).reshape(chips, vec_rows, WIDE)[:, :vec_used].reshape(lay.devices, padded).astype(F32)
    )
    widths = [enc_biases.shape[0], enc_gains.shape[0], dec_biases.shape[0], dec_gains.shape[0]]
    starts = [0]
    for width in widths:
        starts.append(starts[-1] + width)
    v_enc_b, v_enc_g, v_dec_b, v_dec_g = [
        vec_all[:, starts[i] : starts[i + 1]].reshape(-1) for i in range(4)
    ]
    ebias = slices_of(v_enc_b, ENC_WIDTHS)
    egain = slices_of(v_enc_g, (D, D))
    dbias = slices_of(v_dec_b, DEC_WIDTHS)
    dgain = slices_of(v_dec_g, (D, D, D))

    def half_of(vector):
        parts = vector.reshape(2, -1)
        return pick(parts[0], parts[1])

    def hidden_of(vector):
        parts = vector.reshape(chips, 2, f)
        return pick(parts[:, 0], parts[:, 1]).reshape(-1)

    zero_half = jnp.zeros((HALF,), F32)
    lens = jnp.stack([pair(vec[None], vec_got[None], 0)[:, nvec - 2 + i] for i in range(2)])
    lens = lens.astype(F32).astype(jnp.int32)
    src_len, tgt_len = lens[0], lens[1]
    positions = jnp.arange(LEN, dtype=jnp.int32)
    src_valid = (positions[None, :] < src_len[:, None])[:, None, None, None, :]
    onehot = bucket_table(LEN, BUCKETS)

    def both(partial):
        low = partial.astype(BF)
        return low.astype(F32) + swap(low).astype(F32)

    x = pair(source[None], source_got[None], 0).reshape(2 * LEN, D)
    qkv_bias = jnp.concatenate([half_of(ebias[0]), zero_half, half_of(ebias[1])])
    eqkv = (dot(x, w_enc_in) + qkv_bias).astype(BF).reshape(2, LEN, 3, OWN_HEADS, HEAD)
    eq, ek, ev = eqkv[:, None, :, 0], eqkv[:, :, 1], eqkv[:, :, 2]
    ea, eprobs = attention_forward(eq, ek, ev, src_valid)
    ea = ea.reshape(2 * LEN, HALF)
    ez1 = x.astype(F32) + both(dot(ea, w_enc_out)) + ebias[2]
    eh1 = norm(ez1, egain[0], ebias[5])
    eh1_low = eh1.astype(BF)
    eu = dot(eh1_low, w_enc_up) + hidden_of(ebias[3])
    eg = gelu_exact(eu).astype(BF)
    ez2 = eh1 + both(dot(eg, w_enc_down)) + ebias[4]
    enc = norm(ez2, egain[1], ebias[6])
    enc_low = enc.astype(BF)

    rows = 2 * STREAMS * LEN
    y = pair(
        dec_in.transpose(1, 0, 2)[None], dec_in_got.reshape(LEN, STREAMS, D).transpose(1, 0, 2)[None], 0
    ).reshape(rows, D)
    dqkv_bias = jnp.concatenate([half_of(dbias[0]), zero_half, half_of(dbias[1])])
    dqkv = (dot(y, w_dec_in) + dqkv_bias).astype(BF)
    dqkv = dqkv.reshape(2, STREAMS, LEN, 3, OWN_HEADS, HEAD)
    rel = (dot(y, w_rel) + half_of(dbias[2])).reshape(2, STREAMS, LEN, OWN_HEADS, BUCKETS)
    da, dmain, down = ngram_forward(dqkv, rel, tgt_len, onehot)
    da = da.reshape(rows, HALF)
    dz1 = y.astype(F32) + both(dot(da, w_dec_out)) + dbias[3]
    dh1 = norm(dz1, dgain[0], dbias[9])
    dh1_low = dh1.astype(BF)
    cq = (dot(dh1_low, w_cross_q) + half_of(dbias[4])).astype(BF)
    cq = cq.reshape(2, STREAMS, LEN, OWN_HEADS, HEAD)
    ckv = dot(enc_low, w_cross_kv) + jnp.concatenate([zero_half, half_of(dbias[5])])
    ckv = ckv.astype(BF).reshape(2, LEN, 2, OWN_HEADS, HEAD)
    ck, cv = ckv[:, :, 0], ckv[:, :, 1]
    ca, cprobs = attention_forward(cq, ck, cv, src_valid)
    ca = ca.reshape(rows, HALF)
    dz2 = dh1 + both(dot(ca, w_cross_out)) + dbias[6]
    dh2 = norm(dz2, dgain[1], dbias[10])
    dh2_low = dh2.astype(BF)
    du = dot(dh2_low, w_dec_up) + hidden_of(dbias[7])
    dg = gelu_exact(du).astype(BF)
    dz3 = dh2 + both(dot(dg, w_dec_down)) + dbias[8]
    dec = norm(dz3, dgain[2], dbias[11])

    def own_rows_of(total, count):
        blocks = total[: count * 2 * r].reshape(count, 2, r, WIDE)
        keep = pick(blocks[:, 0], blocks[:, 1])
        got = swap(pick(blocks[:, 1], blocks[:, 0]))
        return pair(keep[:, None], got[:, None], 1)

    def chip_blocks(grad):
        n = grad.shape[1] // WIDE
        shape = (lay.ndp, lay.nz, grad.shape[0] // chips, WIDE)
        low = grad.astype(BF)
        return [low[:, WIDE * i : WIDE * i + WIDE].reshape(shape) for i in range(n)]

    def head_blocks(grad):
        parts = grad.astype(BF).reshape(chips // 2, 2, r, D)
        keep = pick(parts[:, 0], parts[:, 1])
        got = swap(pick(parts[:, 1], parts[:, 0]))
        return chip_blocks(pair(keep, got, 0).reshape(chips * r, D))

    def scatter(parts, previous):
        buf = jnp.concatenate(parts, axis=2)
        if previous is not None:
            buf = tie(buf, previous)
        first = scatter_dp(lay, buf)
        return scatter_z(lay, first), first

    def split_rows(total, sizes):
        at = 0
        result = []
        for size in sizes:
            result.append(total[at : at + size])
            at += size
        return result

    dcot_got = swap(dec_cot.reshape(LEN * STREAMS, D)).reshape(LEN, STREAMS, D)
    dcot = pair(dec_cot.transpose(1, 0, 2)[None], dcot_got.transpose(1, 0, 2)[None], 0)
    dcot = dcot.reshape(rows, D).astype(F32)
    gz3, ggain3, gnorm3 = norm_back(dz3, dgain[2], dcot)
    gf = gz3.astype(BF)
    g_down = dot_g(dg, gf)
    gu = gelu_back(du, dot_t(gf, w_dec_down)).astype(BF)
    g_up = dot_g(dh2_low, gu)
    total4, first4 = scatter(chip_blocks(g_up) + chip_blocks(g_down), None)
    gz2, ggain2, gnorm2 = norm_back(dz2, dgain[1], gz3 + both(dot_t(gu, w_dec_up)))
    gx = gz2.astype(BF)
    g_cross_out = dot_g(ca, gx)
    gca = dot_t(gx, w_cross_out).astype(BF).reshape(2, STREAMS, LEN, OWN_HEADS, HEAD)
    gcq, gck, gcv = attention_back(cq, ck, cv, cprobs, gca)
    gcq = gcq.reshape(rows, HALF)
    gckv = jnp.stack([gck, gcv], axis=2).reshape(2 * LEN, D)
    g_cross_q = dot_g(dh1_low, gcq)
    g_cross_kv = dot_g(enc_low, gckv)
    total3, first3 = scatter(
        chip_blocks(g_cross_q) + chip_blocks(g_cross_kv) + head_blocks(g_cross_out), first4
    )
    ecot_got = swap(enc_cot)
    ecot = pair(enc_cot[None], ecot_got[None], 0).reshape(2 * LEN, D).astype(F32)
    genc = ecot + both(dot_t(gckv, w_cross_kv))
    gz1, ggain1, gnorm1 = norm_back(dz1, dgain[0], gz2 + both(dot_t(gcq, w_cross_q)))
    go = gz1.astype(BF)
    g_dec_out = dot_g(da, go)
    gda = dot_t(go, w_dec_out).astype(BF).reshape(2, STREAMS, LEN, OWN_HEADS, HEAD)
    gqkv, grel = ngram_back(dqkv, dmain, down, onehot, gda)
    gqkv = gqkv.reshape(rows, 3 * HALF)
    grel = grel.reshape(rows, REL_HALF)
    g_dec_in = dot_g(y, gqkv)
    g_rel = dot_g(y, grel)
    rel_block = (
        g_rel.astype(BF)
        .reshape(chips, 2, r, REL_HALF)
        .transpose(0, 2, 1, 3)
        .reshape(lay.ndp, lay.nz, r, WIDE)
    )
    total2, first2 = scatter(chip_blocks(g_dec_in) + [rel_block] + head_blocks(g_dec_out), first3)

    def own_sequence(partial, count):
        parts = partial.reshape(2, count, D)
        keep = pick(parts[0], parts[1])
        return keep + swap(pick(parts[1], parts[0]).astype(BF)).astype(F32)

    def own_part(values, count):
        parts = values.reshape(2, count, D)
        return pick(parts[0], parts[1])

    dec_rows = STREAMS * LEN
    g_dec_input = own_part(gz1, dec_rows) + own_sequence(
        dot_t(gqkv, w_dec_in) + dot_t(grel, w_rel), dec_rows
    )

    def widen(vector):
        zeros = jnp.zeros_like(vector)
        return pick(jnp.concatenate([vector, zeros]), jnp.concatenate([zeros, vector]))

    def widen_hidden(vector):
        parts = vector.reshape(chips, 1, f)
        zeros = jnp.zeros_like(parts)
        return pick(
            jnp.concatenate([parts, zeros], axis=1), jnp.concatenate([zeros, parts], axis=1)
        ).reshape(-1)

    column_sums = col_sum(gqkv)
    dec_vec = jnp.concatenate(
        [
            widen(column_sums[:HALF]),
            widen(column_sums[2 * HALF :]),
            widen(col_sum(grel)),
            0.5 * col_sum(go),
            widen(col_sum(gcq)),
            widen(col_sum(gckv)[HALF:]),
            0.5 * col_sum(gx),
            widen_hidden(col_sum(gu)),
            0.5 * col_sum(gf),
            0.5 * gnorm1,
            0.5 * gnorm2,
            0.5 * gnorm3,
            0.5 * ggain1,
            0.5 * ggain2,
            0.5 * ggain3,
        ]
    )

    gz2e, eggain2, egnorm2 = norm_back(ez2, egain[1], genc)
    gfe = gz2e.astype(BF)
    ge_down = dot_g(eg, gfe)
    gue = gelu_back(eu, dot_t(gfe, w_enc_down)).astype(BF)
    ge_up = dot_g(eh1_low, gue)
    total1, first1 = scatter(chip_blocks(ge_up) + chip_blocks(ge_down), first2)
    gz1e, eggain1, egnorm1 = norm_back(ez1, egain[0], gz2e + both(dot_t(gue, w_enc_up)))
    goe = gz1e.astype(BF)
    ge_out = dot_g(ea, goe)
    gae = dot_t(goe, w_enc_out).astype(BF).reshape(2, 1, LEN, OWN_HEADS, HEAD)
    geq, gek, gev = attention_back(eq, ek, ev, eprobs, gae)
    geqkv = jnp.stack([geq[:, 0], gek, gev], axis=2).reshape(2 * LEN, 3 * HALF)
    ge_in = dot_g(x, geqkv)
    total0, first0 = scatter(chip_blocks(ge_in) + head_blocks(ge_out), first1)
    g_source = own_part(gz1e, LEN) + own_sequence(dot_t(geqkv, w_enc_in), LEN)
    ecolumn_sums = col_sum(geqkv)
    enc_vec = jnp.concatenate(
        [
            widen(ecolumn_sums[:HALF]),
            widen(ecolumn_sums[2 * HALF :]),
            0.5 * col_sum(goe),
            widen_hidden(col_sum(gue)),
            0.5 * col_sum(gfe),
            0.5 * egnorm1,
            0.5 * egnorm2,
            0.5 * eggain1,
            0.5 * eggain2,
        ]
    )
    me = lay.dp * lay.nf + lax.axis_index("fsdp")

    def own_slice(vector):
        return take(vector.reshape(lay.devices, -1), me)

    dec_vec = lax.psum(dec_vec, ("dp", "fsdp"))
    enc_vec = lax.psum(enc_vec, ("dp", "fsdp"))
    nb = sum(ENC_WIDTHS)
    g_enc_biases, g_enc_gains = own_slice(enc_vec[:nb]), own_slice(enc_vec[nb:])
    nb = sum(DEC_WIDTHS)
    g_dec_biases, g_dec_gains = own_slice(dec_vec[:nb]), own_slice(dec_vec[nb:])

    def in_rows(blocks):
        return blocks.transpose(2, 0, 1, 3).reshape(r, -1)

    def up_rows(blocks):
        per = WIDE // f
        return blocks.reshape(4, 2, r, per, f).transpose(2, 0, 3, 1, 4).reshape(r, FF)

    def side(low, high):
        return jnp.concatenate([low, high], axis=1)

    t0 = split_rows(total0, [6 * r, r, r])
    o_enc_in, o_enc_out = in_rows(own_rows_of(t0[0], 3)), side(t0[1], t0[2])
    t1 = split_rows(total1, [8 * r, f, f])
    o_enc_up, o_enc_down = up_rows(own_rows_of(t1[0], 4)), side(t1[1], t1[2])
    t2 = split_rows(total2, [6 * r, r, r, r])
    o_dec_in, o_dec_out = in_rows(own_rows_of(t2[0], 3)), side(t2[2], t2[3])
    relp = t2[1].reshape(r, 2, REL_HALF)
    rel_keep = pick(relp[:, 0], relp[:, 1])
    o_rel = pair(rel_keep, swap(pick(relp[:, 1], relp[:, 0])), 1)
    t3 = split_rows(total3, [2 * r, 4 * r, r, r])
    o_cross_q = in_rows(own_rows_of(t3[0], 1))
    o_cross_kv = in_rows(own_rows_of(t3[1], 2))
    o_cross_out = side(t3[2], t3[3])
    t4 = split_rows(total4, [8 * r, f, f])
    o_dec_up, o_dec_down = up_rows(own_rows_of(t4[0], 4)), side(t4[1], t4[2])

    return (
        own_part(enc_low, LEN),
        own_part(dec.astype(BF), dec_rows).reshape(STREAMS, LEN, D).transpose(1, 0, 2),
        g_source,
        g_dec_input.reshape(STREAMS, LEN, D).transpose(1, 0, 2),
        o_enc_in,
        o_enc_out,
        o_enc_up,
        o_enc_down,
        g_enc_gains,
        g_enc_biases,
        o_dec_in,
        o_rel,
        o_dec_out,
        o_cross_q,
        o_cross_kv,
        o_cross_out,
        o_dec_up,
        o_dec_down,
        g_dec_gains,
        g_dec_biases,
    )


BUDGET = 58 * 1024 * 1024
PIECES = 4
HBM_RATE = 3.0e6


def run(body, grid, ins, outs, scratch=(), us=5):
    arrays = [a for a, s in ins]
    return pl.pallas_call(
        body,
        grid=(grid,),
        in_specs=[s for a, s in ins],
        out_specs=[s for a, s in outs],
        out_shape=[a for a, s in outs],
        scratch_shapes=list(scratch),
        compiler_params=pltpu.CompilerParams(vmem_limit_bytes=BUDGET),
        cost_estimate=pl.CostEstimate(
            flops=0, bytes_accessed=int(us * HBM_RATE), transcendentals=0
        ),
    )(*arrays)


def full(array):
    zeros = (0,) * array.ndim
    return array, pl.BlockSpec(array.shape, lambda t: zeros, pipeline_mode=pl.Buffered(1))


def small(array):
    return array, pl.BlockSpec(memory_space=pltpu.SMEM)


def out_full(shape, dtype):
    zeros = (0,) * len(shape)
    return jax.ShapeDtypeStruct(shape, dtype), pl.BlockSpec(shape, lambda t: zeros)


def out_cols(rows, cols, dtype, index):
    return (
        jax.ShapeDtypeStruct((rows, cols), dtype),
        pl.BlockSpec((rows, WIDE), lambda t: (0, index(t))),
    )


def in_cols(array, index, width=WIDE):
    return array, pl.BlockSpec((array.shape[0], width), lambda t: (0, index(t)))


def blocks(pieces, rows, index):
    return [
        (p, pl.BlockSpec((4, rows, WIDE), lambda t: (0, index(t), 0))) for p in pieces
    ]


def wide_blocks(pieces, index):
    return [(p, pl.BlockSpec((4,) + p.shape[1:2] + (WIDE,), lambda t: (0, 0, index(t)))) for p in pieces]


def assemble(refs, scr, place):
    for i in range(4):
        scr[jnp.bitwise_xor(place[0], i)] = refs[i][...]


def weight_scratch(rows, width=WIDE):
    return pltpu.VMEM((4, 4, rows, width), BF)


def matrix_of(scr):
    a, b, c, d = scr.shape
    return scr[...].reshape(a * b * c, d)


def pick_matrix(parity):
    i = lax.broadcasted_iota(jnp.int32, (HALF, HALF // 2), 0)
    j = lax.broadcasted_iota(jnp.int32, (HALF, HALF // 2), 1)
    from_row = ((j >> 5) << 6) + (parity << 5) + (j & 31)
    return jnp.where(i == from_row, 1.0, 0.0).astype(BF)


def head_masks():
    lane = lax.broadcasted_iota(jnp.int32, (1, 128), 1)
    first = jnp.where(lane < HEAD, 1.0, 0.0)
    return first.astype(BF), (1.0 - first).astype(BF)


def first_lanes(rows):
    return lax.broadcasted_iota(jnp.int32, (rows, 128), 1) < HEAD


def soft_rows(scores):
    top = jnp.max(scores, axis=-1, keepdims=True)
    raised = jnp.exp(scores - top)
    return raised * (1.0 / jnp.sum(raised, axis=-1, keepdims=True))


def masked_probs(queries, keys, count):
    scores = dot_t(queries, keys) * SCALE
    column = lax.broadcasted_iota(jnp.int32, scores.shape, 1)
    return soft_rows(jnp.where(column < count, scores, MASKED))


def attend(q, k, v, count):
    rows = q.shape[0]
    out = []
    for mask in head_masks():
        probs = masked_probs(q * mask, k, count).astype(BF)
        out.append(dot(probs, v))
    return jnp.where(first_lanes(rows), out[0], out[1]).astype(BF)


def attend_back(q, k, v, g, count):
    gq, gk, gv = [], 0.0, 0.0
    for mask in head_masks():
        qm, gm = q * mask, g * mask
        probs = masked_probs(qm, k, count)
        gp = dot_t(gm, v)
        ds = (probs * (gp - jnp.sum(probs * gp, axis=-1, keepdims=True))).astype(BF)
        gq.append(dot(ds, k))
        gk = gk + dot_g(ds, qm)
        gv = gv + dot_g(probs.astype(BF), gm)
    gq = jnp.where(first_lanes(q.shape[0]), gq[0], gq[1]) * SCALE
    return gq.astype(BF), (gk * SCALE).astype(BF), gv.astype(BF)


def split_parity(heads, place, keep, send):
    core = place[2]
    keep[...] = dot(heads[...], pick_matrix(core)).astype(BF)
    send[...] = dot(heads[...], pick_matrix(1 - core)).astype(BF)


def join_parity(keep, got, place, heads):
    core = place[2]
    heads[...] = (
        dot_t(keep[...], pick_matrix(core)) + dot_t(got[...], pick_matrix(1 - core))
    ).astype(BF)


def enc_attention(place, x, bias, pieces):
    rows = x.shape[0]

    def body(place, x, bias, *refs):
        w, (qkv, keep, send, scr, heads) = refs[:PIECES], refs[PIECES:]
        t = pl.program_id(0)
        assemble(w, scr, place)
        qkv[:, pl.ds(t * WIDE, WIDE)] = (dot(x[...], matrix_of(scr)) + bias[...]).astype(BF)

        @pl.when(t == 2)
        def _():
            for s in range(2):
                r = slice(s * LEN, s * LEN + LEN)
                for j in range(4):
                    c = [slice(HALF * i + 128 * j, HALF * i + 128 * j + 128) for i in range(3)]
                    heads[r, c[0]] = attend(qkv[r, c[0]], qkv[r, c[1]], qkv[r, c[2]], place[3 + s])
            split_parity(heads, place, keep, send)

    return run(
        body,
        3,
        [small(place), full(x), in_cols(bias, lambda t: t)] + blocks(pieces, 64, lambda t: t),
        [
            out_full((rows, 3 * HALF), BF),
            out_full((rows, HALF // 2), BF),
            out_full((rows, HALF // 2), BF),
        ],
        [weight_scratch(64), pltpu.VMEM((rows, HALF), BF)],
        us=10,
    )


def out_projection(place, keep, got, pieces):
    rows = keep.shape[0]

    def body(place, keep, got, *refs):
        w, (out, scr) = refs[:PIECES], refs[PIECES:]
        assemble(w, scr, place)
        core = place[2]
        mine = scr[pl.ds(2 * core, 2)].reshape(HALF // 2, WIDE)
        theirs = scr[pl.ds(2 - 2 * core, 2)].reshape(HALF // 2, WIDE)
        out[...] = (dot(keep[...], mine) + dot(got[...], theirs)).astype(BF)

    return run(
        body,
        2,
        [small(place), full(keep), full(got)] + blocks(pieces, 32, lambda t: 6 + t),
        [out_cols(rows, D, BF, lambda t: t)],
        [weight_scratch(32)],
        us=3,
    )[0]


def stats(v):
    centered = v - jnp.mean(v, axis=-1, keepdims=True)
    inverse = lax.rsqrt(jnp.mean(centered * centered, axis=-1, keepdims=True) + EPSILON)
    return centered * inverse, inverse


def each_tile(rows, tile, step):
    def loop(m, carry):
        step(pl.multiple_of(m * tile, tile))
        return carry

    lax.fori_loop(0, rows // tile, loop, 0)


def norm_tiles(rows, base, affine, own, other, bias, gain, shift, unit_out, inv_out, low_out, at=0):
    def step(r):
        here = pl.ds(r, LEN)
        v = base[here].astype(F32)
        if affine is not None:
            v = v * affine[0] + affine[1]
        there = pl.ds(r + at, LEN)
        v = v + (own[there].astype(F32) + other[there].astype(F32)) + bias
        unit, inverse = stats(v)
        unit_out[here] = unit
        inv_out[here] = jnp.broadcast_to(inverse, (LEN, 128))
        low_out[here] = (unit * gain + shift).astype(BF)

    each_tile(rows, LEN, step)


ROOT_HALF = math.sqrt(0.5)
ROOT_TWO_PI = math.sqrt(0.5 / math.pi)


def gelu_pair(u):
    phi = 0.5 + 0.5 * lax.erf(u * ROOT_HALF)
    return u * phi, phi + u * (jnp.exp(-0.5 * u * u) * ROOT_TWO_PI)


def ffn_forward(place, base, affine, own, other, vecs, hidden_bias, up_pieces, down_pieces):
    rows = base.shape[0]
    hidden = hidden_bias.shape[1]
    ups = hidden // WIDE
    tile = 256

    def body(place, base, own, other, vecs, hb, *refs):
        wu, wd = refs[:PIECES], refs[PIECES : 2 * PIECES]
        unit, inv, low, g, gp, part, scr_u, scr_d, acts = refs[2 * PIECES :]
        t = pl.program_id(0)

        @pl.when(t == 0)
        def _():
            aff = (vecs[0:1], vecs[1:2]) if affine else None
            norm_tiles(
                rows, base, aff, own, other, vecs[2:3], vecs[3:4], vecs[4:5], unit, inv, low
            )

        @pl.when(t < ups)
        def _():
            assemble(wu, scr_u, place)
            w = matrix_of(scr_u)

            def step(r):
                here = pl.ds(r, tile)
                a, b = gelu_pair(dot(low[here], w) + hb[...])
                a = a.astype(BF)
                g[here] = a
                acts[here, pl.ds(t * WIDE, WIDE)] = a
                gp[here] = b.astype(BF)

            each_tile(rows, tile, step)

        @pl.when(t >= ups)
        def _():
            assemble(wd, scr_d, place)
            part[...] = dot(acts[...], matrix_of(scr_d)).astype(BF)

    up = lambda t: jnp.minimum(t, ups - 1)
    down = lambda t: jnp.maximum(t - ups, 0)
    return run(
        body,
        ups + 2,
        [small(place), full(base), full(own), full(other), full(vecs), in_cols(hidden_bias, up)]
        + blocks(up_pieces, 64, up)
        + wide_blocks(down_pieces, down),
        [
            out_full((rows, D), F32),
            out_full((rows, 128), F32),
            out_full((rows, D), BF),
            out_cols(rows, hidden, BF, up),
            out_cols(rows, hidden, BF, up),
            out_cols(rows, D, BF, down),
        ],
        [weight_scratch(64), weight_scratch(128), pltpu.VMEM((rows, hidden), BF)],
        us=20 if rows > 256 else 11,
    )


def distance_buckets(reverse):
    row = lax.broadcasted_iota(jnp.int32, (128, 128), 0) & (BUCKETS - 1)
    lane = lax.broadcasted_iota(jnp.int32, (128, 128), 1)
    distance = ((lane + 1) if reverse else (128 - lane)) & 127
    bucket = jnp.zeros((128, 128), jnp.int32)
    for target in range(1, BUCKETS):
        at = 1
        while bucket_value(at, BUCKETS) < target:
            at += 1
        bucket = bucket + jnp.where(distance >= at, 1, 0)
    return jnp.where(bucket == row, 1.0, 0.0).astype(BF)


def skew(values):
    parts = [values[128 * n : 128 * n + 128] for n in range(values.shape[0] // 128)]
    return jnp.concatenate(
        [pltpu.roll(part, 0, 1, stride=1, stride_axis=0) for part in parts], axis=0
    )


def mirror():
    row = lax.broadcasted_iota(jnp.int32, (128, 128), 0)
    lane = lax.broadcasted_iota(jnp.int32, (128, 128), 1)
    return jnp.where(row + lane == 127, 1.0, 0.0).astype(BF)


def quarter_mask(h):
    lane = lax.broadcasted_iota(jnp.int32, (1, 128), 1)
    return jnp.where((lane >> 5) == h, 1.0, 0.0).astype(BF)


def ngram_probs(qm, prod, k0, rel_high, rel_low, table, count, h, first):
    mask = quarter_mask(h % 4)
    turned = dot(rel_high * mask, table) + dot(rel_low * mask, table)
    scores = dot_t(qm, k0) * SCALE + skew(turned)
    row = lax.broadcasted_iota(jnp.int32, scores.shape, 0)
    column = lax.broadcasted_iota(jnp.int32, scores.shape, 1)
    token = row & (LEN - 1)
    reach = jnp.where(row < LEN, token, token - 1)
    scores = jnp.where((column <= reach) & (column < count), scores, MASKED)
    own = jnp.sum(prod * first, axis=-1, keepdims=True) * SCALE + turned[:, 0:1]
    main = lax.broadcasted_iota(jnp.int32, own.shape, 0) < LEN
    own = jnp.where(main, 2.0 * MASKED, own)
    top = jnp.maximum(jnp.max(scores, axis=-1, keepdims=True), own)
    raised = jnp.exp(scores - top)
    own = jnp.exp(own - top)
    scale = 1.0 / (jnp.sum(raised, axis=-1, keepdims=True) + own)
    return raised * scale, own * scale


def split_high(values):
    high = values.astype(BF)
    return high, (values - high.astype(F32)).astype(BF)


def half_rows(rows):
    first = jnp.where(lax.broadcasted_iota(jnp.int32, (rows, 128), 1) < HEAD, 1.0, 0.0)
    return first, 1.0 - first


def ngram_attention(place, y, bias, rel_bias, pieces):
    rows = y.shape[0]
    span = STREAMS * LEN

    def body(place, y, bias, rbias, *refs):
        w, wr = refs[:PIECES], refs[PIECES : 2 * PIECES]
        qkv, rel, keep, send, scr, scr_r, heads, table = refs[2 * PIECES :]
        t = pl.program_id(0)

        @pl.when(t < 3)
        def _():
            assemble(w, scr, place)
            qkv[:, pl.ds(pl.multiple_of(t * WIDE, WIDE), WIDE)] = (
                dot(y[...], matrix_of(scr)) + bias[...]
            ).astype(BF)

        @pl.when(t == 3)
        def _():
            assemble_rel(wr, scr_r, place)
            rel[...] = dot(y[...], scr_r[...].reshape(D, REL_HALF)) + rbias[...]
            table[...] = distance_buckets(False)
            lanes = half_rows(span)

            def step(s, carry):
                r = pl.ds(pl.multiple_of(s * span, span), span)
                r0 = pl.ds(pl.multiple_of(s * span, span), LEN)
                count = place[5 + s]
                for j in range(4):
                    c = [slice(HALF * i + 128 * j, HALF * i + 128 * j + 128) for i in range(3)]
                    q, k, v = qkv[r, c[0]], qkv[r, c[1]], qkv[r, c[2]]
                    k0, v0 = qkv[r0, c[1]], qkv[r0, c[2]]
                    high, low = split_high(rel[r, 128 * (j // 2) : 128 * (j // 2) + 128])
                    prod = q.astype(F32) * k.astype(F32)
                    out = []
                    for i, mask in enumerate(head_masks()):
                        probs, own = ngram_probs(
                            q * mask, prod, k0, high, low, table[...], count, 2 * j + i, lanes[i]
                        )
                        own = own.astype(BF).astype(F32)
                        out.append(dot(probs.astype(BF), v0) + own * v.astype(F32))
                    heads[r, c[0]] = jnp.where(first_lanes(span), out[0], out[1]).astype(BF)
                return carry

            lax.fori_loop(0, 2, step, 0)
            split_parity(heads, place, keep, send)

    third = lambda t: jnp.minimum(t, 2)
    return run(
        body,
        4,
        [small(place), full(y), in_cols(bias, third), full(rel_bias)]
        + blocks(pieces, 64, third)
        + blocks(pieces, 32, lambda t: 8),
        [
            out_full((rows, 3 * HALF), BF),
            out_full((rows, REL_HALF), F32),
            out_full((rows, HALF // 2), BF),
            out_full((rows, HALF // 2), BF),
        ],
        [
            weight_scratch(64),
            pltpu.VMEM((4, 4, 2, 32, REL_HALF), BF),
            pltpu.VMEM((rows, HALF), BF),
            pltpu.VMEM((128, 128), BF),
        ],
        us=19,
    )


def assemble_rel(refs, scr, place):
    for i in range(4):
        block = refs[i][...]
        at = jnp.bitwise_xor(place[0], i)
        scr[at, :, 0] = block[:, :, :REL_HALF]
        scr[at, :, 1] = block[:, :, REL_HALF:]


def cross_forward(place, y, own, other, vecs, eunit, evecs, eown, eother, q_bias, kv_bias, pieces):
    rows, mem = y.shape[0], eunit.shape[0]
    span = STREAMS * LEN

    def body(place, y, own, other, vecs, eunit, evecs, eown, eother, qb, kvb, *refs):
        w = refs[:PIECES]
        unit, inv, low, eunit2, einv2, elow, q, kv, keep, send, scr, heads = refs[PIECES:]
        t = pl.program_id(0)
        assemble(w, scr, place)

        @pl.when(t == 0)
        def _():
            norm_tiles(
                rows, y, None, own, other, vecs[0:1], vecs[1:2], vecs[2:3], unit, inv, low
            )
            norm_tiles(
                mem,
                eunit,
                (evecs[0:1], evecs[1:2]),
                eown,
                eother,
                evecs[2:3],
                evecs[3:4],
                evecs[4:5],
                eunit2,
                einv2,
                elow,
            )
            q[...] = (dot(low[...], matrix_of(scr)) + qb[...]).astype(BF)

        @pl.when(t > 0)
        def _():
            at = pl.multiple_of((t - 1) * WIDE, WIDE)
            kv[:, pl.ds(at, WIDE)] = (dot(elow[...], matrix_of(scr)) + kvb[...]).astype(BF)

        @pl.when(t == 2)
        def _():
            for s in range(2):
                r = slice(s * span, s * span + span)
                m = slice(s * LEN, s * LEN + LEN)
                for j in range(4):
                    c = slice(128 * j, 128 * j + 128)
                    c2 = slice(HALF + 128 * j, HALF + 128 * j + 128)
                    heads[r, c] = attend(q[r, c], kv[m, c], kv[m, c2], place[3 + s])
            split_parity(heads, place, keep, send)

    return run(
        body,
        3,
        [small(place)]
        + [full(a) for a in (y, own, other, vecs, eunit, evecs, eown, eother, q_bias)]
        + [in_cols(kv_bias, lambda t: jnp.maximum(t - 1, 0))]
        + blocks(pieces, 64, lambda t: t),
        [
            out_full((rows, D), F32),
            out_full((rows, 128), F32),
            out_full((rows, D), BF),
            out_full((mem, D), F32),
            out_full((mem, 128), F32),
            out_full((mem, D), BF),
            out_full((rows, HALF), BF),
            out_full((mem, D), BF),
            out_full((rows, HALF // 2), BF),
            out_full((rows, HALF // 2), BF),
        ],
        [weight_scratch(64), pltpu.VMEM((rows, HALF), BF)],
        us=15,
    )


def fold(values):
    return jnp.sum(values.reshape(values.shape[0] // 8, 8, values.shape[1]), axis=0)


def norm_back_tile(total, unit, inverse, gain):
    scaled = total * gain
    one = jnp.mean(scaled, axis=-1, keepdims=True)
    two = jnp.mean(scaled * unit, axis=-1, keepdims=True)
    return inverse * (scaled - one - unit * two)


def ffn_back(place, final, total_ins, unit_ins, vecs, gp, up_pieces, down_pieces):
    rows, hidden = gp.shape
    ups = hidden // WIDE
    n_total, n_unit = len(total_ins), len(unit_ins)
    mine = rows // 2

    def body(place, vecs, gp, *refs):
        at = 0

        def take_refs(n):
            nonlocal at
            at += n
            return refs[at - n : at]

        tot, uni = take_refs(n_total), take_refs(n_unit)
        wu, wd = take_refs(PIECES), take_refs(PIECES)
        outs = take_refs(1) if final else ()
        gz, gf, gu, part, s_gain, s_shift, s_gf, s_gu = take_refs(8)
        scr_u, scr_d, all_u, scr_all_u, acc = refs[at:]
        t = pl.program_id(0)

        @pl.when(t == 0)
        def _():
            acc[...] = jnp.zeros_like(acc)

            def step(r):
                here = pl.ds(r, LEN)
                if final:
                    v = uni[0][here] * vecs[0:1] + vecs[1:2]
                    v = v + (uni[1][here].astype(F32) + uni[2][here].astype(F32)) + vecs[2:3]
                    unit, inverse = stats(v)

                    @pl.when((r >= mine) == (place[2] == 1))
                    def _():
                        to = pl.ds(pl.multiple_of(r - mine * place[2], LEN), LEN)
                        outs[0][to] = (unit * vecs[3:4] + vecs[4:5]).astype(BF)

                else:
                    unit, inverse = uni[0][here], uni[1][here, 0:1]
                total = tot[0][here].astype(F32)
                if n_total > 1:
                    there = pl.ds(r + tot[1].shape[0] - rows, LEN)
                    total = total + (tot[1][there].astype(F32) + tot[2][there].astype(F32))
                acc[0:8] += fold(total * unit)
                acc[8:16] += fold(total)
                back = norm_back_tile(total, unit, inverse, vecs[3:4])
                gz[here] = back
                low = back.astype(BF)
                gf[here] = low
                acc[16:24] += fold(low.astype(F32))

            each_tile(rows, LEN, step)
            s_gain[...] = jnp.sum(acc[0:8], axis=0, keepdims=True)
            s_shift[...] = jnp.sum(acc[8:16], axis=0, keepdims=True)
            s_gf[...] = jnp.sum(acc[16:24], axis=0, keepdims=True)

        @pl.when(t < 2)
        def _():
            assemble(wd, scr_d.at[t], place)

        @pl.when(t >= 2)
        def _():
            b = t - 2
            assemble(wu, scr_u, place)
            scr_all_u[:, pl.ds(pl.multiple_of(b * WIDE, WIDE), WIDE)] = matrix_of(scr_u)
            w0 = scr_d[0, b].reshape(WIDE, WIDE)
            w1 = scr_d[1, b].reshape(WIDE, WIDE)
            back = dot_t(gf[:, :WIDE], w0) + dot_t(gf[:, WIDE:], w1)
            low = (back * gp[...].astype(F32)).astype(BF)
            gu[...] = low
            all_u[:, pl.ds(pl.multiple_of(b * WIDE, WIDE), WIDE)] = low
            s_gu[...] = jnp.sum(fold(low.astype(F32)), axis=0, keepdims=True)

        @pl.when(t == ups + 1)
        def _():
            part[...] = dot_t(all_u[...], scr_all_u[...]).astype(BF)

    up = lambda t: jnp.maximum(t - 2, 0)
    down = lambda t: jnp.minimum(t, 1)
    outs = [out_full((mine, D), BF)] if final else []
    outs += [
        out_full((rows, D), F32),
        out_full((rows, D), BF),
        out_cols(rows, hidden, BF, up),
        out_full((rows, D), BF),
        out_full((1, D), F32),
        out_full((1, D), F32),
        out_full((1, D), F32),
        out_cols(1, hidden, F32, up),
    ]
    return run(
        body,
        ups + 2,
        [small(place), full(vecs), in_cols(gp, up)]
        + [full(a) for a in total_ins]
        + [full(a) for a in unit_ins]
        + blocks(up_pieces, 64, up)
        + wide_blocks(down_pieces, down),
        outs,
        [
            weight_scratch(64),
            pltpu.VMEM((2, 4, 4, 128, WIDE), BF),
            pltpu.VMEM((rows, hidden), BF),
            pltpu.VMEM((D, hidden), BF),
            pltpu.VMEM((24, D), F32),
        ],
        us=21 if rows > 256 else 12,
    )


def branch_back(place, resid, own, other, unit, inv, gain, pieces):
    rows = resid.shape[0]

    def body(place, resid, own, other, unit, inv, gain, *refs):
        w = refs[:PIECES]
        gz, gx, keep, send, s_gain, s_shift, s_gx, scr, total_out, acc = refs[PIECES:]
        t = pl.program_id(0)
        assemble(w, scr, place)

        @pl.when(t == 0)
        def _():
            acc[...] = jnp.zeros_like(acc)

            def step(r):
                here = pl.ds(r, LEN)
                total = resid[here] + (own[here].astype(F32) + other[here].astype(F32))
                acc[0:8] += fold(total * unit[here])
                acc[8:16] += fold(total)
                back = norm_back_tile(total, unit[here], inv[here, 0:1], gain[...])
                gz[here] = back
                low = back.astype(BF)
                gx[here] = low
                acc[16:24] += fold(low.astype(F32))

            each_tile(rows, LEN, step)
            s_gain[...] = jnp.sum(acc[0:8], axis=0, keepdims=True)
            s_shift[...] = jnp.sum(acc[8:16], axis=0, keepdims=True)
            s_gx[...] = jnp.sum(acc[16:24], axis=0, keepdims=True)
            total_out[...] = dot_t(gx[:, :WIDE], matrix_of(scr))

        @pl.when(t == 1)
        def _():
            total_out[...] += dot_t(gx[:, WIDE:], matrix_of(scr))
            core = place[2]
            quarter = HALF // 2
            keep[...] = total_out[:, pl.ds(pl.multiple_of(quarter * core, 128), quarter)].astype(BF)
            send[...] = total_out[
                :, pl.ds(pl.multiple_of(quarter * (1 - core), 128), quarter)
            ].astype(BF)

    return run(
        body,
        2,
        [small(place)]
        + [full(a) for a in (resid, own, other, unit, inv, gain)]
        + blocks(pieces, 32, lambda t: 6 + t),
        [
            out_full((rows, D), F32),
            out_full((rows, D), BF),
            out_full((rows, HALF // 2), BF),
            out_full((rows, HALF // 2), BF),
            out_full((1, D), F32),
            out_full((1, D), F32),
            out_full((1, D), F32),
        ],
        [weight_scratch(32), pltpu.VMEM((rows, HALF), F32), pltpu.VMEM((24, D), F32)],
        us=10 if rows > 256 else 5,
    )


def column_sums(out, values):
    out[...] = jnp.sum(fold(values.astype(F32)), axis=0, keepdims=True)


def cross_back(place, q, kv, keep, got, pieces):
    rows, mem = q.shape[0], kv.shape[0]
    span = STREAMS * LEN

    def body(place, q, kv, keep, got, *refs):
        w = refs[:PIECES]
        gq, gkv, part, s_gq, s_gkv, scr, g, acc = refs[PIECES:]
        t = pl.program_id(0)
        assemble(w, scr, place)

        @pl.when(t == 0)
        def _():
            join_parity(keep, got, place, g)
            for s in range(2):
                r = slice(s * span, s * span + span)
                m = slice(s * LEN, s * LEN + LEN)
                for j in range(4):
                    c = slice(128 * j, 128 * j + 128)
                    c2 = slice(HALF + 128 * j, HALF + 128 * j + 128)
                    gq[r, c], gkv[m, c], gkv[m, c2] = attend_back(
                        q[r, c], kv[m, c], kv[m, c2], g[r, c], place[3 + s]
                    )
            column_sums(s_gq, gq[...])
            column_sums(s_gkv, gkv[...])
            part[:rows] = dot_t(gq[...], matrix_of(scr)).astype(BF)

        @pl.when(t == 1)
        def _():
            acc[...] = dot_t(gkv[:, :HALF], matrix_of(scr))

        @pl.when(t == 2)
        def _():
            part[rows:] = (acc[...] + dot_t(gkv[:, HALF:], matrix_of(scr))).astype(BF)

    return run(
        body,
        3,
        [small(place), full(q), full(kv), full(keep), full(got)]
        + blocks(pieces, 64, lambda t: t),
        [
            out_full((rows, HALF), BF),
            out_full((mem, D), BF),
            out_full((rows + mem, D), BF),
            out_full((1, HALF), F32),
            out_full((1, D), F32),
        ],
        [weight_scratch(64), pltpu.VMEM((rows, HALF), BF), pltpu.VMEM((mem, D), F32)],
        us=14,
    )


def input_grads(place, gz, parts, keep, send):
    rows = gz.shape[0] // 2
    core = place[2]
    here = pl.ds(pl.multiple_of(rows * core, LEN), rows)
    there = pl.ds(pl.multiple_of(rows * (1 - core), LEN), rows)
    total = gz[here]
    for g, w in parts:
        total = total + dot_t(g[here], w)
    keep[...] = total
    total = 0.0
    for g, w in parts:
        total = total + dot_t(g[there], w)
    send[...] = total.astype(BF)


def enc_attention_back(place, qkv, keep, got, gz, pieces):
    rows = qkv.shape[0]

    def body(place, qkv, keep, got, gz, *refs):
        w = refs[:PIECES]
        gqkv, out, send, sums, scr, g, win = refs[PIECES:]
        t = pl.program_id(0)
        assemble(w, scr, place)
        win[:, pl.ds(pl.multiple_of(t * WIDE, WIDE), WIDE)] = matrix_of(scr)

        @pl.when(t == 0)
        def _():
            join_parity(keep, got, place, g)
            for s in range(2):
                r = slice(s * LEN, s * LEN + LEN)
                for j in range(4):
                    c = [slice(HALF * i + 128 * j, HALF * i + 128 * j + 128) for i in range(3)]
                    gqkv[r, c[0]], gqkv[r, c[1]], gqkv[r, c[2]] = attend_back(
                        qkv[r, c[0]], qkv[r, c[1]], qkv[r, c[2]], g[r, c[0]], place[3 + s]
                    )
            column_sums(sums, gqkv[...])

        @pl.when(t == 2)
        def _():
            input_grads(place, gz, [(gqkv, win[...])], out, send)

    return run(
        body,
        3,
        [small(place), full(qkv), full(keep), full(got), full(gz)]
        + blocks(pieces, 64, lambda t: t),
        [
            out_full((rows, 3 * HALF), BF),
            out_full((rows // 2, D), F32),
            out_full((rows // 2, D), BF),
            out_full((1, 3 * HALF), F32),
        ],
        [weight_scratch(64), pltpu.VMEM((rows, HALF), BF), pltpu.VMEM((D, 3 * HALF), BF)],
        us=13,
    )


def ngram_back_kernel(place, qkv, rel, keep, got, gz, pieces):
    rows = qkv.shape[0]
    span = STREAMS * LEN

    def body(place, qkv, rel, keep, got, gz, *refs):
        w, wr = refs[:PIECES], refs[PIECES : 2 * PIECES]
        gqkv, grel, out, send, sums, s_rel, scr, scr_r, g, win, *tables = refs[2 * PIECES :]
        table, table_back, flip = tables
        t = pl.program_id(0)

        @pl.when(t < 3)
        def _():
            assemble(w, scr, place)
            win[:, pl.ds(pl.multiple_of(t * WIDE, WIDE), WIDE)] = matrix_of(scr)

        @pl.when(t == 0)
        def _():
            join_parity(keep, got, place, g)
            table[...] = distance_buckets(False)
            table_back[...] = distance_buckets(True)
            flip[...] = mirror()
            lanes = half_rows(span)

            def step(s, carry):
                r = pl.ds(pl.multiple_of(s * span, span), span)
                r0 = pl.ds(pl.multiple_of(s * span, span), LEN)
                r1 = pl.ds(pl.multiple_of(s * span + LEN, LEN), span - LEN)
                count = place[5 + s]
                for j in range(4):
                    c = [slice(HALF * i + 128 * j, HALF * i + 128 * j + 128) for i in range(3)]
                    q, k, v = qkv[r, c[0]], qkv[r, c[1]], qkv[r, c[2]]
                    k0, v0 = qkv[r0, c[1]], qkv[r0, c[2]]
                    go = g[r, c[0]]
                    high, low = split_high(rel[r, 128 * (j // 2) : 128 * (j // 2) + 128])
                    prod = q.astype(F32) * k.astype(F32)
                    prod_g = go.astype(F32) * v.astype(F32)
                    gq, gk0, gv0, p_own, d_own, turned = [], 0.0, 0.0, [], [], []
                    for i, mask in enumerate(head_masks()):
                        qm, gm = q * mask, go * mask
                        h = 2 * j + i
                        probs, own = ngram_probs(
                            qm, prod, k0, high, low, table[...], count, h, lanes[i]
                        )
                        gp = dot_t(gm, v0)
                        g_own = jnp.sum(prod_g * lanes[i], axis=-1, keepdims=True)
                        inner = jnp.sum(probs * gp, axis=-1, keepdims=True) + own * g_own
                        ds = (probs * (gp - inner)).astype(BF)
                        ds_own = (own * (g_own - inner)).astype(BF).astype(F32)
                        gq.append(dot(ds, k0))
                        gk0 = gk0 + dot_g(ds, qm)
                        gv0 = gv0 + dot_g(probs.astype(BF), gm)
                        p_own.append(own.astype(BF).astype(F32))
                        d_own.append(ds_own)
                        back = skew(dot(ds, flip[...]))
                        lane = lax.broadcasted_iota(jnp.int32, back.shape, 1)
                        main = lax.broadcasted_iota(jnp.int32, back.shape, 0) < LEN
                        back = jnp.where((lane == 127) & jnp.logical_not(main), ds_own, back)
                        grads = dot_t(back.astype(BF), table_back[...])
                        turned.append(grads * quarter_mask(h % 4).astype(F32))
                    first = first_lanes(span)
                    d_own = jnp.where(first, d_own[0], d_own[1])
                    p_own = jnp.where(first, p_own[0], p_own[1])
                    gqf = jnp.where(first, gq[0], gq[1]) + d_own * k.astype(F32)
                    gqkv[r, c[0]] = (gqf * SCALE).astype(BF)
                    gkn = d_own * q.astype(F32) * SCALE
                    gvn = p_own * go.astype(F32)
                    gqkv[r0, c[1]] = (gk0 * SCALE).astype(BF)
                    gqkv[r0, c[2]] = gv0.astype(BF)
                    gqkv[r1, c[1]] = gkn[LEN:].astype(BF)
                    gqkv[r1, c[2]] = gvn[LEN:].astype(BF)
                    both = turned[0] + turned[1]
                    at = slice(128 * (j // 2), 128 * (j // 2) + 128)
                    if j % 2 == 0:
                        held = both
                    else:
                        grel[r, at] = (held + both).astype(BF)
                return carry

            lax.fori_loop(0, 2, step, 0)
            column_sums(sums, gqkv[...])
            column_sums(s_rel, grel[...])

        @pl.when(t == 3)
        def _():
            assemble_rel(wr, scr_r, place)
            wrel = scr_r[...].reshape(D, REL_HALF)
            input_grads(place, gz, [(gqkv, win[...]), (grel, wrel)], out, send)

    third = lambda t: jnp.minimum(t, 2)
    return run(
        body,
        4,
        [small(place), full(qkv), full(rel), full(keep), full(got), full(gz)]
        + blocks(pieces, 64, third)
        + blocks(pieces, 32, lambda t: 8),
        [
            out_full((rows, 3 * HALF), BF),
            out_full((rows, REL_HALF), BF),
            out_full((rows // 2, D), F32),
            out_full((rows // 2, D), BF),
            out_full((1, 3 * HALF), F32),
            out_full((1, REL_HALF), F32),
        ],
        [
            weight_scratch(64),
            pltpu.VMEM((4, 4, 2, 32, REL_HALF), BF),
            pltpu.VMEM((rows, HALF), BF),
            pltpu.VMEM((D, 3 * HALF), BF),
        ]
        + [pltpu.VMEM((128, 128), BF)] * 3,
        us=29,
    )


def grad_chunk(place, arrays, terms, total_rows, width=WIDE):
    n = len(arrays)

    def body(place, *refs):
        ins, outs, scr = refs[:n], refs[n : n + 4], refs[n + 4]
        t = pl.program_id(0)
        dp, core = place[0], place[2]

        def spread(value, at, rows, lanes=slice(0, WIDE)):
            v = value.astype(BF).reshape(4, 4, rows, WIDE)
            scr[:, :, :rows] = v
            for i in range(4):
                outs[i][:, at : at + rows, lanes] = scr[jnp.bitwise_xor(dp, i), :, :rows]

        for index, (kind, at, x, g, col) in enumerate(terms):

            @pl.when(t == index)
            def _(kind=kind, at=at, x=x, g=g, col=col):
                if kind == "whole":
                    spread(ins[x][...], at, ins[x].shape[0] // 16)
                    return
                if kind == "heads":
                    right = ins[g][:, col : col + WIDE]
                    mine, theirs = ins[x][...], ins[x + 1][...]
                    keep, got = dot_g(mine, right), dot_g(theirs, right)
                    quarter = (2, 4, 32, WIDE)
                    scr[pl.ds(2 * core, 2), :, :32] = keep.astype(BF).reshape(quarter)
                    scr[pl.ds(2 - 2 * core, 2), :, :32] = got.astype(BF).reshape(quarter)
                    spread(scr[:, :, :32], at, 32)
                    return
                if kind == "rel":
                    v = dot_g(ins[x][...], ins[g][...]).astype(BF).reshape(16, 2, 32, REL_HALF)
                    spread(jnp.concatenate([v[:, 0], v[:, 1]], axis=-1), at, 32)
                    return
                value = dot_g(ins[x][...], ins[g][:, col : col + WIDE])
                lanes = slice(col, col + WIDE) if kind == "rows" else slice(0, WIDE)
                spread(value, at, value.shape[0] // 16, lanes)

    return run(
        body,
        len(terms),
        [small(place)] + [full(a) for a in arrays],
        [out_full((4, total_rows, width), BF)] * 4,
        [weight_scratch(128)],
        us=10,
    )


def vec_chunk(place, pieces):
    def body(place, *refs):
        assemble(refs[:PIECES], refs[PIECES], place)

    return run(
        body,
        1,
        [small(place)] + blocks(pieces, 16, lambda t: 18),
        [out_full((4, 4, 16, WIDE), BF)],
        us=2,
    )[0]


class Order:

    def __init__(self, place):
        self.place = place
        self.last = None

    def after(self, *values):
        if self.last is not None:
            values = (self.last,) + values
        self.place = tie(self.place, *values)
        self.last = None

    def run(self, kernel, *args):
        if self.last is not None:
            self.place = tie(self.place, self.last)
        out = kernel(self.place, *args)
        self.last = out[0] if isinstance(out, (list, tuple)) else out
        return out

    def add(self, first, *others):
        if self.last is not None:
            first = tie(first, self.last)
        self.last = add_low(first, *others)
        return self.last


class Links:

    def __init__(self, lay):
        self.lay = lay
        self.sent = {1: [], 2: []}
        self.gathered = []
        self.far = 2
        self.groups = [list(range(core, lay.nf, 2)) for core in range(2)]

    def send(self, value, mask):
        queue = self.sent[mask]
        if len(queue) >= 2:
            value = tie(value, queue[-2])
        queue.append(self.lay.flip_dp(value, mask))
        return queue[-1]

    def turn(self):
        self.far = 3 - self.far
        return self.far

    def gather(self, buf):
        far = self.turn()
        if len(self.gathered) >= 2:
            buf = tie(buf, self.gathered[-2])
        own = lax.all_gather(buf, "fsdp", axis=0, axis_index_groups=self.groups)
        self.gathered.append(own)
        x, y = self.send(own, 1), self.send(own, 2)
        d = self.send(x, 2) if far == 2 else self.send(y, 1)
        return [own, x, y, d]

    def scatter(self, order, parts):
        far = self.turn()
        own, x, y, d = parts
        d = self.lay.flip_dp(d, far)
        if far == 2:
            y = self.lay.flip_dp(y, 2)
            yield
            x = self.lay.flip_dp(order.add(x, d), 1)
        else:
            x = self.lay.flip_dp(x, 1)
            yield
            y = self.lay.flip_dp(order.add(y, d), 2)
        yield
        total = order.add(own, x, y)
        yield lax.psum_scatter(
            total, "fsdp", scatter_dimension=0, axis_index_groups=self.groups
        ).astype(F32)


def shards_fast(
    ndp,
    nf,
    source,
    dec_in,
    src_lengths,
    tgt_lengths,
    enc_in_proj,
    enc_out_proj,
    enc_ffn_in,
    enc_ffn_out,
    enc_gains,
    enc_biases,
    dec_in_proj,
    dec_rel_proj,
    dec_out_proj,
    cross_query,
    cross_kv,
    cross_out,
    dec_ffn_in,
    dec_ffn_out,
    dec_gains,
    dec_biases,
    enc_cot,
    dec_cot,
):
    lay = Layout(ndp, nf)
    lay.place()
    r, f, chips = lay.r, lay.f, lay.chips
    swap, pick, pair = lay.swap, lay.pick, lay.pair
    core = lay.core
    dec_rows = STREAMS * LEN

    links = Links(lay)
    w = {"dec_down": links.gather(dec_ffn_out), "enc_down": links.gather(enc_ffn_out)}

    def halves(matrix, groups, width):
        parts = matrix.reshape(r, groups, 2, width)
        return (
            pick(parts[:, :, 0], parts[:, :, 1]).reshape(r, groups * width),
            pick(parts[:, :, 1], parts[:, :, 0]).reshape(r, groups * width),
        )

    split = [
        halves(enc_in_proj, 3, HALF),
        halves(enc_ffn_in, chips, f),
        halves(dec_in_proj, 3, HALF),
        halves(cross_query, 1, HALF),
        halves(cross_kv, 2, HALF),
        halves(dec_ffn_in, chips, f),
        halves(dec_rel_proj, 1, REL_HALF),
    ]
    vec = jnp.concatenate(
        [
            enc_biases,
            enc_gains,
            dec_biases,
            dec_gains,
            src_lengths.astype(BF),
            tgt_lengths.astype(BF),
        ]
    )
    nvec = vec.shape[0]
    padded = -(-nvec // WIDE) * WIDE
    vec = jnp.pad(vec, (0, padded - nvec))
    mine = jnp.concatenate([own for own, other in split], axis=1)
    theirs = jnp.concatenate([other for own, other in split], axis=1)
    theirs_got = swap(theirs)
    vec_got = swap(vec)
    source_got = swap(source)
    dec_own = dec_in.transpose(1, 0, 2).reshape(dec_rows, D)
    dec_got = swap(dec_own)

    def column_blocks(start, count):
        return [
            pair(
                mine[:, start + WIDE * i : start + WIDE * i + WIDE],
                theirs_got[:, start + WIDE * i : start + WIDE * i + WIDE],
                0,
            )
            for i in range(count)
        ]

    def row_blocks(matrix):
        return [matrix[:, :WIDE], matrix[:, WIDE:]]

    rel_start = mine.shape[1] - REL_HALF
    rel_block = pair(mine[:, rel_start:], theirs_got[:, rel_start:], 1)
    vec_pair = pair(vec[None], vec_got[None], 0)
    vec_used = 2 * padded // WIDE
    vec_block = jnp.pad(vec_pair.reshape(vec_used, WIDE), ((0, 16 - vec_used), (0, 0)))
    at = [0, 3 * WIDE, 7 * WIDE, 10 * WIDE, 11 * WIDE, 13 * WIDE]
    chunk_parts = {
        "enc": column_blocks(at[0], 3) + row_blocks(enc_out_proj),
        "enc_up": column_blocks(at[1], 4),
        "dec": column_blocks(at[2], 3) + row_blocks(dec_out_proj) + [rel_block, vec_block],
        "cross": column_blocks(at[3], 1) + column_blocks(at[4], 2) + row_blocks(cross_out),
        "dec_up": column_blocks(at[5], 4),
    }
    for name in ("dec", "enc", "enc_up", "cross", "dec_up"):
        w[name] = links.gather(jnp.concatenate(chunk_parts[name], axis=0))

    lens = vec_pair[:, nvec - 2 : nvec].T.reshape(-1).astype(F32).astype(jnp.int32)
    place = jnp.concatenate(
        [jnp.stack([lay.dp, lay.z, core]).astype(jnp.int32), lens, jnp.zeros((1,), jnp.int32)]
    )

    order = Order(place)
    vec_all = order.run(vec_chunk, w["dec"]).reshape(chips, 16, WIDE)[:, :vec_used]
    vec_all = vec_all.reshape(lay.devices, padded).astype(F32)
    widths = [enc_biases.shape[0], enc_gains.shape[0], dec_biases.shape[0], dec_gains.shape[0]]
    starts = [0]
    for width in widths:
        starts.append(starts[-1] + width)
    v_enc_b, v_enc_g, v_dec_b, v_dec_g = [
        vec_all[:, starts[i] : starts[i + 1]].reshape(-1) for i in range(4)
    ]
    eb, eg_rows = v_enc_b.reshape(-1, D), v_enc_g.reshape(2, D)
    dg_rows = v_dec_g.reshape(3, D)
    d_split = 2 * D + HEADS * BUCKETS
    db = v_dec_b[d_split:].reshape(-1, D)

    def half_of(vector):
        parts = vector.reshape(2, -1)
        return pick(parts[0], parts[1])

    def hidden_of(vector):
        parts = vector.reshape(chips, 2, f)
        return pick(parts[:, 0], parts[:, 1]).reshape(1, -1)

    zero_half = jnp.zeros((HALF,), F32)

    def qkv_bias(q, v):
        return jnp.concatenate([half_of(q), zero_half, half_of(v)])[None]

    def rows_of(*vectors):
        return jnp.stack(vectors)

    x = pair(source, source_got, 0)
    y = pair(dec_own, dec_got, 0)
    dcot_own = dec_cot.transpose(1, 0, 2).reshape(dec_rows, D)
    dcot = pair(dcot_own, swap(dcot_own), 0)
    ecot = pair(enc_cot, swap(enc_cot), 0)
    order.after(x, y, dcot, ecot)
    dqkv, rel, da_keep, da_send = order.run(
        ngram_attention,
        y,
        qkv_bias(v_dec_b[:D], v_dec_b[D : 2 * D]),
        half_of(v_dec_b[2 * D : d_split])[None],
        w["dec"],
    )
    da_got = swap(da_send)
    eqkv, ea_keep, ea_send = order.run(enc_attention, x, qkv_bias(eb[0], eb[1]), w["enc"])
    ea_got = swap(ea_send)
    p3 = order.run(out_projection, da_keep, da_got, w["dec"])
    p3_got = swap(p3)
    p1 = order.run(out_projection, ea_keep, ea_got, w["enc"])
    p1_got = swap(p1)
    eunit1, einv1, eh1_low, eg, egp, p2 = order.run(
        ffn_forward,
        x,
        False,
        p1,
        p1_got,
        rows_of(eb[2], eb[2], eb[2], eg_rows[0], eb[8]),
        hidden_of(eb[3:7]),
        w["enc_up"],
        w["enc_down"],
    )
    p2_got = swap(p2)
    dunit1, dinv1, dh1_low, eunit2, einv2, enc_low, cq, ckv, ca_keep, ca_send = order.run(
        cross_forward,
        y,
        p3,
        p3_got,
        rows_of(db[0], dg_rows[0], db[9]),
        eunit1,
        rows_of(eg_rows[0], eb[8], eb[7], eg_rows[1], eb[9]),
        p2,
        p2_got,
        half_of(db[1])[None],
        jnp.concatenate([zero_half, half_of(db[2])])[None],
        w["cross"],
    )
    ca_got = swap(ca_send)
    p4 = order.run(out_projection, ca_keep, ca_got, w["cross"])
    p4_got = swap(p4)
    dunit2, dinv2, dh2_low, dg, dgp, p5 = order.run(
        ffn_forward,
        dunit1,
        True,
        p4,
        p4_got,
        rows_of(dg_rows[0], db[9], db[3], dg_rows[1], db[10]),
        hidden_of(db[4:8]),
        w["dec_up"],
        w["dec_down"],
    )
    p5_got = swap(p5)

    dec_out, gz3, gf, gu, p6, s_gain3, s_shift3, s_gf, s_gu = order.run(
        ffn_back,
        True,
        [dcot],
        [dunit2, p5, p5_got],
        rows_of(dg_rows[1], db[10], db[8], dg_rows[2], db[11]),
        dgp,
        w["dec_up"],
        w["dec_down"],
    )
    p6_got = swap(p6)
    up_terms = [("plain", 64 * b, 0, 1, WIDE * b) for b in range(4)]
    down_terms = [("rows", 0, 0, 1, WIDE * h) for h in range(2)]

    def grads(*args):
        scatter = links.scatter(order, order.run(grad_chunk, *args))
        next(scatter)
        return scatter

    r_dd = grads([dg, gf], down_terms, 128, D)
    r_du = grads([dh2_low, gu], up_terms, 256)
    gz2, gx, gca_keep, gca_send, s_gain2, s_shift2, s_gx = order.run(
        branch_back, gz3, p6, p6_got, dunit2, dinv2, dg_rows[1:2], w["cross"]
    )
    gca_got = swap(gca_send)
    next(r_dd)
    next(r_du)
    gcq, gckv, p7, s_gcq, s_gckv = order.run(
        cross_back, cq, ckv, gca_keep, gca_got, w["cross"]
    )
    p7_got = swap(p7)
    r_cross = grads(
        [dh1_low, gcq, enc_low, gckv, ca_keep, ca_got, gx],
        [
            ("plain", 0, 0, 1, 0),
            ("plain", 64, 2, 3, 0),
            ("plain", 128, 2, 3, WIDE),
            ("heads", 192, 4, 6, 0),
            ("heads", 224, 4, 6, WIDE),
        ],
        256,
    )
    gz1, go, gda_keep, gda_send, s_gain1, s_shift1, s_go = order.run(
        branch_back, gz2, p7, p7_got, dunit1, dinv1, dg_rows[0:1], w["dec"]
    )
    gda_got = swap(gda_send)
    gz2e, gfe, gue, p9, e_gain2, e_shift2, s_gfe, s_gue = order.run(
        ffn_back,
        False,
        [ecot, p7, p7_got],
        [eunit2, einv2],
        rows_of(*([eg_rows[1]] * 5)),
        egp,
        w["enc_up"],
        w["enc_down"],
    )
    p9_got = swap(p9)
    total_dd = next(r_dd)
    next(r_cross)
    total_du = next(r_du)
    r_ed = grads([eg, gfe], down_terms, 128, D)
    r_eu = grads([eh1_low, gue], up_terms, 256)
    gz1e, goe, gea_keep, gea_send, e_gain1, e_shift1, s_goe = order.run(
        branch_back, gz2e, p9, p9_got, eunit1, einv1, eg_rows[0:1], w["enc"]
    )
    gea_got = swap(gea_send)
    gqkv, grel, p8, p8_send, s_gqkv, s_grel = order.run(
        ngram_back_kernel, dqkv, rel, gda_keep, gda_got, gz1, w["dec"]
    )
    p8_got = swap(p8_send)
    next(r_ed)
    next(r_eu)
    total_cross = next(r_cross)
    geqkv, p10, p10_send, s_geqkv = order.run(
        enc_attention_back, eqkv, gea_keep, gea_got, gz1e, w["enc"]
    )
    p10_got = swap(p10_send)
    r_dec = grads(
        [y, gqkv, da_keep, da_got, go, grel],
        [("plain", 64 * b, 0, 1, WIDE * b) for b in range(3)]
        + [("heads", 192, 2, 4, 0), ("heads", 224, 2, 4, WIDE), ("rel", 256, 0, 5, 0)],
        288,
    )
    total_ed = next(r_ed)
    total_eu = next(r_eu)

    def widen(vector):
        zeros = jnp.zeros_like(vector)
        return pick(jnp.concatenate([vector, zeros]), jnp.concatenate([zeros, vector]))

    def widen_hidden(vector):
        parts = vector.reshape(chips, 1, f)
        zeros = jnp.zeros_like(parts)
        return pick(
            jnp.concatenate([parts, zeros], axis=1), jnp.concatenate([zeros, parts], axis=1)
        ).reshape(-1)

    def owned(*vectors):
        return jnp.concatenate(vectors).reshape(lay.devices, -1)

    vec_grads = jnp.concatenate(
        [
            owned(
                widen(s_geqkv[0, :HALF]),
                widen(s_geqkv[0, 2 * HALF :]),
                0.5 * s_goe[0],
                widen_hidden(s_gue),
                0.5 * s_gfe[0],
                0.5 * e_shift1[0],
                0.5 * e_shift2[0],
            ),
            owned(0.5 * e_gain1[0], 0.5 * e_gain2[0]),
            owned(
                widen(s_gqkv[0, :HALF]),
                widen(s_gqkv[0, 2 * HALF :]),
                widen(s_grel[0]),
                0.5 * s_go[0],
                widen(s_gcq[0]),
                widen(s_gckv[0, HALF:]),
                0.5 * s_gx[0],
                widen_hidden(s_gu),
                0.5 * s_gf[0],
                0.5 * s_shift1[0],
                0.5 * s_shift2[0],
                0.5 * s_shift3[0],
            ),
            owned(0.5 * s_gain1[0], 0.5 * s_gain2[0], 0.5 * s_gain3[0]),
        ],
        axis=1,
    ).astype(BF)
    vec_width = vec_grads.shape[1]
    vec_grads = jnp.pad(vec_grads, ((0, 0), (0, padded - vec_width)))
    vec_grads = vec_grads.reshape(chips, vec_used, WIDE)
    vec_grads = jnp.pad(vec_grads, ((0, 0), (0, 16 - vec_used), (0, 0))).reshape(chips * 16, WIDE)
    r_enc = grads(
        [x, geqkv, ea_keep, ea_got, goe, vec_grads],
        [("plain", 64 * b, 0, 1, WIDE * b) for b in range(3)]
        + [("heads", 192, 2, 4, 0), ("heads", 224, 2, 4, WIDE), ("whole", 256, 5, 5, 0)],
        272,
    )
    next(r_dec)
    next(r_enc)
    total2 = next(r_dec)
    total0 = next(r_enc)

    def split_rows(total, sizes):
        at = 0
        result = []
        for size in sizes:
            result.append(total[at : at + size])
            at += size
        return result

    def own_rows_of(total, count):
        rows = total.reshape(count, 2, r, WIDE)
        keep = pick(rows[:, 0], rows[:, 1])
        got = swap(pick(rows[:, 1], rows[:, 0]))
        return pair(keep[:, None], got[:, None], 1)

    def in_rows(rows):
        return rows.transpose(2, 0, 1, 3).reshape(r, -1)

    def up_rows(rows):
        per = WIDE // f
        return rows.reshape(4, 2, r, per, f).transpose(2, 0, 3, 1, 4).reshape(r, FF)

    def side(low, high):
        return jnp.concatenate([low, high], axis=1)

    t0 = split_rows(total0, [6 * r, r, r, 16])
    o_enc_in, o_enc_out = in_rows(own_rows_of(t0[0], 3)), side(t0[1], t0[2])
    vec_sum = t0[3][:vec_used].reshape(2, padded)
    vec_sum = pick(vec_sum[0], vec_sum[1]) + swap(pick(vec_sum[1], vec_sum[0]))
    o_vec = [vec_sum[starts[i] : starts[i + 1]] for i in range(4)]
    o_enc_up = up_rows(own_rows_of(total_eu, 4))
    o_enc_down = total_ed
    t2 = split_rows(total2, [6 * r, r, r, r])
    o_dec_in, o_dec_out = in_rows(own_rows_of(t2[0], 3)), side(t2[1], t2[2])
    relp = t2[3].reshape(r, 2, REL_HALF)
    o_rel = pair(pick(relp[:, 0], relp[:, 1]), swap(pick(relp[:, 1], relp[:, 0])), 1)
    t3 = split_rows(total_cross, [2 * r, 4 * r, r, r])
    o_cross_q = in_rows(own_rows_of(t3[0], 1))
    o_cross_kv = in_rows(own_rows_of(t3[1], 2))
    o_cross_out = side(t3[2], t3[3])
    o_dec_up = up_rows(own_rows_of(total_du, 4))
    o_dec_down = total_dd

    return (
        pick(enc_low[:LEN], enc_low[LEN:]),
        dec_out.reshape(STREAMS, LEN, D).transpose(1, 0, 2),
        p10 + p10_got.astype(F32),
        (p8 + p8_got.astype(F32)).reshape(STREAMS, LEN, D).transpose(1, 0, 2),
        o_enc_in,
        o_enc_out,
        o_enc_up,
        o_enc_down,
        o_vec[1],
        o_vec[0],
        o_dec_in,
        o_rel,
        o_dec_out,
        o_cross_q,
        o_cross_kv,
        o_cross_out,
        o_dec_up,
        o_dec_down,
        o_vec[3],
        o_vec[2],
    )


def solution(mesh):
    ndp, nf = mesh.shape["dp"], mesh.shape["fsdp"]
    whole = ("dp", "fsdp")
    one, two, three = P(whole), P(whole, None), P(whole, None, None)
    args = (two, three, one, one) + (two,) * 4 + (one,) * 2 + (two,) * 8 + (one,) * 2 + (two, three)
    outs = (two, three, two, three) + (two,) * 4 + (one,) * 2 + (two,) * 8 + (one,) * 2

    def body(*arrays):
        if (ndp, nf) == (4, 8):
            return shards_fast(ndp, nf, *arrays)
        return shards(ndp, nf, *arrays)

    return jax.shard_map(body, mesh=mesh, in_specs=args, out_specs=outs, check_vma=False)
```

```python
import math

import jax
import jax.numpy as jnp
from jax import lax
from jax.experimental import pallas as pl
from jax.experimental.pallas import tpu as pltpu
from jax.sharding import PartitionSpec as P

D = 1024
HEADS = 16
HEAD = 64
FF = 4096
NGRAM = 2
STREAMS = NGRAM + 1
BUCKETS = 32
LEN = 128
HALF = D // 2
OWN_HEADS = HEADS // 2
REL_HALF = OWN_HEADS * BUCKETS
HIDDEN_HALF = FF // 2
WIDE = 512
EPSILON = 1e-05
MASKED = -1000000000.0
SCALE = 1.0 / math.sqrt(HEAD)
BF = jnp.bfloat16
F32 = jnp.float32
ENC_WIDTHS = (D, D, D, FF, D, D, D)
DEC_WIDTHS = (D, D, HEADS * BUCKETS, D, D, D, D, FF, D, D, D, D)


def bucket_value(distance, bucket_count):
    exact_count = bucket_count // 2
    if distance < exact_count:
        return distance
    return min(
        bucket_count - 1,
        exact_count
        + int(
            math.log(distance / exact_count)
            / math.log(128 / exact_count)
            * (bucket_count - exact_count)
        ),
    )


def bucket_table(length, bucket_count):
    positions = jnp.arange(length, dtype=jnp.int32)
    distance = positions[:, None] - positions[None, :]
    bucket = jnp.zeros((length, length), jnp.int32)
    for target in range(1, bucket_count):
        distance_at = 1
        while bucket_value(distance_at, bucket_count) < target:
            distance_at += 1
        bucket = bucket + (distance >= distance_at).astype(jnp.int32)
    return (bucket[:, :, None] == jnp.arange(bucket_count, dtype=jnp.int32)).astype(F32)


def slices_of(vector, widths):
    starts = 0
    result = []
    for amount in widths:
        result.append(vector[starts : starts + amount])
        starts += amount
    return result


def dot(a, b):
    return lax.dot_general(a, b, (((1,), (0,)), ((), ())), preferred_element_type=F32)


def dot_t(a, b):
    return lax.dot_general(a, b, (((1,), (1,)), ((), ())), preferred_element_type=F32)


def dot_g(a, b):
    return lax.dot_general(a, b, (((0,), (0,)), ((), ())), preferred_element_type=F32)


def norm_stats(values):
    average = jnp.mean(values, axis=-1, keepdims=True)
    centered = values - average
    variance = jnp.mean(centered * centered, axis=-1, keepdims=True)
    inverse = lax.rsqrt(variance + EPSILON)
    return centered * inverse, inverse


def norm(values, gain, shift):
    unit, inverse = norm_stats(values)
    return unit * gain + shift


def norm_back(values, gain, grads):
    unit, inverse = norm_stats(values)
    scaled = grads * gain
    mean_one = jnp.mean(scaled, axis=-1, keepdims=True)
    mean_two = jnp.mean(scaled * unit, axis=-1, keepdims=True)
    return (
        inverse * (scaled - mean_one - unit * mean_two),
        jnp.sum(grads * unit, axis=0),
        jnp.sum(grads, axis=0),
    )


def gelu_exact(inputs):
    return jax.nn.gelu(inputs, approximate=False)


def gelu_back(inputs, gradients):
    outputs, pullback = jax.vjp(gelu_exact, inputs)
    return pullback(gradients)[0]


def col_sum(values):
    return jnp.sum(values.astype(F32), axis=0)


class Layout:
    def __init__(self, ndp, nf):
        self.ndp = ndp
        self.nf = nf
        self.nz = nf // 2
        self.chips = ndp * self.nz
        self.devices = ndp * nf
        self.r = D // self.devices
        self.f = FF // self.devices

    def place(self):
        self.dp = lax.axis_index("dp")
        fs = lax.axis_index("fsdp")
        self.z = fs // 2
        self.core = fs % 2

    def swap(self, value):
        return lax.ppermute(value, "fsdp", [(i, i ^ 1) for i in range(self.nf)])

    def shift_z(self, value, step):
        return lax.ppermute(
            value, "fsdp", [(i, (i + 2 * step) % self.nf) for i in range(self.nf)]
        )

    def flip_dp(self, value, mask):
        return lax.ppermute(value, "dp", [(i, i ^ mask) for i in range(self.ndp)])

    def shift_dp(self, value, step):
        return lax.ppermute(value, "dp", [(i, (i + step) % self.ndp) for i in range(self.ndp)])

    def pick(self, first, second):
        return jnp.where(self.core == 0, first, second)

    def pair(self, own, other, axis):
        return self.pick(
            jnp.concatenate([own, other], axis=axis), jnp.concatenate([other, own], axis=axis)
        )


def tie(value, *others):
    return lax.optimization_barrier((value,) + others)[0]


def gather_z(lay, buf):
    out = jnp.zeros((lay.nz,) + buf.shape, buf.dtype)
    out = lax.dynamic_update_slice(out, buf[None], (lay.z, 0, 0))
    for step in range(1, lay.nz):
        got = lay.shift_z(buf, step)
        out = lax.dynamic_update_slice(out, got[None], ((lay.z - step) % lay.nz, 0, 0))
    return out


def gather_dp_first(lay, buf):
    if lay.ndp == 4:
        return [lay.flip_dp(buf, 1), lay.flip_dp(buf, 2)]
    return [lay.shift_dp(buf, step) for step in range(1, lay.ndp)]


def gather_dp_rest(lay, buf, first):
    half = lay.nz // 2
    out = jnp.zeros((lay.ndp,) + buf.shape, buf.dtype)
    if lay.ndp == 4:
        low = lay.flip_dp(first[0][:half], 2)
        high = lay.flip_dp(first[1][half:], 1)
        parts = [(0, 0, buf), (1, 0, first[0]), (2, 0, first[1]), (3, 0, low), (3, half, high)]
        for flip, at, part in parts:
            out = lax.dynamic_update_slice(out, part[None], (lay.dp ^ flip, at, 0, 0))
        return out
    out = lax.dynamic_update_slice(out, buf[None], (lay.dp, 0, 0, 0))
    for step in range(1, lay.ndp):
        out = lax.dynamic_update_slice(
            out, first[step - 1][None], ((lay.dp - step) % lay.ndp, 0, 0, 0)
        )
    return out


def gather_all(lay, bufs):
    staged = []
    results = []
    firsts = []
    for i, buf in enumerate(bufs):
        if i >= 2:
            buf = tie(buf, *firsts[i - 2])
        z = gather_z(lay, buf)
        staged.append(z)
        firsts.append(gather_dp_first(lay, z))
    for z, first in zip(staged, firsts):
        results.append(gather_dp_rest(lay, z, first))
    return results


def take(buf, index, axis=0):
    return lax.dynamic_index_in_dim(buf, index, axis, keepdims=False)


def add_low(*values):
    return sum(v.astype(F32) for v in values).astype(BF)


def scatter_dp(lay, buf):
    if lay.ndp == 4:
        half = lay.nz // 2
        far = take(buf, lay.dp ^ 3)
        to_x = take(buf, lay.dp ^ 1)
        to_y = take(buf, lay.dp ^ 2)
        own = take(buf, lay.dp)
        low = lay.flip_dp(far[:half], 2)
        high = lay.flip_dp(far[half:], 1)
        to_x = jnp.concatenate([add_low(to_x[:half], low), to_x[half:]], axis=0)
        to_y = jnp.concatenate([to_y[:half], add_low(to_y[half:], high)], axis=0)
        return add_low(own, lay.flip_dp(to_x, 1), lay.flip_dp(to_y, 2))
    parts = [take(buf, lay.dp)]
    for step in range(1, lay.ndp):
        parts.append(lay.shift_dp(take(buf, (lay.dp + step) % lay.ndp), step))
    return add_low(*parts)


def scatter_z(lay, buf):
    total = take(buf, lay.z).astype(F32)
    for step in range(1, lay.nz):
        total = total + lay.shift_z(take(buf, (lay.z + step) % lay.nz), step).astype(F32)
    return total


def attention_forward(queries, keys, values, allowed):
    scores = jnp.einsum("snihe,sjhe->snhij", queries, keys, preferred_element_type=F32) * SCALE
    probs = jax.nn.softmax(jnp.where(allowed, scores, MASKED), axis=-1)
    out = jnp.einsum("snhij,sjhe->snihe", probs.astype(BF), values, preferred_element_type=F32)
    return out.astype(BF), probs


def attention_back(queries, keys, values, probs, grad_out):
    grad_probs = jnp.einsum("snihe,sjhe->snhij", grad_out, values, preferred_element_type=F32)
    grad_values = jnp.einsum(
        "snhij,snihe->sjhe", probs.astype(BF), grad_out, preferred_element_type=F32
    )
    grad_scores = (
        probs * (grad_probs - jnp.sum(probs * grad_probs, axis=-1, keepdims=True))
    ).astype(BF)
    grad_queries = (
        jnp.einsum("snhij,sjhe->snihe", grad_scores, keys, preferred_element_type=F32) * SCALE
    )
    grad_keys = (
        jnp.einsum("snhij,snihe->sjhe", grad_scores, queries, preferred_element_type=F32) * SCALE
    )
    return grad_queries.astype(BF), grad_keys.astype(BF), grad_values.astype(BF)


def ngram_forward(dqkv, rel, tgt, onehot):
    q, k, v = dqkv[:, :, :, 0], dqkv[:, :, :, 1], dqkv[:, :, :, 2]
    positions = jnp.arange(LEN, dtype=jnp.int32)
    inside = positions[None, :] < tgt[:, None]
    main_valid = (positions[None, :] <= positions[:, None])[None] & inside[:, None]
    pred_valid = (positions[None, :] < positions[:, None])[None] & inside[:, None]
    valid = jnp.stack([main_valid] + [pred_valid] * NGRAM, axis=1)[:, :, None]
    main = jnp.einsum("snihe,sjhe->snhij", q, k[:, 0], preferred_element_type=F32) * SCALE
    main = main + jnp.einsum("snihk,ijk->snhij", rel, onehot, precision=lax.Precision.HIGHEST)
    main = jnp.where(valid, main, MASKED)
    own = jnp.einsum("snihe,snihe->snhi", q, k, preferred_element_type=F32) * SCALE
    own = own + jnp.transpose(rel[..., 0], (0, 1, 3, 2))
    stream = jnp.arange(STREAMS)[None, :, None, None]
    own = jnp.where(stream == 0, -jnp.inf, own)
    top = jnp.maximum(jnp.max(main, axis=-1), own)
    main = jnp.exp(main - top[..., None])
    own = jnp.exp(own - top)
    total = jnp.sum(main, axis=-1) + own
    main = main / total[..., None]
    own = own / total
    out = jnp.einsum("snhij,sjhe->snihe", main.astype(BF), v[:, 0], preferred_element_type=F32)
    own_low = jnp.transpose(own.astype(BF), (0, 1, 3, 2)).astype(F32)[..., None]
    out = out + own_low * v.astype(F32)
    return out.astype(BF), main, own


def ngram_back(dqkv, main, own, onehot, grad_out):
    q, k, v = dqkv[:, :, :, 0], dqkv[:, :, :, 1], dqkv[:, :, :, 2]
    grad_main = jnp.einsum("snihe,sjhe->snhij", grad_out, v[:, 0], preferred_element_type=F32)
    grad_own = jnp.einsum("snihe,snihe->snhi", grad_out, v, preferred_element_type=F32)
    inner = jnp.sum(main * grad_main, axis=-1) + own * grad_own
    ds = (main * (grad_main - inner[..., None])).astype(BF)
    ds_own = (own * (grad_own - inner)).astype(BF)
    own_rows = jnp.transpose(ds_own, (0, 1, 3, 2)).astype(F32)[..., None]
    p_rows = jnp.transpose(own.astype(BF), (0, 1, 3, 2)).astype(F32)[..., None]
    gq = (
        jnp.einsum("snhij,sjhe->snihe", ds, k[:, 0], preferred_element_type=F32)
        + own_rows * k.astype(F32)
    ) * SCALE
    gk0 = jnp.einsum("snhij,snihe->sjhe", ds, q, preferred_element_type=F32) * SCALE
    gv0 = jnp.einsum("snhij,snihe->sjhe", main.astype(BF), grad_out, preferred_element_type=F32)
    gk = own_rows * q.astype(F32) * SCALE
    gv = p_rows * grad_out.astype(F32)
    gk = jnp.concatenate([gk0[:, None], gk[:, 1:]], axis=1)
    gv = jnp.concatenate([gv0[:, None], gv[:, 1:]], axis=1)
    gqkv = jnp.stack([gq, gk, gv], axis=3).astype(BF)
    grel = jnp.einsum("snhij,ijk->snihk", ds, onehot.astype(BF), preferred_element_type=F32)
    first = (jnp.arange(BUCKETS) == 0).astype(F32)
    grel = (grel + own_rows * first).astype(BF)
    return gqkv, grel


def shards(
    ndp,
    nf,
    source,
    dec_in,
    src_lengths,
    tgt_lengths,
    enc_in_proj,
    enc_out_proj,
    enc_ffn_in,
    enc_ffn_out,
    enc_gains,
    enc_biases,
    dec_in_proj,
    dec_rel_proj,
    dec_out_proj,
    cross_query,
    cross_kv,
    cross_out,
    dec_ffn_in,
    dec_ffn_out,
    dec_gains,
    dec_biases,
    enc_cot,
    dec_cot,
):
    lay = Layout(ndp, nf)
    lay.place()
    r, f, chips = lay.r, lay.f, lay.chips
    swap, pick, pair = lay.swap, lay.pick, lay.pair
    core = lay.core

    def halves(matrix, groups, width):
        parts = matrix.reshape(r, groups, 2, width)
        return (
            pick(parts[:, :, 0], parts[:, :, 1]).reshape(r, groups * width),
            pick(parts[:, :, 1], parts[:, :, 0]).reshape(r, groups * width),
        )

    split = [
        halves(enc_in_proj, 3, HALF),
        halves(enc_ffn_in, chips, f),
        halves(dec_in_proj, 3, HALF),
        halves(cross_query, 1, HALF),
        halves(cross_kv, 2, HALF),
        halves(dec_ffn_in, chips, f),
        halves(dec_rel_proj, 1, REL_HALF),
    ]
    vec = jnp.concatenate(
        [
            enc_biases,
            enc_gains,
            dec_biases,
            dec_gains,
            src_lengths.astype(BF),
            tgt_lengths.astype(BF),
        ]
    )
    nvec = vec.shape[0]
    padded = -(-nvec // WIDE) * WIDE
    vec = jnp.pad(vec, (0, padded - nvec))
    mine = jnp.concatenate([own for own, other in split], axis=1)
    theirs = jnp.concatenate([other for own, other in split], axis=1)
    theirs_got = swap(theirs)
    vec_got = swap(vec)
    source_got = swap(source)
    dec_in_got = swap(dec_in.reshape(LEN * STREAMS, D))

    def owner_rows(start, width):
        return pair(mine[:, start : start + width], theirs_got[:, start : start + width], 0)

    def column_blocks(start, count):
        return [owner_rows(start + WIDE * i, WIDE) for i in range(count)]

    def row_blocks(matrix):
        return [matrix[:, :WIDE], matrix[:, WIDE:]]

    rel_start = mine.shape[1] - REL_HALF
    rel_own = mine[:, rel_start:]
    rel_other = theirs_got[:, rel_start:]
    vec_pair = pair(vec[None], vec_got[None], 0).reshape(-1, WIDE)
    vec_rows = -(-vec_pair.shape[0] // 16) * 16
    vec_used = vec_pair.shape[0]
    vec_pair = jnp.pad(vec_pair, ((0, vec_rows - vec_used), (0, 0)))
    wide_at = [0, 3 * WIDE, 7 * WIDE, 10 * WIDE, 11 * WIDE, 13 * WIDE]
    chunk_parts = [
        column_blocks(wide_at[0], 3) + row_blocks(enc_out_proj) + [vec_pair],
        column_blocks(wide_at[1], 4) + row_blocks(enc_ffn_out),
        column_blocks(wide_at[2], 3) + [pair(rel_own, rel_other, 1)] + row_blocks(dec_out_proj),
        column_blocks(wide_at[3], 1) + column_blocks(wide_at[4], 2) + row_blocks(cross_out),
        column_blocks(wide_at[5], 4) + row_blocks(dec_ffn_out),
    ]
    bufs = [jnp.concatenate(parts, axis=0) for parts in chunk_parts]
    full = gather_all(lay, bufs)

    def cut(index, block):
        parts = chunk_parts[index]
        at = sum(p.shape[0] for p in parts[:block])
        rows = parts[block].shape[0]
        return full[index][:, :, at : at + rows].reshape(chips * rows, WIDE)

    def columns(index, first, count):
        return jnp.concatenate([cut(index, first + i) for i in range(count)], axis=1)

    def head_rows(index, first):
        rows = columns(index, first, 2)
        low, high = rows[:HALF // 2], rows[HALF // 2 :]
        keep = pick(low, high).reshape(chips // 2, 1, r, D)
        got = swap(pick(high, low)).reshape(chips // 2, 1, r, D)
        return pair(keep, got, 1).reshape(HALF, D)

    w_enc_in = columns(0, 0, 3)
    w_enc_out = head_rows(0, 3)
    w_enc_up = columns(1, 0, 4)
    w_enc_down = columns(1, 4, 2)
    w_dec_in = columns(2, 0, 3)
    w_rel = (
        cut(2, 3)
        .reshape(chips, r, 2, REL_HALF)
        .transpose(0, 2, 1, 3)
        .reshape(D, REL_HALF)
    )
    w_dec_out = head_rows(2, 4)
    w_cross_q = columns(3, 0, 1)
    w_cross_kv = columns(3, 1, 2)
    w_cross_out = head_rows(3, 3)
    w_dec_up = columns(4, 0, 4)
    w_dec_down = columns(4, 4, 2)

    vec_all = (
        cut(0, 5).reshape(chips, vec_rows, WIDE)[:, :vec_used].reshape(lay.devices, padded).astype(F32)
    )
    widths = [enc_biases.shape[0], enc_gains.shape[0], dec_biases.shape[0], dec_gains.shape[0]]
    starts = [0]
    for width in widths:
        starts.append(starts[-1] + width)
    v_enc_b, v_enc_g, v_dec_b, v_dec_g = [
        vec_all[:, starts[i] : starts[i + 1]].reshape(-1) for i in range(4)
    ]
    ebias = slices_of(v_enc_b, ENC_WIDTHS)
    egain = slices_of(v_enc_g, (D, D))
    dbias = slices_of(v_dec_b, DEC_WIDTHS)
    dgain = slices_of(v_dec_g, (D, D, D))

    def half_of(vector):
        parts = vector.reshape(2, -1)
        return pick(parts[0], parts[1])

    def hidden_of(vector):
        parts = vector.reshape(chips, 2, f)
        return pick(parts[:, 0], parts[:, 1]).reshape(-1)

    zero_half = jnp.zeros((HALF,), F32)
    lens = jnp.stack([pair(vec[None], vec_got[None], 0)[:, nvec - 2 + i] for i in range(2)])
    lens = lens.astype(F32).astype(jnp.int32)
    src_len, tgt_len = lens[0], lens[1]
    positions = jnp.arange(LEN, dtype=jnp.int32)
    src_valid = (positions[None, :] < src_len[:, None])[:, None, None, None, :]
    onehot = bucket_table(LEN, BUCKETS)

    def both(partial):
        low = partial.astype(BF)
        return low.astype(F32) + swap(low).astype(F32)

    x = pair(source[None], source_got[None], 0).reshape(2 * LEN, D)
    qkv_bias = jnp.concatenate([half_of(ebias[0]), zero_half, half_of(ebias[1])])
    eqkv = (dot(x, w_enc_in) + qkv_bias).astype(BF).reshape(2, LEN, 3, OWN_HEADS, HEAD)
    eq, ek, ev = eqkv[:, None, :, 0], eqkv[:, :, 1], eqkv[:, :, 2]
    ea, eprobs = attention_forward(eq, ek, ev, src_valid)
    ea = ea.reshape(2 * LEN, HALF)
    ez1 = x.astype(F32) + both(dot(ea, w_enc_out)) + ebias[2]
    eh1 = norm(ez1, egain[0], ebias[5])
    eh1_low = eh1.astype(BF)
    eu = dot(eh1_low, w_enc_up) + hidden_of(ebias[3])
    eg = gelu_exact(eu).astype(BF)
    ez2 = eh1 + both(dot(eg, w_enc_down)) + ebias[4]
    enc = norm(ez2, egain[1], ebias[6])
    enc_low = enc.astype(BF)

    rows = 2 * STREAMS * LEN
    y = pair(
        dec_in.transpose(1, 0, 2)[None], dec_in_got.reshape(LEN, STREAMS, D).transpose(1, 0, 2)[None], 0
    ).reshape(rows, D)
    dqkv_bias = jnp.concatenate([half_of(dbias[0]), zero_half, half_of(dbias[1])])
    dqkv = (dot(y, w_dec_in) + dqkv_bias).astype(BF)
    dqkv = dqkv.reshape(2, STREAMS, LEN, 3, OWN_HEADS, HEAD)
    rel = (dot(y, w_rel) + half_of(dbias[2])).reshape(2, STREAMS, LEN, OWN_HEADS, BUCKETS)
    da, dmain, down = ngram_forward(dqkv, rel, tgt_len, onehot)
    da = da.reshape(rows, HALF)
    dz1 = y.astype(F32) + both(dot(da, w_dec_out)) + dbias[3]
    dh1 = norm(dz1, dgain[0], dbias[9])
    dh1_low = dh1.astype(BF)
    cq = (dot(dh1_low, w_cross_q) + half_of(dbias[4])).astype(BF)
    cq = cq.reshape(2, STREAMS, LEN, OWN_HEADS, HEAD)
    ckv = dot(enc_low, w_cross_kv) + jnp.concatenate([zero_half, half_of(dbias[5])])
    ckv = ckv.astype(BF).reshape(2, LEN, 2, OWN_HEADS, HEAD)
    ck, cv = ckv[:, :, 0], ckv[:, :, 1]
    ca, cprobs = attention_forward(cq, ck, cv, src_valid)
    ca = ca.reshape(rows, HALF)
    dz2 = dh1 + both(dot(ca, w_cross_out)) + dbias[6]
    dh2 = norm(dz2, dgain[1], dbias[10])
    dh2_low = dh2.astype(BF)
    du = dot(dh2_low, w_dec_up) + hidden_of(dbias[7])
    dg = gelu_exact(du).astype(BF)
    dz3 = dh2 + both(dot(dg, w_dec_down)) + dbias[8]
    dec = norm(dz3, dgain[2], dbias[11])

    def own_rows_of(total, count):
        blocks = total[: count * 2 * r].reshape(count, 2, r, WIDE)
        keep = pick(blocks[:, 0], blocks[:, 1])
        got = swap(pick(blocks[:, 1], blocks[:, 0]))
        return pair(keep[:, None], got[:, None], 1)

    def chip_blocks(grad):
        n = grad.shape[1] // WIDE
        shape = (lay.ndp, lay.nz, grad.shape[0] // chips, WIDE)
        low = grad.astype(BF)
        return [low[:, WIDE * i : WIDE * i + WIDE].reshape(shape) for i in range(n)]

    def head_blocks(grad):
        parts = grad.astype(BF).reshape(chips // 2, 2, r, D)
        keep = pick(parts[:, 0], parts[:, 1])
        got = swap(pick(parts[:, 1], parts[:, 0]))
        return chip_blocks(pair(keep, got, 0).reshape(chips * r, D))

    def scatter(parts, previous):
        buf = jnp.concatenate(parts, axis=2)
        if previous is not None:
            buf = tie(buf, previous)
        first = scatter_dp(lay, buf)
        return scatter_z(lay, first), first

    def split_rows(total, sizes):
        at = 0
        result = []
        for size in sizes:
            result.append(total[at : at + size])
            at += size
        return result

    dcot_got = swap(dec_cot.reshape(LEN * STREAMS, D)).reshape(LEN, STREAMS, D)
    dcot = pair(dec_cot.transpose(1, 0, 2)[None], dcot_got.transpose(1, 0, 2)[None], 0)
    dcot = dcot.reshape(rows, D).astype(F32)
    gz3, ggain3, gnorm3 = norm_back(dz3, dgain[2], dcot)
    gf = gz3.astype(BF)
    g_down = dot_g(dg, gf)
    gu = gelu_back(du, dot_t(gf, w_dec_down)).astype(BF)
    g_up = dot_g(dh2_low, gu)
    total4, first4 = scatter(chip_blocks(g_up) + chip_blocks(g_down), None)
    gz2, ggain2, gnorm2 = norm_back(dz2, dgain[1], gz3 + both(dot_t(gu, w_dec_up)))
    gx = gz2.astype(BF)
    g_cross_out = dot_g(ca, gx)
    gca = dot_t(gx, w_cross_out).astype(BF).reshape(2, STREAMS, LEN, OWN_HEADS, HEAD)
    gcq, gck, gcv = attention_back(cq, ck, cv, cprobs, gca)
    gcq = gcq.reshape(rows, HALF)
    gckv = jnp.stack([gck, gcv], axis=2).reshape(2 * LEN, D)
    g_cross_q = dot_g(dh1_low, gcq)
    g_cross_kv = dot_g(enc_low, gckv)
    total3, first3 = scatter(
        chip_blocks(g_cross_q) + chip_blocks(g_cross_kv) + head_blocks(g_cross_out), first4
    )
    ecot_got = swap(enc_cot)
    ecot = pair(enc_cot[None], ecot_got[None], 0).reshape(2 * LEN, D).astype(F32)
    genc = ecot + both(dot_t(gckv, w_cross_kv))
    gz1, ggain1, gnorm1 = norm_back(dz1, dgain[0], gz2 + both(dot_t(gcq, w_cross_q)))
    go = gz1.astype(BF)
    g_dec_out = dot_g(da, go)
    gda = dot_t(go, w_dec_out).astype(BF).reshape(2, STREAMS, LEN, OWN_HEADS, HEAD)
    gqkv, grel = ngram_back(dqkv, dmain, down, onehot, gda)
    gqkv = gqkv.reshape(rows, 3 * HALF)
    grel = grel.reshape(rows, REL_HALF)
    g_dec_in = dot_g(y, gqkv)
    g_rel = dot_g(y, grel)
    rel_block = (
        g_rel.astype(BF)
        .reshape(chips, 2, r, REL_HALF)
        .transpose(0, 2, 1, 3)
        .reshape(lay.ndp, lay.nz, r, WIDE)
    )
    total2, first2 = scatter(chip_blocks(g_dec_in) + [rel_block] + head_blocks(g_dec_out), first3)

    def own_sequence(partial, count):
        parts = partial.reshape(2, count, D)
        keep = pick(parts[0], parts[1])
        return keep + swap(pick(parts[1], parts[0]).astype(BF)).astype(F32)

    def own_part(values, count):
        parts = values.reshape(2, count, D)
        return pick(parts[0], parts[1])

    dec_rows = STREAMS * LEN
    g_dec_input = own_part(gz1, dec_rows) + own_sequence(
        dot_t(gqkv, w_dec_in) + dot_t(grel, w_rel), dec_rows
    )

    def widen(vector):
        zeros = jnp.zeros_like(vector)
        return pick(jnp.concatenate([vector, zeros]), jnp.concatenate([zeros, vector]))

    def widen_hidden(vector):
        parts = vector.reshape(chips, 1, f)
        zeros = jnp.zeros_like(parts)
        return pick(
            jnp.concatenate([parts, zeros], axis=1), jnp.concatenate([zeros, parts], axis=1)
        ).reshape(-1)

    column_sums = col_sum(gqkv)
    dec_vec = jnp.concatenate(
        [
            widen(column_sums[:HALF]),
            widen(column_sums[2 * HALF :]),
            widen(col_sum(grel)),
            0.5 * col_sum(go),
            widen(col_sum(gcq)),
            widen(col_sum(gckv)[HALF:]),
            0.5 * col_sum(gx),
            widen_hidden(col_sum(gu)),
            0.5 * col_sum(gf),
            0.5 * gnorm1,
            0.5 * gnorm2,
            0.5 * gnorm3,
            0.5 * ggain1,
            0.5 * ggain2,
            0.5 * ggain3,
        ]
    )

    gz2e, eggain2, egnorm2 = norm_back(ez2, egain[1], genc)
    gfe = gz2e.astype(BF)
    ge_down = dot_g(eg, gfe)
    gue = gelu_back(eu, dot_t(gfe, w_enc_down)).astype(BF)
    ge_up = dot_g(eh1_low, gue)
    total1, first1 = scatter(chip_blocks(ge_up) + chip_blocks(ge_down), first2)
    gz1e, eggain1, egnorm1 = norm_back(ez1, egain[0], gz2e + both(dot_t(gue, w_enc_up)))
    goe = gz1e.astype(BF)
    ge_out = dot_g(ea, goe)
    gae = dot_t(goe, w_enc_out).astype(BF).reshape(2, 1, LEN, OWN_HEADS, HEAD)
    geq, gek, gev = attention_back(eq, ek, ev, eprobs, gae)
    geqkv = jnp.stack([geq[:, 0], gek, gev], axis=2).reshape(2 * LEN, 3 * HALF)
    ge_in = dot_g(x, geqkv)
    total0, first0 = scatter(chip_blocks(ge_in) + head_blocks(ge_out), first1)
    g_source = own_part(gz1e, LEN) + own_sequence(dot_t(geqkv, w_enc_in), LEN)
    ecolumn_sums = col_sum(geqkv)
    enc_vec = jnp.concatenate(
        [
            widen(ecolumn_sums[:HALF]),
            widen(ecolumn_sums[2 * HALF :]),
            0.5 * col_sum(goe),
            widen_hidden(col_sum(gue)),
            0.5 * col_sum(gfe),
            0.5 * egnorm1,
            0.5 * egnorm2,
            0.5 * eggain1,
            0.5 * eggain2,
        ]
    )
    me = lay.dp * lay.nf + lax.axis_index("fsdp")

    def own_slice(vector):
        return take(vector.reshape(lay.devices, -1), me)

    dec_vec = lax.psum(dec_vec, ("dp", "fsdp"))
    enc_vec = lax.psum(enc_vec, ("dp", "fsdp"))
    nb = sum(ENC_WIDTHS)
    g_enc_biases, g_enc_gains = own_slice(enc_vec[:nb]), own_slice(enc_vec[nb:])
    nb = sum(DEC_WIDTHS)
    g_dec_biases, g_dec_gains = own_slice(dec_vec[:nb]), own_slice(dec_vec[nb:])

    def in_rows(blocks):
        return blocks.transpose(2, 0, 1, 3).reshape(r, -1)

    def up_rows(blocks):
        per = WIDE // f
        return blocks.reshape(4, 2, r, per, f).transpose(2, 0, 3, 1, 4).reshape(r, FF)

    def side(low, high):
        return jnp.concatenate([low, high], axis=1)

    t0 = split_rows(total0, [6 * r, r, r])
    o_enc_in, o_enc_out = in_rows(own_rows_of(t0[0], 3)), side(t0[1], t0[2])
    t1 = split_rows(total1, [8 * r, f, f])
    o_enc_up, o_enc_down = up_rows(own_rows_of(t1[0], 4)), side(t1[1], t1[2])
    t2 = split_rows(total2, [6 * r, r, r, r])
    o_dec_in, o_dec_out = in_rows(own_rows_of(t2[0], 3)), side(t2[2], t2[3])
    relp = t2[1].reshape(r, 2, REL_HALF)
    rel_keep = pick(relp[:, 0], relp[:, 1])
    o_rel = pair(rel_keep, swap(pick(relp[:, 1], relp[:, 0])), 1)
    t3 = split_rows(total3, [2 * r, 4 * r, r, r])
    o_cross_q = in_rows(own_rows_of(t3[0], 1))
    o_cross_kv = in_rows(own_rows_of(t3[1], 2))
    o_cross_out = side(t3[2], t3[3])
    t4 = split_rows(total4, [8 * r, f, f])
    o_dec_up, o_dec_down = up_rows(own_rows_of(t4[0], 4)), side(t4[1], t4[2])

    return (
        own_part(enc_low, LEN),
        own_part(dec.astype(BF), dec_rows).reshape(STREAMS, LEN, D).transpose(1, 0, 2),
        g_source,
        g_dec_input.reshape(STREAMS, LEN, D).transpose(1, 0, 2),
        o_enc_in,
        o_enc_out,
        o_enc_up,
        o_enc_down,
        g_enc_gains,
        g_enc_biases,
        o_dec_in,
        o_rel,
        o_dec_out,
        o_cross_q,
        o_cross_kv,
        o_cross_out,
        o_dec_up,
        o_dec_down,
        g_dec_gains,
        g_dec_biases,
    )


BUDGET = 36 * 1024 * 1024
PIECES = 4
HBM_RATE = 1.0e6
FLOP_RATE = 1.0e9


def run(body, grid, ins, outs, scratch=(), us=5):
    arrays = [a for a, s in ins]
    return pl.pallas_call(
        body,
        grid=(grid,),
        in_specs=[s for a, s in ins],
        out_specs=[s for a, s in outs],
        out_shape=[a for a, s in outs],
        scratch_shapes=list(scratch),
        compiler_params=pltpu.CompilerParams(vmem_limit_bytes=BUDGET),
        cost_estimate=pl.CostEstimate(
            flops=int(us * FLOP_RATE), bytes_accessed=int(us * HBM_RATE), transcendentals=0
        ),
    )(*arrays)


def full(array):
    zeros = (0,) * array.ndim
    return array, pl.BlockSpec(array.shape, lambda t: zeros, pipeline_mode=pl.Buffered(1))


def small(array):
    return array, pl.BlockSpec(memory_space=pltpu.SMEM)


def out_full(shape, dtype):
    zeros = (0,) * len(shape)
    return jax.ShapeDtypeStruct(shape, dtype), pl.BlockSpec(shape, lambda t: zeros)


def out_cols(rows, cols, dtype, index):
    return (
        jax.ShapeDtypeStruct((rows, cols), dtype),
        pl.BlockSpec((rows, WIDE), lambda t: (0, index(t))),
    )


def in_cols(array, index, width=WIDE):
    return array, pl.BlockSpec((array.shape[0], width), lambda t: (0, index(t)))


def blocks(pieces, rows, index):
    return [
        (p, pl.BlockSpec((4, rows, WIDE), lambda t: (0, index(t), 0))) for p in pieces
    ]


def wide_blocks(pieces, index):
    return [(p, pl.BlockSpec((4,) + p.shape[1:2] + (WIDE,), lambda t: (0, 0, index(t)))) for p in pieces]


def assemble(refs, scr, place):
    for i in range(4):
        scr[jnp.bitwise_xor(place[0], i)] = refs[i][...]


def weight_scratch(rows, width=WIDE):
    return pltpu.VMEM((4, 4, rows, width), BF)


def matrix_of(scr):
    a, b, c, d = scr.shape
    return scr[...].reshape(a * b * c, d)


def pick_matrix(parity):
    i = lax.broadcasted_iota(jnp.int32, (HALF, HALF // 2), 0)
    j = lax.broadcasted_iota(jnp.int32, (HALF, HALF // 2), 1)
    from_row = ((j >> 5) << 6) + (parity << 5) + (j & 31)
    return jnp.where(i == from_row, 1.0, 0.0).astype(BF)


def head_masks():
    lane = lax.broadcasted_iota(jnp.int32, (1, 128), 1)
    first = jnp.where(lane < HEAD, 1.0, 0.0)
    return first.astype(BF), (1.0 - first).astype(BF)


def first_lanes(rows):
    return lax.broadcasted_iota(jnp.int32, (rows, 128), 1) < HEAD


def soft_rows(scores):
    top = jnp.max(scores, axis=-1, keepdims=True)
    raised = jnp.exp(scores - top)
    return raised * (1.0 / jnp.sum(raised, axis=-1, keepdims=True))


def masked_probs(queries, keys, count):
    scores = dot_t(queries, keys) * SCALE
    column = lax.broadcasted_iota(jnp.int32, scores.shape, 1)
    return soft_rows(jnp.where(column < count, scores, MASKED))


def attend(q, k, v, count):
    rows = q.shape[0]
    out = []
    for mask in head_masks():
        probs = masked_probs(q * mask, k, count).astype(BF)
        out.append(dot(probs, v))
    return jnp.where(first_lanes(rows), out[0], out[1]).astype(BF)


def attend_back(q, k, v, g, count):
    gq, gk, gv = [], 0.0, 0.0
    for mask in head_masks():
        qm, gm = q * mask, g * mask
        probs = masked_probs(qm, k, count)
        gp = dot_t(gm, v)
        ds = (probs * (gp - jnp.sum(probs * gp, axis=-1, keepdims=True))).astype(BF)
        gq.append(dot(ds, k))
        gk = gk + dot_g(ds, qm)
        gv = gv + dot_g(probs.astype(BF), gm)
    gq = jnp.where(first_lanes(q.shape[0]), gq[0], gq[1]) * SCALE
    return gq.astype(BF), (gk * SCALE).astype(BF), gv.astype(BF)


def split_parity(heads, place, keep, send):
    core = place[2]
    keep[...] = dot(heads[...], pick_matrix(core)).astype(BF)
    send[...] = dot(heads[...], pick_matrix(1 - core)).astype(BF)


def join_parity(keep, got, place, heads):
    core = place[2]
    heads[...] = (
        dot_t(keep[...], pick_matrix(core)) + dot_t(got[...], pick_matrix(1 - core))
    ).astype(BF)


def enc_attention(place, x, bias, pieces):
    rows = x.shape[0]

    def body(place, x, bias, *refs):
        w, (qkv, keep, send, scr, heads) = refs[:PIECES], refs[PIECES:]
        t = pl.program_id(0)
        assemble(w, scr, place)
        qkv[:, pl.ds(t * WIDE, WIDE)] = (dot(x[...], matrix_of(scr)) + bias[...]).astype(BF)

        @pl.when(t == 2)
        def _():
            for s in range(2):
                r = slice(s * LEN, s * LEN + LEN)
                for j in range(4):
                    c = [slice(HALF * i + 128 * j, HALF * i + 128 * j + 128) for i in range(3)]
                    heads[r, c[0]] = attend(qkv[r, c[0]], qkv[r, c[1]], qkv[r, c[2]], place[3 + s])
            split_parity(heads, place, keep, send)

    return run(
        body,
        3,
        [small(place), full(x), in_cols(bias, lambda t: t)] + blocks(pieces, 64, lambda t: t),
        [
            out_full((rows, 3 * HALF), BF),
            out_full((rows, HALF // 2), BF),
            out_full((rows, HALF // 2), BF),
        ],
        [weight_scratch(64), pltpu.VMEM((rows, HALF), BF)],
        us=10,
    )


def out_projection(place, keep, got, pieces):
    rows = keep.shape[0]

    def body(place, keep, got, *refs):
        w, (out, scr) = refs[:PIECES], refs[PIECES:]
        assemble(w, scr, place)
        core = place[2]
        mine = scr[pl.ds(2 * core, 2)].reshape(HALF // 2, WIDE)
        theirs = scr[pl.ds(2 - 2 * core, 2)].reshape(HALF // 2, WIDE)
        out[...] = (dot(keep[...], mine) + dot(got[...], theirs)).astype(BF)

    return run(
        body,
        2,
        [small(place), full(keep), full(got)] + blocks(pieces, 32, lambda t: 6 + t),
        [out_cols(rows, D, BF, lambda t: t)],
        [weight_scratch(32)],
        us=3,
    )[0]


def stats(v):
    centered = v - jnp.mean(v, axis=-1, keepdims=True)
    inverse = lax.rsqrt(jnp.mean(centered * centered, axis=-1, keepdims=True) + EPSILON)
    return centered * inverse, inverse


def each_tile(rows, tile, step):
    def loop(m, carry):
        step(pl.multiple_of(m * tile, tile))
        return carry

    lax.fori_loop(0, rows // tile, loop, 0)


def norm_tiles(rows, base, affine, own, other, bias, gain, shift, unit_out, inv_out, low_out, at=0):
    def step(r):
        here = pl.ds(r, LEN)
        v = base[here].astype(F32)
        if affine is not None:
            v = v * affine[0] + affine[1]
        there = pl.ds(r + at, LEN)
        v = v + (own[there].astype(F32) + other[there].astype(F32)) + bias
        unit, inverse = stats(v)
        unit_out[here] = unit
        inv_out[here] = jnp.broadcast_to(inverse, (LEN, 128))
        low_out[here] = (unit * gain + shift).astype(BF)

    each_tile(rows, LEN, step)


def norm_forward(place, base, affine, own, other, vecs):
    rows = base.shape[0]

    def body(place, base, own, other, vecs, unit, inv, low):
        aff = (vecs[0:1], vecs[1:2]) if affine else None
        norm_tiles(LEN, base, aff, own, other, vecs[2:3], vecs[3:4], vecs[4:5], unit, inv, low)

    def tiles(array):
        return array, pl.BlockSpec((LEN, array.shape[1]), lambda t: (t, 0))

    def out(width, dtype):
        return jax.ShapeDtypeStruct((rows, width), dtype), pl.BlockSpec((LEN, width), lambda t: (t, 0))

    return run(
        body,
        rows // LEN,
        [small(place), tiles(base), tiles(own), tiles(other), full(vecs)],
        [out(D, F32), out(128, F32), out(D, BF)],
        us=4,
    )


ROOT_HALF = math.sqrt(0.5)
ROOT_TWO_PI = math.sqrt(0.5 / math.pi)
TAIL = (0.254829592, -0.284496736, 1.421413741, -1.453152027, 1.061405429)


def gelu_pair(u):
    depth = 1.0 + (0.3275911 * ROOT_HALF) * jnp.abs(u)
    t = pl.reciprocal(depth, approx=True)
    t = t * (2.0 - depth * t)
    bell = jnp.exp(-0.5 * u * u)
    poly = TAIL[4]
    for c in TAIL[3::-1]:
        poly = poly * t + c
    tail = (0.5 * t) * poly * bell
    phi = jnp.where(u < 0.0, tail, 1.0 - tail)
    return u * phi, phi + u * (bell * ROOT_TWO_PI)


def ffn_forward(place, low, hidden_bias, up_pieces, down_pieces):
    rows = low.shape[0]
    hidden = hidden_bias.shape[1]
    ups = hidden // WIDE
    tile = 256

    def body(place, low, hb, *refs):
        wu, wd = refs[:PIECES], refs[PIECES : 2 * PIECES]
        g, gp, part, scr_u, scr_d, acts = refs[2 * PIECES :]
        t = pl.program_id(0)

        @pl.when(t < ups)
        def _():
            assemble(wu, scr_u, place)
            w = matrix_of(scr_u)

            def step(r):
                here = pl.ds(r, tile)
                a, b = gelu_pair(dot(low[here], w) + hb[...])
                a = a.astype(BF)
                g[here] = a
                acts[here, pl.ds(t * WIDE, WIDE)] = a
                gp[here] = b.astype(BF)

            each_tile(rows, tile, step)

        @pl.when(t >= ups)
        def _():
            assemble(wd, scr_d, place)
            part[...] = dot(acts[...], matrix_of(scr_d)).astype(BF)

    up = lambda t: jnp.minimum(t, ups - 1)
    down = lambda t: jnp.maximum(t - ups, 0)
    return run(
        body,
        ups + 2,
        [small(place), full(low), in_cols(hidden_bias, up)]
        + blocks(up_pieces, 64, up)
        + wide_blocks(down_pieces, down),
        [
            out_cols(rows, hidden, BF, up),
            out_cols(rows, hidden, BF, up),
            out_cols(rows, D, BF, down),
        ],
        [weight_scratch(64), weight_scratch(128), pltpu.VMEM((rows, hidden), BF)],
        us=14 if rows > 256 else 8,
    )


def distance_buckets(reverse):
    row = lax.broadcasted_iota(jnp.int32, (128, 128), 0) & (BUCKETS - 1)
    lane = lax.broadcasted_iota(jnp.int32, (128, 128), 1)
    distance = ((lane + 1) if reverse else (128 - lane)) & 127
    bucket = jnp.zeros((128, 128), jnp.int32)
    for target in range(1, BUCKETS):
        at = 1
        while bucket_value(at, BUCKETS) < target:
            at += 1
        bucket = bucket + jnp.where(distance >= at, 1, 0)
    return jnp.where(bucket == row, 1.0, 0.0).astype(BF)


def skew(values):
    parts = [values[128 * n : 128 * n + 128] for n in range(values.shape[0] // 128)]
    return jnp.concatenate(
        [pltpu.roll(part, 0, 1, stride=1, stride_axis=0) for part in parts], axis=0
    )


def mirror():
    row = lax.broadcasted_iota(jnp.int32, (128, 128), 0)
    lane = lax.broadcasted_iota(jnp.int32, (128, 128), 1)
    return jnp.where(row + lane == 127, 1.0, 0.0).astype(BF)


def quarter_mask(h):
    lane = lax.broadcasted_iota(jnp.int32, (1, 128), 1)
    return jnp.where((lane >> 5) == h, 1.0, 0.0).astype(BF)


def ngram_probs(qm, prod, k0, rel_high, rel_low, table, count, h, first):
    mask = quarter_mask(h % 4)
    turned = dot(rel_high * mask, table) + dot(rel_low * mask, table)
    scores = dot_t(qm, k0) * SCALE + skew(turned)
    row = lax.broadcasted_iota(jnp.int32, scores.shape, 0)
    column = lax.broadcasted_iota(jnp.int32, scores.shape, 1)
    token = row & (LEN - 1)
    reach = jnp.where(row < LEN, token, token - 1)
    scores = jnp.where((column <= reach) & (column < count), scores, MASKED)
    own = jnp.sum(prod * first, axis=-1, keepdims=True) * SCALE + turned[:, 0:1]
    main = lax.broadcasted_iota(jnp.int32, own.shape, 0) < LEN
    own = jnp.where(main, 2.0 * MASKED, own)
    top = jnp.maximum(jnp.max(scores, axis=-1, keepdims=True), own)
    raised = jnp.exp(scores - top)
    own = jnp.exp(own - top)
    scale = 1.0 / (jnp.sum(raised, axis=-1, keepdims=True) + own)
    return raised * scale, own * scale


def split_high(values):
    high = values.astype(BF)
    return high, (values - high.astype(F32)).astype(BF)


def half_rows(rows):
    first = jnp.where(lax.broadcasted_iota(jnp.int32, (rows, 128), 1) < HEAD, 1.0, 0.0)
    return first, 1.0 - first


def ngram_attention(place, y, bias, rel_bias, pieces):
    rows = y.shape[0]
    span = STREAMS * LEN

    def body(place, y, bias, rbias, *refs):
        w, wr = refs[:PIECES], refs[PIECES : 2 * PIECES]
        qkv, rel, keep, send, scr, scr_r, heads, table = refs[2 * PIECES :]
        t = pl.program_id(0)

        @pl.when(t < 3)
        def _():
            assemble(w, scr, place)
            qkv[:, pl.ds(pl.multiple_of(t * WIDE, WIDE), WIDE)] = (
                dot(y[...], matrix_of(scr)) + bias[...]
            ).astype(BF)

        @pl.when(t == 3)
        def _():
            assemble_rel(wr, scr_r, place)
            rel[...] = dot(y[...], scr_r[...].reshape(D, REL_HALF)) + rbias[...]
            table[...] = distance_buckets(False)
            lanes = half_rows(span)

            def step(s, carry):
                r = pl.ds(pl.multiple_of(s * span, span), span)
                r0 = pl.ds(pl.multiple_of(s * span, span), LEN)
                count = place[5 + s]
                for j in range(4):
                    c = [slice(HALF * i + 128 * j, HALF * i + 128 * j + 128) for i in range(3)]
                    q, k, v = qkv[r, c[0]], qkv[r, c[1]], qkv[r, c[2]]
                    k0, v0 = qkv[r0, c[1]], qkv[r0, c[2]]
                    high, low = split_high(rel[r, 128 * (j // 2) : 128 * (j // 2) + 128])
                    prod = q.astype(F32) * k.astype(F32)
                    out = []
                    for i, mask in enumerate(head_masks()):
                        probs, own = ngram_probs(
                            q * mask, prod, k0, high, low, table[...], count, 2 * j + i, lanes[i]
                        )
                        own = own.astype(BF).astype(F32)
                        out.append(dot(probs.astype(BF), v0) + own * v.astype(F32))
                    heads[r, c[0]] = jnp.where(first_lanes(span), out[0], out[1]).astype(BF)
                return carry

            lax.fori_loop(0, 2, step, 0)
            split_parity(heads, place, keep, send)

    third = lambda t: jnp.minimum(t, 2)
    return run(
        body,
        4,
        [small(place), full(y), in_cols(bias, third), full(rel_bias)]
        + blocks(pieces, 64, third)
        + blocks(pieces, 32, lambda t: 8),
        [
            out_full((rows, 3 * HALF), BF),
            out_full((rows, REL_HALF), F32),
            out_full((rows, HALF // 2), BF),
            out_full((rows, HALF // 2), BF),
        ],
        [
            weight_scratch(64),
            pltpu.VMEM((4, 4, 2, 32, REL_HALF), BF),
            pltpu.VMEM((rows, HALF), BF),
            pltpu.VMEM((128, 128), BF),
        ],
        us=19,
    )


def assemble_rel(refs, scr, place):
    for i in range(4):
        block = refs[i][...]
        at = jnp.bitwise_xor(place[0], i)
        scr[at, :, 0] = block[:, :, :REL_HALF]
        scr[at, :, 1] = block[:, :, REL_HALF:]


def cross_forward(place, y, own, other, vecs, eunit, evecs, eown, eother, q_bias, kv_bias, pieces):
    rows, mem = y.shape[0], eunit.shape[0]
    span = STREAMS * LEN

    def body(place, y, own, other, vecs, eunit, evecs, eown, eother, qb, kvb, *refs):
        w = refs[:PIECES]
        unit, inv, low, eunit2, einv2, elow, q, kv, keep, send, scr, heads = refs[PIECES:]
        t = pl.program_id(0)
        assemble(w, scr, place)

        @pl.when(t == 0)
        def _():
            norm_tiles(
                rows, y, None, own, other, vecs[0:1], vecs[1:2], vecs[2:3], unit, inv, low
            )
            norm_tiles(
                mem,
                eunit,
                (evecs[0:1], evecs[1:2]),
                eown,
                eother,
                evecs[2:3],
                evecs[3:4],
                evecs[4:5],
                eunit2,
                einv2,
                elow,
            )
            q[...] = (dot(low[...], matrix_of(scr)) + qb[...]).astype(BF)

        @pl.when(t > 0)
        def _():
            at = pl.multiple_of((t - 1) * WIDE, WIDE)
            kv[:, pl.ds(at, WIDE)] = (dot(elow[...], matrix_of(scr)) + kvb[...]).astype(BF)

        @pl.when(t == 2)
        def _():
            for s in range(2):
                r = slice(s * span, s * span + span)
                m = slice(s * LEN, s * LEN + LEN)
                for j in range(4):
                    c = slice(128 * j, 128 * j + 128)
                    c2 = slice(HALF + 128 * j, HALF + 128 * j + 128)
                    heads[r, c] = attend(q[r, c], kv[m, c], kv[m, c2], place[3 + s])
            split_parity(heads, place, keep, send)

    return run(
        body,
        3,
        [small(place)]
        + [full(a) for a in (y, own, other, vecs, eunit, evecs, eown, eother, q_bias)]
        + [in_cols(kv_bias, lambda t: jnp.maximum(t - 1, 0))]
        + blocks(pieces, 64, lambda t: t),
        [
            out_full((rows, D), F32),
            out_full((rows, 128), F32),
            out_full((rows, D), BF),
            out_full((mem, D), F32),
            out_full((mem, 128), F32),
            out_full((mem, D), BF),
            out_full((rows, HALF), BF),
            out_full((mem, D), BF),
            out_full((rows, HALF // 2), BF),
            out_full((rows, HALF // 2), BF),
        ],
        [weight_scratch(64), pltpu.VMEM((rows, HALF), BF)],
        us=15,
    )


def fold(values):
    return jnp.sum(values.reshape(values.shape[0] // 8, 8, values.shape[1]), axis=0)


def norm_back_tile(total, unit, inverse, gain):
    scaled = total * gain
    one = jnp.mean(scaled, axis=-1, keepdims=True)
    two = jnp.mean(scaled * unit, axis=-1, keepdims=True)
    return inverse * (scaled - one - unit * two)


def norm_backward(place, final, total_ins, unit_ins, vecs):
    rows = total_ins[0].shape[0]
    n_total, n_unit = len(total_ins), len(unit_ins)
    steps = rows // LEN
    mine = steps // 2

    def body(place, vecs, *refs):
        tot, uni = refs[:n_total], refs[n_total : n_total + n_unit]
        *outs, gz, gf, s_gain, s_shift, s_gf, acc = refs[n_total + n_unit :]
        t = pl.program_id(0)

        @pl.when(t == 0)
        def _():
            acc[...] = jnp.zeros_like(acc)

        if final:
            v = uni[0][...] * vecs[0:1] + vecs[1:2]
            v = v + (uni[1][...].astype(F32) + uni[2][...].astype(F32)) + vecs[2:3]
            unit, inverse = stats(v)

            @pl.when((t >= mine) == (place[2] == 1))
            def _():
                outs[0][...] = (unit * vecs[3:4] + vecs[4:5]).astype(BF)

        else:
            unit, inverse = uni[0][...], uni[1][:, 0:1]
        total = tot[0][...].astype(F32)
        if n_total > 1:
            total = total + (tot[1][...].astype(F32) + tot[2][...].astype(F32))
        acc[0:8] += fold(total * unit)
        acc[8:16] += fold(total)
        back = norm_back_tile(total, unit, inverse, vecs[3:4])
        gz[...] = back
        low = back.astype(BF)
        gf[...] = low
        acc[16:24] += fold(low.astype(F32))

        @pl.when(t == steps - 1)
        def _():
            s_gain[...] = jnp.sum(acc[0:8], axis=0, keepdims=True)
            s_shift[...] = jnp.sum(acc[8:16], axis=0, keepdims=True)
            s_gf[...] = jnp.sum(acc[16:24], axis=0, keepdims=True)

    def tiles(array):
        skip = (array.shape[0] - rows) // LEN
        return array, pl.BlockSpec((LEN, array.shape[1]), lambda t: (t + skip, 0))

    def out(dtype):
        return jax.ShapeDtypeStruct((rows, D), dtype), pl.BlockSpec((LEN, D), lambda t: (t, 0))

    def own_tile(t, place):
        return (jnp.clip(t - mine * place[2], 0, mine - 1), 0)

    outs = [out(F32), out(BF)] + [out_full((1, D), F32)] * 3
    specs = [s for a, s in outs]
    shapes = [a for a, s in outs]
    ins = [full(vecs)] + [tiles(a) for a in total_ins + unit_ins]

    def with_place(spec):
        index = spec.index_map
        return pl.BlockSpec(
            spec.block_shape, lambda t, place: index(t), pipeline_mode=spec.pipeline_mode
        )

    specs = [with_place(s) for s in specs]
    if final:
        shapes = [jax.ShapeDtypeStruct((rows // 2, D), BF)] + shapes
        specs = [pl.BlockSpec((LEN, D), own_tile)] + specs
    return pl.pallas_call(
        body,
        grid_spec=pltpu.PrefetchScalarGridSpec(
            num_scalar_prefetch=1,
            grid=(steps,),
            in_specs=[with_place(s) for a, s in ins],
            out_specs=specs,
            scratch_shapes=[pltpu.VMEM((24, D), F32)],
        ),
        out_shape=shapes,
        compiler_params=pltpu.CompilerParams(vmem_limit_bytes=BUDGET),
        cost_estimate=pl.CostEstimate(
            flops=int(5 * FLOP_RATE), bytes_accessed=int(5 * HBM_RATE), transcendentals=0
        ),
    )(place, *[a for a, s in ins])


def ffn_back(place, gf, gp, up_pieces, down_pieces):
    rows, hidden = gp.shape
    ups = hidden // WIDE

    def body(place, gf, gp, *refs):
        wu, wd = refs[:PIECES], refs[PIECES : 2 * PIECES]
        gu, part, s_gu, scr_u, scr_d, all_u, scr_all_u = refs[2 * PIECES :]
        t = pl.program_id(0)

        @pl.when(t < 2)
        def _():
            assemble(wd, scr_d.at[t], place)

        @pl.when(t >= 2)
        def _():
            b = t - 2
            assemble(wu, scr_u, place)
            scr_all_u[:, pl.ds(pl.multiple_of(b * WIDE, WIDE), WIDE)] = matrix_of(scr_u)
            w0 = scr_d[0, b].reshape(WIDE, WIDE)
            w1 = scr_d[1, b].reshape(WIDE, WIDE)
            back = dot_t(gf[:, :WIDE], w0) + dot_t(gf[:, WIDE:], w1)
            low = (back * gp[...].astype(F32)).astype(BF)
            gu[...] = low
            all_u[:, pl.ds(pl.multiple_of(b * WIDE, WIDE), WIDE)] = low
            s_gu[...] = jnp.sum(fold(low.astype(F32)), axis=0, keepdims=True)

        @pl.when(t == ups + 1)
        def _():
            part[...] = dot_t(all_u[...], scr_all_u[...]).astype(BF)

    up = lambda t: jnp.maximum(t - 2, 0)
    down = lambda t: jnp.minimum(t, 1)
    return run(
        body,
        ups + 2,
        [small(place), full(gf), in_cols(gp, up)]
        + blocks(up_pieces, 64, up)
        + wide_blocks(down_pieces, down),
        [
            out_cols(rows, hidden, BF, up),
            out_full((rows, D), BF),
            out_cols(1, hidden, F32, up),
        ],
        [
            weight_scratch(64),
            pltpu.VMEM((2, 4, 4, 128, WIDE), BF),
            pltpu.VMEM((rows, hidden), BF),
            pltpu.VMEM((D, hidden), BF),
        ],
        us=14 if rows > 256 else 8,
    )


def branch_back(place, resid, own, other, unit, inv, gain, pieces):
    rows = resid.shape[0]

    def body(place, resid, own, other, unit, inv, gain, *refs):
        w = refs[:PIECES]
        gz, gx, keep, send, s_gain, s_shift, s_gx, scr, total_out, acc = refs[PIECES:]
        t = pl.program_id(0)
        assemble(w, scr, place)

        @pl.when(t == 0)
        def _():
            acc[...] = jnp.zeros_like(acc)

            def step(r):
                here = pl.ds(r, LEN)
                total = resid[here] + (own[here].astype(F32) + other[here].astype(F32))
                acc[0:8] += fold(total * unit[here])
                acc[8:16] += fold(total)
                back = norm_back_tile(total, unit[here], inv[here, 0:1], gain[...])
                gz[here] = back
                low = back.astype(BF)
                gx[here] = low
                acc[16:24] += fold(low.astype(F32))

            each_tile(rows, LEN, step)
            s_gain[...] = jnp.sum(acc[0:8], axis=0, keepdims=True)
            s_shift[...] = jnp.sum(acc[8:16], axis=0, keepdims=True)
            s_gx[...] = jnp.sum(acc[16:24], axis=0, keepdims=True)
            total_out[...] = dot_t(gx[:, :WIDE], matrix_of(scr))

        @pl.when(t == 1)
        def _():
            total_out[...] += dot_t(gx[:, WIDE:], matrix_of(scr))
            core = place[2]
            quarter = HALF // 2
            keep[...] = total_out[:, pl.ds(pl.multiple_of(quarter * core, 128), quarter)].astype(BF)
            send[...] = total_out[
                :, pl.ds(pl.multiple_of(quarter * (1 - core), 128), quarter)
            ].astype(BF)

    return run(
        body,
        2,
        [small(place)]
        + [full(a) for a in (resid, own, other, unit, inv, gain)]
        + blocks(pieces, 32, lambda t: 6 + t),
        [
            out_full((rows, D), F32),
            out_full((rows, D), BF),
            out_full((rows, HALF // 2), BF),
            out_full((rows, HALF // 2), BF),
            out_full((1, D), F32),
            out_full((1, D), F32),
            out_full((1, D), F32),
        ],
        [weight_scratch(32), pltpu.VMEM((rows, HALF), F32), pltpu.VMEM((24, D), F32)],
        us=10 if rows > 256 else 5,
    )


def column_sums(out, values):
    out[...] = jnp.sum(fold(values.astype(F32)), axis=0, keepdims=True)


def cross_back(place, q, kv, keep, got, pieces):
    rows, mem = q.shape[0], kv.shape[0]
    span = STREAMS * LEN

    def body(place, q, kv, keep, got, *refs):
        w = refs[:PIECES]
        gq, gkv, part, s_gq, s_gkv, scr, g, acc = refs[PIECES:]
        t = pl.program_id(0)
        assemble(w, scr, place)

        @pl.when(t == 0)
        def _():
            join_parity(keep, got, place, g)
            for s in range(2):
                r = slice(s * span, s * span + span)
                m = slice(s * LEN, s * LEN + LEN)
                for j in range(4):
                    c = slice(128 * j, 128 * j + 128)
                    c2 = slice(HALF + 128 * j, HALF + 128 * j + 128)
                    gq[r, c], gkv[m, c], gkv[m, c2] = attend_back(
                        q[r, c], kv[m, c], kv[m, c2], g[r, c], place[3 + s]
                    )
            column_sums(s_gq, gq[...])
            column_sums(s_gkv, gkv[...])
            part[:rows] = dot_t(gq[...], matrix_of(scr)).astype(BF)

        @pl.when(t == 1)
        def _():
            acc[...] = dot_t(gkv[:, :HALF], matrix_of(scr))

        @pl.when(t == 2)
        def _():
            part[rows:] = (acc[...] + dot_t(gkv[:, HALF:], matrix_of(scr))).astype(BF)

    return run(
        body,
        3,
        [small(place), full(q), full(kv), full(keep), full(got)]
        + blocks(pieces, 64, lambda t: t),
        [
            out_full((rows, HALF), BF),
            out_full((mem, D), BF),
            out_full((rows + mem, D), BF),
            out_full((1, HALF), F32),
            out_full((1, D), F32),
        ],
        [weight_scratch(64), pltpu.VMEM((rows, HALF), BF), pltpu.VMEM((mem, D), F32)],
        us=14,
    )


def input_grads(place, gz, parts, keep, send):
    rows = gz.shape[0] // 2
    core = place[2]
    here = pl.ds(pl.multiple_of(rows * core, LEN), rows)
    there = pl.ds(pl.multiple_of(rows * (1 - core), LEN), rows)
    total = gz[here]
    for g, w in parts:
        total = total + dot_t(g[here], w)
    keep[...] = total
    total = 0.0
    for g, w in parts:
        total = total + dot_t(g[there], w)
    send[...] = total.astype(BF)


def enc_attention_back(place, qkv, keep, got, gz, pieces):
    rows = qkv.shape[0]

    def body(place, qkv, keep, got, gz, *refs):
        w = refs[:PIECES]
        gqkv, out, send, sums, scr, g, win = refs[PIECES:]
        t = pl.program_id(0)
        assemble(w, scr, place)
        win[:, pl.ds(pl.multiple_of(t * WIDE, WIDE), WIDE)] = matrix_of(scr)

        @pl.when(t == 0)
        def _():
            join_parity(keep, got, place, g)
            for s in range(2):
                r = slice(s * LEN, s * LEN + LEN)
                for j in range(4):
                    c = [slice(HALF * i + 128 * j, HALF * i + 128 * j + 128) for i in range(3)]
                    gqkv[r, c[0]], gqkv[r, c[1]], gqkv[r, c[2]] = attend_back(
                        qkv[r, c[0]], qkv[r, c[1]], qkv[r, c[2]], g[r, c[0]], place[3 + s]
                    )
            column_sums(sums, gqkv[...])

        @pl.when(t == 2)
        def _():
            input_grads(place, gz, [(gqkv, win[...])], out, send)

    return run(
        body,
        3,
        [small(place), full(qkv), full(keep), full(got), full(gz)]
        + blocks(pieces, 64, lambda t: t),
        [
            out_full((rows, 3 * HALF), BF),
            out_full((rows // 2, D), F32),
            out_full((rows // 2, D), BF),
            out_full((1, 3 * HALF), F32),
        ],
        [weight_scratch(64), pltpu.VMEM((rows, HALF), BF), pltpu.VMEM((D, 3 * HALF), BF)],
        us=13,
    )


def ngram_back_kernel(place, qkv, rel, keep, got, gz, pieces):
    rows = qkv.shape[0]
    span = STREAMS * LEN

    def body(place, qkv, rel, keep, got, gz, *refs):
        w, wr = refs[:PIECES], refs[PIECES : 2 * PIECES]
        gqkv, grel, out, send, sums, s_rel, scr, scr_r, g, win, *tables = refs[2 * PIECES :]
        table, table_back, flip = tables
        t = pl.program_id(0)

        @pl.when(t < 3)
        def _():
            assemble(w, scr, place)
            win[:, pl.ds(pl.multiple_of(t * WIDE, WIDE), WIDE)] = matrix_of(scr)

        @pl.when(t == 0)
        def _():
            join_parity(keep, got, place, g)
            table[...] = distance_buckets(False)
            table_back[...] = distance_buckets(True)
            flip[...] = mirror()
            lanes = half_rows(span)

            def step(s, carry):
                r = pl.ds(pl.multiple_of(s * span, span), span)
                r0 = pl.ds(pl.multiple_of(s * span, span), LEN)
                r1 = pl.ds(pl.multiple_of(s * span + LEN, LEN), span - LEN)
                count = place[5 + s]
                for j in range(4):
                    c = [slice(HALF * i + 128 * j, HALF * i + 128 * j + 128) for i in range(3)]
                    q, k, v = qkv[r, c[0]], qkv[r, c[1]], qkv[r, c[2]]
                    k0, v0 = qkv[r0, c[1]], qkv[r0, c[2]]
                    go = g[r, c[0]]
                    high, low = split_high(rel[r, 128 * (j // 2) : 128 * (j // 2) + 128])
                    prod = q.astype(F32) * k.astype(F32)
                    prod_g = go.astype(F32) * v.astype(F32)
                    gq, gk0, gv0, p_own, d_own, turned = [], 0.0, 0.0, [], [], []
                    for i, mask in enumerate(head_masks()):
                        qm, gm = q * mask, go * mask
                        h = 2 * j + i
                        probs, own = ngram_probs(
                            qm, prod, k0, high, low, table[...], count, h, lanes[i]
                        )
                        gp = dot_t(gm, v0)
                        g_own = jnp.sum(prod_g * lanes[i], axis=-1, keepdims=True)
                        inner = jnp.sum(probs * gp, axis=-1, keepdims=True) + own * g_own
                        ds = (probs * (gp - inner)).astype(BF)
                        ds_own = (own * (g_own - inner)).astype(BF).astype(F32)
                        gq.append(dot(ds, k0))
                        gk0 = gk0 + dot_g(ds, qm)
                        gv0 = gv0 + dot_g(probs.astype(BF), gm)
                        p_own.append(own.astype(BF).astype(F32))
                        d_own.append(ds_own)
                        back = skew(dot(ds, flip[...]))
                        lane = lax.broadcasted_iota(jnp.int32, back.shape, 1)
                        main = lax.broadcasted_iota(jnp.int32, back.shape, 0) < LEN
                        back = jnp.where((lane == 127) & jnp.logical_not(main), ds_own, back)
                        grads = dot_t(back.astype(BF), table_back[...])
                        turned.append(grads * quarter_mask(h % 4).astype(F32))
                    first = first_lanes(span)
                    d_own = jnp.where(first, d_own[0], d_own[1])
                    p_own = jnp.where(first, p_own[0], p_own[1])
                    gqf = jnp.where(first, gq[0], gq[1]) + d_own * k.astype(F32)
                    gqkv[r, c[0]] = (gqf * SCALE).astype(BF)
                    gkn = d_own * q.astype(F32) * SCALE
                    gvn = p_own * go.astype(F32)
                    gqkv[r0, c[1]] = (gk0 * SCALE).astype(BF)
                    gqkv[r0, c[2]] = gv0.astype(BF)
                    gqkv[r1, c[1]] = gkn[LEN:].astype(BF)
                    gqkv[r1, c[2]] = gvn[LEN:].astype(BF)
                    both = turned[0] + turned[1]
                    at = slice(128 * (j // 2), 128 * (j // 2) + 128)
                    if j % 2 == 0:
                        held = both
                    else:
                        grel[r, at] = (held + both).astype(BF)
                return carry

            lax.fori_loop(0, 2, step, 0)
            column_sums(sums, gqkv[...])
            column_sums(s_rel, grel[...])

        @pl.when(t == 3)
        def _():
            assemble_rel(wr, scr_r, place)
            wrel = scr_r[...].reshape(D, REL_HALF)
            input_grads(place, gz, [(gqkv, win[...]), (grel, wrel)], out, send)

    third = lambda t: jnp.minimum(t, 2)
    return run(
        body,
        4,
        [small(place), full(qkv), full(rel), full(keep), full(got), full(gz)]
        + blocks(pieces, 64, third)
        + blocks(pieces, 32, lambda t: 8),
        [
            out_full((rows, 3 * HALF), BF),
            out_full((rows, REL_HALF), BF),
            out_full((rows // 2, D), F32),
            out_full((rows // 2, D), BF),
            out_full((1, 3 * HALF), F32),
            out_full((1, REL_HALF), F32),
        ],
        [
            weight_scratch(64),
            pltpu.VMEM((4, 4, 2, 32, REL_HALF), BF),
            pltpu.VMEM((rows, HALF), BF),
            pltpu.VMEM((D, 3 * HALF), BF),
        ]
        + [pltpu.VMEM((128, 128), BF)] * 3,
        us=29,
    )


def grad_chunk(place, arrays, terms, total_rows, width=WIDE):
    n = len(arrays)

    def body(place, *refs):
        ins, outs, scr = refs[:n], refs[n : n + 4], refs[n + 4]
        t = pl.program_id(0)
        dp, core = place[0], place[2]

        def spread(value, at, rows, lanes=slice(0, WIDE)):
            v = value.astype(BF).reshape(4, 4, rows, WIDE)
            scr[:, :, :rows] = v
            for i in range(4):
                outs[i][:, at : at + rows, lanes] = scr[jnp.bitwise_xor(dp, i), :, :rows]

        for index, (kind, at, x, g, col) in enumerate(terms):

            @pl.when(t == index)
            def _(kind=kind, at=at, x=x, g=g, col=col):
                if kind == "whole":
                    spread(ins[x][...], at, ins[x].shape[0] // 16)
                    return
                if kind == "heads":
                    right = ins[g][:, col : col + WIDE]
                    mine, theirs = ins[x][...], ins[x + 1][...]
                    keep, got = dot_g(mine, right), dot_g(theirs, right)
                    quarter = (2, 4, 32, WIDE)
                    scr[pl.ds(2 * core, 2), :, :32] = keep.astype(BF).reshape(quarter)
                    scr[pl.ds(2 - 2 * core, 2), :, :32] = got.astype(BF).reshape(quarter)
                    spread(scr[:, :, :32], at, 32)
                    return
                if kind == "rel":
                    v = dot_g(ins[x][...], ins[g][...]).astype(BF).reshape(16, 2, 32, REL_HALF)
                    spread(jnp.concatenate([v[:, 0], v[:, 1]], axis=-1), at, 32)
                    return
                value = dot_g(ins[x][...], ins[g][:, col : col + WIDE])
                lanes = slice(col, col + WIDE) if kind == "rows" else slice(0, WIDE)
                spread(value, at, value.shape[0] // 16, lanes)

    return run(
        body,
        len(terms),
        [small(place)] + [full(a) for a in arrays],
        [out_full((4, total_rows, width), BF)] * 4,
        [weight_scratch(128)],
        us=10,
    )


def vec_chunk(place, pieces):
    def body(place, *refs):
        assemble(refs[:PIECES], refs[PIECES], place)

    return run(
        body,
        1,
        [small(place)] + blocks(pieces, 16, lambda t: 18),
        [out_full((4, 4, 16, WIDE), BF)],
        us=2,
    )[0]


class Order:

    def __init__(self, place):
        self.place = place
        self.last = None

    def after(self, *values):
        if self.last is not None:
            values = (self.last,) + values
        self.place = tie(self.place, *values)
        self.last = None

    def run(self, kernel, *args):
        if self.last is not None:
            self.place = tie(self.place, self.last)
        out = kernel(self.place, *args)
        self.last = out[0] if isinstance(out, (list, tuple)) else out
        return out

    def matmul(self, left, right):
        if self.last is not None:
            right = tie(right, self.last)
        self.last = dot_g(left, right).astype(BF)
        return self.last

    def add(self, first, *others, dtype=BF):
        if self.last is not None:
            first = tie(first, self.last)
        self.last = sum((v.astype(F32) for v in others), first.astype(F32)).astype(dtype)
        return self.last


class Links:

    def __init__(self, lay):
        self.lay = lay
        self.gathered = []
        self.first = []
        self.second = []
        self.far = 2
        self.groups = [list(range(core, lay.nf, 2)) for core in range(2)]

    def turn(self):
        self.far = 3 - self.far
        return self.far

    def gather(self, buf, direct=False):
        far = 3 if direct else self.turn()
        if len(self.gathered) >= 2:
            buf = tie(buf, self.gathered[-2])
        own = lax.all_gather(buf, "fsdp", axis=0, axis_index_groups=self.groups)
        self.gathered.append(own)
        ready = own
        if self.first:
            ready = tie(ready, *self.first[-1])
        if len(self.second) >= 3:
            ready = tie(ready, self.second[-3])
        x, y = self.lay.flip_dp(ready, 1), self.lay.flip_dp(ready, 2)
        self.first.append((x, y))
        if direct:
            d = self.lay.flip_dp(ready, 3)
        else:
            d = self.lay.flip_dp(x, 2) if far == 2 else self.lay.flip_dp(y, 1)
        self.second.append(d)
        return [own, x, y, d]

    def scatter_whole(self, value):
        lay = self.lay
        groups = [
            [dp * lay.nf + fs for dp in range(lay.ndp) for fs in range(core, lay.nf, 2)]
            for core in range(2)
        ]
        return lax.psum_scatter(
            value, ("dp", "fsdp"), scatter_dimension=0, tiled=True, axis_index_groups=groups
        ).astype(F32)

    def scatter(self, order, parts, direct=False):
        own, x, y, d = parts
        if direct:
            moved = [self.lay.flip_dp(part, i + 1) for i, part in enumerate((x, y, d))]
            yield
            yield
            total = order.add(own, *moved)
        else:
            far = self.turn()
            d = self.lay.flip_dp(d, far)
            if far == 2:
                y = self.lay.flip_dp(y, 2)
                yield
                x = self.lay.flip_dp(order.add(x, d), 1)
            else:
                x = self.lay.flip_dp(x, 1)
                yield
                y = self.lay.flip_dp(order.add(y, d), 2)
            yield
            total = order.add(own, x, y)
        yield lax.psum_scatter(
            total, "fsdp", scatter_dimension=0, axis_index_groups=self.groups
        ).astype(F32)


def shards_fast(
    ndp,
    nf,
    source,
    dec_in,
    src_lengths,
    tgt_lengths,
    enc_in_proj,
    enc_out_proj,
    enc_ffn_in,
    enc_ffn_out,
    enc_gains,
    enc_biases,
    dec_in_proj,
    dec_rel_proj,
    dec_out_proj,
    cross_query,
    cross_kv,
    cross_out,
    dec_ffn_in,
    dec_ffn_out,
    dec_gains,
    dec_biases,
    enc_cot,
    dec_cot,
):
    lay = Layout(ndp, nf)
    lay.place()
    r, f, chips = lay.r, lay.f, lay.chips
    swap, pick, pair = lay.swap, lay.pick, lay.pair
    core = lay.core
    dec_rows = STREAMS * LEN

    links = Links(lay)
    w = {"dec_down": links.gather(dec_ffn_out), "enc_down": links.gather(enc_ffn_out)}

    def halves(matrix, groups, width):
        parts = matrix.reshape(r, groups, 2, width)
        return (
            pick(parts[:, :, 0], parts[:, :, 1]).reshape(r, groups * width),
            pick(parts[:, :, 1], parts[:, :, 0]).reshape(r, groups * width),
        )

    split = [
        halves(enc_in_proj, 3, HALF),
        halves(enc_ffn_in, chips, f),
        halves(dec_in_proj, 3, HALF),
        halves(cross_query, 1, HALF),
        halves(cross_kv, 2, HALF),
        halves(dec_ffn_in, chips, f),
        halves(dec_rel_proj, 1, REL_HALF),
    ]
    vec = jnp.concatenate(
        [
            enc_biases,
            enc_gains,
            dec_biases,
            dec_gains,
            src_lengths.astype(BF),
            tgt_lengths.astype(BF),
        ]
    )
    nvec = vec.shape[0]
    padded = -(-nvec // WIDE) * WIDE
    vec = jnp.pad(vec, (0, padded - nvec))
    mine = jnp.concatenate([own for own, other in split], axis=1)
    theirs = jnp.concatenate([other for own, other in split], axis=1)
    theirs_got = swap(theirs)
    vec_got = swap(vec)
    source_got = swap(source)
    dec_own = dec_in.transpose(1, 0, 2).reshape(dec_rows, D)
    dec_got = swap(dec_own)

    def column_blocks(start, count):
        return [
            pair(
                mine[:, start + WIDE * i : start + WIDE * i + WIDE],
                theirs_got[:, start + WIDE * i : start + WIDE * i + WIDE],
                0,
            )
            for i in range(count)
        ]

    def row_blocks(matrix):
        return [matrix[:, :WIDE], matrix[:, WIDE:]]

    rel_start = mine.shape[1] - REL_HALF
    rel_block = pair(mine[:, rel_start:], theirs_got[:, rel_start:], 1)
    vec_pair = pair(vec[None], vec_got[None], 0)
    vec_used = 2 * padded // WIDE
    vec_block = jnp.pad(vec_pair.reshape(vec_used, WIDE), ((0, 16 - vec_used), (0, 0)))
    at = [0, 3 * WIDE, 7 * WIDE, 10 * WIDE, 11 * WIDE, 13 * WIDE]
    chunk_parts = {
        "enc": column_blocks(at[0], 3) + row_blocks(enc_out_proj),
        "enc_up": column_blocks(at[1], 4),
        "dec": column_blocks(at[2], 3) + row_blocks(dec_out_proj) + [rel_block, vec_block],
        "cross": column_blocks(at[3], 1) + column_blocks(at[4], 2) + row_blocks(cross_out),
        "dec_up": column_blocks(at[5], 4),
    }
    for name in ("dec", "enc", "enc_up", "cross", "dec_up"):
        w[name] = links.gather(jnp.concatenate(chunk_parts[name], axis=0))

    lens = vec_pair[:, nvec - 2 : nvec].T.reshape(-1).astype(F32).astype(jnp.int32)
    place = jnp.concatenate(
        [jnp.stack([lay.dp, lay.z, core]).astype(jnp.int32), lens, jnp.zeros((1,), jnp.int32)]
    )

    order = Order(place)
    vec_all = order.run(vec_chunk, w["dec"]).reshape(chips, 16, WIDE)[:, :vec_used]
    vec_all = vec_all.reshape(lay.devices, padded).astype(F32)
    widths = [enc_biases.shape[0], enc_gains.shape[0], dec_biases.shape[0], dec_gains.shape[0]]
    starts = [0]
    for width in widths:
        starts.append(starts[-1] + width)
    v_enc_b, v_enc_g, v_dec_b, v_dec_g = [
        vec_all[:, starts[i] : starts[i + 1]].reshape(-1) for i in range(4)
    ]
    eb, eg_rows = v_enc_b.reshape(-1, D), v_enc_g.reshape(2, D)
    dg_rows = v_dec_g.reshape(3, D)
    d_split = 2 * D + HEADS * BUCKETS
    db = v_dec_b[d_split:].reshape(-1, D)

    def half_of(vector):
        parts = vector.reshape(2, -1)
        return pick(parts[0], parts[1])

    def hidden_of(vector):
        parts = vector.reshape(chips, 2, f)
        return pick(parts[:, 0], parts[:, 1]).reshape(1, -1)

    zero_half = jnp.zeros((HALF,), F32)

    def qkv_bias(q, v):
        return jnp.concatenate([half_of(q), zero_half, half_of(v)])[None]

    def rows_of(*vectors):
        return jnp.stack(vectors)

    x = pair(source, source_got, 0)
    y = pair(dec_own, dec_got, 0)
    dcot_own = dec_cot.transpose(1, 0, 2).reshape(dec_rows, D)
    dcot = pair(dcot_own, swap(dcot_own), 0)
    ecot = pair(enc_cot, swap(enc_cot), 0)
    order.after(x, y, dcot, ecot)
    order.after(links.gathered[5], *links.first[3], links.second[1])
    dqkv, rel, da_keep, da_send = order.run(
        ngram_attention,
        y,
        qkv_bias(v_dec_b[:D], v_dec_b[D : 2 * D]),
        half_of(v_dec_b[2 * D : d_split])[None],
        w["dec"],
    )
    da_got = swap(da_send)
    order.after(links.gathered[6], *links.first[4])
    eqkv, ea_keep, ea_send = order.run(enc_attention, x, qkv_bias(eb[0], eb[1]), w["enc"])
    ea_got = swap(ea_send)
    order.after(*links.first[5])
    p3 = order.run(out_projection, da_keep, da_got, w["dec"])
    p3_got = swap(p3)
    p1 = order.run(out_projection, ea_keep, ea_got, w["enc"])
    p1_got = swap(p1)
    eunit1, einv1, eh1_low = order.run(
        norm_forward,
        x,
        False,
        p1,
        p1_got,
        rows_of(eb[2], eb[2], eb[2], eg_rows[0], eb[8]),
    )
    order.after(links.second[5], *links.first[6])
    eg, egp, p2 = order.run(
        ffn_forward, eh1_low, hidden_of(eb[3:7]), w["enc_up"], w["enc_down"]
    )
    p2_got = swap(p2)
    order.after(links.second[6])
    dunit1, dinv1, dh1_low, eunit2, einv2, enc_low, cq, ckv, ca_keep, ca_send = order.run(
        cross_forward,
        y,
        p3,
        p3_got,
        rows_of(db[0], dg_rows[0], db[9]),
        eunit1,
        rows_of(eg_rows[0], eb[8], eb[7], eg_rows[1], eb[9]),
        p2,
        p2_got,
        half_of(db[1])[None],
        jnp.concatenate([zero_half, half_of(db[2])])[None],
        w["cross"],
    )
    ca_got = swap(ca_send)
    p4 = order.run(out_projection, ca_keep, ca_got, w["cross"])
    p4_got = swap(p4)
    dunit2, dinv2, dh2_low = order.run(
        norm_forward,
        dunit1,
        True,
        p4,
        p4_got,
        rows_of(dg_rows[0], db[9], db[3], dg_rows[1], db[10]),
    )
    dg, dgp, p5 = order.run(
        ffn_forward, dh2_low, hidden_of(db[4:8]), w["dec_up"], w["dec_down"]
    )
    p5_got = swap(p5)

    up_terms = [("plain", 64 * b, 0, 1, WIDE * b) for b in range(4)]
    down_terms = [("rows", 0, 0, 1, WIDE * h) for h in range(2)]

    def grads(*args):
        scatter = links.scatter(order, order.run(grad_chunk, *args))
        next(scatter)
        return scatter

    dec_out, gz3, gf, s_gain3, s_shift3, s_gf = order.run(
        norm_backward,
        True,
        [dcot],
        [dunit2, p5, p5_got],
        rows_of(dg_rows[1], db[10], db[8], dg_rows[2], db[11]),
    )
    r_dd = grads([dg, gf], down_terms, 128, D)
    gu, p6, s_gu = order.run(ffn_back, gf, dgp, w["dec_up"], w["dec_down"])
    p6_got = swap(p6)
    r_du = grads([dh2_low, gu], up_terms, 256)
    gz2, gx, gca_keep, gca_send, s_gain2, s_shift2, s_gx = order.run(
        branch_back, gz3, p6, p6_got, dunit2, dinv2, dg_rows[1:2], w["cross"]
    )
    gca_got = swap(gca_send)
    next(r_dd)
    next(r_du)
    gcq, gckv, p7, s_gcq, s_gckv = order.run(
        cross_back, cq, ckv, gca_keep, gca_got, w["cross"]
    )
    p7_got = swap(p7)
    r_cross = grads(
        [dh1_low, gcq, enc_low, gckv, ca_keep, ca_got, gx],
        [
            ("plain", 0, 0, 1, 0),
            ("plain", 64, 2, 3, 0),
            ("plain", 128, 2, 3, WIDE),
            ("heads", 192, 4, 6, 0),
            ("heads", 224, 4, 6, WIDE),
        ],
        256,
    )
    gz1, go, gda_keep, gda_send, s_gain1, s_shift1, s_go = order.run(
        branch_back, gz2, p7, p7_got, dunit1, dinv1, dg_rows[0:1], w["dec"]
    )
    gda_got = swap(gda_send)
    gz2e, gfe, e_gain2, e_shift2, s_gfe = order.run(
        norm_backward, False, [ecot, p7, p7_got], [eunit2, einv2], rows_of(*([eg_rows[1]] * 5))
    )
    gue, p9, s_gue = order.run(ffn_back, gfe, egp, w["enc_up"], w["enc_down"])
    p9_got = swap(p9)
    total_dd = next(r_dd)
    next(r_cross)
    r_ed = grads([eg, gfe], down_terms, 128, D)
    r_eu = grads([eh1_low, gue], up_terms, 256)
    total_du = next(r_du)
    gz1e, goe, gea_keep, gea_send, e_gain1, e_shift1, s_goe = order.run(
        branch_back, gz2e, p9, p9_got, eunit1, einv1, eg_rows[0:1], w["enc"]
    )
    gea_got = swap(gea_send)
    gqkv, grel, p8, p8_send, s_gqkv, s_grel = order.run(
        ngram_back_kernel, dqkv, rel, gda_keep, gda_got, gz1, w["dec"]
    )
    p8_got = swap(p8_send)
    next(r_ed)
    next(r_eu)
    total_cross = next(r_cross)
    geqkv, p10, p10_send, s_geqkv = order.run(
        enc_attention_back, eqkv, gea_keep, gea_got, gz1e, w["enc"]
    )
    p10_got = swap(p10_send)
    g_dec_in = order.add(p8, p8_got, dtype=F32)
    r_dec = grads(
        [y, gqkv, da_keep, da_got, go, grel],
        [("plain", 64 * b, 0, 1, WIDE * b) for b in range(3)]
        + [("heads", 192, 2, 4, 0), ("heads", 224, 2, 4, WIDE), ("rel", 256, 0, 5, 0)],
        288,
    )
    g_source = order.add(p10, p10_got, dtype=F32)
    total_ed = next(r_ed)
    total_eu = next(r_eu)

    def widen(vector):
        zeros = jnp.zeros_like(vector)
        return pick(jnp.concatenate([vector, zeros]), jnp.concatenate([zeros, vector]))

    def widen_hidden(vector):
        parts = vector.reshape(chips, 1, f)
        zeros = jnp.zeros_like(parts)
        return pick(
            jnp.concatenate([parts, zeros], axis=1), jnp.concatenate([zeros, parts], axis=1)
        ).reshape(-1)

    def owned(*vectors):
        return jnp.concatenate(vectors).reshape(lay.devices, -1)

    vec_grads = jnp.concatenate(
        [
            owned(
                widen(s_geqkv[0, :HALF]),
                widen(s_geqkv[0, 2 * HALF :]),
                0.5 * s_goe[0],
                widen_hidden(s_gue),
                0.5 * s_gfe[0],
                0.5 * e_shift1[0],
                0.5 * e_shift2[0],
            ),
            owned(0.5 * e_gain1[0], 0.5 * e_gain2[0]),
            owned(
                widen(s_gqkv[0, :HALF]),
                widen(s_gqkv[0, 2 * HALF :]),
                widen(s_grel[0]),
                0.5 * s_go[0],
                widen(s_gcq[0]),
                widen(s_gckv[0, HALF:]),
                0.5 * s_gx[0],
                widen_hidden(s_gu),
                0.5 * s_gf[0],
                0.5 * s_shift1[0],
                0.5 * s_shift2[0],
                0.5 * s_shift3[0],
            ),
            owned(0.5 * s_gain1[0], 0.5 * s_gain2[0], 0.5 * s_gain3[0]),
        ],
        axis=1,
    ).astype(BF)
    vec_width = vec_grads.shape[1]
    vec_grads = jnp.pad(vec_grads, ((0, 0), (0, padded - vec_width)))
    vec_grads = vec_grads.reshape(chips, vec_used, WIDE)
    vec_grads = jnp.pad(vec_grads, ((0, 0), (0, 16 - vec_used), (0, 0))).reshape(chips * 16, WIDE)
    r_enc = grads(
        [x, geqkv, ea_keep, ea_got, goe, vec_grads],
        [("plain", 64 * b, 0, 1, WIDE * b) for b in range(3)]
        + [("heads", 192, 2, 4, 0), ("heads", 224, 2, 4, WIDE), ("whole", 256, 5, 5, 0)],
        272,
    )
    next(r_dec)
    next(r_enc)
    total2 = next(r_dec)
    total0 = next(r_enc)

    def split_rows(total, sizes):
        at = 0
        result = []
        for size in sizes:
            result.append(total[at : at + size])
            at += size
        return result

    def own_rows_of(total, count):
        rows = total.reshape(count, 2, r, WIDE)
        keep = pick(rows[:, 0], rows[:, 1])
        got = swap(pick(rows[:, 1], rows[:, 0]))
        return pair(keep[:, None], got[:, None], 1)

    def in_rows(rows):
        return rows.transpose(2, 0, 1, 3).reshape(r, -1)

    def up_rows(rows):
        per = WIDE // f
        return rows.reshape(4, 2, r, per, f).transpose(2, 0, 3, 1, 4).reshape(r, FF)

    def side(low, high):
        return jnp.concatenate([low, high], axis=1)

    t0 = split_rows(total0, [6 * r, r, r, 16])
    o_enc_in, o_enc_out = in_rows(own_rows_of(t0[0], 3)), side(t0[1], t0[2])
    vec_sum = t0[3][:vec_used].reshape(2, padded)
    vec_sum = pick(vec_sum[0], vec_sum[1]) + swap(pick(vec_sum[1], vec_sum[0]))
    o_vec = [vec_sum[starts[i] : starts[i + 1]] for i in range(4)]
    o_enc_up = up_rows(own_rows_of(total_eu, 4))
    o_enc_down = total_ed
    t2 = split_rows(total2, [6 * r, r, r, r])
    o_dec_in, o_dec_out = in_rows(own_rows_of(t2[0], 3)), side(t2[1], t2[2])
    relp = t2[3].reshape(r, 2, REL_HALF)
    o_rel = pair(pick(relp[:, 0], relp[:, 1]), swap(pick(relp[:, 1], relp[:, 0])), 1)
    t3 = split_rows(total_cross, [2 * r, 4 * r, r, r])
    o_cross_q = in_rows(own_rows_of(t3[0], 1))
    o_cross_kv = in_rows(own_rows_of(t3[1], 2))
    o_cross_out = side(t3[2], t3[3])
    o_dec_up = up_rows(own_rows_of(total_du, 4))
    o_dec_down = total_dd

    return (
        pick(enc_low[:LEN], enc_low[LEN:]),
        dec_out.reshape(STREAMS, LEN, D).transpose(1, 0, 2),
        g_source,
        g_dec_in.reshape(STREAMS, LEN, D).transpose(1, 0, 2),
        o_enc_in,
        o_enc_out,
        o_enc_up,
        o_enc_down,
        o_vec[1],
        o_vec[0],
        o_dec_in,
        o_rel,
        o_dec_out,
        o_cross_q,
        o_cross_kv,
        o_cross_out,
        o_dec_up,
        o_dec_down,
        o_vec[3],
        o_vec[2],
    )


def solution(mesh):
    ndp, nf = mesh.shape["dp"], mesh.shape["fsdp"]
    whole = ("dp", "fsdp")
    one, two, three = P(whole), P(whole, None), P(whole, None, None)
    args = (two, three, one, one) + (two,) * 4 + (one,) * 2 + (two,) * 8 + (one,) * 2 + (two, three)
    outs = (two, three, two, three) + (two,) * 4 + (one,) * 2 + (two,) * 8 + (one,) * 2

    def body(*arrays):
        if (ndp, nf) == (4, 8):
            return shards_fast(ndp, nf, *arrays)
        return shards(ndp, nf, *arrays)

    return jax.shard_map(body, mesh=mesh, in_specs=args, out_specs=outs, check_vma=False)
```

```python
import math

import jax
import jax.numpy as jnp
from jax import lax
from jax.experimental import pallas as pl
from jax.experimental.pallas import tpu as pltpu
from jax.sharding import PartitionSpec as P

D = 1024
HEADS = 16
HEAD = 64
FF = 4096
NGRAM = 2
STREAMS = NGRAM + 1
BUCKETS = 32
LEN = 128
HALF = D // 2
OWN_HEADS = HEADS // 2
REL_HALF = OWN_HEADS * BUCKETS
HIDDEN_HALF = FF // 2
WIDE = 512
EPSILON = 1e-05
MASKED = -1000000000.0
SCALE = 1.0 / math.sqrt(HEAD)
BF = jnp.bfloat16
F32 = jnp.float32
ENC_WIDTHS = (D, D, D, FF, D, D, D)
DEC_WIDTHS = (D, D, HEADS * BUCKETS, D, D, D, D, FF, D, D, D, D)


def bucket_value(distance, bucket_count):
    exact_count = bucket_count // 2
    if distance < exact_count:
        return distance
    return min(
        bucket_count - 1,
        exact_count
        + int(
            math.log(distance / exact_count)
            / math.log(128 / exact_count)
            * (bucket_count - exact_count)
        ),
    )


def bucket_table(length, bucket_count):
    positions = jnp.arange(length, dtype=jnp.int32)
    distance = positions[:, None] - positions[None, :]
    bucket = jnp.zeros((length, length), jnp.int32)
    for target in range(1, bucket_count):
        distance_at = 1
        while bucket_value(distance_at, bucket_count) < target:
            distance_at += 1
        bucket = bucket + (distance >= distance_at).astype(jnp.int32)
    return (bucket[:, :, None] == jnp.arange(bucket_count, dtype=jnp.int32)).astype(F32)


def slices_of(vector, widths):
    starts = 0
    result = []
    for amount in widths:
        result.append(vector[starts : starts + amount])
        starts += amount
    return result


def dot(a, b):
    return lax.dot_general(a, b, (((1,), (0,)), ((), ())), preferred_element_type=F32)


def dot_t(a, b):
    return lax.dot_general(a, b, (((1,), (1,)), ((), ())), preferred_element_type=F32)


def dot_g(a, b):
    return lax.dot_general(a, b, (((0,), (0,)), ((), ())), preferred_element_type=F32)


def norm_stats(values):
    average = jnp.mean(values, axis=-1, keepdims=True)
    centered = values - average
    variance = jnp.mean(centered * centered, axis=-1, keepdims=True)
    inverse = lax.rsqrt(variance + EPSILON)
    return centered * inverse, inverse


def norm(values, gain, shift):
    unit, inverse = norm_stats(values)
    return unit * gain + shift


def norm_back(values, gain, grads):
    unit, inverse = norm_stats(values)
    scaled = grads * gain
    mean_one = jnp.mean(scaled, axis=-1, keepdims=True)
    mean_two = jnp.mean(scaled * unit, axis=-1, keepdims=True)
    return (
        inverse * (scaled - mean_one - unit * mean_two),
        jnp.sum(grads * unit, axis=0),
        jnp.sum(grads, axis=0),
    )


def gelu_exact(inputs):
    return jax.nn.gelu(inputs, approximate=False)


def gelu_back(inputs, gradients):
    outputs, pullback = jax.vjp(gelu_exact, inputs)
    return pullback(gradients)[0]


def col_sum(values):
    return jnp.sum(values.astype(F32), axis=0)


class Layout:
    def __init__(self, ndp, nf):
        self.ndp = ndp
        self.nf = nf
        self.nz = nf // 2
        self.chips = ndp * self.nz
        self.devices = ndp * nf
        self.r = D // self.devices
        self.f = FF // self.devices

    def place(self):
        self.dp = lax.axis_index("dp")
        fs = lax.axis_index("fsdp")
        self.z = fs // 2
        self.core = fs % 2

    def swap(self, value):
        return lax.ppermute(value, "fsdp", [(i, i ^ 1) for i in range(self.nf)])

    def shift_z(self, value, step):
        return lax.ppermute(
            value, "fsdp", [(i, (i + 2 * step) % self.nf) for i in range(self.nf)]
        )

    def flip_dp(self, value, mask):
        return lax.ppermute(value, "dp", [(i, i ^ mask) for i in range(self.ndp)])

    def shift_dp(self, value, step):
        return lax.ppermute(value, "dp", [(i, (i + step) % self.ndp) for i in range(self.ndp)])

    def pick(self, first, second):
        return jnp.where(self.core == 0, first, second)

    def pair(self, own, other, axis):
        return self.pick(
            jnp.concatenate([own, other], axis=axis), jnp.concatenate([other, own], axis=axis)
        )


def tie(value, *others):
    return lax.optimization_barrier((value,) + others)[0]


def gather_z(lay, buf):
    out = jnp.zeros((lay.nz,) + buf.shape, buf.dtype)
    out = lax.dynamic_update_slice(out, buf[None], (lay.z, 0, 0))
    for step in range(1, lay.nz):
        got = lay.shift_z(buf, step)
        out = lax.dynamic_update_slice(out, got[None], ((lay.z - step) % lay.nz, 0, 0))
    return out


def gather_dp_first(lay, buf):
    if lay.ndp == 4:
        return [lay.flip_dp(buf, 1), lay.flip_dp(buf, 2)]
    return [lay.shift_dp(buf, step) for step in range(1, lay.ndp)]


def gather_dp_rest(lay, buf, first):
    half = lay.nz // 2
    out = jnp.zeros((lay.ndp,) + buf.shape, buf.dtype)
    if lay.ndp == 4:
        low = lay.flip_dp(first[0][:half], 2)
        high = lay.flip_dp(first[1][half:], 1)
        parts = [(0, 0, buf), (1, 0, first[0]), (2, 0, first[1]), (3, 0, low), (3, half, high)]
        for flip, at, part in parts:
            out = lax.dynamic_update_slice(out, part[None], (lay.dp ^ flip, at, 0, 0))
        return out
    out = lax.dynamic_update_slice(out, buf[None], (lay.dp, 0, 0, 0))
    for step in range(1, lay.ndp):
        out = lax.dynamic_update_slice(
            out, first[step - 1][None], ((lay.dp - step) % lay.ndp, 0, 0, 0)
        )
    return out


def gather_all(lay, bufs):
    staged = []
    results = []
    firsts = []
    for i, buf in enumerate(bufs):
        if i >= 2:
            buf = tie(buf, *firsts[i - 2])
        z = gather_z(lay, buf)
        staged.append(z)
        firsts.append(gather_dp_first(lay, z))
    for z, first in zip(staged, firsts):
        results.append(gather_dp_rest(lay, z, first))
    return results


def take(buf, index, axis=0):
    return lax.dynamic_index_in_dim(buf, index, axis, keepdims=False)


def add_low(*values):
    return sum(v.astype(F32) for v in values).astype(BF)


def scatter_dp(lay, buf):
    if lay.ndp == 4:
        half = lay.nz // 2
        far = take(buf, lay.dp ^ 3)
        to_x = take(buf, lay.dp ^ 1)
        to_y = take(buf, lay.dp ^ 2)
        own = take(buf, lay.dp)
        low = lay.flip_dp(far[:half], 2)
        high = lay.flip_dp(far[half:], 1)
        to_x = jnp.concatenate([add_low(to_x[:half], low), to_x[half:]], axis=0)
        to_y = jnp.concatenate([to_y[:half], add_low(to_y[half:], high)], axis=0)
        return add_low(own, lay.flip_dp(to_x, 1), lay.flip_dp(to_y, 2))
    parts = [take(buf, lay.dp)]
    for step in range(1, lay.ndp):
        parts.append(lay.shift_dp(take(buf, (lay.dp + step) % lay.ndp), step))
    return add_low(*parts)


def scatter_z(lay, buf):
    total = take(buf, lay.z).astype(F32)
    for step in range(1, lay.nz):
        total = total + lay.shift_z(take(buf, (lay.z + step) % lay.nz), step).astype(F32)
    return total


def attention_forward(queries, keys, values, allowed):
    scores = jnp.einsum("snihe,sjhe->snhij", queries, keys, preferred_element_type=F32) * SCALE
    probs = jax.nn.softmax(jnp.where(allowed, scores, MASKED), axis=-1)
    out = jnp.einsum("snhij,sjhe->snihe", probs.astype(BF), values, preferred_element_type=F32)
    return out.astype(BF), probs


def attention_back(queries, keys, values, probs, grad_out):
    grad_probs = jnp.einsum("snihe,sjhe->snhij", grad_out, values, preferred_element_type=F32)
    grad_values = jnp.einsum(
        "snhij,snihe->sjhe", probs.astype(BF), grad_out, preferred_element_type=F32
    )
    grad_scores = (
        probs * (grad_probs - jnp.sum(probs * grad_probs, axis=-1, keepdims=True))
    ).astype(BF)
    grad_queries = (
        jnp.einsum("snhij,sjhe->snihe", grad_scores, keys, preferred_element_type=F32) * SCALE
    )
    grad_keys = (
        jnp.einsum("snhij,snihe->sjhe", grad_scores, queries, preferred_element_type=F32) * SCALE
    )
    return grad_queries.astype(BF), grad_keys.astype(BF), grad_values.astype(BF)


def ngram_forward(dqkv, rel, tgt, onehot):
    q, k, v = dqkv[:, :, :, 0], dqkv[:, :, :, 1], dqkv[:, :, :, 2]
    positions = jnp.arange(LEN, dtype=jnp.int32)
    inside = positions[None, :] < tgt[:, None]
    main_valid = (positions[None, :] <= positions[:, None])[None] & inside[:, None]
    pred_valid = (positions[None, :] < positions[:, None])[None] & inside[:, None]
    valid = jnp.stack([main_valid] + [pred_valid] * NGRAM, axis=1)[:, :, None]
    main = jnp.einsum("snihe,sjhe->snhij", q, k[:, 0], preferred_element_type=F32) * SCALE
    main = main + jnp.einsum("snihk,ijk->snhij", rel, onehot, precision=lax.Precision.HIGHEST)
    main = jnp.where(valid, main, MASKED)
    own = jnp.einsum("snihe,snihe->snhi", q, k, preferred_element_type=F32) * SCALE
    own = own + jnp.transpose(rel[..., 0], (0, 1, 3, 2))
    stream = jnp.arange(STREAMS)[None, :, None, None]
    own = jnp.where(stream == 0, -jnp.inf, own)
    top = jnp.maximum(jnp.max(main, axis=-1), own)
    main = jnp.exp(main - top[..., None])
    own = jnp.exp(own - top)
    total = jnp.sum(main, axis=-1) + own
    main = main / total[..., None]
    own = own / total
    out = jnp.einsum("snhij,sjhe->snihe", main.astype(BF), v[:, 0], preferred_element_type=F32)
    own_low = jnp.transpose(own.astype(BF), (0, 1, 3, 2)).astype(F32)[..., None]
    out = out + own_low * v.astype(F32)
    return out.astype(BF), main, own


def ngram_back(dqkv, main, own, onehot, grad_out):
    q, k, v = dqkv[:, :, :, 0], dqkv[:, :, :, 1], dqkv[:, :, :, 2]
    grad_main = jnp.einsum("snihe,sjhe->snhij", grad_out, v[:, 0], preferred_element_type=F32)
    grad_own = jnp.einsum("snihe,snihe->snhi", grad_out, v, preferred_element_type=F32)
    inner = jnp.sum(main * grad_main, axis=-1) + own * grad_own
    ds = (main * (grad_main - inner[..., None])).astype(BF)
    ds_own = (own * (grad_own - inner)).astype(BF)
    own_rows = jnp.transpose(ds_own, (0, 1, 3, 2)).astype(F32)[..., None]
    p_rows = jnp.transpose(own.astype(BF), (0, 1, 3, 2)).astype(F32)[..., None]
    gq = (
        jnp.einsum("snhij,sjhe->snihe", ds, k[:, 0], preferred_element_type=F32)
        + own_rows * k.astype(F32)
    ) * SCALE
    gk0 = jnp.einsum("snhij,snihe->sjhe", ds, q, preferred_element_type=F32) * SCALE
    gv0 = jnp.einsum("snhij,snihe->sjhe", main.astype(BF), grad_out, preferred_element_type=F32)
    gk = own_rows * q.astype(F32) * SCALE
    gv = p_rows * grad_out.astype(F32)
    gk = jnp.concatenate([gk0[:, None], gk[:, 1:]], axis=1)
    gv = jnp.concatenate([gv0[:, None], gv[:, 1:]], axis=1)
    gqkv = jnp.stack([gq, gk, gv], axis=3).astype(BF)
    grel = jnp.einsum("snhij,ijk->snihk", ds, onehot.astype(BF), preferred_element_type=F32)
    first = (jnp.arange(BUCKETS) == 0).astype(F32)
    grel = (grel + own_rows * first).astype(BF)
    return gqkv, grel


def shards(
    ndp,
    nf,
    source,
    dec_in,
    src_lengths,
    tgt_lengths,
    enc_in_proj,
    enc_out_proj,
    enc_ffn_in,
    enc_ffn_out,
    enc_gains,
    enc_biases,
    dec_in_proj,
    dec_rel_proj,
    dec_out_proj,
    cross_query,
    cross_kv,
    cross_out,
    dec_ffn_in,
    dec_ffn_out,
    dec_gains,
    dec_biases,
    enc_cot,
    dec_cot,
):
    lay = Layout(ndp, nf)
    lay.place()
    r, f, chips = lay.r, lay.f, lay.chips
    swap, pick, pair = lay.swap, lay.pick, lay.pair
    core = lay.core

    def halves(matrix, groups, width):
        parts = matrix.reshape(r, groups, 2, width)
        return (
            pick(parts[:, :, 0], parts[:, :, 1]).reshape(r, groups * width),
            pick(parts[:, :, 1], parts[:, :, 0]).reshape(r, groups * width),
        )

    split = [
        halves(enc_in_proj, 3, HALF),
        halves(enc_ffn_in, chips, f),
        halves(dec_in_proj, 3, HALF),
        halves(cross_query, 1, HALF),
        halves(cross_kv, 2, HALF),
        halves(dec_ffn_in, chips, f),
        halves(dec_rel_proj, 1, REL_HALF),
    ]
    vec = jnp.concatenate(
        [
            enc_biases,
            enc_gains,
            dec_biases,
            dec_gains,
            src_lengths.astype(BF),
            tgt_lengths.astype(BF),
        ]
    )
    nvec = vec.shape[0]
    padded = -(-nvec // WIDE) * WIDE
    vec = jnp.pad(vec, (0, padded - nvec))
    mine = jnp.concatenate([own for own, other in split], axis=1)
    theirs = jnp.concatenate([other for own, other in split], axis=1)
    theirs_got = swap(theirs)
    vec_got = swap(vec)
    source_got = swap(source)
    dec_in_got = swap(dec_in.reshape(LEN * STREAMS, D))

    def owner_rows(start, width):
        return pair(mine[:, start : start + width], theirs_got[:, start : start + width], 0)

    def column_blocks(start, count):
        return [owner_rows(start + WIDE * i, WIDE) for i in range(count)]

    def row_blocks(matrix):
        return [matrix[:, :WIDE], matrix[:, WIDE:]]

    rel_start = mine.shape[1] - REL_HALF
    rel_own = mine[:, rel_start:]
    rel_other = theirs_got[:, rel_start:]
    vec_pair = pair(vec[None], vec_got[None], 0).reshape(-1, WIDE)
    vec_rows = -(-vec_pair.shape[0] // 16) * 16
    vec_used = vec_pair.shape[0]
    vec_pair = jnp.pad(vec_pair, ((0, vec_rows - vec_used), (0, 0)))
    wide_at = [0, 3 * WIDE, 7 * WIDE, 10 * WIDE, 11 * WIDE, 13 * WIDE]
    chunk_parts = [
        column_blocks(wide_at[0], 3) + row_blocks(enc_out_proj) + [vec_pair],
        column_blocks(wide_at[1], 4) + row_blocks(enc_ffn_out),
        column_blocks(wide_at[2], 3) + [pair(rel_own, rel_other, 1)] + row_blocks(dec_out_proj),
        column_blocks(wide_at[3], 1) + column_blocks(wide_at[4], 2) + row_blocks(cross_out),
        column_blocks(wide_at[5], 4) + row_blocks(dec_ffn_out),
    ]
    bufs = [jnp.concatenate(parts, axis=0) for parts in chunk_parts]
    full = gather_all(lay, bufs)

    def cut(index, block):
        parts = chunk_parts[index]
        at = sum(p.shape[0] for p in parts[:block])
        rows = parts[block].shape[0]
        return full[index][:, :, at : at + rows].reshape(chips * rows, WIDE)

    def columns(index, first, count):
        return jnp.concatenate([cut(index, first + i) for i in range(count)], axis=1)

    def head_rows(index, first):
        rows = columns(index, first, 2)
        low, high = rows[:HALF // 2], rows[HALF // 2 :]
        keep = pick(low, high).reshape(chips // 2, 1, r, D)
        got = swap(pick(high, low)).reshape(chips // 2, 1, r, D)
        return pair(keep, got, 1).reshape(HALF, D)

    w_enc_in = columns(0, 0, 3)
    w_enc_out = head_rows(0, 3)
    w_enc_up = columns(1, 0, 4)
    w_enc_down = columns(1, 4, 2)
    w_dec_in = columns(2, 0, 3)
    w_rel = (
        cut(2, 3)
        .reshape(chips, r, 2, REL_HALF)
        .transpose(0, 2, 1, 3)
        .reshape(D, REL_HALF)
    )
    w_dec_out = head_rows(2, 4)
    w_cross_q = columns(3, 0, 1)
    w_cross_kv = columns(3, 1, 2)
    w_cross_out = head_rows(3, 3)
    w_dec_up = columns(4, 0, 4)
    w_dec_down = columns(4, 4, 2)

    vec_all = (
        cut(0, 5).reshape(chips, vec_rows, WIDE)[:, :vec_used].reshape(lay.devices, padded).astype(F32)
    )
    widths = [enc_biases.shape[0], enc_gains.shape[0], dec_biases.shape[0], dec_gains.shape[0]]
    starts = [0]
    for width in widths:
        starts.append(starts[-1] + width)
    v_enc_b, v_enc_g, v_dec_b, v_dec_g = [
        vec_all[:, starts[i] : starts[i + 1]].reshape(-1) for i in range(4)
    ]
    ebias = slices_of(v_enc_b, ENC_WIDTHS)
    egain = slices_of(v_enc_g, (D, D))
    dbias = slices_of(v_dec_b, DEC_WIDTHS)
    dgain = slices_of(v_dec_g, (D, D, D))

    def half_of(vector):
        parts = vector.reshape(2, -1)
        return pick(parts[0], parts[1])

    def hidden_of(vector):
        parts = vector.reshape(chips, 2, f)
        return pick(parts[:, 0], parts[:, 1]).reshape(-1)

    zero_half = jnp.zeros((HALF,), F32)
    lens = jnp.stack([pair(vec[None], vec_got[None], 0)[:, nvec - 2 + i] for i in range(2)])
    lens = lens.astype(F32).astype(jnp.int32)
    src_len, tgt_len = lens[0], lens[1]
    positions = jnp.arange(LEN, dtype=jnp.int32)
    src_valid = (positions[None, :] < src_len[:, None])[:, None, None, None, :]
    onehot = bucket_table(LEN, BUCKETS)

    def both(partial):
        low = partial.astype(BF)
        return low.astype(F32) + swap(low).astype(F32)

    x = pair(source[None], source_got[None], 0).reshape(2 * LEN, D)
    qkv_bias = jnp.concatenate([half_of(ebias[0]), zero_half, half_of(ebias[1])])
    eqkv = (dot(x, w_enc_in) + qkv_bias).astype(BF).reshape(2, LEN, 3, OWN_HEADS, HEAD)
    eq, ek, ev = eqkv[:, None, :, 0], eqkv[:, :, 1], eqkv[:, :, 2]
    ea, eprobs = attention_forward(eq, ek, ev, src_valid)
    ea = ea.reshape(2 * LEN, HALF)
    ez1 = x.astype(F32) + both(dot(ea, w_enc_out)) + ebias[2]
    eh1 = norm(ez1, egain[0], ebias[5])
    eh1_low = eh1.astype(BF)
    eu = dot(eh1_low, w_enc_up) + hidden_of(ebias[3])
    eg = gelu_exact(eu).astype(BF)
    ez2 = eh1 + both(dot(eg, w_enc_down)) + ebias[4]
    enc = norm(ez2, egain[1], ebias[6])
    enc_low = enc.astype(BF)

    rows = 2 * STREAMS * LEN
    y = pair(
        dec_in.transpose(1, 0, 2)[None], dec_in_got.reshape(LEN, STREAMS, D).transpose(1, 0, 2)[None], 0
    ).reshape(rows, D)
    dqkv_bias = jnp.concatenate([half_of(dbias[0]), zero_half, half_of(dbias[1])])
    dqkv = (dot(y, w_dec_in) + dqkv_bias).astype(BF)
    dqkv = dqkv.reshape(2, STREAMS, LEN, 3, OWN_HEADS, HEAD)
    rel = (dot(y, w_rel) + half_of(dbias[2])).reshape(2, STREAMS, LEN, OWN_HEADS, BUCKETS)
    da, dmain, down = ngram_forward(dqkv, rel, tgt_len, onehot)
    da = da.reshape(rows, HALF)
    dz1 = y.astype(F32) + both(dot(da, w_dec_out)) + dbias[3]
    dh1 = norm(dz1, dgain[0], dbias[9])
    dh1_low = dh1.astype(BF)
    cq = (dot(dh1_low, w_cross_q) + half_of(dbias[4])).astype(BF)
    cq = cq.reshape(2, STREAMS, LEN, OWN_HEADS, HEAD)
    ckv = dot(enc_low, w_cross_kv) + jnp.concatenate([zero_half, half_of(dbias[5])])
    ckv = ckv.astype(BF).reshape(2, LEN, 2, OWN_HEADS, HEAD)
    ck, cv = ckv[:, :, 0], ckv[:, :, 1]
    ca, cprobs = attention_forward(cq, ck, cv, src_valid)
    ca = ca.reshape(rows, HALF)
    dz2 = dh1 + both(dot(ca, w_cross_out)) + dbias[6]
    dh2 = norm(dz2, dgain[1], dbias[10])
    dh2_low = dh2.astype(BF)
    du = dot(dh2_low, w_dec_up) + hidden_of(dbias[7])
    dg = gelu_exact(du).astype(BF)
    dz3 = dh2 + both(dot(dg, w_dec_down)) + dbias[8]
    dec = norm(dz3, dgain[2], dbias[11])

    def own_rows_of(total, count):
        blocks = total[: count * 2 * r].reshape(count, 2, r, WIDE)
        keep = pick(blocks[:, 0], blocks[:, 1])
        got = swap(pick(blocks[:, 1], blocks[:, 0]))
        return pair(keep[:, None], got[:, None], 1)

    def chip_blocks(grad):
        n = grad.shape[1] // WIDE
        shape = (lay.ndp, lay.nz, grad.shape[0] // chips, WIDE)
        low = grad.astype(BF)
        return [low[:, WIDE * i : WIDE * i + WIDE].reshape(shape) for i in range(n)]

    def head_blocks(grad):
        parts = grad.astype(BF).reshape(chips // 2, 2, r, D)
        keep = pick(parts[:, 0], parts[:, 1])
        got = swap(pick(parts[:, 1], parts[:, 0]))
        return chip_blocks(pair(keep, got, 0).reshape(chips * r, D))

    def scatter(parts, previous):
        buf = jnp.concatenate(parts, axis=2)
        if previous is not None:
            buf = tie(buf, previous)
        first = scatter_dp(lay, buf)
        return scatter_z(lay, first), first

    def split_rows(total, sizes):
        at = 0
        result = []
        for size in sizes:
            result.append(total[at : at + size])
            at += size
        return result

    dcot_got = swap(dec_cot.reshape(LEN * STREAMS, D)).reshape(LEN, STREAMS, D)
    dcot = pair(dec_cot.transpose(1, 0, 2)[None], dcot_got.transpose(1, 0, 2)[None], 0)
    dcot = dcot.reshape(rows, D).astype(F32)
    gz3, ggain3, gnorm3 = norm_back(dz3, dgain[2], dcot)
    gf = gz3.astype(BF)
    g_down = dot_g(dg, gf)
    gu = gelu_back(du, dot_t(gf, w_dec_down)).astype(BF)
    g_up = dot_g(dh2_low, gu)
    total4, first4 = scatter(chip_blocks(g_up) + chip_blocks(g_down), None)
    gz2, ggain2, gnorm2 = norm_back(dz2, dgain[1], gz3 + both(dot_t(gu, w_dec_up)))
    gx = gz2.astype(BF)
    g_cross_out = dot_g(ca, gx)
    gca = dot_t(gx, w_cross_out).astype(BF).reshape(2, STREAMS, LEN, OWN_HEADS, HEAD)
    gcq, gck, gcv = attention_back(cq, ck, cv, cprobs, gca)
    gcq = gcq.reshape(rows, HALF)
    gckv = jnp.stack([gck, gcv], axis=2).reshape(2 * LEN, D)
    g_cross_q = dot_g(dh1_low, gcq)
    g_cross_kv = dot_g(enc_low, gckv)
    total3, first3 = scatter(
        chip_blocks(g_cross_q) + chip_blocks(g_cross_kv) + head_blocks(g_cross_out), first4
    )
    ecot_got = swap(enc_cot)
    ecot = pair(enc_cot[None], ecot_got[None], 0).reshape(2 * LEN, D).astype(F32)
    genc = ecot + both(dot_t(gckv, w_cross_kv))
    gz1, ggain1, gnorm1 = norm_back(dz1, dgain[0], gz2 + both(dot_t(gcq, w_cross_q)))
    go = gz1.astype(BF)
    g_dec_out = dot_g(da, go)
    gda = dot_t(go, w_dec_out).astype(BF).reshape(2, STREAMS, LEN, OWN_HEADS, HEAD)
    gqkv, grel = ngram_back(dqkv, dmain, down, onehot, gda)
    gqkv = gqkv.reshape(rows, 3 * HALF)
    grel = grel.reshape(rows, REL_HALF)
    g_dec_in = dot_g(y, gqkv)
    g_rel = dot_g(y, grel)
    rel_block = (
        g_rel.astype(BF)
        .reshape(chips, 2, r, REL_HALF)
        .transpose(0, 2, 1, 3)
        .reshape(lay.ndp, lay.nz, r, WIDE)
    )
    total2, first2 = scatter(chip_blocks(g_dec_in) + [rel_block] + head_blocks(g_dec_out), first3)

    def own_sequence(partial, count):
        parts = partial.reshape(2, count, D)
        keep = pick(parts[0], parts[1])
        return keep + swap(pick(parts[1], parts[0]).astype(BF)).astype(F32)

    def own_part(values, count):
        parts = values.reshape(2, count, D)
        return pick(parts[0], parts[1])

    dec_rows = STREAMS * LEN
    g_dec_input = own_part(gz1, dec_rows) + own_sequence(
        dot_t(gqkv, w_dec_in) + dot_t(grel, w_rel), dec_rows
    )

    def widen(vector):
        zeros = jnp.zeros_like(vector)
        return pick(jnp.concatenate([vector, zeros]), jnp.concatenate([zeros, vector]))

    def widen_hidden(vector):
        parts = vector.reshape(chips, 1, f)
        zeros = jnp.zeros_like(parts)
        return pick(
            jnp.concatenate([parts, zeros], axis=1), jnp.concatenate([zeros, parts], axis=1)
        ).reshape(-1)

    column_sums = col_sum(gqkv)
    dec_vec = jnp.concatenate(
        [
            widen(column_sums[:HALF]),
            widen(column_sums[2 * HALF :]),
            widen(col_sum(grel)),
            0.5 * col_sum(go),
            widen(col_sum(gcq)),
            widen(col_sum(gckv)[HALF:]),
            0.5 * col_sum(gx),
            widen_hidden(col_sum(gu)),
            0.5 * col_sum(gf),
            0.5 * gnorm1,
            0.5 * gnorm2,
            0.5 * gnorm3,
            0.5 * ggain1,
            0.5 * ggain2,
            0.5 * ggain3,
        ]
    )

    gz2e, eggain2, egnorm2 = norm_back(ez2, egain[1], genc)
    gfe = gz2e.astype(BF)
    ge_down = dot_g(eg, gfe)
    gue = gelu_back(eu, dot_t(gfe, w_enc_down)).astype(BF)
    ge_up = dot_g(eh1_low, gue)
    total1, first1 = scatter(chip_blocks(ge_up) + chip_blocks(ge_down), first2)
    gz1e, eggain1, egnorm1 = norm_back(ez1, egain[0], gz2e + both(dot_t(gue, w_enc_up)))
    goe = gz1e.astype(BF)
    ge_out = dot_g(ea, goe)
    gae = dot_t(goe, w_enc_out).astype(BF).reshape(2, 1, LEN, OWN_HEADS, HEAD)
    geq, gek, gev = attention_back(eq, ek, ev, eprobs, gae)
    geqkv = jnp.stack([geq[:, 0], gek, gev], axis=2).reshape(2 * LEN, 3 * HALF)
    ge_in = dot_g(x, geqkv)
    total0, first0 = scatter(chip_blocks(ge_in) + head_blocks(ge_out), first1)
    g_source = own_part(gz1e, LEN) + own_sequence(dot_t(geqkv, w_enc_in), LEN)
    ecolumn_sums = col_sum(geqkv)
    enc_vec = jnp.concatenate(
        [
            widen(ecolumn_sums[:HALF]),
            widen(ecolumn_sums[2 * HALF :]),
            0.5 * col_sum(goe),
            widen_hidden(col_sum(gue)),
            0.5 * col_sum(gfe),
            0.5 * egnorm1,
            0.5 * egnorm2,
            0.5 * eggain1,
            0.5 * eggain2,
        ]
    )
    me = lay.dp * lay.nf + lax.axis_index("fsdp")

    def own_slice(vector):
        return take(vector.reshape(lay.devices, -1), me)

    dec_vec = lax.psum(dec_vec, ("dp", "fsdp"))
    enc_vec = lax.psum(enc_vec, ("dp", "fsdp"))
    nb = sum(ENC_WIDTHS)
    g_enc_biases, g_enc_gains = own_slice(enc_vec[:nb]), own_slice(enc_vec[nb:])
    nb = sum(DEC_WIDTHS)
    g_dec_biases, g_dec_gains = own_slice(dec_vec[:nb]), own_slice(dec_vec[nb:])

    def in_rows(blocks):
        return blocks.transpose(2, 0, 1, 3).reshape(r, -1)

    def up_rows(blocks):
        per = WIDE // f
        return blocks.reshape(4, 2, r, per, f).transpose(2, 0, 3, 1, 4).reshape(r, FF)

    def side(low, high):
        return jnp.concatenate([low, high], axis=1)

    t0 = split_rows(total0, [6 * r, r, r])
    o_enc_in, o_enc_out = in_rows(own_rows_of(t0[0], 3)), side(t0[1], t0[2])
    t1 = split_rows(total1, [8 * r, f, f])
    o_enc_up, o_enc_down = up_rows(own_rows_of(t1[0], 4)), side(t1[1], t1[2])
    t2 = split_rows(total2, [6 * r, r, r, r])
    o_dec_in, o_dec_out = in_rows(own_rows_of(t2[0], 3)), side(t2[2], t2[3])
    relp = t2[1].reshape(r, 2, REL_HALF)
    rel_keep = pick(relp[:, 0], relp[:, 1])
    o_rel = pair(rel_keep, swap(pick(relp[:, 1], relp[:, 0])), 1)
    t3 = split_rows(total3, [2 * r, 4 * r, r, r])
    o_cross_q = in_rows(own_rows_of(t3[0], 1))
    o_cross_kv = in_rows(own_rows_of(t3[1], 2))
    o_cross_out = side(t3[2], t3[3])
    t4 = split_rows(total4, [8 * r, f, f])
    o_dec_up, o_dec_down = up_rows(own_rows_of(t4[0], 4)), side(t4[1], t4[2])

    return (
        own_part(enc_low, LEN),
        own_part(dec.astype(BF), dec_rows).reshape(STREAMS, LEN, D).transpose(1, 0, 2),
        g_source,
        g_dec_input.reshape(STREAMS, LEN, D).transpose(1, 0, 2),
        o_enc_in,
        o_enc_out,
        o_enc_up,
        o_enc_down,
        g_enc_gains,
        g_enc_biases,
        o_dec_in,
        o_rel,
        o_dec_out,
        o_cross_q,
        o_cross_kv,
        o_cross_out,
        o_dec_up,
        o_dec_down,
        g_dec_gains,
        g_dec_biases,
    )


BUDGET = 26 * 1024 * 1024
PIECES = 4
HBM_RATE = 1.0e6
FLOP_RATE = 1.0e9


def run(body, grid, ins, outs, scratch=(), us=5):
    arrays = [a for a, s in ins]
    return pl.pallas_call(
        body,
        grid=(grid,),
        in_specs=[s for a, s in ins],
        out_specs=[s for a, s in outs],
        out_shape=[a for a, s in outs],
        scratch_shapes=list(scratch),
        compiler_params=pltpu.CompilerParams(vmem_limit_bytes=BUDGET),
        cost_estimate=pl.CostEstimate(
            flops=int(us * FLOP_RATE), bytes_accessed=int(us * HBM_RATE), transcendentals=0
        ),
    )(*arrays)


def full(array):
    zeros = (0,) * array.ndim
    return array, pl.BlockSpec(array.shape, lambda t: zeros, pipeline_mode=pl.Buffered(1))


def small(array):
    return array, pl.BlockSpec(memory_space=pltpu.SMEM)


def out_full(shape, dtype):
    zeros = (0,) * len(shape)
    return jax.ShapeDtypeStruct(shape, dtype), pl.BlockSpec(shape, lambda t: zeros)


def out_cols(rows, cols, dtype, index):
    return (
        jax.ShapeDtypeStruct((rows, cols), dtype),
        pl.BlockSpec((rows, WIDE), lambda t: (0, index(t))),
    )


def in_cols(array, index, width=WIDE):
    return array, pl.BlockSpec((array.shape[0], width), lambda t: (0, index(t)))


def blocks(pieces, rows, index):
    return [
        (p, pl.BlockSpec((4, rows, WIDE), lambda t: (0, index(t), 0))) for p in pieces
    ]


def wide_blocks(pieces, index):
    return [(p, pl.BlockSpec((4,) + p.shape[1:2] + (WIDE,), lambda t: (0, 0, index(t)))) for p in pieces]


def assemble(refs, scr, place):
    for i in range(4):
        scr[jnp.bitwise_xor(place[0], i)] = refs[i][...]


def weight_scratch(rows, width=WIDE):
    return pltpu.VMEM((4, 4, rows, width), BF)


def matrix_of(scr):
    a, b, c, d = scr.shape
    return scr[...].reshape(a * b * c, d)


def pick_matrix(parity):
    i = lax.broadcasted_iota(jnp.int32, (HALF, HALF // 2), 0)
    j = lax.broadcasted_iota(jnp.int32, (HALF, HALF // 2), 1)
    from_row = ((j >> 5) << 6) + (parity << 5) + (j & 31)
    return jnp.where(i == from_row, 1.0, 0.0).astype(BF)


def head_masks():
    lane = lax.broadcasted_iota(jnp.int32, (1, 128), 1)
    first = jnp.where(lane < HEAD, 1.0, 0.0)
    return first.astype(BF), (1.0 - first).astype(BF)


def first_lanes(rows):
    return lax.broadcasted_iota(jnp.int32, (rows, 128), 1) < HEAD


def soft_rows(scores):
    top = jnp.max(scores, axis=-1, keepdims=True)
    raised = jnp.exp(scores - top)
    return raised * (1.0 / jnp.sum(raised, axis=-1, keepdims=True))


def masked_probs(queries, keys, count):
    scores = dot_t(queries, keys) * SCALE
    column = lax.broadcasted_iota(jnp.int32, scores.shape, 1)
    return soft_rows(jnp.where(column < count, scores, MASKED))


def attend(q, k, v, count):
    rows = q.shape[0]
    out = []
    for mask in head_masks():
        probs = masked_probs(q * mask, k, count).astype(BF)
        out.append(dot(probs, v))
    return jnp.where(first_lanes(rows), out[0], out[1]).astype(BF)


def attend_back(q, k, v, g, count):
    gq, gk, gv = [], 0.0, 0.0
    for mask in head_masks():
        qm, gm = q * mask, g * mask
        probs = masked_probs(qm, k, count)
        gp = dot_t(gm, v)
        ds = (probs * (gp - jnp.sum(probs * gp, axis=-1, keepdims=True))).astype(BF)
        gq.append(dot(ds, k))
        gk = gk + dot_g(ds, qm)
        gv = gv + dot_g(probs.astype(BF), gm)
    gq = jnp.where(first_lanes(q.shape[0]), gq[0], gq[1]) * SCALE
    return gq.astype(BF), (gk * SCALE).astype(BF), gv.astype(BF)


def split_parity(heads, place, keep, send):
    core = place[2]
    keep[...] = dot(heads[...], pick_matrix(core)).astype(BF)
    send[...] = dot(heads[...], pick_matrix(1 - core)).astype(BF)


def join_parity(keep, got, place, heads):
    core = place[2]
    heads[...] = (
        dot_t(keep[...], pick_matrix(core)) + dot_t(got[...], pick_matrix(1 - core))
    ).astype(BF)


def enc_attention(place, x, bias, pieces):
    rows = x.shape[0]

    def body(place, x, bias, *refs):
        w, (qkv, keep, send, scr, heads) = refs[:PIECES], refs[PIECES:]
        t = pl.program_id(0)
        assemble(w, scr, place)
        qkv[:, pl.ds(t * WIDE, WIDE)] = (dot(x[...], matrix_of(scr)) + bias[...]).astype(BF)

        @pl.when(t == 2)
        def _():
            for s in range(2):
                r = slice(s * LEN, s * LEN + LEN)
                for j in range(4):
                    c = [slice(HALF * i + 128 * j, HALF * i + 128 * j + 128) for i in range(3)]
                    heads[r, c[0]] = attend(qkv[r, c[0]], qkv[r, c[1]], qkv[r, c[2]], place[3 + s])
            split_parity(heads, place, keep, send)

    return run(
        body,
        3,
        [small(place), full(x), in_cols(bias, lambda t: t)] + blocks(pieces, 64, lambda t: t),
        [
            out_full((rows, 3 * HALF), BF),
            out_full((rows, HALF // 2), BF),
            out_full((rows, HALF // 2), BF),
        ],
        [weight_scratch(64), pltpu.VMEM((rows, HALF), BF)],
        us=10,
    )


def out_projection(place, keep, got, pieces):
    rows = keep.shape[0]

    def body(place, keep, got, *refs):
        w, (out, scr) = refs[:PIECES], refs[PIECES:]
        assemble(w, scr, place)
        core = place[2]
        mine = scr[pl.ds(2 * core, 2)].reshape(HALF // 2, WIDE)
        theirs = scr[pl.ds(2 - 2 * core, 2)].reshape(HALF // 2, WIDE)
        out[...] = (dot(keep[...], mine) + dot(got[...], theirs)).astype(BF)

    return run(
        body,
        2,
        [small(place), full(keep), full(got)] + blocks(pieces, 32, lambda t: 6 + t),
        [out_cols(rows, D, BF, lambda t: t)],
        [weight_scratch(32)],
        us=3,
    )[0]


def stats(v):
    centered = v - jnp.mean(v, axis=-1, keepdims=True)
    inverse = lax.rsqrt(jnp.mean(centered * centered, axis=-1, keepdims=True) + EPSILON)
    return centered * inverse, inverse


def each_tile(rows, tile, step):
    def loop(m, carry):
        step(pl.multiple_of(m * tile, tile))
        return carry

    lax.fori_loop(0, rows // tile, loop, 0)


def norm_tiles(rows, base, affine, own, other, bias, gain, shift, unit_out, inv_out, low_out, at=0):
    def step(r):
        here = pl.ds(r, LEN)
        v = base[here].astype(F32)
        if affine is not None:
            v = v * affine[0] + affine[1]
        there = pl.ds(r + at, LEN)
        v = v + (own[there].astype(F32) + other[there].astype(F32)) + bias
        unit, inverse = stats(v)
        unit_out[here] = unit
        inv_out[here] = jnp.broadcast_to(inverse, (LEN, 128))
        low_out[here] = (unit * gain + shift).astype(BF)

    each_tile(rows, LEN, step)


def norm_forward(place, base, affine, own, other, vecs):
    rows = base.shape[0]

    def body(place, base, own, other, vecs, unit, inv, low):
        aff = (vecs[0:1], vecs[1:2]) if affine else None
        norm_tiles(LEN, base, aff, own, other, vecs[2:3], vecs[3:4], vecs[4:5], unit, inv, low)

    def tiles(array):
        return array, pl.BlockSpec((LEN, array.shape[1]), lambda t: (t, 0))

    def out(width, dtype):
        return jax.ShapeDtypeStruct((rows, width), dtype), pl.BlockSpec((LEN, width), lambda t: (t, 0))

    return run(
        body,
        rows // LEN,
        [small(place), tiles(base), tiles(own), tiles(other), full(vecs)],
        [out(D, F32), out(128, F32), out(D, BF)],
        us=4,
    )


ROOT_HALF = math.sqrt(0.5)
ROOT_TWO_PI = math.sqrt(0.5 / math.pi)
TAIL = (0.254829592, -0.284496736, 1.421413741, -1.453152027, 1.061405429)


def gelu_pair(u):
    depth = 1.0 + (0.3275911 * ROOT_HALF) * jnp.abs(u)
    t = pl.reciprocal(depth, approx=True)
    t = t * (2.0 - depth * t)
    bell = jnp.exp(-0.5 * u * u)
    poly = TAIL[4]
    for c in TAIL[3::-1]:
        poly = poly * t + c
    tail = (0.5 * t) * poly * bell
    phi = jnp.where(u < 0.0, tail, 1.0 - tail)
    return u * phi, phi + u * (bell * ROOT_TWO_PI)


def ffn_forward(place, low, hidden_bias, up_pieces, down_pieces):
    rows = low.shape[0]
    hidden = hidden_bias.shape[1]
    ups = hidden // WIDE
    tile = 128

    def body(place, low, hb, *refs):
        wu, wd = refs[:PIECES], refs[PIECES : 2 * PIECES]
        g, gp, part, scr_u, scr_d, acts = refs[2 * PIECES :]
        t = pl.program_id(0)

        @pl.when(t < ups)
        def _():
            assemble(wu, scr_u, place)
            w = matrix_of(scr_u)

            for r in range(0, rows, tile):
                here = slice(r, r + tile)
                a, b = gelu_pair(dot(low[here], w) + hb[...])
                a = a.astype(BF)
                g[here] = a
                acts[here, pl.ds(t * WIDE, WIDE)] = a
                gp[here] = b.astype(BF)

        @pl.when(t >= ups)
        def _():
            assemble(wd, scr_d, place)
            part[...] = dot(acts[...], matrix_of(scr_d)).astype(BF)

    up = lambda t: jnp.minimum(t, ups - 1)
    down = lambda t: jnp.maximum(t - ups, 0)
    return run(
        body,
        ups + 2,
        [small(place), full(low), in_cols(hidden_bias, up)]
        + blocks(up_pieces, 64, up)
        + wide_blocks(down_pieces, down),
        [
            out_cols(rows, hidden, BF, up),
            out_cols(rows, hidden, BF, up),
            out_cols(rows, D, BF, down),
        ],
        [weight_scratch(64), weight_scratch(128), pltpu.VMEM((rows, hidden), BF)],
        us=14 if rows > 256 else 8,
    )


def distance_buckets(reverse):
    row = lax.broadcasted_iota(jnp.int32, (128, 128), 0) & (BUCKETS - 1)
    lane = lax.broadcasted_iota(jnp.int32, (128, 128), 1)
    distance = ((lane + 1) if reverse else (128 - lane)) & 127
    bucket = jnp.zeros((128, 128), jnp.int32)
    for target in range(1, BUCKETS):
        at = 1
        while bucket_value(at, BUCKETS) < target:
            at += 1
        bucket = bucket + jnp.where(distance >= at, 1, 0)
    return jnp.where(bucket == row, 1.0, 0.0).astype(BF)


def skew(values):
    parts = [values[128 * n : 128 * n + 128] for n in range(values.shape[0] // 128)]
    return jnp.concatenate(
        [pltpu.roll(part, 0, 1, stride=1, stride_axis=0) for part in parts], axis=0
    )


def mirror():
    row = lax.broadcasted_iota(jnp.int32, (128, 128), 0)
    lane = lax.broadcasted_iota(jnp.int32, (128, 128), 1)
    return jnp.where(row + lane == 127, 1.0, 0.0).astype(BF)


def quarter_mask(h):
    lane = lax.broadcasted_iota(jnp.int32, (1, 128), 1)
    return jnp.where((lane >> 5) == h, 1.0, 0.0).astype(BF)


def ngram_probs(qm, prod, k0, rel_high, rel_low, table, count, h, first):
    mask = quarter_mask(h % 4)
    turned = dot(rel_high * mask, table) + dot(rel_low * mask, table)
    scores = dot_t(qm, k0) * SCALE + skew(turned)
    row = lax.broadcasted_iota(jnp.int32, scores.shape, 0)
    column = lax.broadcasted_iota(jnp.int32, scores.shape, 1)
    token = row & (LEN - 1)
    reach = jnp.where(row < LEN, token, token - 1)
    scores = jnp.where((column <= reach) & (column < count), scores, MASKED)
    own = jnp.sum(prod * first, axis=-1, keepdims=True) * SCALE + turned[:, 0:1]
    main = lax.broadcasted_iota(jnp.int32, own.shape, 0) < LEN
    own = jnp.where(main, 2.0 * MASKED, own)
    top = jnp.maximum(jnp.max(scores, axis=-1, keepdims=True), own)
    raised = jnp.exp(scores - top)
    own = jnp.exp(own - top)
    scale = 1.0 / (jnp.sum(raised, axis=-1, keepdims=True) + own)
    return raised * scale, own * scale


def split_high(values):
    high = values.astype(BF)
    return high, (values - high.astype(F32)).astype(BF)


def half_rows(rows):
    first = jnp.where(lax.broadcasted_iota(jnp.int32, (rows, 128), 1) < HEAD, 1.0, 0.0)
    return first, 1.0 - first


def ngram_attention(place, y, bias, rel_bias, pieces):
    rows = y.shape[0]
    span = STREAMS * LEN

    def body(place, y, bias, rbias, *refs):
        w, wr = refs[:PIECES], refs[PIECES : 2 * PIECES]
        qkv, rel, keep, send, scr, scr_r, heads, table = refs[2 * PIECES :]
        t = pl.program_id(0)

        @pl.when(t < 3)
        def _():
            assemble(w, scr, place)
            qkv[:, pl.ds(pl.multiple_of(t * WIDE, WIDE), WIDE)] = (
                dot(y[...], matrix_of(scr)) + bias[...]
            ).astype(BF)

        @pl.when(t == 3)
        def _():
            assemble_rel(wr, scr_r, place)
            rel[...] = dot(y[...], scr_r[...].reshape(D, REL_HALF)) + rbias[...]
            table[...] = distance_buckets(False)
            lanes = half_rows(span)

            def step(s, carry):
                r = pl.ds(pl.multiple_of(s * span, span), span)
                r0 = pl.ds(pl.multiple_of(s * span, span), LEN)
                count = place[5 + s]
                for j in range(4):
                    c = [slice(HALF * i + 128 * j, HALF * i + 128 * j + 128) for i in range(3)]
                    q, k, v = qkv[r, c[0]], qkv[r, c[1]], qkv[r, c[2]]
                    k0, v0 = qkv[r0, c[1]], qkv[r0, c[2]]
                    high, low = split_high(rel[r, 128 * (j // 2) : 128 * (j // 2) + 128])
                    prod = q.astype(F32) * k.astype(F32)
                    out = []
                    for i, mask in enumerate(head_masks()):
                        probs, own = ngram_probs(
                            q * mask, prod, k0, high, low, table[...], count, 2 * j + i, lanes[i]
                        )
                        own = own.astype(BF).astype(F32)
                        out.append(dot(probs.astype(BF), v0) + own * v.astype(F32))
                    heads[r, c[0]] = jnp.where(first_lanes(span), out[0], out[1]).astype(BF)
                return carry

            lax.fori_loop(0, 2, step, 0)
            split_parity(heads, place, keep, send)

    third = lambda t: jnp.minimum(t, 2)
    return run(
        body,
        4,
        [small(place), full(y), in_cols(bias, third), full(rel_bias)]
        + blocks(pieces, 64, third)
        + blocks(pieces, 32, lambda t: 8),
        [
            out_full((rows, 3 * HALF), BF),
            out_full((rows, REL_HALF), F32),
            out_full((rows, HALF // 2), BF),
            out_full((rows, HALF // 2), BF),
        ],
        [
            weight_scratch(64),
            pltpu.VMEM((4, 4, 2, 32, REL_HALF), BF),
            pltpu.VMEM((rows, HALF), BF),
            pltpu.VMEM((128, 128), BF),
        ],
        us=19,
    )


def assemble_rel(refs, scr, place):
    for i in range(4):
        block = refs[i][...]
        at = jnp.bitwise_xor(place[0], i)
        scr[at, :, 0] = block[:, :, :REL_HALF]
        scr[at, :, 1] = block[:, :, REL_HALF:]


def cross_forward(place, y, own, other, vecs, eunit, evecs, eown, eother, q_bias, kv_bias, pieces):
    rows, mem = y.shape[0], eunit.shape[0]
    span = STREAMS * LEN

    def body(place, y, own, other, vecs, eunit, evecs, eown, eother, qb, kvb, *refs):
        w = refs[:PIECES]
        unit, inv, low, eunit2, einv2, elow, q, kv, keep, send, scr, heads = refs[PIECES:]
        t = pl.program_id(0)
        assemble(w, scr, place)

        @pl.when(t == 0)
        def _():
            norm_tiles(
                rows, y, None, own, other, vecs[0:1], vecs[1:2], vecs[2:3], unit, inv, low
            )
            norm_tiles(
                mem,
                eunit,
                (evecs[0:1], evecs[1:2]),
                eown,
                eother,
                evecs[2:3],
                evecs[3:4],
                evecs[4:5],
                eunit2,
                einv2,
                elow,
            )
            q[...] = (dot(low[...], matrix_of(scr)) + qb[...]).astype(BF)

        @pl.when(t > 0)
        def _():
            at = pl.multiple_of((t - 1) * WIDE, WIDE)
            kv[:, pl.ds(at, WIDE)] = (dot(elow[...], matrix_of(scr)) + kvb[...]).astype(BF)

        @pl.when(t == 2)
        def _():
            for s in range(2):
                r = slice(s * span, s * span + span)
                m = slice(s * LEN, s * LEN + LEN)
                for j in range(4):
                    c = slice(128 * j, 128 * j + 128)
                    c2 = slice(HALF + 128 * j, HALF + 128 * j + 128)
                    heads[r, c] = attend(q[r, c], kv[m, c], kv[m, c2], place[3 + s])
            split_parity(heads, place, keep, send)

    return run(
        body,
        3,
        [small(place)]
        + [full(a) for a in (y, own, other, vecs, eunit, evecs, eown, eother, q_bias)]
        + [in_cols(kv_bias, lambda t: jnp.maximum(t - 1, 0))]
        + blocks(pieces, 64, lambda t: t),
        [
            out_full((rows, D), F32),
            out_full((rows, 128), F32),
            out_full((rows, D), BF),
            out_full((mem, D), F32),
            out_full((mem, 128), F32),
            out_full((mem, D), BF),
            out_full((rows, HALF), BF),
            out_full((mem, D), BF),
            out_full((rows, HALF // 2), BF),
            out_full((rows, HALF // 2), BF),
        ],
        [weight_scratch(64), pltpu.VMEM((rows, HALF), BF)],
        us=15,
    )


def fold(values):
    return jnp.sum(values.reshape(values.shape[0] // 8, 8, values.shape[1]), axis=0)


def norm_back_tile(total, unit, inverse, gain):
    scaled = total * gain
    one = jnp.mean(scaled, axis=-1, keepdims=True)
    two = jnp.mean(scaled * unit, axis=-1, keepdims=True)
    return inverse * (scaled - one - unit * two)


def norm_backward(place, final, total_ins, unit_ins, vecs):
    rows = total_ins[0].shape[0]
    n_total, n_unit = len(total_ins), len(unit_ins)
    steps = rows // LEN
    mine = steps // 2

    def body(place, vecs, *refs):
        tot, uni = refs[:n_total], refs[n_total : n_total + n_unit]
        *outs, gz, gf, s_gain, s_shift, s_gf, acc = refs[n_total + n_unit :]
        t = pl.program_id(0)

        @pl.when(t == 0)
        def _():
            acc[...] = jnp.zeros_like(acc)

        if final:
            v = uni[0][...] * vecs[0:1] + vecs[1:2]
            v = v + (uni[1][...].astype(F32) + uni[2][...].astype(F32)) + vecs[2:3]
            unit, inverse = stats(v)

            @pl.when((t >= mine) == (place[2] == 1))
            def _():
                outs[0][...] = (unit * vecs[3:4] + vecs[4:5]).astype(BF)

        else:
            unit, inverse = uni[0][...], uni[1][:, 0:1]
        total = tot[0][...].astype(F32)
        if n_total > 1:
            total = total + (tot[1][...].astype(F32) + tot[2][...].astype(F32))
        acc[0:8] += fold(total * unit)
        acc[8:16] += fold(total)
        back = norm_back_tile(total, unit, inverse, vecs[3:4])
        gz[...] = back
        low = back.astype(BF)
        gf[...] = low
        acc[16:24] += fold(low.astype(F32))

        @pl.when(t == steps - 1)
        def _():
            s_gain[...] = jnp.sum(acc[0:8], axis=0, keepdims=True)
            s_shift[...] = jnp.sum(acc[8:16], axis=0, keepdims=True)
            s_gf[...] = jnp.sum(acc[16:24], axis=0, keepdims=True)

    def tiles(array):
        skip = (array.shape[0] - rows) // LEN
        return array, pl.BlockSpec((LEN, array.shape[1]), lambda t: (t + skip, 0))

    def out(dtype):
        return jax.ShapeDtypeStruct((rows, D), dtype), pl.BlockSpec((LEN, D), lambda t: (t, 0))

    def own_tile(t, place):
        return (jnp.clip(t - mine * place[2], 0, mine - 1), 0)

    outs = [out(F32), out(BF)] + [out_full((1, D), F32)] * 3
    specs = [s for a, s in outs]
    shapes = [a for a, s in outs]
    ins = [full(vecs)] + [tiles(a) for a in total_ins + unit_ins]

    def with_place(spec):
        index = spec.index_map
        return pl.BlockSpec(
            spec.block_shape, lambda t, place: index(t), pipeline_mode=spec.pipeline_mode
        )

    specs = [with_place(s) for s in specs]
    if final:
        shapes = [jax.ShapeDtypeStruct((rows // 2, D), BF)] + shapes
        specs = [pl.BlockSpec((LEN, D), own_tile)] + specs
    return pl.pallas_call(
        body,
        grid_spec=pltpu.PrefetchScalarGridSpec(
            num_scalar_prefetch=1,
            grid=(steps,),
            in_specs=[with_place(s) for a, s in ins],
            out_specs=specs,
            scratch_shapes=[pltpu.VMEM((24, D), F32)],
        ),
        out_shape=shapes,
        compiler_params=pltpu.CompilerParams(vmem_limit_bytes=BUDGET),
        cost_estimate=pl.CostEstimate(
            flops=int(5 * FLOP_RATE), bytes_accessed=int(5 * HBM_RATE), transcendentals=0
        ),
    )(place, *[a for a, s in ins])


def ffn_back(place, gf, gp, up_pieces, down_pieces):
    rows, hidden = gp.shape
    ups = hidden // WIDE

    def body(place, gf, gp, *refs):
        wu, wd = refs[:PIECES], refs[PIECES : 2 * PIECES]
        gu, part, s_gu, scr_u, scr_d, all_u, scr_all_u = refs[2 * PIECES :]
        t = pl.program_id(0)

        @pl.when(t < 2)
        def _():
            assemble(wd, scr_d.at[t], place)

        @pl.when(t >= 2)
        def _():
            b = t - 2
            assemble(wu, scr_u, place)
            scr_all_u[:, pl.ds(pl.multiple_of(b * WIDE, WIDE), WIDE)] = matrix_of(scr_u)
            w0 = scr_d[0, b].reshape(WIDE, WIDE)
            w1 = scr_d[1, b].reshape(WIDE, WIDE)
            back = dot_t(gf[:, :WIDE], w0) + dot_t(gf[:, WIDE:], w1)
            low = (back * gp[...].astype(F32)).astype(BF)
            gu[...] = low
            all_u[:, pl.ds(pl.multiple_of(b * WIDE, WIDE), WIDE)] = low
            s_gu[...] = jnp.sum(fold(low.astype(F32)), axis=0, keepdims=True)

        @pl.when(t == ups + 1)
        def _():
            part[...] = dot_t(all_u[...], scr_all_u[...]).astype(BF)

    up = lambda t: jnp.maximum(t - 2, 0)
    down = lambda t: jnp.minimum(t, 1)
    return run(
        body,
        ups + 2,
        [small(place), full(gf), in_cols(gp, up)]
        + blocks(up_pieces, 64, up)
        + wide_blocks(down_pieces, down),
        [
            out_cols(rows, hidden, BF, up),
            out_full((rows, D), BF),
            out_cols(1, hidden, F32, up),
        ],
        [
            weight_scratch(64),
            pltpu.VMEM((2, 4, 4, 128, WIDE), BF),
            pltpu.VMEM((rows, hidden), BF),
            pltpu.VMEM((D, hidden), BF),
        ],
        us=14 if rows > 256 else 8,
    )


def branch_back(place, resid, own, other, unit, inv, gain, pieces):
    rows = resid.shape[0]

    def body(place, resid, own, other, unit, inv, gain, *refs):
        w = refs[:PIECES]
        gz, gx, keep, send, s_gain, s_shift, s_gx, scr, total_out, acc = refs[PIECES:]
        t = pl.program_id(0)
        assemble(w, scr, place)

        @pl.when(t == 0)
        def _():
            acc[...] = jnp.zeros_like(acc)

            def step(r):
                here = pl.ds(r, LEN)
                total = resid[here] + (own[here].astype(F32) + other[here].astype(F32))
                acc[0:8] += fold(total * unit[here])
                acc[8:16] += fold(total)
                back = norm_back_tile(total, unit[here], inv[here, 0:1], gain[...])
                gz[here] = back
                low = back.astype(BF)
                gx[here] = low
                acc[16:24] += fold(low.astype(F32))

            each_tile(rows, LEN, step)
            s_gain[...] = jnp.sum(acc[0:8], axis=0, keepdims=True)
            s_shift[...] = jnp.sum(acc[8:16], axis=0, keepdims=True)
            s_gx[...] = jnp.sum(acc[16:24], axis=0, keepdims=True)
            total_out[...] = dot_t(gx[:, :WIDE], matrix_of(scr))

        @pl.when(t == 1)
        def _():
            total_out[...] += dot_t(gx[:, WIDE:], matrix_of(scr))
            core = place[2]
            quarter = HALF // 2
            keep[...] = total_out[:, pl.ds(pl.multiple_of(quarter * core, 128), quarter)].astype(BF)
            send[...] = total_out[
                :, pl.ds(pl.multiple_of(quarter * (1 - core), 128), quarter)
            ].astype(BF)

    return run(
        body,
        2,
        [small(place)]
        + [full(a) for a in (resid, own, other, unit, inv, gain)]
        + blocks(pieces, 32, lambda t: 6 + t),
        [
            out_full((rows, D), F32),
            out_full((rows, D), BF),
            out_full((rows, HALF // 2), BF),
            out_full((rows, HALF // 2), BF),
            out_full((1, D), F32),
            out_full((1, D), F32),
            out_full((1, D), F32),
        ],
        [weight_scratch(32), pltpu.VMEM((rows, HALF), F32), pltpu.VMEM((24, D), F32)],
        us=10 if rows > 256 else 5,
    )


def column_sums(out, values):
    out[...] = jnp.sum(fold(values.astype(F32)), axis=0, keepdims=True)


def cross_back(place, q, kv, keep, got, pieces):
    rows, mem = q.shape[0], kv.shape[0]
    span = STREAMS * LEN

    def body(place, q, kv, keep, got, *refs):
        w = refs[:PIECES]
        gq, gkv, part, s_gq, s_gkv, scr, g, acc = refs[PIECES:]
        t = pl.program_id(0)
        assemble(w, scr, place)

        @pl.when(t == 0)
        def _():
            join_parity(keep, got, place, g)
            for s in range(2):
                r = slice(s * span, s * span + span)
                m = slice(s * LEN, s * LEN + LEN)
                for j in range(4):
                    c = slice(128 * j, 128 * j + 128)
                    c2 = slice(HALF + 128 * j, HALF + 128 * j + 128)
                    gq[r, c], gkv[m, c], gkv[m, c2] = attend_back(
                        q[r, c], kv[m, c], kv[m, c2], g[r, c], place[3 + s]
                    )
            column_sums(s_gq, gq[...])
            column_sums(s_gkv, gkv[...])
            part[:rows] = dot_t(gq[...], matrix_of(scr)).astype(BF)

        @pl.when(t == 1)
        def _():
            acc[...] = dot_t(gkv[:, :HALF], matrix_of(scr))

        @pl.when(t == 2)
        def _():
            part[rows:] = (acc[...] + dot_t(gkv[:, HALF:], matrix_of(scr))).astype(BF)

    return run(
        body,
        3,
        [small(place), full(q), full(kv), full(keep), full(got)]
        + blocks(pieces, 64, lambda t: t),
        [
            out_full((rows, HALF), BF),
            out_full((mem, D), BF),
            out_full((rows + mem, D), BF),
            out_full((1, HALF), F32),
            out_full((1, D), F32),
        ],
        [weight_scratch(64), pltpu.VMEM((rows, HALF), BF), pltpu.VMEM((mem, D), F32)],
        us=14,
    )


def input_grads(place, gz, parts, keep, send):
    rows = gz.shape[0] // 2
    core = place[2]
    here = pl.ds(pl.multiple_of(rows * core, LEN), rows)
    there = pl.ds(pl.multiple_of(rows * (1 - core), LEN), rows)
    total = gz[here]
    for g, w in parts:
        total = total + dot_t(g[here], w)
    keep[...] = total
    total = 0.0
    for g, w in parts:
        total = total + dot_t(g[there], w)
    send[...] = total.astype(BF)


def enc_attention_back(place, qkv, keep, got, gz, pieces):
    rows = qkv.shape[0]

    def body(place, qkv, keep, got, gz, *refs):
        w = refs[:PIECES]
        gqkv, out, send, sums, scr, g, win = refs[PIECES:]
        t = pl.program_id(0)
        assemble(w, scr, place)
        win[:, pl.ds(pl.multiple_of(t * WIDE, WIDE), WIDE)] = matrix_of(scr)

        @pl.when(t == 0)
        def _():
            join_parity(keep, got, place, g)
            for s in range(2):
                r = slice(s * LEN, s * LEN + LEN)
                for j in range(4):
                    c = [slice(HALF * i + 128 * j, HALF * i + 128 * j + 128) for i in range(3)]
                    gqkv[r, c[0]], gqkv[r, c[1]], gqkv[r, c[2]] = attend_back(
                        qkv[r, c[0]], qkv[r, c[1]], qkv[r, c[2]], g[r, c[0]], place[3 + s]
                    )
            column_sums(sums, gqkv[...])

        @pl.when(t == 2)
        def _():
            input_grads(place, gz, [(gqkv, win[...])], out, send)

    return run(
        body,
        3,
        [small(place), full(qkv), full(keep), full(got), full(gz)]
        + blocks(pieces, 64, lambda t: t),
        [
            out_full((rows, 3 * HALF), BF),
            out_full((rows // 2, D), F32),
            out_full((rows // 2, D), BF),
            out_full((1, 3 * HALF), F32),
        ],
        [weight_scratch(64), pltpu.VMEM((rows, HALF), BF), pltpu.VMEM((D, 3 * HALF), BF)],
        us=13,
    )


def ngram_back_kernel(place, qkv, rel, keep, got, gz, pieces):
    rows = qkv.shape[0]
    span = STREAMS * LEN

    def body(place, qkv, rel, keep, got, gz, *refs):
        w, wr = refs[:PIECES], refs[PIECES : 2 * PIECES]
        gqkv, grel, out, send, sums, s_rel, scr, scr_r, g, win, *tables = refs[2 * PIECES :]
        table, table_back, flip = tables
        t = pl.program_id(0)

        @pl.when(t < 3)
        def _():
            assemble(w, scr, place)
            win[:, pl.ds(pl.multiple_of(t * WIDE, WIDE), WIDE)] = matrix_of(scr)

        @pl.when(t == 0)
        def _():
            join_parity(keep, got, place, g)
            table[...] = distance_buckets(False)
            table_back[...] = distance_buckets(True)
            flip[...] = mirror()
            lanes = half_rows(span)

            def step(s, carry):
                r = pl.ds(pl.multiple_of(s * span, span), span)
                r0 = pl.ds(pl.multiple_of(s * span, span), LEN)
                r1 = pl.ds(pl.multiple_of(s * span + LEN, LEN), span - LEN)
                count = place[5 + s]
                for j in range(4):
                    c = [slice(HALF * i + 128 * j, HALF * i + 128 * j + 128) for i in range(3)]
                    q, k, v = qkv[r, c[0]], qkv[r, c[1]], qkv[r, c[2]]
                    k0, v0 = qkv[r0, c[1]], qkv[r0, c[2]]
                    go = g[r, c[0]]
                    high, low = split_high(rel[r, 128 * (j // 2) : 128 * (j // 2) + 128])
                    prod = q.astype(F32) * k.astype(F32)
                    prod_g = go.astype(F32) * v.astype(F32)
                    gq, gk0, gv0, p_own, d_own, turned = [], 0.0, 0.0, [], [], []
                    for i, mask in enumerate(head_masks()):
                        qm, gm = q * mask, go * mask
                        h = 2 * j + i
                        probs, own = ngram_probs(
                            qm, prod, k0, high, low, table[...], count, h, lanes[i]
                        )
                        gp = dot_t(gm, v0)
                        g_own = jnp.sum(prod_g * lanes[i], axis=-1, keepdims=True)
                        inner = jnp.sum(probs * gp, axis=-1, keepdims=True) + own * g_own
                        ds = (probs * (gp - inner)).astype(BF)
                        ds_own = (own * (g_own - inner)).astype(BF).astype(F32)
                        gq.append(dot(ds, k0))
                        gk0 = gk0 + dot_g(ds, qm)
                        gv0 = gv0 + dot_g(probs.astype(BF), gm)
                        p_own.append(own.astype(BF).astype(F32))
                        d_own.append(ds_own)
                        back = skew(dot(ds, flip[...]))
                        lane = lax.broadcasted_iota(jnp.int32, back.shape, 1)
                        main = lax.broadcasted_iota(jnp.int32, back.shape, 0) < LEN
                        back = jnp.where((lane == 127) & jnp.logical_not(main), ds_own, back)
                        grads = dot_t(back.astype(BF), table_back[...])
                        turned.append(grads * quarter_mask(h % 4).astype(F32))
                    first = first_lanes(span)
                    d_own = jnp.where(first, d_own[0], d_own[1])
                    p_own = jnp.where(first, p_own[0], p_own[1])
                    gqf = jnp.where(first, gq[0], gq[1]) + d_own * k.astype(F32)
                    gqkv[r, c[0]] = (gqf * SCALE).astype(BF)
                    gkn = d_own * q.astype(F32) * SCALE
                    gvn = p_own * go.astype(F32)
                    gqkv[r0, c[1]] = (gk0 * SCALE).astype(BF)
                    gqkv[r0, c[2]] = gv0.astype(BF)
                    gqkv[r1, c[1]] = gkn[LEN:].astype(BF)
                    gqkv[r1, c[2]] = gvn[LEN:].astype(BF)
                    both = turned[0] + turned[1]
                    at = slice(128 * (j // 2), 128 * (j // 2) + 128)
                    if j % 2 == 0:
                        held = both
                    else:
                        grel[r, at] = (held + both).astype(BF)
                return carry

            lax.fori_loop(0, 2, step, 0)
            column_sums(sums, gqkv[...])
            column_sums(s_rel, grel[...])

        @pl.when(t == 3)
        def _():
            assemble_rel(wr, scr_r, place)
            wrel = scr_r[...].reshape(D, REL_HALF)
            input_grads(place, gz, [(gqkv, win[...]), (grel, wrel)], out, send)

    third = lambda t: jnp.minimum(t, 2)
    return run(
        body,
        4,
        [small(place), full(qkv), full(rel), full(keep), full(got), full(gz)]
        + blocks(pieces, 64, third)
        + blocks(pieces, 32, lambda t: 8),
        [
            out_full((rows, 3 * HALF), BF),
            out_full((rows, REL_HALF), BF),
            out_full((rows // 2, D), F32),
            out_full((rows // 2, D), BF),
            out_full((1, 3 * HALF), F32),
            out_full((1, REL_HALF), F32),
        ],
        [
            weight_scratch(64),
            pltpu.VMEM((4, 4, 2, 32, REL_HALF), BF),
            pltpu.VMEM((rows, HALF), BF),
            pltpu.VMEM((D, 3 * HALF), BF),
        ]
        + [pltpu.VMEM((128, 128), BF)] * 3,
        us=29,
    )


def grad_chunk(place, arrays, terms, total_rows, width=WIDE):
    n = len(arrays)

    def body(place, *refs):
        ins, outs, scr = refs[:n], refs[n : n + 4], refs[n + 4]
        t = pl.program_id(0)
        dp, core = place[0], place[2]

        def spread(value, at, rows, lanes=slice(0, WIDE)):
            v = value.astype(BF).reshape(4, 4, rows, WIDE)
            scr[:, :, :rows] = v
            for i in range(4):
                outs[i][:, at : at + rows, lanes] = scr[jnp.bitwise_xor(dp, i), :, :rows]

        for index, (kind, at, x, g, col) in enumerate(terms):

            @pl.when(t == index)
            def _(kind=kind, at=at, x=x, g=g, col=col):
                if kind == "whole":
                    spread(ins[x][...], at, ins[x].shape[0] // 16)
                    return
                if kind == "heads":
                    right = ins[g][:, col : col + WIDE]
                    mine, theirs = ins[x][...], ins[x + 1][...]
                    keep, got = dot_g(mine, right), dot_g(theirs, right)
                    quarter = (2, 4, 32, WIDE)
                    scr[pl.ds(2 * core, 2), :, :32] = keep.astype(BF).reshape(quarter)
                    scr[pl.ds(2 - 2 * core, 2), :, :32] = got.astype(BF).reshape(quarter)
                    spread(scr[:, :, :32], at, 32)
                    return
                if kind == "rel":
                    v = dot_g(ins[x][...], ins[g][...]).astype(BF).reshape(16, 2, 32, REL_HALF)
                    spread(jnp.concatenate([v[:, 0], v[:, 1]], axis=-1), at, 32)
                    return
                value = dot_g(ins[x][...], ins[g][:, col : col + WIDE])
                lanes = slice(col, col + WIDE) if kind == "rows" else slice(0, WIDE)
                spread(value, at, value.shape[0] // 16, lanes)

    return run(
        body,
        len(terms),
        [small(place)] + [full(a) for a in arrays],
        [out_full((4, total_rows, width), BF)] * 4,
        [weight_scratch(128)],
        us=10,
    )


def vec_chunk(place, pieces):
    def body(place, *refs):
        assemble(refs[:PIECES], refs[PIECES], place)

    return run(
        body,
        1,
        [small(place)] + blocks(pieces, 16, lambda t: 18),
        [out_full((4, 4, 16, WIDE), BF)],
        us=2,
    )[0]


class Order:

    def __init__(self, place):
        self.place = place
        self.last = None

    def after(self, *values):
        if self.last is not None:
            values = (self.last,) + values
        self.place = tie(self.place, *values)
        self.last = None

    def run(self, kernel, *args):
        if self.last is not None:
            self.place = tie(self.place, self.last)
        out = kernel(self.place, *args)
        self.last = out[0] if isinstance(out, (list, tuple)) else out
        return out

    def matmul(self, left, right):
        if self.last is not None:
            right = tie(right, self.last)
        self.last = dot_g(left, right).astype(BF)
        return self.last

    def add(self, first, *others, dtype=BF):
        if self.last is not None:
            first = tie(first, self.last)
        self.last = sum((v.astype(F32) for v in others), first.astype(F32)).astype(dtype)
        return self.last


class Links:

    def __init__(self, lay, before):
        self.lay = lay
        self.gathered = []
        self.first = []
        self.before = before
        self.second = []
        self.far = 2
        self.groups = [list(range(core, lay.nf, 2)) for core in range(2)]

    def turn(self):
        self.far = 3 - self.far
        return self.far

    def gather(self, buf, direct=False):
        far = 3 if direct else self.turn()
        if len(self.gathered) >= 2:
            buf = tie(buf, self.gathered[-2])
        own = lax.all_gather(buf, "fsdp", axis=0, axis_index_groups=self.groups)
        self.gathered.append(own)
        ready = tie(own, *(self.first[-1] if self.first else self.before))
        if len(self.second) >= 3:
            ready = tie(ready, self.second[-3])
        x, y = self.lay.flip_dp(ready, 1), self.lay.flip_dp(ready, 2)
        self.first.append((x, y))
        if direct:
            d = self.lay.flip_dp(ready, 3)
        else:
            d = self.lay.flip_dp(x, 2) if far == 2 else self.lay.flip_dp(y, 1)
        self.second.append(d)
        return [own, x, y, d]

    def scatter_whole(self, value):
        lay = self.lay
        groups = [
            [dp * lay.nf + fs for dp in range(lay.ndp) for fs in range(core, lay.nf, 2)]
            for core in range(2)
        ]
        return lax.psum_scatter(
            value, ("dp", "fsdp"), scatter_dimension=0, tiled=True, axis_index_groups=groups
        ).astype(F32)

    def scatter(self, order, parts, direct=False):
        own, x, y, d = parts
        if direct:
            moved = [self.lay.flip_dp(part, i + 1) for i, part in enumerate((x, y, d))]
            yield
            yield
            total = order.add(own, *moved)
        else:
            far = self.turn()
            d = self.lay.flip_dp(d, far)
            if far == 2:
                y = self.lay.flip_dp(y, 2)
                yield
                x = self.lay.flip_dp(order.add(x, d), 1)
            else:
                x = self.lay.flip_dp(x, 1)
                yield
                y = self.lay.flip_dp(order.add(y, d), 2)
            yield
            total = order.add(own, x, y)
        yield lax.psum_scatter(
            total, "fsdp", scatter_dimension=0, axis_index_groups=self.groups
        ).astype(F32)


def shards_fast(
    ndp,
    nf,
    source,
    dec_in,
    src_lengths,
    tgt_lengths,
    enc_in_proj,
    enc_out_proj,
    enc_ffn_in,
    enc_ffn_out,
    enc_gains,
    enc_biases,
    dec_in_proj,
    dec_rel_proj,
    dec_out_proj,
    cross_query,
    cross_kv,
    cross_out,
    dec_ffn_in,
    dec_ffn_out,
    dec_gains,
    dec_biases,
    enc_cot,
    dec_cot,
):
    lay = Layout(ndp, nf)
    lay.place()
    r, f, chips = lay.r, lay.f, lay.chips
    swap, pick, pair = lay.swap, lay.pick, lay.pair
    core = lay.core
    dec_rows = STREAMS * LEN

    def halves(matrix, groups, width):
        parts = matrix.reshape(r, groups, 2, width)
        return (
            pick(parts[:, :, 0], parts[:, :, 1]).reshape(r, groups * width),
            pick(parts[:, :, 1], parts[:, :, 0]).reshape(r, groups * width),
        )

    split = [
        halves(enc_in_proj, 3, HALF),
        halves(enc_ffn_in, chips, f),
        halves(dec_in_proj, 3, HALF),
        halves(cross_query, 1, HALF),
        halves(cross_kv, 2, HALF),
        halves(dec_ffn_in, chips, f),
        halves(dec_rel_proj, 1, REL_HALF),
    ]
    vec = jnp.concatenate(
        [
            enc_biases,
            enc_gains,
            dec_biases,
            dec_gains,
            src_lengths.astype(BF),
            tgt_lengths.astype(BF),
        ]
    )
    nvec = vec.shape[0]
    padded = -(-nvec // WIDE) * WIDE
    vec = jnp.pad(vec, (0, padded - nvec))
    mine = jnp.concatenate([own for own, other in split], axis=1)
    theirs = jnp.concatenate([other for own, other in split], axis=1)
    theirs_got = swap(theirs)
    vec_got = swap(vec)
    source_got = swap(source)
    dec_own = dec_in.transpose(1, 0, 2).reshape(dec_rows, D)
    dec_got = swap(dec_own)
    dcot_own = dec_cot.transpose(1, 0, 2).reshape(dec_rows, D)
    dcot_got = swap(dcot_own)
    ecot_got = swap(enc_cot)
    links = Links(lay, (theirs_got, vec_got, source_got, dec_got, dcot_got, ecot_got))
    w = {"dec_down": links.gather(dec_ffn_out), "enc_down": links.gather(enc_ffn_out)}

    def column_blocks(start, count):
        return [
            pair(
                mine[:, start + WIDE * i : start + WIDE * i + WIDE],
                theirs_got[:, start + WIDE * i : start + WIDE * i + WIDE],
                0,
            )
            for i in range(count)
        ]

    def row_blocks(matrix):
        return [matrix[:, :WIDE], matrix[:, WIDE:]]

    rel_start = mine.shape[1] - REL_HALF
    rel_block = pair(mine[:, rel_start:], theirs_got[:, rel_start:], 1)
    vec_pair = pair(vec[None], vec_got[None], 0)
    vec_used = 2 * padded // WIDE
    vec_block = jnp.pad(vec_pair.reshape(vec_used, WIDE), ((0, 16 - vec_used), (0, 0)))
    at = [0, 3 * WIDE, 7 * WIDE, 10 * WIDE, 11 * WIDE, 13 * WIDE]
    chunk_parts = {
        "enc": column_blocks(at[0], 3) + row_blocks(enc_out_proj),
        "enc_up": column_blocks(at[1], 4),
        "dec": column_blocks(at[2], 3) + row_blocks(dec_out_proj) + [rel_block, vec_block],
        "cross": column_blocks(at[3], 1) + column_blocks(at[4], 2) + row_blocks(cross_out),
        "dec_up": column_blocks(at[5], 4),
    }
    for name in ("dec", "enc", "enc_up", "cross", "dec_up"):
        w[name] = links.gather(jnp.concatenate(chunk_parts[name], axis=0))

    lens = vec_pair[:, nvec - 2 : nvec].T.reshape(-1).astype(F32).astype(jnp.int32)
    place = jnp.concatenate(
        [jnp.stack([lay.dp, lay.z, core]).astype(jnp.int32), lens, jnp.zeros((1,), jnp.int32)]
    )

    order = Order(place)
    vec_all = order.run(vec_chunk, w["dec"]).reshape(chips, 16, WIDE)[:, :vec_used]
    vec_all = vec_all.reshape(lay.devices, padded).astype(F32)
    widths = [enc_biases.shape[0], enc_gains.shape[0], dec_biases.shape[0], dec_gains.shape[0]]
    starts = [0]
    for width in widths:
        starts.append(starts[-1] + width)
    v_enc_b, v_enc_g, v_dec_b, v_dec_g = [
        vec_all[:, starts[i] : starts[i + 1]].reshape(-1) for i in range(4)
    ]
    eb, eg_rows = v_enc_b.reshape(-1, D), v_enc_g.reshape(2, D)
    dg_rows = v_dec_g.reshape(3, D)
    d_split = 2 * D + HEADS * BUCKETS
    db = v_dec_b[d_split:].reshape(-1, D)

    def half_of(vector):
        parts = vector.reshape(2, -1)
        return pick(parts[0], parts[1])

    def hidden_of(vector):
        parts = vector.reshape(chips, 2, f)
        return pick(parts[:, 0], parts[:, 1]).reshape(1, -1)

    zero_half = jnp.zeros((HALF,), F32)

    def qkv_bias(q, v):
        return jnp.concatenate([half_of(q), zero_half, half_of(v)])[None]

    def rows_of(*vectors):
        return jnp.stack(vectors)

    x = pair(source, source_got, 0)
    y = pair(dec_own, dec_got, 0)
    dcot = pair(dcot_own, dcot_got, 0)
    ecot = pair(enc_cot, ecot_got, 0)
    order.after(x, y, dcot, ecot)
    order.after(links.gathered[5], *links.first[3], links.second[1])
    dqkv, rel, da_keep, da_send = order.run(
        ngram_attention,
        y,
        qkv_bias(v_dec_b[:D], v_dec_b[D : 2 * D]),
        half_of(v_dec_b[2 * D : d_split])[None],
        w["dec"],
    )
    da_got = swap(da_send)
    order.after(links.gathered[6], *links.first[4])
    eqkv, ea_keep, ea_send = order.run(enc_attention, x, qkv_bias(eb[0], eb[1]), w["enc"])
    ea_got = swap(ea_send)
    order.after(*links.first[5])
    p3 = order.run(out_projection, da_keep, da_got, w["dec"])
    p3_got = swap(p3)
    p1 = order.run(out_projection, ea_keep, ea_got, w["enc"])
    p1_got = swap(p1)
    eunit1, einv1, eh1_low = order.run(
        norm_forward,
        x,
        False,
        p1,
        p1_got,
        rows_of(eb[2], eb[2], eb[2], eg_rows[0], eb[8]),
    )
    order.after(links.second[5], *links.first[6])
    eg, egp, p2 = order.run(
        ffn_forward, eh1_low, hidden_of(eb[3:7]), w["enc_up"], w["enc_down"]
    )
    p2_got = swap(p2)
    order.after(links.second[6])
    dunit1, dinv1, dh1_low, eunit2, einv2, enc_low, cq, ckv, ca_keep, ca_send = order.run(
        cross_forward,
        y,
        p3,
        p3_got,
        rows_of(db[0], dg_rows[0], db[9]),
        eunit1,
        rows_of(eg_rows[0], eb[8], eb[7], eg_rows[1], eb[9]),
        p2,
        p2_got,
        half_of(db[1])[None],
        jnp.concatenate([zero_half, half_of(db[2])])[None],
        w["cross"],
    )
    ca_got = swap(ca_send)
    p4 = order.run(out_projection, ca_keep, ca_got, w["cross"])
    p4_got = swap(p4)
    dunit2, dinv2, dh2_low = order.run(
        norm_forward,
        dunit1,
        True,
        p4,
        p4_got,
        rows_of(dg_rows[0], db[9], db[3], dg_rows[1], db[10]),
    )
    dg, dgp, p5 = order.run(
        ffn_forward, dh2_low, hidden_of(db[4:8]), w["dec_up"], w["dec_down"]
    )
    p5_got = swap(p5)

    up_terms = [("plain", 64 * b, 0, 1, WIDE * b) for b in range(4)]
    down_terms = [("rows", 0, 0, 1, WIDE * h) for h in range(2)]

    def grads(*args):
        scatter = links.scatter(order, order.run(grad_chunk, *args))
        next(scatter)
        return scatter

    dec_out, gz3, gf, s_gain3, s_shift3, s_gf = order.run(
        norm_backward,
        True,
        [dcot],
        [dunit2, p5, p5_got],
        rows_of(dg_rows[1], db[10], db[8], dg_rows[2], db[11]),
    )
    r_dd = grads([dg, gf], down_terms, 128, D)
    gu, p6, s_gu = order.run(ffn_back, gf, dgp, w["dec_up"], w["dec_down"])
    p6_got = swap(p6)
    r_du = grads([dh2_low, gu], up_terms, 256)
    gz2, gx, gca_keep, gca_send, s_gain2, s_shift2, s_gx = order.run(
        branch_back, gz3, p6, p6_got, dunit2, dinv2, dg_rows[1:2], w["cross"]
    )
    gca_got = swap(gca_send)
    next(r_dd)
    next(r_du)
    gcq, gckv, p7, s_gcq, s_gckv = order.run(
        cross_back, cq, ckv, gca_keep, gca_got, w["cross"]
    )
    p7_got = swap(p7)
    r_cross = grads(
        [dh1_low, gcq, enc_low, gckv, ca_keep, ca_got, gx],
        [
            ("plain", 0, 0, 1, 0),
            ("plain", 64, 2, 3, 0),
            ("plain", 128, 2, 3, WIDE),
            ("heads", 192, 4, 6, 0),
            ("heads", 224, 4, 6, WIDE),
        ],
        256,
    )
    gz1, go, gda_keep, gda_send, s_gain1, s_shift1, s_go = order.run(
        branch_back, gz2, p7, p7_got, dunit1, dinv1, dg_rows[0:1], w["dec"]
    )
    gda_got = swap(gda_send)
    gz2e, gfe, e_gain2, e_shift2, s_gfe = order.run(
        norm_backward, False, [ecot, p7, p7_got], [eunit2, einv2], rows_of(*([eg_rows[1]] * 5))
    )
    gue, p9, s_gue = order.run(ffn_back, gfe, egp, w["enc_up"], w["enc_down"])
    p9_got = swap(p9)
    total_dd = next(r_dd)
    next(r_cross)
    r_ed = grads([eg, gfe], down_terms, 128, D)
    r_eu = grads([eh1_low, gue], up_terms, 256)
    total_du = next(r_du)
    gz1e, goe, gea_keep, gea_send, e_gain1, e_shift1, s_goe = order.run(
        branch_back, gz2e, p9, p9_got, eunit1, einv1, eg_rows[0:1], w["enc"]
    )
    gea_got = swap(gea_send)
    gqkv, grel, p8, p8_send, s_gqkv, s_grel = order.run(
        ngram_back_kernel, dqkv, rel, gda_keep, gda_got, gz1, w["dec"]
    )
    p8_got = swap(p8_send)
    next(r_ed)
    next(r_eu)
    total_cross = next(r_cross)
    geqkv, p10, p10_send, s_geqkv = order.run(
        enc_attention_back, eqkv, gea_keep, gea_got, gz1e, w["enc"]
    )
    p10_got = swap(p10_send)
    g_dec_in = order.add(p8, p8_got, dtype=F32)
    r_dec = grads(
        [y, gqkv, da_keep, da_got, go, grel],
        [("plain", 64 * b, 0, 1, WIDE * b) for b in range(3)]
        + [("heads", 192, 2, 4, 0), ("heads", 224, 2, 4, WIDE), ("rel", 256, 0, 5, 0)],
        288,
    )
    g_source = order.add(p10, p10_got, dtype=F32)
    total_ed = next(r_ed)
    total_eu = next(r_eu)

    def widen(vector):
        zeros = jnp.zeros_like(vector)
        return pick(jnp.concatenate([vector, zeros]), jnp.concatenate([zeros, vector]))

    def widen_hidden(vector):
        parts = vector.reshape(chips, 1, f)
        zeros = jnp.zeros_like(parts)
        return pick(
            jnp.concatenate([parts, zeros], axis=1), jnp.concatenate([zeros, parts], axis=1)
        ).reshape(-1)

    def owned(*vectors):
        return jnp.concatenate(vectors).reshape(lay.devices, -1)

    vec_grads = jnp.concatenate(
        [
            owned(
                widen(s_geqkv[0, :HALF]),
                widen(s_geqkv[0, 2 * HALF :]),
                0.5 * s_goe[0],
                widen_hidden(s_gue),
                0.5 * s_gfe[0],
                0.5 * e_shift1[0],
                0.5 * e_shift2[0],
            ),
            owned(0.5 * e_gain1[0], 0.5 * e_gain2[0]),
            owned(
                widen(s_gqkv[0, :HALF]),
                widen(s_gqkv[0, 2 * HALF :]),
                widen(s_grel[0]),
                0.5 * s_go[0],
                widen(s_gcq[0]),
                widen(s_gckv[0, HALF:]),
                0.5 * s_gx[0],
                widen_hidden(s_gu),
                0.5 * s_gf[0],
                0.5 * s_shift1[0],
                0.5 * s_shift2[0],
                0.5 * s_shift3[0],
            ),
            owned(0.5 * s_gain1[0], 0.5 * s_gain2[0], 0.5 * s_gain3[0]),
        ],
        axis=1,
    ).astype(BF)
    vec_width = vec_grads.shape[1]
    vec_grads = jnp.pad(vec_grads, ((0, 0), (0, padded - vec_width)))
    vec_grads = vec_grads.reshape(chips, vec_used, WIDE)
    vec_grads = jnp.pad(vec_grads, ((0, 0), (0, 16 - vec_used), (0, 0))).reshape(chips * 16, WIDE)
    r_enc = grads(
        [x, geqkv, ea_keep, ea_got, goe, vec_grads],
        [("plain", 64 * b, 0, 1, WIDE * b) for b in range(3)]
        + [("heads", 192, 2, 4, 0), ("heads", 224, 2, 4, WIDE), ("whole", 256, 5, 5, 0)],
        272,
    )
    next(r_dec)
    next(r_enc)
    total2 = next(r_dec)
    total0 = next(r_enc)

    def split_rows(total, sizes):
        at = 0
        result = []
        for size in sizes:
            result.append(total[at : at + size])
            at += size
        return result

    def own_rows_of(total, count):
        rows = total.reshape(count, 2, r, WIDE)
        keep = pick(rows[:, 0], rows[:, 1])
        got = swap(pick(rows[:, 1], rows[:, 0]))
        return pair(keep[:, None], got[:, None], 1)

    def in_rows(rows):
        return rows.transpose(2, 0, 1, 3).reshape(r, -1)

    def up_rows(rows):
        per = WIDE // f
        return rows.reshape(4, 2, r, per, f).transpose(2, 0, 3, 1, 4).reshape(r, FF)

    def side(low, high):
        return jnp.concatenate([low, high], axis=1)

    t0 = split_rows(total0, [6 * r, r, r, 16])
    o_enc_in, o_enc_out = in_rows(own_rows_of(t0[0], 3)), side(t0[1], t0[2])
    vec_sum = t0[3][:vec_used].reshape(2, padded)
    vec_sum = pick(vec_sum[0], vec_sum[1]) + swap(pick(vec_sum[1], vec_sum[0]))
    o_vec = [vec_sum[starts[i] : starts[i + 1]] for i in range(4)]
    o_enc_up = up_rows(own_rows_of(total_eu, 4))
    o_enc_down = total_ed
    t2 = split_rows(total2, [6 * r, r, r, r])
    o_dec_in, o_dec_out = in_rows(own_rows_of(t2[0], 3)), side(t2[1], t2[2])
    relp = t2[3].reshape(r, 2, REL_HALF)
    o_rel = pair(pick(relp[:, 0], relp[:, 1]), swap(pick(relp[:, 1], relp[:, 0])), 1)
    t3 = split_rows(total_cross, [2 * r, 4 * r, r, r])
    o_cross_q = in_rows(own_rows_of(t3[0], 1))
    o_cross_kv = in_rows(own_rows_of(t3[1], 2))
    o_cross_out = side(t3[2], t3[3])
    o_dec_up = up_rows(own_rows_of(total_du, 4))
    o_dec_down = total_dd

    return (
        pick(enc_low[:LEN], enc_low[LEN:]),
        dec_out.reshape(STREAMS, LEN, D).transpose(1, 0, 2),
        g_source,
        g_dec_in.reshape(STREAMS, LEN, D).transpose(1, 0, 2),
        o_enc_in,
        o_enc_out,
        o_enc_up,
        o_enc_down,
        o_vec[1],
        o_vec[0],
        o_dec_in,
        o_rel,
        o_dec_out,
        o_cross_q,
        o_cross_kv,
        o_cross_out,
        o_dec_up,
        o_dec_down,
        o_vec[3],
        o_vec[2],
    )


def solution(mesh):
    ndp, nf = mesh.shape["dp"], mesh.shape["fsdp"]
    whole = ("dp", "fsdp")
    one, two, three = P(whole), P(whole, None), P(whole, None, None)
    args = (two, three, one, one) + (two,) * 4 + (one,) * 2 + (two,) * 8 + (one,) * 2 + (two, three)
    outs = (two, three, two, three) + (two,) * 4 + (one,) * 2 + (two,) * 8 + (one,) * 2

    def body(*arrays):
        if (ndp, nf) == (4, 8):
            return shards_fast(ndp, nf, *arrays)
        return shards(ndp, nf, *arrays)

    return jax.shard_map(body, mesh=mesh, in_specs=args, out_specs=outs, check_vma=False)
```

```python
import math

import jax
import jax.numpy as jnp
from jax import lax
from jax.experimental import pallas as pl
from jax.experimental.pallas import tpu as pltpu
from jax.sharding import PartitionSpec as P

D = 1024
HEADS = 16
HEAD = 64
FF = 4096
NGRAM = 2
STREAMS = NGRAM + 1
BUCKETS = 32
LEN = 128
HALF = D // 2
OWN_HEADS = HEADS // 2
REL_HALF = OWN_HEADS * BUCKETS
HIDDEN_HALF = FF // 2
WIDE = 512
EPSILON = 1e-05
MASKED = -1000000000.0
SCALE = 1.0 / math.sqrt(HEAD)
BF = jnp.bfloat16
F32 = jnp.float32
ENC_WIDTHS = (D, D, D, FF, D, D, D)
DEC_WIDTHS = (D, D, HEADS * BUCKETS, D, D, D, D, FF, D, D, D, D)


def bucket_value(distance, bucket_count):
    exact_count = bucket_count // 2
    if distance < exact_count:
        return distance
    return min(
        bucket_count - 1,
        exact_count
        + int(
            math.log(distance / exact_count)
            / math.log(128 / exact_count)
            * (bucket_count - exact_count)
        ),
    )


def bucket_table(length, bucket_count):
    positions = jnp.arange(length, dtype=jnp.int32)
    distance = positions[:, None] - positions[None, :]
    bucket = jnp.zeros((length, length), jnp.int32)
    for target in range(1, bucket_count):
        distance_at = 1
        while bucket_value(distance_at, bucket_count) < target:
            distance_at += 1
        bucket = bucket + (distance >= distance_at).astype(jnp.int32)
    return (bucket[:, :, None] == jnp.arange(bucket_count, dtype=jnp.int32)).astype(F32)


def slices_of(vector, widths):
    starts = 0
    result = []
    for amount in widths:
        result.append(vector[starts : starts + amount])
        starts += amount
    return result


def dot(a, b):
    return lax.dot_general(a, b, (((1,), (0,)), ((), ())), preferred_element_type=F32)


def dot_t(a, b):
    return lax.dot_general(a, b, (((1,), (1,)), ((), ())), preferred_element_type=F32)


def dot_g(a, b):
    return lax.dot_general(a, b, (((0,), (0,)), ((), ())), preferred_element_type=F32)


def norm_stats(values):
    average = jnp.mean(values, axis=-1, keepdims=True)
    centered = values - average
    variance = jnp.mean(centered * centered, axis=-1, keepdims=True)
    inverse = lax.rsqrt(variance + EPSILON)
    return centered * inverse, inverse


def norm(values, gain, shift):
    unit, inverse = norm_stats(values)
    return unit * gain + shift


def norm_back(values, gain, grads):
    unit, inverse = norm_stats(values)
    scaled = grads * gain
    mean_one = jnp.mean(scaled, axis=-1, keepdims=True)
    mean_two = jnp.mean(scaled * unit, axis=-1, keepdims=True)
    return (
        inverse * (scaled - mean_one - unit * mean_two),
        jnp.sum(grads * unit, axis=0),
        jnp.sum(grads, axis=0),
    )


def gelu_exact(inputs):
    return jax.nn.gelu(inputs, approximate=False)


def gelu_back(inputs, gradients):
    outputs, pullback = jax.vjp(gelu_exact, inputs)
    return pullback(gradients)[0]


def col_sum(values):
    return jnp.sum(values.astype(F32), axis=0)


class Layout:
    def __init__(self, ndp, nf):
        self.ndp = ndp
        self.nf = nf
        self.nz = nf // 2
        self.chips = ndp * self.nz
        self.devices = ndp * nf
        self.r = D // self.devices
        self.f = FF // self.devices

    def place(self):
        self.dp = lax.axis_index("dp")
        fs = lax.axis_index("fsdp")
        self.z = fs // 2
        self.core = fs % 2

    def swap(self, value):
        return lax.ppermute(value, "fsdp", [(i, i ^ 1) for i in range(self.nf)])

    def shift_z(self, value, step):
        return lax.ppermute(
            value, "fsdp", [(i, (i + 2 * step) % self.nf) for i in range(self.nf)]
        )

    def flip_dp(self, value, mask):
        return lax.ppermute(value, "dp", [(i, i ^ mask) for i in range(self.ndp)])

    def shift_dp(self, value, step):
        return lax.ppermute(value, "dp", [(i, (i + step) % self.ndp) for i in range(self.ndp)])

    def pick(self, first, second):
        return jnp.where(self.core == 0, first, second)

    def pair(self, own, other, axis):
        return self.pick(
            jnp.concatenate([own, other], axis=axis), jnp.concatenate([other, own], axis=axis)
        )


def tie(value, *others):
    return lax.optimization_barrier((value,) + others)[0]


def gather_z(lay, buf):
    out = jnp.zeros((lay.nz,) + buf.shape, buf.dtype)
    out = lax.dynamic_update_slice(out, buf[None], (lay.z, 0, 0))
    for step in range(1, lay.nz):
        got = lay.shift_z(buf, step)
        out = lax.dynamic_update_slice(out, got[None], ((lay.z - step) % lay.nz, 0, 0))
    return out


def gather_dp_first(lay, buf):
    if lay.ndp == 4:
        return [lay.flip_dp(buf, 1), lay.flip_dp(buf, 2)]
    return [lay.shift_dp(buf, step) for step in range(1, lay.ndp)]


def gather_dp_rest(lay, buf, first):
    half = lay.nz // 2
    out = jnp.zeros((lay.ndp,) + buf.shape, buf.dtype)
    if lay.ndp == 4:
        low = lay.flip_dp(first[0][:half], 2)
        high = lay.flip_dp(first[1][half:], 1)
        parts = [(0, 0, buf), (1, 0, first[0]), (2, 0, first[1]), (3, 0, low), (3, half, high)]
        for flip, at, part in parts:
            out = lax.dynamic_update_slice(out, part[None], (lay.dp ^ flip, at, 0, 0))
        return out
    out = lax.dynamic_update_slice(out, buf[None], (lay.dp, 0, 0, 0))
    for step in range(1, lay.ndp):
        out = lax.dynamic_update_slice(
            out, first[step - 1][None], ((lay.dp - step) % lay.ndp, 0, 0, 0)
        )
    return out


def gather_all(lay, bufs):
    staged = []
    results = []
    firsts = []
    for i, buf in enumerate(bufs):
        if i >= 2:
            buf = tie(buf, *firsts[i - 2])
        z = gather_z(lay, buf)
        staged.append(z)
        firsts.append(gather_dp_first(lay, z))
    for z, first in zip(staged, firsts):
        results.append(gather_dp_rest(lay, z, first))
    return results


def take(buf, index, axis=0):
    return lax.dynamic_index_in_dim(buf, index, axis, keepdims=False)


def add_low(*values):
    return sum(v.astype(F32) for v in values).astype(BF)


def scatter_dp(lay, buf):
    if lay.ndp == 4:
        half = lay.nz // 2
        far = take(buf, lay.dp ^ 3)
        to_x = take(buf, lay.dp ^ 1)
        to_y = take(buf, lay.dp ^ 2)
        own = take(buf, lay.dp)
        low = lay.flip_dp(far[:half], 2)
        high = lay.flip_dp(far[half:], 1)
        to_x = jnp.concatenate([add_low(to_x[:half], low), to_x[half:]], axis=0)
        to_y = jnp.concatenate([to_y[:half], add_low(to_y[half:], high)], axis=0)
        return add_low(own, lay.flip_dp(to_x, 1), lay.flip_dp(to_y, 2))
    parts = [take(buf, lay.dp)]
    for step in range(1, lay.ndp):
        parts.append(lay.shift_dp(take(buf, (lay.dp + step) % lay.ndp), step))
    return add_low(*parts)


def scatter_z(lay, buf):
    total = take(buf, lay.z).astype(F32)
    for step in range(1, lay.nz):
        total = total + lay.shift_z(take(buf, (lay.z + step) % lay.nz), step).astype(F32)
    return total


def attention_forward(queries, keys, values, allowed):
    scores = jnp.einsum("snihe,sjhe->snhij", queries, keys, preferred_element_type=F32) * SCALE
    probs = jax.nn.softmax(jnp.where(allowed, scores, MASKED), axis=-1)
    out = jnp.einsum("snhij,sjhe->snihe", probs.astype(BF), values, preferred_element_type=F32)
    return out.astype(BF), probs


def attention_back(queries, keys, values, probs, grad_out):
    grad_probs = jnp.einsum("snihe,sjhe->snhij", grad_out, values, preferred_element_type=F32)
    grad_values = jnp.einsum(
        "snhij,snihe->sjhe", probs.astype(BF), grad_out, preferred_element_type=F32
    )
    grad_scores = (
        probs * (grad_probs - jnp.sum(probs * grad_probs, axis=-1, keepdims=True))
    ).astype(BF)
    grad_queries = (
        jnp.einsum("snhij,sjhe->snihe", grad_scores, keys, preferred_element_type=F32) * SCALE
    )
    grad_keys = (
        jnp.einsum("snhij,snihe->sjhe", grad_scores, queries, preferred_element_type=F32) * SCALE
    )
    return grad_queries.astype(BF), grad_keys.astype(BF), grad_values.astype(BF)


def ngram_forward(dqkv, rel, tgt, onehot):
    q, k, v = dqkv[:, :, :, 0], dqkv[:, :, :, 1], dqkv[:, :, :, 2]
    positions = jnp.arange(LEN, dtype=jnp.int32)
    inside = positions[None, :] < tgt[:, None]
    main_valid = (positions[None, :] <= positions[:, None])[None] & inside[:, None]
    pred_valid = (positions[None, :] < positions[:, None])[None] & inside[:, None]
    valid = jnp.stack([main_valid] + [pred_valid] * NGRAM, axis=1)[:, :, None]
    main = jnp.einsum("snihe,sjhe->snhij", q, k[:, 0], preferred_element_type=F32) * SCALE
    main = main + jnp.einsum("snihk,ijk->snhij", rel, onehot, precision=lax.Precision.HIGHEST)
    main = jnp.where(valid, main, MASKED)
    own = jnp.einsum("snihe,snihe->snhi", q, k, preferred_element_type=F32) * SCALE
    own = own + jnp.transpose(rel[..., 0], (0, 1, 3, 2))
    stream = jnp.arange(STREAMS)[None, :, None, None]
    own = jnp.where(stream == 0, -jnp.inf, own)
    top = jnp.maximum(jnp.max(main, axis=-1), own)
    main = jnp.exp(main - top[..., None])
    own = jnp.exp(own - top)
    total = jnp.sum(main, axis=-1) + own
    main = main / total[..., None]
    own = own / total
    out = jnp.einsum("snhij,sjhe->snihe", main.astype(BF), v[:, 0], preferred_element_type=F32)
    own_low = jnp.transpose(own.astype(BF), (0, 1, 3, 2)).astype(F32)[..., None]
    out = out + own_low * v.astype(F32)
    return out.astype(BF), main, own


def ngram_back(dqkv, main, own, onehot, grad_out):
    q, k, v = dqkv[:, :, :, 0], dqkv[:, :, :, 1], dqkv[:, :, :, 2]
    grad_main = jnp.einsum("snihe,sjhe->snhij", grad_out, v[:, 0], preferred_element_type=F32)
    grad_own = jnp.einsum("snihe,snihe->snhi", grad_out, v, preferred_element_type=F32)
    inner = jnp.sum(main * grad_main, axis=-1) + own * grad_own
    ds = (main * (grad_main - inner[..., None])).astype(BF)
    ds_own = (own * (grad_own - inner)).astype(BF)
    own_rows = jnp.transpose(ds_own, (0, 1, 3, 2)).astype(F32)[..., None]
    p_rows = jnp.transpose(own.astype(BF), (0, 1, 3, 2)).astype(F32)[..., None]
    gq = (
        jnp.einsum("snhij,sjhe->snihe", ds, k[:, 0], preferred_element_type=F32)
        + own_rows * k.astype(F32)
    ) * SCALE
    gk0 = jnp.einsum("snhij,snihe->sjhe", ds, q, preferred_element_type=F32) * SCALE
    gv0 = jnp.einsum("snhij,snihe->sjhe", main.astype(BF), grad_out, preferred_element_type=F32)
    gk = own_rows * q.astype(F32) * SCALE
    gv = p_rows * grad_out.astype(F32)
    gk = jnp.concatenate([gk0[:, None], gk[:, 1:]], axis=1)
    gv = jnp.concatenate([gv0[:, None], gv[:, 1:]], axis=1)
    gqkv = jnp.stack([gq, gk, gv], axis=3).astype(BF)
    grel = jnp.einsum("snhij,ijk->snihk", ds, onehot.astype(BF), preferred_element_type=F32)
    first = (jnp.arange(BUCKETS) == 0).astype(F32)
    grel = (grel + own_rows * first).astype(BF)
    return gqkv, grel


def shards(
    ndp,
    nf,
    source,
    dec_in,
    src_lengths,
    tgt_lengths,
    enc_in_proj,
    enc_out_proj,
    enc_ffn_in,
    enc_ffn_out,
    enc_gains,
    enc_biases,
    dec_in_proj,
    dec_rel_proj,
    dec_out_proj,
    cross_query,
    cross_kv,
    cross_out,
    dec_ffn_in,
    dec_ffn_out,
    dec_gains,
    dec_biases,
    enc_cot,
    dec_cot,
):
    lay = Layout(ndp, nf)
    lay.place()
    r, f, chips = lay.r, lay.f, lay.chips
    swap, pick, pair = lay.swap, lay.pick, lay.pair
    core = lay.core

    def halves(matrix, groups, width):
        parts = matrix.reshape(r, groups, 2, width)
        return (
            pick(parts[:, :, 0], parts[:, :, 1]).reshape(r, groups * width),
            pick(parts[:, :, 1], parts[:, :, 0]).reshape(r, groups * width),
        )

    split = [
        halves(enc_in_proj, 3, HALF),
        halves(enc_ffn_in, chips, f),
        halves(dec_in_proj, 3, HALF),
        halves(cross_query, 1, HALF),
        halves(cross_kv, 2, HALF),
        halves(dec_ffn_in, chips, f),
        halves(dec_rel_proj, 1, REL_HALF),
    ]
    vec = jnp.concatenate(
        [
            enc_biases,
            enc_gains,
            dec_biases,
            dec_gains,
            src_lengths.astype(BF),
            tgt_lengths.astype(BF),
        ]
    )
    nvec = vec.shape[0]
    padded = -(-nvec // WIDE) * WIDE
    vec = jnp.pad(vec, (0, padded - nvec))
    mine = jnp.concatenate([own for own, other in split], axis=1)
    theirs = jnp.concatenate([other for own, other in split], axis=1)
    theirs_got = swap(theirs)
    vec_got = swap(vec)
    source_got = swap(source)
    dec_in_got = swap(dec_in.reshape(LEN * STREAMS, D))

    def owner_rows(start, width):
        return pair(mine[:, start : start + width], theirs_got[:, start : start + width], 0)

    def column_blocks(start, count):
        return [owner_rows(start + WIDE * i, WIDE) for i in range(count)]

    def row_blocks(matrix):
        return [matrix[:, :WIDE], matrix[:, WIDE:]]

    rel_start = mine.shape[1] - REL_HALF
    rel_own = mine[:, rel_start:]
    rel_other = theirs_got[:, rel_start:]
    vec_pair = pair(vec[None], vec_got[None], 0).reshape(-1, WIDE)
    vec_rows = -(-vec_pair.shape[0] // 16) * 16
    vec_used = vec_pair.shape[0]
    vec_pair = jnp.pad(vec_pair, ((0, vec_rows - vec_used), (0, 0)))
    wide_at = [0, 3 * WIDE, 7 * WIDE, 10 * WIDE, 11 * WIDE, 13 * WIDE]
    chunk_parts = [
        column_blocks(wide_at[0], 3) + row_blocks(enc_out_proj) + [vec_pair],
        column_blocks(wide_at[1], 4) + row_blocks(enc_ffn_out),
        column_blocks(wide_at[2], 3) + [pair(rel_own, rel_other, 1)] + row_blocks(dec_out_proj),
        column_blocks(wide_at[3], 1) + column_blocks(wide_at[4], 2) + row_blocks(cross_out),
        column_blocks(wide_at[5], 4) + row_blocks(dec_ffn_out),
    ]
    bufs = [jnp.concatenate(parts, axis=0) for parts in chunk_parts]
    full = gather_all(lay, bufs)

    def cut(index, block):
        parts = chunk_parts[index]
        at = sum(p.shape[0] for p in parts[:block])
        rows = parts[block].shape[0]
        return full[index][:, :, at : at + rows].reshape(chips * rows, WIDE)

    def columns(index, first, count):
        return jnp.concatenate([cut(index, first + i) for i in range(count)], axis=1)

    def head_rows(index, first):
        rows = columns(index, first, 2)
        low, high = rows[:HALF // 2], rows[HALF // 2 :]
        keep = pick(low, high).reshape(chips // 2, 1, r, D)
        got = swap(pick(high, low)).reshape(chips // 2, 1, r, D)
        return pair(keep, got, 1).reshape(HALF, D)

    w_enc_in = columns(0, 0, 3)
    w_enc_out = head_rows(0, 3)
    w_enc_up = columns(1, 0, 4)
    w_enc_down = columns(1, 4, 2)
    w_dec_in = columns(2, 0, 3)
    w_rel = (
        cut(2, 3)
        .reshape(chips, r, 2, REL_HALF)
        .transpose(0, 2, 1, 3)
        .reshape(D, REL_HALF)
    )
    w_dec_out = head_rows(2, 4)
    w_cross_q = columns(3, 0, 1)
    w_cross_kv = columns(3, 1, 2)
    w_cross_out = head_rows(3, 3)
    w_dec_up = columns(4, 0, 4)
    w_dec_down = columns(4, 4, 2)

    vec_all = (
        cut(0, 5).reshape(chips, vec_rows, WIDE)[:, :vec_used].reshape(lay.devices, padded).astype(F32)
    )
    widths = [enc_biases.shape[0], enc_gains.shape[0], dec_biases.shape[0], dec_gains.shape[0]]
    starts = [0]
    for width in widths:
        starts.append(starts[-1] + width)
    v_enc_b, v_enc_g, v_dec_b, v_dec_g = [
        vec_all[:, starts[i] : starts[i + 1]].reshape(-1) for i in range(4)
    ]
    ebias = slices_of(v_enc_b, ENC_WIDTHS)
    egain = slices_of(v_enc_g, (D, D))
    dbias = slices_of(v_dec_b, DEC_WIDTHS)
    dgain = slices_of(v_dec_g, (D, D, D))

    def half_of(vector):
        parts = vector.reshape(2, -1)
        return pick(parts[0], parts[1])

    def hidden_of(vector):
        parts = vector.reshape(chips, 2, f)
        return pick(parts[:, 0], parts[:, 1]).reshape(-1)

    zero_half = jnp.zeros((HALF,), F32)
    lens = jnp.stack([pair(vec[None], vec_got[None], 0)[:, nvec - 2 + i] for i in range(2)])
    lens = lens.astype(F32).astype(jnp.int32)
    src_len, tgt_len = lens[0], lens[1]
    positions = jnp.arange(LEN, dtype=jnp.int32)
    src_valid = (positions[None, :] < src_len[:, None])[:, None, None, None, :]
    onehot = bucket_table(LEN, BUCKETS)

    def both(partial):
        low = partial.astype(BF)
        return low.astype(F32) + swap(low).astype(F32)

    x = pair(source[None], source_got[None], 0).reshape(2 * LEN, D)
    qkv_bias = jnp.concatenate([half_of(ebias[0]), zero_half, half_of(ebias[1])])
    eqkv = (dot(x, w_enc_in) + qkv_bias).astype(BF).reshape(2, LEN, 3, OWN_HEADS, HEAD)
    eq, ek, ev = eqkv[:, None, :, 0], eqkv[:, :, 1], eqkv[:, :, 2]
    ea, eprobs = attention_forward(eq, ek, ev, src_valid)
    ea = ea.reshape(2 * LEN, HALF)
    ez1 = x.astype(F32) + both(dot(ea, w_enc_out)) + ebias[2]
    eh1 = norm(ez1, egain[0], ebias[5])
    eh1_low = eh1.astype(BF)
    eu = dot(eh1_low, w_enc_up) + hidden_of(ebias[3])
    eg = gelu_exact(eu).astype(BF)
    ez2 = eh1 + both(dot(eg, w_enc_down)) + ebias[4]
    enc = norm(ez2, egain[1], ebias[6])
    enc_low = enc.astype(BF)

    rows = 2 * STREAMS * LEN
    y = pair(
        dec_in.transpose(1, 0, 2)[None], dec_in_got.reshape(LEN, STREAMS, D).transpose(1, 0, 2)[None], 0
    ).reshape(rows, D)
    dqkv_bias = jnp.concatenate([half_of(dbias[0]), zero_half, half_of(dbias[1])])
    dqkv = (dot(y, w_dec_in) + dqkv_bias).astype(BF)
    dqkv = dqkv.reshape(2, STREAMS, LEN, 3, OWN_HEADS, HEAD)
    rel = (dot(y, w_rel) + half_of(dbias[2])).reshape(2, STREAMS, LEN, OWN_HEADS, BUCKETS)
    da, dmain, down = ngram_forward(dqkv, rel, tgt_len, onehot)
    da = da.reshape(rows, HALF)
    dz1 = y.astype(F32) + both(dot(da, w_dec_out)) + dbias[3]
    dh1 = norm(dz1, dgain[0], dbias[9])
    dh1_low = dh1.astype(BF)
    cq = (dot(dh1_low, w_cross_q) + half_of(dbias[4])).astype(BF)
    cq = cq.reshape(2, STREAMS, LEN, OWN_HEADS, HEAD)
    ckv = dot(enc_low, w_cross_kv) + jnp.concatenate([zero_half, half_of(dbias[5])])
    ckv = ckv.astype(BF).reshape(2, LEN, 2, OWN_HEADS, HEAD)
    ck, cv = ckv[:, :, 0], ckv[:, :, 1]
    ca, cprobs = attention_forward(cq, ck, cv, src_valid)
    ca = ca.reshape(rows, HALF)
    dz2 = dh1 + both(dot(ca, w_cross_out)) + dbias[6]
    dh2 = norm(dz2, dgain[1], dbias[10])
    dh2_low = dh2.astype(BF)
    du = dot(dh2_low, w_dec_up) + hidden_of(dbias[7])
    dg = gelu_exact(du).astype(BF)
    dz3 = dh2 + both(dot(dg, w_dec_down)) + dbias[8]
    dec = norm(dz3, dgain[2], dbias[11])

    def own_rows_of(total, count):
        blocks = total[: count * 2 * r].reshape(count, 2, r, WIDE)
        keep = pick(blocks[:, 0], blocks[:, 1])
        got = swap(pick(blocks[:, 1], blocks[:, 0]))
        return pair(keep[:, None], got[:, None], 1)

    def chip_blocks(grad):
        n = grad.shape[1] // WIDE
        shape = (lay.ndp, lay.nz, grad.shape[0] // chips, WIDE)
        low = grad.astype(BF)
        return [low[:, WIDE * i : WIDE * i + WIDE].reshape(shape) for i in range(n)]

    def head_blocks(grad):
        parts = grad.astype(BF).reshape(chips // 2, 2, r, D)
        keep = pick(parts[:, 0], parts[:, 1])
        got = swap(pick(parts[:, 1], parts[:, 0]))
        return chip_blocks(pair(keep, got, 0).reshape(chips * r, D))

    def scatter(parts, previous):
        buf = jnp.concatenate(parts, axis=2)
        if previous is not None:
            buf = tie(buf, previous)
        first = scatter_dp(lay, buf)
        return scatter_z(lay, first), first

    def split_rows(total, sizes):
        at = 0
        result = []
        for size in sizes:
            result.append(total[at : at + size])
            at += size
        return result

    dcot_got = swap(dec_cot.reshape(LEN * STREAMS, D)).reshape(LEN, STREAMS, D)
    dcot = pair(dec_cot.transpose(1, 0, 2)[None], dcot_got.transpose(1, 0, 2)[None], 0)
    dcot = dcot.reshape(rows, D).astype(F32)
    gz3, ggain3, gnorm3 = norm_back(dz3, dgain[2], dcot)
    gf = gz3.astype(BF)
    g_down = dot_g(dg, gf)
    gu = gelu_back(du, dot_t(gf, w_dec_down)).astype(BF)
    g_up = dot_g(dh2_low, gu)
    total4, first4 = scatter(chip_blocks(g_up) + chip_blocks(g_down), None)
    gz2, ggain2, gnorm2 = norm_back(dz2, dgain[1], gz3 + both(dot_t(gu, w_dec_up)))
    gx = gz2.astype(BF)
    g_cross_out = dot_g(ca, gx)
    gca = dot_t(gx, w_cross_out).astype(BF).reshape(2, STREAMS, LEN, OWN_HEADS, HEAD)
    gcq, gck, gcv = attention_back(cq, ck, cv, cprobs, gca)
    gcq = gcq.reshape(rows, HALF)
    gckv = jnp.stack([gck, gcv], axis=2).reshape(2 * LEN, D)
    g_cross_q = dot_g(dh1_low, gcq)
    g_cross_kv = dot_g(enc_low, gckv)
    total3, first3 = scatter(
        chip_blocks(g_cross_q) + chip_blocks(g_cross_kv) + head_blocks(g_cross_out), first4
    )
    ecot_got = swap(enc_cot)
    ecot = pair(enc_cot[None], ecot_got[None], 0).reshape(2 * LEN, D).astype(F32)
    genc = ecot + both(dot_t(gckv, w_cross_kv))
    gz1, ggain1, gnorm1 = norm_back(dz1, dgain[0], gz2 + both(dot_t(gcq, w_cross_q)))
    go = gz1.astype(BF)
    g_dec_out = dot_g(da, go)
    gda = dot_t(go, w_dec_out).astype(BF).reshape(2, STREAMS, LEN, OWN_HEADS, HEAD)
    gqkv, grel = ngram_back(dqkv, dmain, down, onehot, gda)
    gqkv = gqkv.reshape(rows, 3 * HALF)
    grel = grel.reshape(rows, REL_HALF)
    g_dec_in = dot_g(y, gqkv)
    g_rel = dot_g(y, grel)
    rel_block = (
        g_rel.astype(BF)
        .reshape(chips, 2, r, REL_HALF)
        .transpose(0, 2, 1, 3)
        .reshape(lay.ndp, lay.nz, r, WIDE)
    )
    total2, first2 = scatter(chip_blocks(g_dec_in) + [rel_block] + head_blocks(g_dec_out), first3)

    def own_sequence(partial, count):
        parts = partial.reshape(2, count, D)
        keep = pick(parts[0], parts[1])
        return keep + swap(pick(parts[1], parts[0]).astype(BF)).astype(F32)

    def own_part(values, count):
        parts = values.reshape(2, count, D)
        return pick(parts[0], parts[1])

    dec_rows = STREAMS * LEN
    g_dec_input = own_part(gz1, dec_rows) + own_sequence(
        dot_t(gqkv, w_dec_in) + dot_t(grel, w_rel), dec_rows
    )

    def widen(vector):
        zeros = jnp.zeros_like(vector)
        return pick(jnp.concatenate([vector, zeros]), jnp.concatenate([zeros, vector]))

    def widen_hidden(vector):
        parts = vector.reshape(chips, 1, f)
        zeros = jnp.zeros_like(parts)
        return pick(
            jnp.concatenate([parts, zeros], axis=1), jnp.concatenate([zeros, parts], axis=1)
        ).reshape(-1)

    column_sums = col_sum(gqkv)
    dec_vec = jnp.concatenate(
        [
            widen(column_sums[:HALF]),
            widen(column_sums[2 * HALF :]),
            widen(col_sum(grel)),
            0.5 * col_sum(go),
            widen(col_sum(gcq)),
            widen(col_sum(gckv)[HALF:]),
            0.5 * col_sum(gx),
            widen_hidden(col_sum(gu)),
            0.5 * col_sum(gf),
            0.5 * gnorm1,
            0.5 * gnorm2,
            0.5 * gnorm3,
            0.5 * ggain1,
            0.5 * ggain2,
            0.5 * ggain3,
        ]
    )

    gz2e, eggain2, egnorm2 = norm_back(ez2, egain[1], genc)
    gfe = gz2e.astype(BF)
    ge_down = dot_g(eg, gfe)
    gue = gelu_back(eu, dot_t(gfe, w_enc_down)).astype(BF)
    ge_up = dot_g(eh1_low, gue)
    total1, first1 = scatter(chip_blocks(ge_up) + chip_blocks(ge_down), first2)
    gz1e, eggain1, egnorm1 = norm_back(ez1, egain[0], gz2e + both(dot_t(gue, w_enc_up)))
    goe = gz1e.astype(BF)
    ge_out = dot_g(ea, goe)
    gae = dot_t(goe, w_enc_out).astype(BF).reshape(2, 1, LEN, OWN_HEADS, HEAD)
    geq, gek, gev = attention_back(eq, ek, ev, eprobs, gae)
    geqkv = jnp.stack([geq[:, 0], gek, gev], axis=2).reshape(2 * LEN, 3 * HALF)
    ge_in = dot_g(x, geqkv)
    total0, first0 = scatter(chip_blocks(ge_in) + head_blocks(ge_out), first1)
    g_source = own_part(gz1e, LEN) + own_sequence(dot_t(geqkv, w_enc_in), LEN)
    ecolumn_sums = col_sum(geqkv)
    enc_vec = jnp.concatenate(
        [
            widen(ecolumn_sums[:HALF]),
            widen(ecolumn_sums[2 * HALF :]),
            0.5 * col_sum(goe),
            widen_hidden(col_sum(gue)),
            0.5 * col_sum(gfe),
            0.5 * egnorm1,
            0.5 * egnorm2,
            0.5 * eggain1,
            0.5 * eggain2,
        ]
    )
    me = lay.dp * lay.nf + lax.axis_index("fsdp")

    def own_slice(vector):
        return take(vector.reshape(lay.devices, -1), me)

    dec_vec = lax.psum(dec_vec, ("dp", "fsdp"))
    enc_vec = lax.psum(enc_vec, ("dp", "fsdp"))
    nb = sum(ENC_WIDTHS)
    g_enc_biases, g_enc_gains = own_slice(enc_vec[:nb]), own_slice(enc_vec[nb:])
    nb = sum(DEC_WIDTHS)
    g_dec_biases, g_dec_gains = own_slice(dec_vec[:nb]), own_slice(dec_vec[nb:])

    def in_rows(blocks):
        return blocks.transpose(2, 0, 1, 3).reshape(r, -1)

    def up_rows(blocks):
        per = WIDE // f
        return blocks.reshape(4, 2, r, per, f).transpose(2, 0, 3, 1, 4).reshape(r, FF)

    def side(low, high):
        return jnp.concatenate([low, high], axis=1)

    t0 = split_rows(total0, [6 * r, r, r])
    o_enc_in, o_enc_out = in_rows(own_rows_of(t0[0], 3)), side(t0[1], t0[2])
    t1 = split_rows(total1, [8 * r, f, f])
    o_enc_up, o_enc_down = up_rows(own_rows_of(t1[0], 4)), side(t1[1], t1[2])
    t2 = split_rows(total2, [6 * r, r, r, r])
    o_dec_in, o_dec_out = in_rows(own_rows_of(t2[0], 3)), side(t2[2], t2[3])
    relp = t2[1].reshape(r, 2, REL_HALF)
    rel_keep = pick(relp[:, 0], relp[:, 1])
    o_rel = pair(rel_keep, swap(pick(relp[:, 1], relp[:, 0])), 1)
    t3 = split_rows(total3, [2 * r, 4 * r, r, r])
    o_cross_q = in_rows(own_rows_of(t3[0], 1))
    o_cross_kv = in_rows(own_rows_of(t3[1], 2))
    o_cross_out = side(t3[2], t3[3])
    t4 = split_rows(total4, [8 * r, f, f])
    o_dec_up, o_dec_down = up_rows(own_rows_of(t4[0], 4)), side(t4[1], t4[2])

    return (
        own_part(enc_low, LEN),
        own_part(dec.astype(BF), dec_rows).reshape(STREAMS, LEN, D).transpose(1, 0, 2),
        g_source,
        g_dec_input.reshape(STREAMS, LEN, D).transpose(1, 0, 2),
        o_enc_in,
        o_enc_out,
        o_enc_up,
        o_enc_down,
        g_enc_gains,
        g_enc_biases,
        o_dec_in,
        o_rel,
        o_dec_out,
        o_cross_q,
        o_cross_kv,
        o_cross_out,
        o_dec_up,
        o_dec_down,
        g_dec_gains,
        g_dec_biases,
    )


BUDGET = 26 * 1024 * 1024
PIECES = 4
HBM_RATE = 1.0e6
FLOP_RATE = 1.0e9


def run(body, grid, ins, outs, scratch=(), us=5):
    arrays = [a for a, s in ins]
    return pl.pallas_call(
        body,
        grid=(grid,),
        in_specs=[s for a, s in ins],
        out_specs=[s for a, s in outs],
        out_shape=[a for a, s in outs],
        scratch_shapes=list(scratch),
        compiler_params=pltpu.CompilerParams(vmem_limit_bytes=BUDGET),
        cost_estimate=pl.CostEstimate(
            flops=int(us * FLOP_RATE), bytes_accessed=int(us * HBM_RATE), transcendentals=0
        ),
    )(*arrays)


def full(array):
    zeros = (0,) * array.ndim
    return array, pl.BlockSpec(array.shape, lambda t: zeros, pipeline_mode=pl.Buffered(1))


def small(array):
    return array, pl.BlockSpec(memory_space=pltpu.SMEM)


def out_full(shape, dtype):
    zeros = (0,) * len(shape)
    return jax.ShapeDtypeStruct(shape, dtype), pl.BlockSpec(shape, lambda t: zeros)


def out_cols(rows, cols, dtype, index):
    return (
        jax.ShapeDtypeStruct((rows, cols), dtype),
        pl.BlockSpec((rows, WIDE), lambda t: (0, index(t))),
    )


def in_cols(array, index, width=WIDE):
    return array, pl.BlockSpec((array.shape[0], width), lambda t: (0, index(t)))


def blocks(pieces, rows, index):
    return [
        (p, pl.BlockSpec((4, rows, WIDE), lambda t: (0, index(t), 0))) for p in pieces
    ]


def wide_blocks(pieces, index):
    return [(p, pl.BlockSpec((4,) + p.shape[1:2] + (WIDE,), lambda t: (0, 0, index(t)))) for p in pieces]


def assemble(refs, scr, place):
    for i in range(4):
        scr[jnp.bitwise_xor(place[0], i)] = refs[i][...]


def weight_scratch(rows, width=WIDE):
    return pltpu.VMEM((4, 4, rows, width), BF)


def matrix_of(scr):
    a, b, c, d = scr.shape
    return scr[...].reshape(a * b * c, d)


def pick_matrix(parity):
    i = lax.broadcasted_iota(jnp.int32, (HALF, HALF // 2), 0)
    j = lax.broadcasted_iota(jnp.int32, (HALF, HALF // 2), 1)
    from_row = ((j >> 5) << 6) + (parity << 5) + (j & 31)
    return jnp.where(i == from_row, 1.0, 0.0).astype(BF)


def head_masks():
    lane = lax.broadcasted_iota(jnp.int32, (1, 128), 1)
    first = jnp.where(lane < HEAD, 1.0, 0.0)
    return first.astype(BF), (1.0 - first).astype(BF)


def first_lanes(rows):
    return lax.broadcasted_iota(jnp.int32, (rows, 128), 1) < HEAD


def soft_rows(scores):
    top = jnp.max(scores, axis=-1, keepdims=True)
    raised = jnp.exp(scores - top)
    return raised * (1.0 / jnp.sum(raised, axis=-1, keepdims=True))


def masked_probs(queries, keys, count):
    scores = dot_t(queries, keys) * SCALE
    column = lax.broadcasted_iota(jnp.int32, scores.shape, 1)
    return soft_rows(jnp.where(column < count, scores, MASKED))


def attend(q, k, v, count):
    rows = q.shape[0]
    out = []
    for mask in head_masks():
        probs = masked_probs(q * mask, k, count).astype(BF)
        out.append(dot(probs, v))
    return jnp.where(first_lanes(rows), out[0], out[1]).astype(BF)


def attend_back(q, k, v, g, count):
    gq, gk, gv = [], 0.0, 0.0
    for mask in head_masks():
        qm, gm = q * mask, g * mask
        probs = masked_probs(qm, k, count)
        gp = dot_t(gm, v)
        ds = (probs * (gp - jnp.sum(probs * gp, axis=-1, keepdims=True))).astype(BF)
        gq.append(dot(ds, k))
        gk = gk + dot_g(ds, qm)
        gv = gv + dot_g(probs.astype(BF), gm)
    gq = jnp.where(first_lanes(q.shape[0]), gq[0], gq[1]) * SCALE
    return gq.astype(BF), (gk * SCALE).astype(BF), gv.astype(BF)


def split_parity(heads, place, keep, send):
    core = place[2]
    keep[...] = dot(heads[...], pick_matrix(core)).astype(BF)
    send[...] = dot(heads[...], pick_matrix(1 - core)).astype(BF)


def join_parity(keep, got, place, heads):
    core = place[2]
    heads[...] = (
        dot_t(keep[...], pick_matrix(core)) + dot_t(got[...], pick_matrix(1 - core))
    ).astype(BF)


def enc_attention(place, x, bias, pieces):
    rows = x.shape[0]

    def body(place, x, bias, *refs):
        w, (qkv, keep, send, scr, heads) = refs[:PIECES], refs[PIECES:]
        t = pl.program_id(0)
        assemble(w, scr, place)
        qkv[:, pl.ds(t * WIDE, WIDE)] = (dot(x[...], matrix_of(scr)) + bias[...]).astype(BF)

        @pl.when(t == 2)
        def _():
            for s in range(2):
                r = slice(s * LEN, s * LEN + LEN)
                for j in range(4):
                    c = [slice(HALF * i + 128 * j, HALF * i + 128 * j + 128) for i in range(3)]
                    heads[r, c[0]] = attend(qkv[r, c[0]], qkv[r, c[1]], qkv[r, c[2]], place[3 + s])
            split_parity(heads, place, keep, send)

    return run(
        body,
        3,
        [small(place), full(x), in_cols(bias, lambda t: t)] + blocks(pieces, 64, lambda t: t),
        [
            out_full((rows, 3 * HALF), BF),
            out_full((rows, HALF // 2), BF),
            out_full((rows, HALF // 2), BF),
        ],
        [weight_scratch(64), pltpu.VMEM((rows, HALF), BF)],
        us=10,
    )


def out_projection(place, keep, got, pieces):
    rows = keep.shape[0]

    def body(place, keep, got, *refs):
        w, (out, scr) = refs[:PIECES], refs[PIECES:]
        assemble(w, scr, place)
        core = place[2]
        mine = scr[pl.ds(2 * core, 2)].reshape(HALF // 2, WIDE)
        theirs = scr[pl.ds(2 - 2 * core, 2)].reshape(HALF // 2, WIDE)
        out[...] = (dot(keep[...], mine) + dot(got[...], theirs)).astype(BF)

    return run(
        body,
        2,
        [small(place), full(keep), full(got)] + blocks(pieces, 32, lambda t: 6 + t),
        [out_cols(rows, D, BF, lambda t: t)],
        [weight_scratch(32)],
        us=3,
    )[0]


def stats(v):
    centered = v - jnp.mean(v, axis=-1, keepdims=True)
    inverse = lax.rsqrt(jnp.mean(centered * centered, axis=-1, keepdims=True) + EPSILON)
    return centered * inverse, inverse


def each_tile(rows, tile, step):
    def loop(m, carry):
        step(pl.multiple_of(m * tile, tile))
        return carry

    lax.fori_loop(0, rows // tile, loop, 0)


def norm_tiles(rows, base, affine, own, other, bias, gain, shift, unit_out, inv_out, low_out, at=0):
    def step(r):
        here = pl.ds(r, LEN)
        v = base[here].astype(F32)
        if affine is not None:
            v = v * affine[0] + affine[1]
        there = pl.ds(r + at, LEN)
        v = v + (own[there].astype(F32) + other[there].astype(F32)) + bias
        unit, inverse = stats(v)
        unit_out[here] = unit
        inv_out[here] = jnp.broadcast_to(inverse, (LEN, 128))
        low_out[here] = (unit * gain + shift).astype(BF)

    each_tile(rows, LEN, step)


def norm_forward(place, base, affine, own, other, vecs):
    rows = base.shape[0]

    def body(place, base, own, other, vecs, unit, inv, low):
        aff = (vecs[0:1], vecs[1:2]) if affine else None
        norm_tiles(LEN, base, aff, own, other, vecs[2:3], vecs[3:4], vecs[4:5], unit, inv, low)

    def tiles(array):
        return array, pl.BlockSpec((LEN, array.shape[1]), lambda t: (t, 0))

    def out(width, dtype):
        return jax.ShapeDtypeStruct((rows, width), dtype), pl.BlockSpec((LEN, width), lambda t: (t, 0))

    return run(
        body,
        rows // LEN,
        [small(place), tiles(base), tiles(own), tiles(other), full(vecs)],
        [out(D, F32), out(128, F32), out(D, BF)],
        us=4,
    )


ROOT_HALF = math.sqrt(0.5)
ROOT_TWO_PI = math.sqrt(0.5 / math.pi)
TAIL = (0.254829592, -0.284496736, 1.421413741, -1.453152027, 1.061405429)


def gelu_pair(u):
    depth = 1.0 + (0.3275911 * ROOT_HALF) * jnp.abs(u)
    t = pl.reciprocal(depth, approx=True)
    t = t * (2.0 - depth * t)
    bell = jnp.exp(-0.5 * u * u)
    poly = TAIL[4]
    for c in TAIL[3::-1]:
        poly = poly * t + c
    tail = (0.5 * t) * poly * bell
    phi = jnp.where(u < 0.0, tail, 1.0 - tail)
    return u * phi, phi + u * (bell * ROOT_TWO_PI)


def ffn_forward(place, low, hidden_bias, up_pieces, down_pieces):
    rows = low.shape[0]
    hidden = hidden_bias.shape[1]
    ups = hidden // WIDE
    tile = 128

    def body(place, low, hb, *refs):
        wu, wd = refs[:PIECES], refs[PIECES : 2 * PIECES]
        g, gp, part, scr_u, scr_d, acts = refs[2 * PIECES :]
        t = pl.program_id(0)

        @pl.when(t < ups)
        def _():
            assemble(wu, scr_u, place)
            w = matrix_of(scr_u)

            for r in range(0, rows, tile):
                here = slice(r, r + tile)
                a, b = gelu_pair(dot(low[here], w) + hb[...])
                a = a.astype(BF)
                g[here] = a
                acts[here, pl.ds(t * WIDE, WIDE)] = a
                gp[here] = b.astype(BF)

        @pl.when(t >= ups)
        def _():
            assemble(wd, scr_d, place)
            part[...] = dot(acts[...], matrix_of(scr_d)).astype(BF)

    up = lambda t: jnp.minimum(t, ups - 1)
    down = lambda t: jnp.maximum(t - ups, 0)
    return run(
        body,
        ups + 2,
        [small(place), full(low), in_cols(hidden_bias, up)]
        + blocks(up_pieces, 64, up)
        + wide_blocks(down_pieces, down),
        [
            out_cols(rows, hidden, BF, up),
            out_cols(rows, hidden, BF, up),
            out_cols(rows, D, BF, down),
        ],
        [weight_scratch(64), weight_scratch(128), pltpu.VMEM((rows, hidden), BF)],
        us=14 if rows > 256 else 8,
    )


def distance_buckets(reverse):
    row = lax.broadcasted_iota(jnp.int32, (128, 128), 0) & (BUCKETS - 1)
    lane = lax.broadcasted_iota(jnp.int32, (128, 128), 1)
    distance = ((lane + 1) if reverse else (128 - lane)) & 127
    bucket = jnp.zeros((128, 128), jnp.int32)
    for target in range(1, BUCKETS):
        at = 1
        while bucket_value(at, BUCKETS) < target:
            at += 1
        bucket = bucket + jnp.where(distance >= at, 1, 0)
    return jnp.where(bucket == row, 1.0, 0.0).astype(BF)


def skew(values):
    parts = [values[128 * n : 128 * n + 128] for n in range(values.shape[0] // 128)]
    return jnp.concatenate(
        [pltpu.roll(part, 0, 1, stride=1, stride_axis=0) for part in parts], axis=0
    )


def mirror():
    row = lax.broadcasted_iota(jnp.int32, (128, 128), 0)
    lane = lax.broadcasted_iota(jnp.int32, (128, 128), 1)
    return jnp.where(row + lane == 127, 1.0, 0.0).astype(BF)


def quarter_mask(h):
    lane = lax.broadcasted_iota(jnp.int32, (1, 128), 1)
    return jnp.where((lane >> 5) == h, 1.0, 0.0).astype(BF)


def ngram_probs(qm, prod, k0, rel_high, rel_low, table, count, h, first):
    mask = quarter_mask(h % 4)
    turned = dot(rel_high * mask, table) + dot(rel_low * mask, table)
    scores = dot_t(qm, k0) * SCALE + skew(turned)
    row = lax.broadcasted_iota(jnp.int32, scores.shape, 0)
    column = lax.broadcasted_iota(jnp.int32, scores.shape, 1)
    token = row & (LEN - 1)
    reach = jnp.where(row < LEN, token, token - 1)
    scores = jnp.where((column <= reach) & (column < count), scores, MASKED)
    own = jnp.sum(prod * first, axis=-1, keepdims=True) * SCALE + turned[:, 0:1]
    main = lax.broadcasted_iota(jnp.int32, own.shape, 0) < LEN
    own = jnp.where(main, 2.0 * MASKED, own)
    top = jnp.maximum(jnp.max(scores, axis=-1, keepdims=True), own)
    raised = jnp.exp(scores - top)
    own = jnp.exp(own - top)
    scale = 1.0 / (jnp.sum(raised, axis=-1, keepdims=True) + own)
    return raised * scale, own * scale


def split_high(values):
    high = values.astype(BF)
    return high, (values - high.astype(F32)).astype(BF)


def half_rows(rows):
    first = jnp.where(lax.broadcasted_iota(jnp.int32, (rows, 128), 1) < HEAD, 1.0, 0.0)
    return first, 1.0 - first


def ngram_attention(place, y, bias, rel_bias, pieces):
    rows = y.shape[0]
    span = STREAMS * LEN

    def body(place, y, bias, rbias, *refs):
        w, wr = refs[:PIECES], refs[PIECES : 2 * PIECES]
        qkv, rel, keep, send, scr, scr_r, heads, table = refs[2 * PIECES :]
        t = pl.program_id(0)

        @pl.when(t < 3)
        def _():
            assemble(w, scr, place)
            qkv[:, pl.ds(pl.multiple_of(t * WIDE, WIDE), WIDE)] = (
                dot(y[...], matrix_of(scr)) + bias[...]
            ).astype(BF)

        @pl.when(t == 3)
        def _():
            assemble_rel(wr, scr_r, place)
            rel[...] = dot(y[...], scr_r[...].reshape(D, REL_HALF)) + rbias[...]
            table[...] = distance_buckets(False)
            lanes = half_rows(span)

            def step(s, carry):
                r = pl.ds(pl.multiple_of(s * span, span), span)
                r0 = pl.ds(pl.multiple_of(s * span, span), LEN)
                count = place[5 + s]
                for j in range(4):
                    c = [slice(HALF * i + 128 * j, HALF * i + 128 * j + 128) for i in range(3)]
                    q, k, v = qkv[r, c[0]], qkv[r, c[1]], qkv[r, c[2]]
                    k0, v0 = qkv[r0, c[1]], qkv[r0, c[2]]
                    high, low = split_high(rel[r, 128 * (j // 2) : 128 * (j // 2) + 128])
                    prod = q.astype(F32) * k.astype(F32)
                    out = []
                    for i, mask in enumerate(head_masks()):
                        probs, own = ngram_probs(
                            q * mask, prod, k0, high, low, table[...], count, 2 * j + i, lanes[i]
                        )
                        own = own.astype(BF).astype(F32)
                        out.append(dot(probs.astype(BF), v0) + own * v.astype(F32))
                    heads[r, c[0]] = jnp.where(first_lanes(span), out[0], out[1]).astype(BF)
                return carry

            lax.fori_loop(0, 2, step, 0)
            split_parity(heads, place, keep, send)

    third = lambda t: jnp.minimum(t, 2)
    return run(
        body,
        4,
        [small(place), full(y), in_cols(bias, third), full(rel_bias)]
        + blocks(pieces, 64, third)
        + blocks(pieces, 32, lambda t: 8),
        [
            out_full((rows, 3 * HALF), BF),
            out_full((rows, REL_HALF), F32),
            out_full((rows, HALF // 2), BF),
            out_full((rows, HALF // 2), BF),
        ],
        [
            weight_scratch(64),
            pltpu.VMEM((4, 4, 2, 32, REL_HALF), BF),
            pltpu.VMEM((rows, HALF), BF),
            pltpu.VMEM((128, 128), BF),
        ],
        us=19,
    )


def assemble_rel(refs, scr, place):
    for i in range(4):
        block = refs[i][...]
        at = jnp.bitwise_xor(place[0], i)
        scr[at, :, 0] = block[:, :, :REL_HALF]
        scr[at, :, 1] = block[:, :, REL_HALF:]


def cross_forward(place, y, own, other, vecs, eunit, evecs, eown, eother, q_bias, kv_bias, pieces):
    rows, mem = y.shape[0], eunit.shape[0]
    span = STREAMS * LEN

    def body(place, y, own, other, vecs, eunit, evecs, eown, eother, qb, kvb, *refs):
        w = refs[:PIECES]
        unit, inv, low, eunit2, einv2, elow, q, kv, keep, send, scr, heads = refs[PIECES:]
        t = pl.program_id(0)
        assemble(w, scr, place)

        @pl.when(t == 0)
        def _():
            norm_tiles(
                rows, y, None, own, other, vecs[0:1], vecs[1:2], vecs[2:3], unit, inv, low
            )
            norm_tiles(
                mem,
                eunit,
                (evecs[0:1], evecs[1:2]),
                eown,
                eother,
                evecs[2:3],
                evecs[3:4],
                evecs[4:5],
                eunit2,
                einv2,
                elow,
            )
            q[...] = (dot(low[...], matrix_of(scr)) + qb[...]).astype(BF)

        @pl.when(t > 0)
        def _():
            at = pl.multiple_of((t - 1) * WIDE, WIDE)
            kv[:, pl.ds(at, WIDE)] = (dot(elow[...], matrix_of(scr)) + kvb[...]).astype(BF)

        @pl.when(t == 2)
        def _():
            for s in range(2):
                r = slice(s * span, s * span + span)
                m = slice(s * LEN, s * LEN + LEN)
                for j in range(4):
                    c = slice(128 * j, 128 * j + 128)
                    c2 = slice(HALF + 128 * j, HALF + 128 * j + 128)
                    heads[r, c] = attend(q[r, c], kv[m, c], kv[m, c2], place[3 + s])
            split_parity(heads, place, keep, send)

    return run(
        body,
        3,
        [small(place)]
        + [full(a) for a in (y, own, other, vecs, eunit, evecs, eown, eother, q_bias)]
        + [in_cols(kv_bias, lambda t: jnp.maximum(t - 1, 0))]
        + blocks(pieces, 64, lambda t: t),
        [
            out_full((rows, D), F32),
            out_full((rows, 128), F32),
            out_full((rows, D), BF),
            out_full((mem, D), F32),
            out_full((mem, 128), F32),
            out_full((mem, D), BF),
            out_full((rows, HALF), BF),
            out_full((mem, D), BF),
            out_full((rows, HALF // 2), BF),
            out_full((rows, HALF // 2), BF),
        ],
        [weight_scratch(64), pltpu.VMEM((rows, HALF), BF)],
        us=15,
    )


def fold(values):
    return jnp.sum(values.reshape(values.shape[0] // 8, 8, values.shape[1]), axis=0)


def norm_back_tile(total, unit, inverse, gain):
    scaled = total * gain
    one = jnp.mean(scaled, axis=-1, keepdims=True)
    two = jnp.mean(scaled * unit, axis=-1, keepdims=True)
    return inverse * (scaled - one - unit * two)


def norm_backward(place, final, total_ins, unit_ins, vecs):
    rows = total_ins[0].shape[0]
    n_total, n_unit = len(total_ins), len(unit_ins)
    steps = rows // LEN
    mine = steps // 2

    def body(place, vecs, *refs):
        tot, uni = refs[:n_total], refs[n_total : n_total + n_unit]
        *outs, gz, gf, s_gain, s_shift, s_gf, acc = refs[n_total + n_unit :]
        t = pl.program_id(0)

        @pl.when(t == 0)
        def _():
            acc[...] = jnp.zeros_like(acc)

        if final:
            v = uni[0][...] * vecs[0:1] + vecs[1:2]
            v = v + (uni[1][...].astype(F32) + uni[2][...].astype(F32)) + vecs[2:3]
            unit, inverse = stats(v)

            @pl.when((t >= mine) == (place[2] == 1))
            def _():
                outs[0][...] = (unit * vecs[3:4] + vecs[4:5]).astype(BF)

        else:
            unit, inverse = uni[0][...], uni[1][:, 0:1]
        total = tot[0][...].astype(F32)
        if n_total > 1:
            total = total + (tot[1][...].astype(F32) + tot[2][...].astype(F32))
        acc[0:8] += fold(total * unit)
        acc[8:16] += fold(total)
        back = norm_back_tile(total, unit, inverse, vecs[3:4])
        gz[...] = back
        low = back.astype(BF)
        gf[...] = low
        acc[16:24] += fold(low.astype(F32))

        @pl.when(t == steps - 1)
        def _():
            s_gain[...] = jnp.sum(acc[0:8], axis=0, keepdims=True)
            s_shift[...] = jnp.sum(acc[8:16], axis=0, keepdims=True)
            s_gf[...] = jnp.sum(acc[16:24], axis=0, keepdims=True)

    def tiles(array):
        skip = (array.shape[0] - rows) // LEN
        return array, pl.BlockSpec((LEN, array.shape[1]), lambda t: (t + skip, 0))

    def out(dtype):
        return jax.ShapeDtypeStruct((rows, D), dtype), pl.BlockSpec((LEN, D), lambda t: (t, 0))

    def own_tile(t, place):
        return (jnp.clip(t - mine * place[2], 0, mine - 1), 0)

    outs = [out(F32), out(BF)] + [out_full((1, D), F32)] * 3
    specs = [s for a, s in outs]
    shapes = [a for a, s in outs]
    ins = [full(vecs)] + [tiles(a) for a in total_ins + unit_ins]

    def with_place(spec):
        index = spec.index_map
        return pl.BlockSpec(
            spec.block_shape, lambda t, place: index(t), pipeline_mode=spec.pipeline_mode
        )

    specs = [with_place(s) for s in specs]
    if final:
        shapes = [jax.ShapeDtypeStruct((rows // 2, D), BF)] + shapes
        specs = [pl.BlockSpec((LEN, D), own_tile)] + specs
    return pl.pallas_call(
        body,
        grid_spec=pltpu.PrefetchScalarGridSpec(
            num_scalar_prefetch=1,
            grid=(steps,),
            in_specs=[with_place(s) for a, s in ins],
            out_specs=specs,
            scratch_shapes=[pltpu.VMEM((24, D), F32)],
        ),
        out_shape=shapes,
        compiler_params=pltpu.CompilerParams(vmem_limit_bytes=BUDGET),
        cost_estimate=pl.CostEstimate(
            flops=int(5 * FLOP_RATE), bytes_accessed=int(5 * HBM_RATE), transcendentals=0
        ),
    )(place, *[a for a, s in ins])


def ffn_back(place, gf, gp, up_pieces, down_pieces):
    rows, hidden = gp.shape
    ups = hidden // WIDE

    def body(place, gf, gp, *refs):
        wu, wd = refs[:PIECES], refs[PIECES : 2 * PIECES]
        gu, part, s_gu, scr_u, scr_d, all_u, scr_all_u = refs[2 * PIECES :]
        t = pl.program_id(0)

        @pl.when(t < 2)
        def _():
            assemble(wd, scr_d.at[t], place)

        @pl.when(t >= 2)
        def _():
            b = t - 2
            assemble(wu, scr_u, place)
            scr_all_u[:, pl.ds(pl.multiple_of(b * WIDE, WIDE), WIDE)] = matrix_of(scr_u)
            w0 = scr_d[0, b].reshape(WIDE, WIDE)
            w1 = scr_d[1, b].reshape(WIDE, WIDE)
            back = dot_t(gf[:, :WIDE], w0) + dot_t(gf[:, WIDE:], w1)
            low = (back * gp[...].astype(F32)).astype(BF)
            gu[...] = low
            all_u[:, pl.ds(pl.multiple_of(b * WIDE, WIDE), WIDE)] = low
            s_gu[...] = jnp.sum(fold(low.astype(F32)), axis=0, keepdims=True)

        @pl.when(t == ups + 1)
        def _():
            part[...] = dot_t(all_u[...], scr_all_u[...]).astype(BF)

    up = lambda t: jnp.maximum(t - 2, 0)
    down = lambda t: jnp.minimum(t, 1)
    return run(
        body,
        ups + 2,
        [small(place), full(gf), in_cols(gp, up)]
        + blocks(up_pieces, 64, up)
        + wide_blocks(down_pieces, down),
        [
            out_cols(rows, hidden, BF, up),
            out_full((rows, D), BF),
            out_cols(1, hidden, F32, up),
        ],
        [
            weight_scratch(64),
            pltpu.VMEM((2, 4, 4, 128, WIDE), BF),
            pltpu.VMEM((rows, hidden), BF),
            pltpu.VMEM((D, hidden), BF),
        ],
        us=14 if rows > 256 else 8,
    )


def branch_back(place, resid, own, other, unit, inv, gain, pieces):
    rows = resid.shape[0]

    def body(place, resid, own, other, unit, inv, gain, *refs):
        w = refs[:PIECES]
        gz, gx, keep, send, s_gain, s_shift, s_gx, scr, total_out, acc = refs[PIECES:]
        t = pl.program_id(0)
        assemble(w, scr, place)

        @pl.when(t == 0)
        def _():
            acc[...] = jnp.zeros_like(acc)

            def step(r):
                here = pl.ds(r, LEN)
                total = resid[here] + (own[here].astype(F32) + other[here].astype(F32))
                acc[0:8] += fold(total * unit[here])
                acc[8:16] += fold(total)
                back = norm_back_tile(total, unit[here], inv[here, 0:1], gain[...])
                gz[here] = back
                low = back.astype(BF)
                gx[here] = low
                acc[16:24] += fold(low.astype(F32))

            each_tile(rows, LEN, step)
            s_gain[...] = jnp.sum(acc[0:8], axis=0, keepdims=True)
            s_shift[...] = jnp.sum(acc[8:16], axis=0, keepdims=True)
            s_gx[...] = jnp.sum(acc[16:24], axis=0, keepdims=True)
            total_out[...] = dot_t(gx[:, :WIDE], matrix_of(scr))

        @pl.when(t == 1)
        def _():
            total_out[...] += dot_t(gx[:, WIDE:], matrix_of(scr))
            core = place[2]
            quarter = HALF // 2
            keep[...] = total_out[:, pl.ds(pl.multiple_of(quarter * core, 128), quarter)].astype(BF)
            send[...] = total_out[
                :, pl.ds(pl.multiple_of(quarter * (1 - core), 128), quarter)
            ].astype(BF)

    return run(
        body,
        2,
        [small(place)]
        + [full(a) for a in (resid, own, other, unit, inv, gain)]
        + blocks(pieces, 32, lambda t: 6 + t),
        [
            out_full((rows, D), F32),
            out_full((rows, D), BF),
            out_full((rows, HALF // 2), BF),
            out_full((rows, HALF // 2), BF),
            out_full((1, D), F32),
            out_full((1, D), F32),
            out_full((1, D), F32),
        ],
        [weight_scratch(32), pltpu.VMEM((rows, HALF), F32), pltpu.VMEM((24, D), F32)],
        us=10 if rows > 256 else 5,
    )


def column_sums(out, values):
    out[...] = jnp.sum(fold(values.astype(F32)), axis=0, keepdims=True)


def cross_back(place, q, kv, keep, got, pieces):
    rows, mem = q.shape[0], kv.shape[0]
    span = STREAMS * LEN

    def body(place, q, kv, keep, got, *refs):
        w = refs[:PIECES]
        gq, gkv, part, s_gq, s_gkv, scr, g, acc = refs[PIECES:]
        t = pl.program_id(0)
        assemble(w, scr, place)

        @pl.when(t == 0)
        def _():
            join_parity(keep, got, place, g)
            for s in range(2):
                r = slice(s * span, s * span + span)
                m = slice(s * LEN, s * LEN + LEN)
                for j in range(4):
                    c = slice(128 * j, 128 * j + 128)
                    c2 = slice(HALF + 128 * j, HALF + 128 * j + 128)
                    gq[r, c], gkv[m, c], gkv[m, c2] = attend_back(
                        q[r, c], kv[m, c], kv[m, c2], g[r, c], place[3 + s]
                    )
            column_sums(s_gq, gq[...])
            column_sums(s_gkv, gkv[...])
            part[:rows] = dot_t(gq[...], matrix_of(scr)).astype(BF)

        @pl.when(t == 1)
        def _():
            acc[...] = dot_t(gkv[:, :HALF], matrix_of(scr))

        @pl.when(t == 2)
        def _():
            part[rows:] = (acc[...] + dot_t(gkv[:, HALF:], matrix_of(scr))).astype(BF)

    return run(
        body,
        3,
        [small(place), full(q), full(kv), full(keep), full(got)]
        + blocks(pieces, 64, lambda t: t),
        [
            out_full((rows, HALF), BF),
            out_full((mem, D), BF),
            out_full((rows + mem, D), BF),
            out_full((1, HALF), F32),
            out_full((1, D), F32),
        ],
        [weight_scratch(64), pltpu.VMEM((rows, HALF), BF), pltpu.VMEM((mem, D), F32)],
        us=14,
    )


def input_grads(place, gz, parts, keep, send):
    rows = gz.shape[0] // 2
    core = place[2]
    here = pl.ds(pl.multiple_of(rows * core, LEN), rows)
    there = pl.ds(pl.multiple_of(rows * (1 - core), LEN), rows)
    total = gz[here]
    for g, w in parts:
        total = total + dot_t(g[here], w)
    keep[...] = total
    total = 0.0
    for g, w in parts:
        total = total + dot_t(g[there], w)
    send[...] = total.astype(BF)


def enc_attention_back(place, qkv, keep, got, gz, pieces):
    rows = qkv.shape[0]

    def body(place, qkv, keep, got, gz, *refs):
        w = refs[:PIECES]
        gqkv, out, send, sums, scr, g, win = refs[PIECES:]
        t = pl.program_id(0)
        assemble(w, scr, place)
        win[:, pl.ds(pl.multiple_of(t * WIDE, WIDE), WIDE)] = matrix_of(scr)

        @pl.when(t == 0)
        def _():
            join_parity(keep, got, place, g)
            for s in range(2):
                r = slice(s * LEN, s * LEN + LEN)
                for j in range(4):
                    c = [slice(HALF * i + 128 * j, HALF * i + 128 * j + 128) for i in range(3)]
                    gqkv[r, c[0]], gqkv[r, c[1]], gqkv[r, c[2]] = attend_back(
                        qkv[r, c[0]], qkv[r, c[1]], qkv[r, c[2]], g[r, c[0]], place[3 + s]
                    )
            column_sums(sums, gqkv[...])

        @pl.when(t == 2)
        def _():
            input_grads(place, gz, [(gqkv, win[...])], out, send)

    return run(
        body,
        3,
        [small(place), full(qkv), full(keep), full(got), full(gz)]
        + blocks(pieces, 64, lambda t: t),
        [
            out_full((rows, 3 * HALF), BF),
            out_full((rows // 2, D), F32),
            out_full((rows // 2, D), BF),
            out_full((1, 3 * HALF), F32),
        ],
        [weight_scratch(64), pltpu.VMEM((rows, HALF), BF), pltpu.VMEM((D, 3 * HALF), BF)],
        us=13,
    )


def ngram_back_kernel(place, qkv, rel, keep, got, gz, pieces):
    rows = qkv.shape[0]
    span = STREAMS * LEN

    def body(place, qkv, rel, keep, got, gz, *refs):
        w, wr = refs[:PIECES], refs[PIECES : 2 * PIECES]
        gqkv, grel, out, send, sums, s_rel, scr, scr_r, g, win, *tables = refs[2 * PIECES :]
        table, table_back, flip = tables
        t = pl.program_id(0)

        @pl.when(t < 3)
        def _():
            assemble(w, scr, place)
            win[:, pl.ds(pl.multiple_of(t * WIDE, WIDE), WIDE)] = matrix_of(scr)

        @pl.when(t == 0)
        def _():
            join_parity(keep, got, place, g)
            table[...] = distance_buckets(False)
            table_back[...] = distance_buckets(True)
            flip[...] = mirror()
            lanes = half_rows(span)

            def step(s, carry):
                r = pl.ds(pl.multiple_of(s * span, span), span)
                r0 = pl.ds(pl.multiple_of(s * span, span), LEN)
                r1 = pl.ds(pl.multiple_of(s * span + LEN, LEN), span - LEN)
                count = place[5 + s]
                for j in range(4):
                    c = [slice(HALF * i + 128 * j, HALF * i + 128 * j + 128) for i in range(3)]
                    q, k, v = qkv[r, c[0]], qkv[r, c[1]], qkv[r, c[2]]
                    k0, v0 = qkv[r0, c[1]], qkv[r0, c[2]]
                    go = g[r, c[0]]
                    high, low = split_high(rel[r, 128 * (j // 2) : 128 * (j // 2) + 128])
                    prod = q.astype(F32) * k.astype(F32)
                    prod_g = go.astype(F32) * v.astype(F32)
                    gq, gk0, gv0, p_own, d_own, turned = [], 0.0, 0.0, [], [], []
                    for i, mask in enumerate(head_masks()):
                        qm, gm = q * mask, go * mask
                        h = 2 * j + i
                        probs, own = ngram_probs(
                            qm, prod, k0, high, low, table[...], count, h, lanes[i]
                        )
                        gp = dot_t(gm, v0)
                        g_own = jnp.sum(prod_g * lanes[i], axis=-1, keepdims=True)
                        inner = jnp.sum(probs * gp, axis=-1, keepdims=True) + own * g_own
                        ds = (probs * (gp - inner)).astype(BF)
                        ds_own = (own * (g_own - inner)).astype(BF).astype(F32)
                        gq.append(dot(ds, k0))
                        gk0 = gk0 + dot_g(ds, qm)
                        gv0 = gv0 + dot_g(probs.astype(BF), gm)
                        p_own.append(own.astype(BF).astype(F32))
                        d_own.append(ds_own)
                        back = skew(dot(ds, flip[...]))
                        lane = lax.broadcasted_iota(jnp.int32, back.shape, 1)
                        main = lax.broadcasted_iota(jnp.int32, back.shape, 0) < LEN
                        back = jnp.where((lane == 127) & jnp.logical_not(main), ds_own, back)
                        grads = dot_t(back.astype(BF), table_back[...])
                        turned.append(grads * quarter_mask(h % 4).astype(F32))
                    first = first_lanes(span)
                    d_own = jnp.where(first, d_own[0], d_own[1])
                    p_own = jnp.where(first, p_own[0], p_own[1])
                    gqf = jnp.where(first, gq[0], gq[1]) + d_own * k.astype(F32)
                    gqkv[r, c[0]] = (gqf * SCALE).astype(BF)
                    gkn = d_own * q.astype(F32) * SCALE
                    gvn = p_own * go.astype(F32)
                    gqkv[r0, c[1]] = (gk0 * SCALE).astype(BF)
                    gqkv[r0, c[2]] = gv0.astype(BF)
                    gqkv[r1, c[1]] = gkn[LEN:].astype(BF)
                    gqkv[r1, c[2]] = gvn[LEN:].astype(BF)
                    both = turned[0] + turned[1]
                    at = slice(128 * (j // 2), 128 * (j // 2) + 128)
                    if j % 2 == 0:
                        held = both
                    else:
                        grel[r, at] = (held + both).astype(BF)
                return carry

            lax.fori_loop(0, 2, step, 0)
            column_sums(sums, gqkv[...])
            column_sums(s_rel, grel[...])

        @pl.when(t == 3)
        def _():
            assemble_rel(wr, scr_r, place)
            wrel = scr_r[...].reshape(D, REL_HALF)
            input_grads(place, gz, [(gqkv, win[...]), (grel, wrel)], out, send)

    third = lambda t: jnp.minimum(t, 2)
    return run(
        body,
        4,
        [small(place), full(qkv), full(rel), full(keep), full(got), full(gz)]
        + blocks(pieces, 64, third)
        + blocks(pieces, 32, lambda t: 8),
        [
            out_full((rows, 3 * HALF), BF),
            out_full((rows, REL_HALF), BF),
            out_full((rows // 2, D), F32),
            out_full((rows // 2, D), BF),
            out_full((1, 3 * HALF), F32),
            out_full((1, REL_HALF), F32),
        ],
        [
            weight_scratch(64),
            pltpu.VMEM((4, 4, 2, 32, REL_HALF), BF),
            pltpu.VMEM((rows, HALF), BF),
            pltpu.VMEM((D, 3 * HALF), BF),
        ]
        + [pltpu.VMEM((128, 128), BF)] * 3,
        us=29,
    )


def grad_chunk(place, arrays, terms, total_rows, width=WIDE):
    n = len(arrays)

    def body(place, *refs):
        ins, outs, scr = refs[:n], refs[n : n + 4], refs[n + 4]
        t = pl.program_id(0)
        dp, core = place[0], place[2]

        def spread(value, at, rows, lanes=slice(0, WIDE)):
            v = value.astype(BF).reshape(4, 4, rows, WIDE)
            scr[:, :, :rows] = v
            for i in range(4):
                outs[i][:, at : at + rows, lanes] = scr[jnp.bitwise_xor(dp, i), :, :rows]

        for index, (kind, at, x, g, col) in enumerate(terms):

            @pl.when(t == index)
            def _(kind=kind, at=at, x=x, g=g, col=col):
                if kind == "whole":
                    spread(ins[x][...], at, ins[x].shape[0] // 16)
                    return
                if kind == "heads":
                    right = ins[g][:, col : col + WIDE]
                    mine, theirs = ins[x][...], ins[x + 1][...]
                    keep, got = dot_g(mine, right), dot_g(theirs, right)
                    quarter = (2, 4, 32, WIDE)
                    scr[pl.ds(2 * core, 2), :, :32] = keep.astype(BF).reshape(quarter)
                    scr[pl.ds(2 - 2 * core, 2), :, :32] = got.astype(BF).reshape(quarter)
                    spread(scr[:, :, :32], at, 32)
                    return
                if kind == "rel":
                    v = dot_g(ins[x][...], ins[g][...]).astype(BF).reshape(16, 2, 32, REL_HALF)
                    spread(jnp.concatenate([v[:, 0], v[:, 1]], axis=-1), at, 32)
                    return
                value = dot_g(ins[x][...], ins[g][:, col : col + WIDE])
                lanes = slice(col, col + WIDE) if kind == "rows" else slice(0, WIDE)
                spread(value, at, value.shape[0] // 16, lanes)

    return run(
        body,
        len(terms),
        [small(place)] + [full(a) for a in arrays],
        [out_full((4, total_rows, width), BF)] * 4,
        [weight_scratch(128)],
        us=10,
    )


def vec_chunk(place, pieces):
    def body(place, *refs):
        assemble(refs[:PIECES], refs[PIECES], place)

    return run(
        body,
        1,
        [small(place)] + blocks(pieces, 16, lambda t: 18),
        [out_full((4, 4, 16, WIDE), BF)],
        us=2,
    )[0]


class Order:

    def __init__(self, place):
        self.place = place
        self.last = None

    def after(self, *values):
        if self.last is not None:
            values = (self.last,) + values
        self.place = tie(self.place, *values)
        self.last = None

    def run(self, kernel, *args):
        if self.last is not None:
            self.place = tie(self.place, self.last)
        out = kernel(self.place, *args)
        self.last = out[0] if isinstance(out, (list, tuple)) else out
        return out

    def matmul(self, left, right):
        if self.last is not None:
            right = tie(right, self.last)
        self.last = dot_g(left, right).astype(BF)
        return self.last

    def add(self, first, *others, dtype=BF):
        if self.last is not None:
            first = tie(first, self.last)
        self.last = sum((v.astype(F32) for v in others), first.astype(F32)).astype(dtype)
        return self.last


class Links:

    def __init__(self, lay, before):
        self.lay = lay
        self.gathered = []
        self.first = []
        self.before = before
        self.second = []
        self.far = 2
        self.groups = [list(range(core, lay.nf, 2)) for core in range(2)]

    def turn(self):
        self.far = 3 - self.far
        return self.far

    def gather(self, buf, direct=False):
        far = 3 if direct else self.turn()
        if len(self.gathered) >= 2:
            buf = tie(buf, self.gathered[-2])
        own = lax.all_gather(buf, "fsdp", axis=0, axis_index_groups=self.groups)
        self.gathered.append(own)
        ready = tie(own, *(self.first[-1] if self.first else self.before))
        if len(self.second) >= 3:
            ready = tie(ready, self.second[-3])
        x, y = self.lay.flip_dp(ready, 1), self.lay.flip_dp(ready, 2)
        self.first.append((x, y))
        if direct:
            d = self.lay.flip_dp(ready, 3)
        else:
            d = self.lay.flip_dp(x, 2) if far == 2 else self.lay.flip_dp(y, 1)
        self.second.append(d)
        return [own, x, y, d]

    def scatter_whole(self, value):
        lay = self.lay
        groups = [
            [dp * lay.nf + fs for dp in range(lay.ndp) for fs in range(core, lay.nf, 2)]
            for core in range(2)
        ]
        return lax.psum_scatter(
            value, ("dp", "fsdp"), scatter_dimension=0, tiled=True, axis_index_groups=groups
        ).astype(F32)

    def scatter(self, order, parts, direct=False):
        own, x, y, d = parts
        if direct:
            moved = [self.lay.flip_dp(part, i + 1) for i, part in enumerate((x, y, d))]
            yield
            yield
            total = order.add(own, *moved)
        else:
            far = self.turn()
            d = self.lay.flip_dp(d, far)
            if far == 2:
                y = self.lay.flip_dp(y, 2)
                yield
                x = self.lay.flip_dp(order.add(x, d), 1)
            else:
                x = self.lay.flip_dp(x, 1)
                yield
                y = self.lay.flip_dp(order.add(y, d), 2)
            yield
            total = order.add(own, x, y)
        yield lax.psum_scatter(
            total, "fsdp", scatter_dimension=0, axis_index_groups=self.groups
        ).astype(F32)


def shards_fast(
    ndp,
    nf,
    source,
    dec_in,
    src_lengths,
    tgt_lengths,
    enc_in_proj,
    enc_out_proj,
    enc_ffn_in,
    enc_ffn_out,
    enc_gains,
    enc_biases,
    dec_in_proj,
    dec_rel_proj,
    dec_out_proj,
    cross_query,
    cross_kv,
    cross_out,
    dec_ffn_in,
    dec_ffn_out,
    dec_gains,
    dec_biases,
    enc_cot,
    dec_cot,
):
    lay = Layout(ndp, nf)
    lay.place()
    r, f, chips = lay.r, lay.f, lay.chips
    swap, pick, pair = lay.swap, lay.pick, lay.pair
    core = lay.core
    dec_rows = STREAMS * LEN

    def halves(matrix, groups, width):
        parts = matrix.reshape(r, groups, 2, width)
        return (
            pick(parts[:, :, 0], parts[:, :, 1]).reshape(r, groups * width),
            pick(parts[:, :, 1], parts[:, :, 0]).reshape(r, groups * width),
        )

    split = [
        halves(enc_in_proj, 3, HALF),
        halves(enc_ffn_in, chips, f),
        halves(dec_in_proj, 3, HALF),
        halves(cross_query, 1, HALF),
        halves(cross_kv, 2, HALF),
        halves(dec_ffn_in, chips, f),
        halves(dec_rel_proj, 1, REL_HALF),
    ]
    vec = jnp.concatenate(
        [
            enc_biases,
            enc_gains,
            dec_biases,
            dec_gains,
            src_lengths.astype(BF),
            tgt_lengths.astype(BF),
        ]
    )
    nvec = vec.shape[0]
    padded = -(-nvec // WIDE) * WIDE
    vec = jnp.pad(vec, (0, padded - nvec))
    mine = jnp.concatenate([own for own, other in split], axis=1)
    theirs = jnp.concatenate([other for own, other in split], axis=1)
    theirs_got = swap(theirs)
    vec_got = swap(vec)
    source_got = swap(source)
    dec_own = dec_in.transpose(1, 0, 2).reshape(dec_rows, D)
    dec_got = swap(dec_own)
    dcot_own = dec_cot.transpose(1, 0, 2).reshape(dec_rows, D)
    dcot_got = swap(dcot_own)
    ecot_got = swap(enc_cot)
    links = Links(lay, (theirs_got, vec_got, source_got, dec_got, dcot_got, ecot_got))
    w = {"dec_down": links.gather(dec_ffn_out), "enc_down": links.gather(enc_ffn_out)}

    def column_blocks(start, count):
        return [
            pair(
                mine[:, start + WIDE * i : start + WIDE * i + WIDE],
                theirs_got[:, start + WIDE * i : start + WIDE * i + WIDE],
                0,
            )
            for i in range(count)
        ]

    def row_blocks(matrix):
        return [matrix[:, :WIDE], matrix[:, WIDE:]]

    rel_start = mine.shape[1] - REL_HALF
    rel_block = pair(mine[:, rel_start:], theirs_got[:, rel_start:], 1)
    vec_pair = pair(vec[None], vec_got[None], 0)
    vec_used = 2 * padded // WIDE
    vec_block = jnp.pad(vec_pair.reshape(vec_used, WIDE), ((0, 16 - vec_used), (0, 0)))
    at = [0, 3 * WIDE, 7 * WIDE, 10 * WIDE, 11 * WIDE, 13 * WIDE]
    chunk_parts = {
        "enc": column_blocks(at[0], 3) + row_blocks(enc_out_proj),
        "enc_up": column_blocks(at[1], 4),
        "dec": column_blocks(at[2], 3) + row_blocks(dec_out_proj) + [rel_block, vec_block],
        "cross": column_blocks(at[3], 1) + column_blocks(at[4], 2) + row_blocks(cross_out),
        "dec_up": column_blocks(at[5], 4),
    }
    for name in ("dec", "enc", "enc_up", "cross", "dec_up"):
        w[name] = links.gather(jnp.concatenate(chunk_parts[name], axis=0))

    lens = vec_pair[:, nvec - 2 : nvec].T.reshape(-1).astype(F32).astype(jnp.int32)
    place = jnp.concatenate(
        [jnp.stack([lay.dp, lay.z, core]).astype(jnp.int32), lens, jnp.zeros((1,), jnp.int32)]
    )

    order = Order(place)
    vec_all = order.run(vec_chunk, w["dec"]).reshape(chips, 16, WIDE)[:, :vec_used]
    vec_all = vec_all.reshape(lay.devices, padded).astype(F32)
    widths = [enc_biases.shape[0], enc_gains.shape[0], dec_biases.shape[0], dec_gains.shape[0]]
    starts = [0]
    for width in widths:
        starts.append(starts[-1] + width)
    v_enc_b, v_enc_g, v_dec_b, v_dec_g = [
        vec_all[:, starts[i] : starts[i + 1]].reshape(-1) for i in range(4)
    ]
    eb, eg_rows = v_enc_b.reshape(-1, D), v_enc_g.reshape(2, D)
    dg_rows = v_dec_g.reshape(3, D)
    d_split = 2 * D + HEADS * BUCKETS
    db = v_dec_b[d_split:].reshape(-1, D)

    def half_of(vector):
        parts = vector.reshape(2, -1)
        return pick(parts[0], parts[1])

    def hidden_of(vector):
        parts = vector.reshape(chips, 2, f)
        return pick(parts[:, 0], parts[:, 1]).reshape(1, -1)

    zero_half = jnp.zeros((HALF,), F32)

    def qkv_bias(q, v):
        return jnp.concatenate([half_of(q), zero_half, half_of(v)])[None]

    def rows_of(*vectors):
        return jnp.stack(vectors)

    x = pair(source, source_got, 0)
    y = pair(dec_own, dec_got, 0)
    dcot = pair(dcot_own, dcot_got, 0)
    ecot = pair(enc_cot, ecot_got, 0)
    order.after(x, y, dcot, ecot)
    order.after(links.gathered[5], *links.first[3], links.second[1])
    dqkv, rel, da_keep, da_send = order.run(
        ngram_attention,
        y,
        qkv_bias(v_dec_b[:D], v_dec_b[D : 2 * D]),
        half_of(v_dec_b[2 * D : d_split])[None],
        w["dec"],
    )
    da_got = swap(da_send)
    order.after(links.gathered[6], *links.first[4])
    eqkv, ea_keep, ea_send = order.run(enc_attention, x, qkv_bias(eb[0], eb[1]), w["enc"])
    ea_got = swap(ea_send)
    order.after(*links.first[5])
    p3 = order.run(out_projection, da_keep, da_got, w["dec"])
    p3_got = swap(p3)
    p1 = order.run(out_projection, ea_keep, ea_got, w["enc"])
    p1_got = swap(p1)
    eunit1, einv1, eh1_low = order.run(
        norm_forward,
        x,
        False,
        p1,
        p1_got,
        rows_of(eb[2], eb[2], eb[2], eg_rows[0], eb[8]),
    )
    order.after(links.second[5], *links.first[6])
    eg, egp, p2 = order.run(
        ffn_forward, eh1_low, hidden_of(eb[3:7]), w["enc_up"], w["enc_down"]
    )
    p2_got = swap(p2)
    order.after(links.second[6])
    dunit1, dinv1, dh1_low, eunit2, einv2, enc_low, cq, ckv, ca_keep, ca_send = order.run(
        cross_forward,
        y,
        p3,
        p3_got,
        rows_of(db[0], dg_rows[0], db[9]),
        eunit1,
        rows_of(eg_rows[0], eb[8], eb[7], eg_rows[1], eb[9]),
        p2,
        p2_got,
        half_of(db[1])[None],
        jnp.concatenate([zero_half, half_of(db[2])])[None],
        w["cross"],
    )
    ca_got = swap(ca_send)
    p4 = order.run(out_projection, ca_keep, ca_got, w["cross"])
    p4_got = swap(p4)
    dunit2, dinv2, dh2_low = order.run(
        norm_forward,
        dunit1,
        True,
        p4,
        p4_got,
        rows_of(dg_rows[0], db[9], db[3], dg_rows[1], db[10]),
    )
    dg, dgp, p5 = order.run(
        ffn_forward, dh2_low, hidden_of(db[4:8]), w["dec_up"], w["dec_down"]
    )
    p5_got = swap(p5)

    up_terms = [("plain", 64 * b, 0, 1, WIDE * b) for b in range(4)]
    down_terms = [("rows", 0, 0, 1, WIDE * h) for h in range(2)]

    def grads(*args):
        scatter = links.scatter(order, order.run(grad_chunk, *args))
        next(scatter)
        return scatter

    dec_out, gz3, gf, s_gain3, s_shift3, s_gf = order.run(
        norm_backward,
        True,
        [dcot],
        [dunit2, p5, p5_got],
        rows_of(dg_rows[1], db[10], db[8], dg_rows[2], db[11]),
    )
    r_dd = grads([dg, gf], down_terms, 128, D)
    gu, p6, s_gu = order.run(ffn_back, gf, dgp, w["dec_up"], w["dec_down"])
    p6_got = swap(p6)
    r_du = grads([dh2_low, gu], up_terms, 256)
    gz2, gx, gca_keep, gca_send, s_gain2, s_shift2, s_gx = order.run(
        branch_back, gz3, p6, p6_got, dunit2, dinv2, dg_rows[1:2], w["cross"]
    )
    gca_got = swap(gca_send)
    next(r_dd)
    next(r_du)
    gcq, gckv, p7, s_gcq, s_gckv = order.run(
        cross_back, cq, ckv, gca_keep, gca_got, w["cross"]
    )
    p7_got = swap(p7)
    r_cross = grads(
        [dh1_low, gcq, enc_low, gckv, ca_keep, ca_got, gx],
        [
            ("plain", 0, 0, 1, 0),
            ("plain", 64, 2, 3, 0),
            ("plain", 128, 2, 3, WIDE),
            ("heads", 192, 4, 6, 0),
            ("heads", 224, 4, 6, WIDE),
        ],
        256,
    )
    gz1, go, gda_keep, gda_send, s_gain1, s_shift1, s_go = order.run(
        branch_back, gz2, p7, p7_got, dunit1, dinv1, dg_rows[0:1], w["dec"]
    )
    gda_got = swap(gda_send)
    gz2e, gfe, e_gain2, e_shift2, s_gfe = order.run(
        norm_backward, False, [ecot, p7, p7_got], [eunit2, einv2], rows_of(*([eg_rows[1]] * 5))
    )
    gue, p9, s_gue = order.run(ffn_back, gfe, egp, w["enc_up"], w["enc_down"])
    p9_got = swap(p9)
    r_ed = grads([eg, gfe], down_terms, 128, D)
    r_eu = grads([eh1_low, gue], up_terms, 256)
    total_dd = next(r_dd)
    next(r_cross)
    total_du = next(r_du)
    gz1e, goe, gea_keep, gea_send, e_gain1, e_shift1, s_goe = order.run(
        branch_back, gz2e, p9, p9_got, eunit1, einv1, eg_rows[0:1], w["enc"]
    )
    gea_got = swap(gea_send)
    gqkv, grel, p8, p8_send, s_gqkv, s_grel = order.run(
        ngram_back_kernel, dqkv, rel, gda_keep, gda_got, gz1, w["dec"]
    )
    p8_got = swap(p8_send)
    next(r_ed)
    next(r_eu)
    total_cross = next(r_cross)
    geqkv, p10, p10_send, s_geqkv = order.run(
        enc_attention_back, eqkv, gea_keep, gea_got, gz1e, w["enc"]
    )
    p10_got = swap(p10_send)
    g_dec_in = order.add(p8, p8_got, dtype=F32)
    r_dec = grads(
        [y, gqkv, da_keep, da_got, go, grel],
        [("plain", 64 * b, 0, 1, WIDE * b) for b in range(3)]
        + [("heads", 192, 2, 4, 0), ("heads", 224, 2, 4, WIDE), ("rel", 256, 0, 5, 0)],
        288,
    )
    g_source = order.add(p10, p10_got, dtype=F32)
    total_ed = next(r_ed)
    total_eu = next(r_eu)

    def widen(vector):
        zeros = jnp.zeros_like(vector)
        return pick(jnp.concatenate([vector, zeros]), jnp.concatenate([zeros, vector]))

    def widen_hidden(vector):
        parts = vector.reshape(chips, 1, f)
        zeros = jnp.zeros_like(parts)
        return pick(
            jnp.concatenate([parts, zeros], axis=1), jnp.concatenate([zeros, parts], axis=1)
        ).reshape(-1)

    def owned(*vectors):
        return jnp.concatenate(vectors).reshape(lay.devices, -1)

    vec_grads = jnp.concatenate(
        [
            owned(
                widen(s_geqkv[0, :HALF]),
                widen(s_geqkv[0, 2 * HALF :]),
                0.5 * s_goe[0],
                widen_hidden(s_gue),
                0.5 * s_gfe[0],
                0.5 * e_shift1[0],
                0.5 * e_shift2[0],
            ),
            owned(0.5 * e_gain1[0], 0.5 * e_gain2[0]),
            owned(
                widen(s_gqkv[0, :HALF]),
                widen(s_gqkv[0, 2 * HALF :]),
                widen(s_grel[0]),
                0.5 * s_go[0],
                widen(s_gcq[0]),
                widen(s_gckv[0, HALF:]),
                0.5 * s_gx[0],
                widen_hidden(s_gu),
                0.5 * s_gf[0],
                0.5 * s_shift1[0],
                0.5 * s_shift2[0],
                0.5 * s_shift3[0],
            ),
            owned(0.5 * s_gain1[0], 0.5 * s_gain2[0], 0.5 * s_gain3[0]),
        ],
        axis=1,
    ).astype(BF)
    vec_width = vec_grads.shape[1]
    vec_grads = jnp.pad(vec_grads, ((0, 0), (0, padded - vec_width)))
    vec_grads = vec_grads.reshape(chips, vec_used, WIDE)
    vec_grads = jnp.pad(vec_grads, ((0, 0), (0, 16 - vec_used), (0, 0))).reshape(chips * 16, WIDE)
    r_enc = grads(
        [x, geqkv, ea_keep, ea_got, goe, vec_grads],
        [("plain", 64 * b, 0, 1, WIDE * b) for b in range(3)]
        + [("heads", 192, 2, 4, 0), ("heads", 224, 2, 4, WIDE), ("whole", 256, 5, 5, 0)],
        272,
    )
    next(r_dec)
    next(r_enc)
    total2 = next(r_dec)
    total0 = next(r_enc)

    def split_rows(total, sizes):
        at = 0
        result = []
        for size in sizes:
            result.append(total[at : at + size])
            at += size
        return result

    def own_rows_of(total, count):
        rows = total.reshape(count, 2, r, WIDE)
        keep = pick(rows[:, 0], rows[:, 1])
        got = swap(pick(rows[:, 1], rows[:, 0]))
        return pair(keep[:, None], got[:, None], 1)

    def in_rows(rows):
        return rows.transpose(2, 0, 1, 3).reshape(r, -1)

    def up_rows(rows):
        per = WIDE // f
        return rows.reshape(4, 2, r, per, f).transpose(2, 0, 3, 1, 4).reshape(r, FF)

    def side(low, high):
        return jnp.concatenate([low, high], axis=1)

    t0 = split_rows(total0, [6 * r, r, r, 16])
    o_enc_in, o_enc_out = in_rows(own_rows_of(t0[0], 3)), side(t0[1], t0[2])
    vec_sum = t0[3][:vec_used].reshape(2, padded)
    vec_sum = pick(vec_sum[0], vec_sum[1]) + swap(pick(vec_sum[1], vec_sum[0]))
    o_vec = [vec_sum[starts[i] : starts[i + 1]] for i in range(4)]
    o_enc_up = up_rows(own_rows_of(total_eu, 4))
    o_enc_down = total_ed
    t2 = split_rows(total2, [6 * r, r, r, r])
    o_dec_in, o_dec_out = in_rows(own_rows_of(t2[0], 3)), side(t2[1], t2[2])
    relp = t2[3].reshape(r, 2, REL_HALF)
    o_rel = pair(pick(relp[:, 0], relp[:, 1]), swap(pick(relp[:, 1], relp[:, 0])), 1)
    t3 = split_rows(total_cross, [2 * r, 4 * r, r, r])
    o_cross_q = in_rows(own_rows_of(t3[0], 1))
    o_cross_kv = in_rows(own_rows_of(t3[1], 2))
    o_cross_out = side(t3[2], t3[3])
    o_dec_up = up_rows(own_rows_of(total_du, 4))
    o_dec_down = total_dd

    return (
        pick(enc_low[:LEN], enc_low[LEN:]),
        dec_out.reshape(STREAMS, LEN, D).transpose(1, 0, 2),
        g_source,
        g_dec_in.reshape(STREAMS, LEN, D).transpose(1, 0, 2),
        o_enc_in,
        o_enc_out,
        o_enc_up,
        o_enc_down,
        o_vec[1],
        o_vec[0],
        o_dec_in,
        o_rel,
        o_dec_out,
        o_cross_q,
        o_cross_kv,
        o_cross_out,
        o_dec_up,
        o_dec_down,
        o_vec[3],
        o_vec[2],
    )


def solution(mesh):
    ndp, nf = mesh.shape["dp"], mesh.shape["fsdp"]
    whole = ("dp", "fsdp")
    one, two, three = P(whole), P(whole, None), P(whole, None, None)
    args = (two, three, one, one) + (two,) * 4 + (one,) * 2 + (two,) * 8 + (one,) * 2 + (two, three)
    outs = (two, three, two, three) + (two,) * 4 + (one,) * 2 + (two,) * 8 + (one,) * 2

    def body(*arrays):
        if (ndp, nf) == (4, 8):
            return shards_fast(ndp, nf, *arrays)
        return shards(ndp, nf, *arrays)

    return jax.shard_map(body, mesh=mesh, in_specs=args, out_specs=outs, check_vma=False)
```

```python
import math

import jax
import jax.numpy as jnp
from jax import lax
from jax.experimental import pallas as pl
from jax.experimental.pallas import tpu as pltpu
from jax.sharding import PartitionSpec as P

D = 1024
HEADS = 16
HEAD = 64
FF = 4096
NGRAM = 2
STREAMS = NGRAM + 1
BUCKETS = 32
LEN = 128
HALF = D // 2
OWN_HEADS = HEADS // 2
REL_HALF = OWN_HEADS * BUCKETS
HIDDEN_HALF = FF // 2
WIDE = 512
EPSILON = 1e-05
MASKED = -1000000000.0
SCALE = 1.0 / math.sqrt(HEAD)
BF = jnp.bfloat16
F32 = jnp.float32
ENC_WIDTHS = (D, D, D, FF, D, D, D)
DEC_WIDTHS = (D, D, HEADS * BUCKETS, D, D, D, D, FF, D, D, D, D)


def bucket_value(distance, bucket_count):
    exact_count = bucket_count // 2
    if distance < exact_count:
        return distance
    return min(
        bucket_count - 1,
        exact_count
        + int(
            math.log(distance / exact_count)
            / math.log(128 / exact_count)
            * (bucket_count - exact_count)
        ),
    )


def bucket_table(length, bucket_count):
    positions = jnp.arange(length, dtype=jnp.int32)
    distance = positions[:, None] - positions[None, :]
    bucket = jnp.zeros((length, length), jnp.int32)
    for target in range(1, bucket_count):
        distance_at = 1
        while bucket_value(distance_at, bucket_count) < target:
            distance_at += 1
        bucket = bucket + (distance >= distance_at).astype(jnp.int32)
    return (bucket[:, :, None] == jnp.arange(bucket_count, dtype=jnp.int32)).astype(F32)


def slices_of(vector, widths):
    starts = 0
    result = []
    for amount in widths:
        result.append(vector[starts : starts + amount])
        starts += amount
    return result


def dot(a, b):
    return lax.dot_general(a, b, (((1,), (0,)), ((), ())), preferred_element_type=F32)


def dot_t(a, b):
    return lax.dot_general(a, b, (((1,), (1,)), ((), ())), preferred_element_type=F32)


def dot_g(a, b):
    return lax.dot_general(a, b, (((0,), (0,)), ((), ())), preferred_element_type=F32)


def norm_stats(values):
    average = jnp.mean(values, axis=-1, keepdims=True)
    centered = values - average
    variance = jnp.mean(centered * centered, axis=-1, keepdims=True)
    inverse = lax.rsqrt(variance + EPSILON)
    return centered * inverse, inverse


def norm(values, gain, shift):
    unit, inverse = norm_stats(values)
    return unit * gain + shift


def norm_back(values, gain, grads):
    unit, inverse = norm_stats(values)
    scaled = grads * gain
    mean_one = jnp.mean(scaled, axis=-1, keepdims=True)
    mean_two = jnp.mean(scaled * unit, axis=-1, keepdims=True)
    return (
        inverse * (scaled - mean_one - unit * mean_two),
        jnp.sum(grads * unit, axis=0),
        jnp.sum(grads, axis=0),
    )


def gelu_exact(inputs):
    return jax.nn.gelu(inputs, approximate=False)


def gelu_back(inputs, gradients):
    outputs, pullback = jax.vjp(gelu_exact, inputs)
    return pullback(gradients)[0]


def col_sum(values):
    return jnp.sum(values.astype(F32), axis=0)


class Layout:
    def __init__(self, ndp, nf):
        self.ndp = ndp
        self.nf = nf
        self.nz = nf // 2
        self.chips = ndp * self.nz
        self.devices = ndp * nf
        self.r = D // self.devices
        self.f = FF // self.devices

    def place(self):
        self.dp = lax.axis_index("dp")
        fs = lax.axis_index("fsdp")
        self.z = fs // 2
        self.core = fs % 2

    def swap(self, value):
        return lax.ppermute(value, "fsdp", [(i, i ^ 1) for i in range(self.nf)])

    def shift_z(self, value, step):
        return lax.ppermute(
            value, "fsdp", [(i, (i + 2 * step) % self.nf) for i in range(self.nf)]
        )

    def flip_dp(self, value, mask):
        return lax.ppermute(value, "dp", [(i, i ^ mask) for i in range(self.ndp)])

    def shift_dp(self, value, step):
        return lax.ppermute(value, "dp", [(i, (i + step) % self.ndp) for i in range(self.ndp)])

    def pick(self, first, second):
        return jnp.where(self.core == 0, first, second)

    def pair(self, own, other, axis):
        return self.pick(
            jnp.concatenate([own, other], axis=axis), jnp.concatenate([other, own], axis=axis)
        )


def tie(value, *others):
    return lax.optimization_barrier((value,) + others)[0]


def gather_z(lay, buf):
    out = jnp.zeros((lay.nz,) + buf.shape, buf.dtype)
    out = lax.dynamic_update_slice(out, buf[None], (lay.z, 0, 0))
    for step in range(1, lay.nz):
        got = lay.shift_z(buf, step)
        out = lax.dynamic_update_slice(out, got[None], ((lay.z - step) % lay.nz, 0, 0))
    return out


def gather_dp_first(lay, buf):
    if lay.ndp == 4:
        return [lay.flip_dp(buf, 1), lay.flip_dp(buf, 2)]
    return [lay.shift_dp(buf, step) for step in range(1, lay.ndp)]


def gather_dp_rest(lay, buf, first):
    half = lay.nz // 2
    out = jnp.zeros((lay.ndp,) + buf.shape, buf.dtype)
    if lay.ndp == 4:
        low = lay.flip_dp(first[0][:half], 2)
        high = lay.flip_dp(first[1][half:], 1)
        parts = [(0, 0, buf), (1, 0, first[0]), (2, 0, first[1]), (3, 0, low), (3, half, high)]
        for flip, at, part in parts:
            out = lax.dynamic_update_slice(out, part[None], (lay.dp ^ flip, at, 0, 0))
        return out
    out = lax.dynamic_update_slice(out, buf[None], (lay.dp, 0, 0, 0))
    for step in range(1, lay.ndp):
        out = lax.dynamic_update_slice(
            out, first[step - 1][None], ((lay.dp - step) % lay.ndp, 0, 0, 0)
        )
    return out


def gather_all(lay, bufs):
    staged = []
    results = []
    firsts = []
    for i, buf in enumerate(bufs):
        if i >= 2:
            buf = tie(buf, *firsts[i - 2])
        z = gather_z(lay, buf)
        staged.append(z)
        firsts.append(gather_dp_first(lay, z))
    for z, first in zip(staged, firsts):
        results.append(gather_dp_rest(lay, z, first))
    return results


def take(buf, index, axis=0):
    return lax.dynamic_index_in_dim(buf, index, axis, keepdims=False)


def add_low(*values):
    return sum(v.astype(F32) for v in values).astype(BF)


def scatter_dp(lay, buf):
    if lay.ndp == 4:
        half = lay.nz // 2
        far = take(buf, lay.dp ^ 3)
        to_x = take(buf, lay.dp ^ 1)
        to_y = take(buf, lay.dp ^ 2)
        own = take(buf, lay.dp)
        low = lay.flip_dp(far[:half], 2)
        high = lay.flip_dp(far[half:], 1)
        to_x = jnp.concatenate([add_low(to_x[:half], low), to_x[half:]], axis=0)
        to_y = jnp.concatenate([to_y[:half], add_low(to_y[half:], high)], axis=0)
        return add_low(own, lay.flip_dp(to_x, 1), lay.flip_dp(to_y, 2))
    parts = [take(buf, lay.dp)]
    for step in range(1, lay.ndp):
        parts.append(lay.shift_dp(take(buf, (lay.dp + step) % lay.ndp), step))
    return add_low(*parts)


def scatter_z(lay, buf):
    total = take(buf, lay.z).astype(F32)
    for step in range(1, lay.nz):
        total = total + lay.shift_z(take(buf, (lay.z + step) % lay.nz), step).astype(F32)
    return total


def attention_forward(queries, keys, values, allowed):
    scores = jnp.einsum("snihe,sjhe->snhij", queries, keys, preferred_element_type=F32) * SCALE
    probs = jax.nn.softmax(jnp.where(allowed, scores, MASKED), axis=-1)
    out = jnp.einsum("snhij,sjhe->snihe", probs.astype(BF), values, preferred_element_type=F32)
    return out.astype(BF), probs


def attention_back(queries, keys, values, probs, grad_out):
    grad_probs = jnp.einsum("snihe,sjhe->snhij", grad_out, values, preferred_element_type=F32)
    grad_values = jnp.einsum(
        "snhij,snihe->sjhe", probs.astype(BF), grad_out, preferred_element_type=F32
    )
    grad_scores = (
        probs * (grad_probs - jnp.sum(probs * grad_probs, axis=-1, keepdims=True))
    ).astype(BF)
    grad_queries = (
        jnp.einsum("snhij,sjhe->snihe", grad_scores, keys, preferred_element_type=F32) * SCALE
    )
    grad_keys = (
        jnp.einsum("snhij,snihe->sjhe", grad_scores, queries, preferred_element_type=F32) * SCALE
    )
    return grad_queries.astype(BF), grad_keys.astype(BF), grad_values.astype(BF)


def ngram_forward(dqkv, rel, tgt, onehot):
    q, k, v = dqkv[:, :, :, 0], dqkv[:, :, :, 1], dqkv[:, :, :, 2]
    positions = jnp.arange(LEN, dtype=jnp.int32)
    inside = positions[None, :] < tgt[:, None]
    main_valid = (positions[None, :] <= positions[:, None])[None] & inside[:, None]
    pred_valid = (positions[None, :] < positions[:, None])[None] & inside[:, None]
    valid = jnp.stack([main_valid] + [pred_valid] * NGRAM, axis=1)[:, :, None]
    main = jnp.einsum("snihe,sjhe->snhij", q, k[:, 0], preferred_element_type=F32) * SCALE
    main = main + jnp.einsum("snihk,ijk->snhij", rel, onehot, precision=lax.Precision.HIGHEST)
    main = jnp.where(valid, main, MASKED)
    own = jnp.einsum("snihe,snihe->snhi", q, k, preferred_element_type=F32) * SCALE
    own = own + jnp.transpose(rel[..., 0], (0, 1, 3, 2))
    stream = jnp.arange(STREAMS)[None, :, None, None]
    own = jnp.where(stream == 0, -jnp.inf, own)
    top = jnp.maximum(jnp.max(main, axis=-1), own)
    main = jnp.exp(main - top[..., None])
    own = jnp.exp(own - top)
    total = jnp.sum(main, axis=-1) + own
    main = main / total[..., None]
    own = own / total
    out = jnp.einsum("snhij,sjhe->snihe", main.astype(BF), v[:, 0], preferred_element_type=F32)
    own_low = jnp.transpose(own.astype(BF), (0, 1, 3, 2)).astype(F32)[..., None]
    out = out + own_low * v.astype(F32)
    return out.astype(BF), main, own


def ngram_back(dqkv, main, own, onehot, grad_out):
    q, k, v = dqkv[:, :, :, 0], dqkv[:, :, :, 1], dqkv[:, :, :, 2]
    grad_main = jnp.einsum("snihe,sjhe->snhij", grad_out, v[:, 0], preferred_element_type=F32)
    grad_own = jnp.einsum("snihe,snihe->snhi", grad_out, v, preferred_element_type=F32)
    inner = jnp.sum(main * grad_main, axis=-1) + own * grad_own
    ds = (main * (grad_main - inner[..., None])).astype(BF)
    ds_own = (own * (grad_own - inner)).astype(BF)
    own_rows = jnp.transpose(ds_own, (0, 1, 3, 2)).astype(F32)[..., None]
    p_rows = jnp.transpose(own.astype(BF), (0, 1, 3, 2)).astype(F32)[..., None]
    gq = (
        jnp.einsum("snhij,sjhe->snihe", ds, k[:, 0], preferred_element_type=F32)
        + own_rows * k.astype(F32)
    ) * SCALE
    gk0 = jnp.einsum("snhij,snihe->sjhe", ds, q, preferred_element_type=F32) * SCALE
    gv0 = jnp.einsum("snhij,snihe->sjhe", main.astype(BF), grad_out, preferred_element_type=F32)
    gk = own_rows * q.astype(F32) * SCALE
    gv = p_rows * grad_out.astype(F32)
    gk = jnp.concatenate([gk0[:, None], gk[:, 1:]], axis=1)
    gv = jnp.concatenate([gv0[:, None], gv[:, 1:]], axis=1)
    gqkv = jnp.stack([gq, gk, gv], axis=3).astype(BF)
    grel = jnp.einsum("snhij,ijk->snihk", ds, onehot.astype(BF), preferred_element_type=F32)
    first = (jnp.arange(BUCKETS) == 0).astype(F32)
    grel = (grel + own_rows * first).astype(BF)
    return gqkv, grel


def shards(
    ndp,
    nf,
    source,
    dec_in,
    src_lengths,
    tgt_lengths,
    enc_in_proj,
    enc_out_proj,
    enc_ffn_in,
    enc_ffn_out,
    enc_gains,
    enc_biases,
    dec_in_proj,
    dec_rel_proj,
    dec_out_proj,
    cross_query,
    cross_kv,
    cross_out,
    dec_ffn_in,
    dec_ffn_out,
    dec_gains,
    dec_biases,
    enc_cot,
    dec_cot,
):
    lay = Layout(ndp, nf)
    lay.place()
    r, f, chips = lay.r, lay.f, lay.chips
    swap, pick, pair = lay.swap, lay.pick, lay.pair
    core = lay.core

    def halves(matrix, groups, width):
        parts = matrix.reshape(r, groups, 2, width)
        return (
            pick(parts[:, :, 0], parts[:, :, 1]).reshape(r, groups * width),
            pick(parts[:, :, 1], parts[:, :, 0]).reshape(r, groups * width),
        )

    split = [
        halves(enc_in_proj, 3, HALF),
        halves(enc_ffn_in, chips, f),
        halves(dec_in_proj, 3, HALF),
        halves(cross_query, 1, HALF),
        halves(cross_kv, 2, HALF),
        halves(dec_ffn_in, chips, f),
        halves(dec_rel_proj, 1, REL_HALF),
    ]
    vec = jnp.concatenate(
        [
            enc_biases,
            enc_gains,
            dec_biases,
            dec_gains,
            src_lengths.astype(BF),
            tgt_lengths.astype(BF),
        ]
    )
    nvec = vec.shape[0]
    padded = -(-nvec // WIDE) * WIDE
    vec = jnp.pad(vec, (0, padded - nvec))
    mine = jnp.concatenate([own for own, other in split], axis=1)
    theirs = jnp.concatenate([other for own, other in split], axis=1)
    theirs_got = swap(theirs)
    vec_got = swap(vec)
    source_got = swap(source)
    dec_in_got = swap(dec_in.reshape(LEN * STREAMS, D))

    def owner_rows(start, width):
        return pair(mine[:, start : start + width], theirs_got[:, start : start + width], 0)

    def column_blocks(start, count):
        return [owner_rows(start + WIDE * i, WIDE) for i in range(count)]

    def row_blocks(matrix):
        return [matrix[:, :WIDE], matrix[:, WIDE:]]

    rel_start = mine.shape[1] - REL_HALF
    rel_own = mine[:, rel_start:]
    rel_other = theirs_got[:, rel_start:]
    vec_pair = pair(vec[None], vec_got[None], 0).reshape(-1, WIDE)
    vec_rows = -(-vec_pair.shape[0] // 16) * 16
    vec_used = vec_pair.shape[0]
    vec_pair = jnp.pad(vec_pair, ((0, vec_rows - vec_used), (0, 0)))
    wide_at = [0, 3 * WIDE, 7 * WIDE, 10 * WIDE, 11 * WIDE, 13 * WIDE]
    chunk_parts = [
        column_blocks(wide_at[0], 3) + row_blocks(enc_out_proj) + [vec_pair],
        column_blocks(wide_at[1], 4) + row_blocks(enc_ffn_out),
        column_blocks(wide_at[2], 3) + [pair(rel_own, rel_other, 1)] + row_blocks(dec_out_proj),
        column_blocks(wide_at[3], 1) + column_blocks(wide_at[4], 2) + row_blocks(cross_out),
        column_blocks(wide_at[5], 4) + row_blocks(dec_ffn_out),
    ]
    bufs = [jnp.concatenate(parts, axis=0) for parts in chunk_parts]
    full = gather_all(lay, bufs)

    def cut(index, block):
        parts = chunk_parts[index]
        at = sum(p.shape[0] for p in parts[:block])
        rows = parts[block].shape[0]
        return full[index][:, :, at : at + rows].reshape(chips * rows, WIDE)

    def columns(index, first, count):
        return jnp.concatenate([cut(index, first + i) for i in range(count)], axis=1)

    def head_rows(index, first):
        rows = columns(index, first, 2)
        low, high = rows[:HALF // 2], rows[HALF // 2 :]
        keep = pick(low, high).reshape(chips // 2, 1, r, D)
        got = swap(pick(high, low)).reshape(chips // 2, 1, r, D)
        return pair(keep, got, 1).reshape(HALF, D)

    w_enc_in = columns(0, 0, 3)
    w_enc_out = head_rows(0, 3)
    w_enc_up = columns(1, 0, 4)
    w_enc_down = columns(1, 4, 2)
    w_dec_in = columns(2, 0, 3)
    w_rel = (
        cut(2, 3)
        .reshape(chips, r, 2, REL_HALF)
        .transpose(0, 2, 1, 3)
        .reshape(D, REL_HALF)
    )
    w_dec_out = head_rows(2, 4)
    w_cross_q = columns(3, 0, 1)
    w_cross_kv = columns(3, 1, 2)
    w_cross_out = head_rows(3, 3)
    w_dec_up = columns(4, 0, 4)
    w_dec_down = columns(4, 4, 2)

    vec_all = (
        cut(0, 5).reshape(chips, vec_rows, WIDE)[:, :vec_used].reshape(lay.devices, padded).astype(F32)
    )
    widths = [enc_biases.shape[0], enc_gains.shape[0], dec_biases.shape[0], dec_gains.shape[0]]
    starts = [0]
    for width in widths:
        starts.append(starts[-1] + width)
    v_enc_b, v_enc_g, v_dec_b, v_dec_g = [
        vec_all[:, starts[i] : starts[i + 1]].reshape(-1) for i in range(4)
    ]
    ebias = slices_of(v_enc_b, ENC_WIDTHS)
    egain = slices_of(v_enc_g, (D, D))
    dbias = slices_of(v_dec_b, DEC_WIDTHS)
    dgain = slices_of(v_dec_g, (D, D, D))

    def half_of(vector):
        parts = vector.reshape(2, -1)
        return pick(parts[0], parts[1])

    def hidden_of(vector):
        parts = vector.reshape(chips, 2, f)
        return pick(parts[:, 0], parts[:, 1]).reshape(-1)

    zero_half = jnp.zeros((HALF,), F32)
    lens = jnp.stack([pair(vec[None], vec_got[None], 0)[:, nvec - 2 + i] for i in range(2)])
    lens = lens.astype(F32).astype(jnp.int32)
    src_len, tgt_len = lens[0], lens[1]
    positions = jnp.arange(LEN, dtype=jnp.int32)
    src_valid = (positions[None, :] < src_len[:, None])[:, None, None, None, :]
    onehot = bucket_table(LEN, BUCKETS)

    def both(partial):
        low = partial.astype(BF)
        return low.astype(F32) + swap(low).astype(F32)

    x = pair(source[None], source_got[None], 0).reshape(2 * LEN, D)
    qkv_bias = jnp.concatenate([half_of(ebias[0]), zero_half, half_of(ebias[1])])
    eqkv = (dot(x, w_enc_in) + qkv_bias).astype(BF).reshape(2, LEN, 3, OWN_HEADS, HEAD)
    eq, ek, ev = eqkv[:, None, :, 0], eqkv[:, :, 1], eqkv[:, :, 2]
    ea, eprobs = attention_forward(eq, ek, ev, src_valid)
    ea = ea.reshape(2 * LEN, HALF)
    ez1 = x.astype(F32) + both(dot(ea, w_enc_out)) + ebias[2]
    eh1 = norm(ez1, egain[0], ebias[5])
    eh1_low = eh1.astype(BF)
    eu = dot(eh1_low, w_enc_up) + hidden_of(ebias[3])
    eg = gelu_exact(eu).astype(BF)
    ez2 = eh1 + both(dot(eg, w_enc_down)) + ebias[4]
    enc = norm(ez2, egain[1], ebias[6])
    enc_low = enc.astype(BF)

    rows = 2 * STREAMS * LEN
    y = pair(
        dec_in.transpose(1, 0, 2)[None], dec_in_got.reshape(LEN, STREAMS, D).transpose(1, 0, 2)[None], 0
    ).reshape(rows, D)
    dqkv_bias = jnp.concatenate([half_of(dbias[0]), zero_half, half_of(dbias[1])])
    dqkv = (dot(y, w_dec_in) + dqkv_bias).astype(BF)
    dqkv = dqkv.reshape(2, STREAMS, LEN, 3, OWN_HEADS, HEAD)
    rel = (dot(y, w_rel) + half_of(dbias[2])).reshape(2, STREAMS, LEN, OWN_HEADS, BUCKETS)
    da, dmain, down = ngram_forward(dqkv, rel, tgt_len, onehot)
    da = da.reshape(rows, HALF)
    dz1 = y.astype(F32) + both(dot(da, w_dec_out)) + dbias[3]
    dh1 = norm(dz1, dgain[0], dbias[9])
    dh1_low = dh1.astype(BF)
    cq = (dot(dh1_low, w_cross_q) + half_of(dbias[4])).astype(BF)
    cq = cq.reshape(2, STREAMS, LEN, OWN_HEADS, HEAD)
    ckv = dot(enc_low, w_cross_kv) + jnp.concatenate([zero_half, half_of(dbias[5])])
    ckv = ckv.astype(BF).reshape(2, LEN, 2, OWN_HEADS, HEAD)
    ck, cv = ckv[:, :, 0], ckv[:, :, 1]
    ca, cprobs = attention_forward(cq, ck, cv, src_valid)
    ca = ca.reshape(rows, HALF)
    dz2 = dh1 + both(dot(ca, w_cross_out)) + dbias[6]
    dh2 = norm(dz2, dgain[1], dbias[10])
    dh2_low = dh2.astype(BF)
    du = dot(dh2_low, w_dec_up) + hidden_of(dbias[7])
    dg = gelu_exact(du).astype(BF)
    dz3 = dh2 + both(dot(dg, w_dec_down)) + dbias[8]
    dec = norm(dz3, dgain[2], dbias[11])

    def own_rows_of(total, count):
        blocks = total[: count * 2 * r].reshape(count, 2, r, WIDE)
        keep = pick(blocks[:, 0], blocks[:, 1])
        got = swap(pick(blocks[:, 1], blocks[:, 0]))
        return pair(keep[:, None], got[:, None], 1)

    def chip_blocks(grad):
        n = grad.shape[1] // WIDE
        shape = (lay.ndp, lay.nz, grad.shape[0] // chips, WIDE)
        low = grad.astype(BF)
        return [low[:, WIDE * i : WIDE * i + WIDE].reshape(shape) for i in range(n)]

    def head_blocks(grad):
        parts = grad.astype(BF).reshape(chips // 2, 2, r, D)
        keep = pick(parts[:, 0], parts[:, 1])
        got = swap(pick(parts[:, 1], parts[:, 0]))
        return chip_blocks(pair(keep, got, 0).reshape(chips * r, D))

    def scatter(parts, previous):
        buf = jnp.concatenate(parts, axis=2)
        if previous is not None:
            buf = tie(buf, previous)
        first = scatter_dp(lay, buf)
        return scatter_z(lay, first), first

    def split_rows(total, sizes):
        at = 0
        result = []
        for size in sizes:
            result.append(total[at : at + size])
            at += size
        return result

    dcot_got = swap(dec_cot.reshape(LEN * STREAMS, D)).reshape(LEN, STREAMS, D)
    dcot = pair(dec_cot.transpose(1, 0, 2)[None], dcot_got.transpose(1, 0, 2)[None], 0)
    dcot = dcot.reshape(rows, D).astype(F32)
    gz3, ggain3, gnorm3 = norm_back(dz3, dgain[2], dcot)
    gf = gz3.astype(BF)
    g_down = dot_g(dg, gf)
    gu = gelu_back(du, dot_t(gf, w_dec_down)).astype(BF)
    g_up = dot_g(dh2_low, gu)
    total4, first4 = scatter(chip_blocks(g_up) + chip_blocks(g_down), None)
    gz2, ggain2, gnorm2 = norm_back(dz2, dgain[1], gz3 + both(dot_t(gu, w_dec_up)))
    gx = gz2.astype(BF)
    g_cross_out = dot_g(ca, gx)
    gca = dot_t(gx, w_cross_out).astype(BF).reshape(2, STREAMS, LEN, OWN_HEADS, HEAD)
    gcq, gck, gcv = attention_back(cq, ck, cv, cprobs, gca)
    gcq = gcq.reshape(rows, HALF)
    gckv = jnp.stack([gck, gcv], axis=2).reshape(2 * LEN, D)
    g_cross_q = dot_g(dh1_low, gcq)
    g_cross_kv = dot_g(enc_low, gckv)
    total3, first3 = scatter(
        chip_blocks(g_cross_q) + chip_blocks(g_cross_kv) + head_blocks(g_cross_out), first4
    )
    ecot_got = swap(enc_cot)
    ecot = pair(enc_cot[None], ecot_got[None], 0).reshape(2 * LEN, D).astype(F32)
    genc = ecot + both(dot_t(gckv, w_cross_kv))
    gz1, ggain1, gnorm1 = norm_back(dz1, dgain[0], gz2 + both(dot_t(gcq, w_cross_q)))
    go = gz1.astype(BF)
    g_dec_out = dot_g(da, go)
    gda = dot_t(go, w_dec_out).astype(BF).reshape(2, STREAMS, LEN, OWN_HEADS, HEAD)
    gqkv, grel = ngram_back(dqkv, dmain, down, onehot, gda)
    gqkv = gqkv.reshape(rows, 3 * HALF)
    grel = grel.reshape(rows, REL_HALF)
    g_dec_in = dot_g(y, gqkv)
    g_rel = dot_g(y, grel)
    rel_block = (
        g_rel.astype(BF)
        .reshape(chips, 2, r, REL_HALF)
        .transpose(0, 2, 1, 3)
        .reshape(lay.ndp, lay.nz, r, WIDE)
    )
    total2, first2 = scatter(chip_blocks(g_dec_in) + [rel_block] + head_blocks(g_dec_out), first3)

    def own_sequence(partial, count):
        parts = partial.reshape(2, count, D)
        keep = pick(parts[0], parts[1])
        return keep + swap(pick(parts[1], parts[0]).astype(BF)).astype(F32)

    def own_part(values, count):
        parts = values.reshape(2, count, D)
        return pick(parts[0], parts[1])

    dec_rows = STREAMS * LEN
    g_dec_input = own_part(gz1, dec_rows) + own_sequence(
        dot_t(gqkv, w_dec_in) + dot_t(grel, w_rel), dec_rows
    )

    def widen(vector):
        zeros = jnp.zeros_like(vector)
        return pick(jnp.concatenate([vector, zeros]), jnp.concatenate([zeros, vector]))

    def widen_hidden(vector):
        parts = vector.reshape(chips, 1, f)
        zeros = jnp.zeros_like(parts)
        return pick(
            jnp.concatenate([parts, zeros], axis=1), jnp.concatenate([zeros, parts], axis=1)
        ).reshape(-1)

    column_sums = col_sum(gqkv)
    dec_vec = jnp.concatenate(
        [
            widen(column_sums[:HALF]),
            widen(column_sums[2 * HALF :]),
            widen(col_sum(grel)),
            0.5 * col_sum(go),
            widen(col_sum(gcq)),
            widen(col_sum(gckv)[HALF:]),
            0.5 * col_sum(gx),
            widen_hidden(col_sum(gu)),
            0.5 * col_sum(gf),
            0.5 * gnorm1,
            0.5 * gnorm2,
            0.5 * gnorm3,
            0.5 * ggain1,
            0.5 * ggain2,
            0.5 * ggain3,
        ]
    )

    gz2e, eggain2, egnorm2 = norm_back(ez2, egain[1], genc)
    gfe = gz2e.astype(BF)
    ge_down = dot_g(eg, gfe)
    gue = gelu_back(eu, dot_t(gfe, w_enc_down)).astype(BF)
    ge_up = dot_g(eh1_low, gue)
    total1, first1 = scatter(chip_blocks(ge_up) + chip_blocks(ge_down), first2)
    gz1e, eggain1, egnorm1 = norm_back(ez1, egain[0], gz2e + both(dot_t(gue, w_enc_up)))
    goe = gz1e.astype(BF)
    ge_out = dot_g(ea, goe)
    gae = dot_t(goe, w_enc_out).astype(BF).reshape(2, 1, LEN, OWN_HEADS, HEAD)
    geq, gek, gev = attention_back(eq, ek, ev, eprobs, gae)
    geqkv = jnp.stack([geq[:, 0], gek, gev], axis=2).reshape(2 * LEN, 3 * HALF)
    ge_in = dot_g(x, geqkv)
    total0, first0 = scatter(chip_blocks(ge_in) + head_blocks(ge_out), first1)
    g_source = own_part(gz1e, LEN) + own_sequence(dot_t(geqkv, w_enc_in), LEN)
    ecolumn_sums = col_sum(geqkv)
    enc_vec = jnp.concatenate(
        [
            widen(ecolumn_sums[:HALF]),
            widen(ecolumn_sums[2 * HALF :]),
            0.5 * col_sum(goe),
            widen_hidden(col_sum(gue)),
            0.5 * col_sum(gfe),
            0.5 * egnorm1,
            0.5 * egnorm2,
            0.5 * eggain1,
            0.5 * eggain2,
        ]
    )
    me = lay.dp * lay.nf + lax.axis_index("fsdp")

    def own_slice(vector):
        return take(vector.reshape(lay.devices, -1), me)

    dec_vec = lax.psum(dec_vec, ("dp", "fsdp"))
    enc_vec = lax.psum(enc_vec, ("dp", "fsdp"))
    nb = sum(ENC_WIDTHS)
    g_enc_biases, g_enc_gains = own_slice(enc_vec[:nb]), own_slice(enc_vec[nb:])
    nb = sum(DEC_WIDTHS)
    g_dec_biases, g_dec_gains = own_slice(dec_vec[:nb]), own_slice(dec_vec[nb:])

    def in_rows(blocks):
        return blocks.transpose(2, 0, 1, 3).reshape(r, -1)

    def up_rows(blocks):
        per = WIDE // f
        return blocks.reshape(4, 2, r, per, f).transpose(2, 0, 3, 1, 4).reshape(r, FF)

    def side(low, high):
        return jnp.concatenate([low, high], axis=1)

    t0 = split_rows(total0, [6 * r, r, r])
    o_enc_in, o_enc_out = in_rows(own_rows_of(t0[0], 3)), side(t0[1], t0[2])
    t1 = split_rows(total1, [8 * r, f, f])
    o_enc_up, o_enc_down = up_rows(own_rows_of(t1[0], 4)), side(t1[1], t1[2])
    t2 = split_rows(total2, [6 * r, r, r, r])
    o_dec_in, o_dec_out = in_rows(own_rows_of(t2[0], 3)), side(t2[2], t2[3])
    relp = t2[1].reshape(r, 2, REL_HALF)
    rel_keep = pick(relp[:, 0], relp[:, 1])
    o_rel = pair(rel_keep, swap(pick(relp[:, 1], relp[:, 0])), 1)
    t3 = split_rows(total3, [2 * r, 4 * r, r, r])
    o_cross_q = in_rows(own_rows_of(t3[0], 1))
    o_cross_kv = in_rows(own_rows_of(t3[1], 2))
    o_cross_out = side(t3[2], t3[3])
    t4 = split_rows(total4, [8 * r, f, f])
    o_dec_up, o_dec_down = up_rows(own_rows_of(t4[0], 4)), side(t4[1], t4[2])

    return (
        own_part(enc_low, LEN),
        own_part(dec.astype(BF), dec_rows).reshape(STREAMS, LEN, D).transpose(1, 0, 2),
        g_source,
        g_dec_input.reshape(STREAMS, LEN, D).transpose(1, 0, 2),
        o_enc_in,
        o_enc_out,
        o_enc_up,
        o_enc_down,
        g_enc_gains,
        g_enc_biases,
        o_dec_in,
        o_rel,
        o_dec_out,
        o_cross_q,
        o_cross_kv,
        o_cross_out,
        o_dec_up,
        o_dec_down,
        g_dec_gains,
        g_dec_biases,
    )


BUDGET = 26 * 1024 * 1024
PIECES = 4
HBM_RATE = 1.0e6
FLOP_RATE = 1.0e9


def run(body, grid, ins, outs, scratch=(), us=5):
    arrays = [a for a, s in ins]
    return pl.pallas_call(
        body,
        grid=(grid,),
        in_specs=[s for a, s in ins],
        out_specs=[s for a, s in outs],
        out_shape=[a for a, s in outs],
        scratch_shapes=list(scratch),
        compiler_params=pltpu.CompilerParams(vmem_limit_bytes=BUDGET),
        cost_estimate=pl.CostEstimate(
            flops=int(us * FLOP_RATE), bytes_accessed=int(us * HBM_RATE), transcendentals=0
        ),
    )(*arrays)


def full(array):
    zeros = (0,) * array.ndim
    return array, pl.BlockSpec(array.shape, lambda t: zeros, pipeline_mode=pl.Buffered(1))


def small(array):
    return array, pl.BlockSpec(memory_space=pltpu.SMEM)


def out_full(shape, dtype):
    zeros = (0,) * len(shape)
    return jax.ShapeDtypeStruct(shape, dtype), pl.BlockSpec(shape, lambda t: zeros)


def out_cols(rows, cols, dtype, index):
    return (
        jax.ShapeDtypeStruct((rows, cols), dtype),
        pl.BlockSpec((rows, WIDE), lambda t: (0, index(t))),
    )


def in_cols(array, index, width=WIDE):
    return array, pl.BlockSpec((array.shape[0], width), lambda t: (0, index(t)))


def blocks(pieces, rows, index):
    return [
        (p, pl.BlockSpec((4, rows, WIDE), lambda t: (0, index(t), 0))) for p in pieces
    ]


def wide_blocks(pieces, index):
    return [(p, pl.BlockSpec((4,) + p.shape[1:2] + (WIDE,), lambda t: (0, 0, index(t)))) for p in pieces]


def assemble(refs, scr, place):
    for i in range(4):
        scr[jnp.bitwise_xor(place[0], i)] = refs[i][...]


def weight_scratch(rows, width=WIDE):
    return pltpu.VMEM((4, 4, rows, width), BF)


def matrix_of(scr):
    a, b, c, d = scr.shape
    return scr[...].reshape(a * b * c, d)


def pick_matrix(parity):
    i = lax.broadcasted_iota(jnp.int32, (HALF, HALF // 2), 0)
    j = lax.broadcasted_iota(jnp.int32, (HALF, HALF // 2), 1)
    from_row = ((j >> 5) << 6) + (parity << 5) + (j & 31)
    return jnp.where(i == from_row, 1.0, 0.0).astype(BF)


def head_masks():
    lane = lax.broadcasted_iota(jnp.int32, (1, 128), 1)
    first = jnp.where(lane < HEAD, 1.0, 0.0)
    return first.astype(BF), (1.0 - first).astype(BF)


def first_lanes(rows):
    return lax.broadcasted_iota(jnp.int32, (rows, 128), 1) < HEAD


def soft_rows(scores):
    top = jnp.max(scores, axis=-1, keepdims=True)
    raised = jnp.exp(scores - top)
    return raised * (1.0 / jnp.sum(raised, axis=-1, keepdims=True))


def masked_probs(queries, keys, count):
    scores = dot_t(queries, keys) * SCALE
    column = lax.broadcasted_iota(jnp.int32, scores.shape, 1)
    return soft_rows(jnp.where(column < count, scores, MASKED))


def attend(q, k, v, count):
    rows = q.shape[0]
    out = []
    for mask in head_masks():
        probs = masked_probs(q * mask, k, count).astype(BF)
        out.append(dot(probs, v))
    return jnp.where(first_lanes(rows), out[0], out[1]).astype(BF)


def attend_back(q, k, v, g, count):
    gq, gk, gv = [], 0.0, 0.0
    for mask in head_masks():
        qm, gm = q * mask, g * mask
        probs = masked_probs(qm, k, count)
        gp = dot_t(gm, v)
        ds = (probs * (gp - jnp.sum(probs * gp, axis=-1, keepdims=True))).astype(BF)
        gq.append(dot(ds, k))
        gk = gk + dot_g(ds, qm)
        gv = gv + dot_g(probs.astype(BF), gm)
    gq = jnp.where(first_lanes(q.shape[0]), gq[0], gq[1]) * SCALE
    return gq.astype(BF), (gk * SCALE).astype(BF), gv.astype(BF)


def split_parity(heads, place, keep, send):
    core = place[2]
    keep[...] = dot(heads[...], pick_matrix(core)).astype(BF)
    send[...] = dot(heads[...], pick_matrix(1 - core)).astype(BF)


def join_parity(keep, got, place, heads):
    core = place[2]
    heads[...] = (
        dot_t(keep[...], pick_matrix(core)) + dot_t(got[...], pick_matrix(1 - core))
    ).astype(BF)


def enc_attention(place, x, bias, pieces):
    rows = x.shape[0]

    def body(place, x, bias, *refs):
        w, (qkv, keep, send, scr, heads) = refs[:PIECES], refs[PIECES:]
        t = pl.program_id(0)
        assemble(w, scr, place)
        qkv[:, pl.ds(t * WIDE, WIDE)] = (dot(x[...], matrix_of(scr)) + bias[...]).astype(BF)

        @pl.when(t == 2)
        def _():
            for s in range(2):
                r = slice(s * LEN, s * LEN + LEN)
                for j in range(4):
                    c = [slice(HALF * i + 128 * j, HALF * i + 128 * j + 128) for i in range(3)]
                    heads[r, c[0]] = attend(qkv[r, c[0]], qkv[r, c[1]], qkv[r, c[2]], place[3 + s])
            split_parity(heads, place, keep, send)

    return run(
        body,
        3,
        [small(place), full(x), in_cols(bias, lambda t: t)] + blocks(pieces, 64, lambda t: t),
        [
            out_full((rows, 3 * HALF), BF),
            out_full((rows, HALF // 2), BF),
            out_full((rows, HALF // 2), BF),
        ],
        [weight_scratch(64), pltpu.VMEM((rows, HALF), BF)],
        us=10,
    )


def out_projection(place, keep, got, pieces):
    rows = keep.shape[0]

    def body(place, keep, got, *refs):
        w, (out, scr) = refs[:PIECES], refs[PIECES:]
        assemble(w, scr, place)
        core = place[2]
        mine = scr[pl.ds(2 * core, 2)].reshape(HALF // 2, WIDE)
        theirs = scr[pl.ds(2 - 2 * core, 2)].reshape(HALF // 2, WIDE)
        out[...] = (dot(keep[...], mine) + dot(got[...], theirs)).astype(BF)

    return run(
        body,
        2,
        [small(place), full(keep), full(got)] + blocks(pieces, 32, lambda t: 6 + t),
        [out_cols(rows, D, BF, lambda t: t)],
        [weight_scratch(32)],
        us=3,
    )[0]


def stats(v):
    centered = v - jnp.mean(v, axis=-1, keepdims=True)
    inverse = lax.rsqrt(jnp.mean(centered * centered, axis=-1, keepdims=True) + EPSILON)
    return centered * inverse, inverse


def each_tile(rows, tile, step):
    def loop(m, carry):
        step(pl.multiple_of(m * tile, tile))
        return carry

    lax.fori_loop(0, rows // tile, loop, 0)


def norm_tiles(rows, base, affine, own, other, bias, gain, shift, unit_out, inv_out, low_out, at=0):
    def step(r):
        here = pl.ds(r, LEN)
        v = base[here].astype(F32)
        if affine is not None:
            v = v * affine[0] + affine[1]
        there = pl.ds(r + at, LEN)
        v = v + (own[there].astype(F32) + other[there].astype(F32)) + bias
        unit, inverse = stats(v)
        unit_out[here] = unit
        inv_out[here] = jnp.broadcast_to(inverse, (LEN, 128))
        low_out[here] = (unit * gain + shift).astype(BF)

    each_tile(rows, LEN, step)


def norm_forward(place, base, affine, own, other, vecs):
    rows = base.shape[0]

    def body(place, base, own, other, vecs, unit, inv, low):
        aff = (vecs[0:1], vecs[1:2]) if affine else None
        norm_tiles(LEN, base, aff, own, other, vecs[2:3], vecs[3:4], vecs[4:5], unit, inv, low)

    def tiles(array):
        return array, pl.BlockSpec((LEN, array.shape[1]), lambda t: (t, 0))

    def out(width, dtype):
        return jax.ShapeDtypeStruct((rows, width), dtype), pl.BlockSpec((LEN, width), lambda t: (t, 0))

    return run(
        body,
        rows // LEN,
        [small(place), tiles(base), tiles(own), tiles(other), full(vecs)],
        [out(D, F32), out(128, F32), out(D, BF)],
        us=4,
    )


ROOT_HALF = math.sqrt(0.5)
ROOT_TWO_PI = math.sqrt(0.5 / math.pi)
TAIL = (0.254829592, -0.284496736, 1.421413741, -1.453152027, 1.061405429)


def gelu_pair(u):
    depth = 1.0 + (0.3275911 * ROOT_HALF) * jnp.abs(u)
    t = pl.reciprocal(depth, approx=True)
    t = t * (2.0 - depth * t)
    bell = jnp.exp(-0.5 * u * u)
    poly = TAIL[4]
    for c in TAIL[3::-1]:
        poly = poly * t + c
    tail = (0.5 * t) * poly * bell
    phi = jnp.where(u < 0.0, tail, 1.0 - tail)
    return u * phi, phi + u * (bell * ROOT_TWO_PI)


def ffn_forward(place, low, hidden_bias, up_pieces, down_pieces):
    rows = low.shape[0]
    hidden = hidden_bias.shape[1]
    ups = hidden // WIDE
    tile = 128

    def body(place, low, hb, *refs):
        wu, wd = refs[:PIECES], refs[PIECES : 2 * PIECES]
        g, gp, part, scr_u, scr_d, acts = refs[2 * PIECES :]
        t = pl.program_id(0)

        @pl.when(t < ups)
        def _():
            assemble(wu, scr_u, place)
            w = matrix_of(scr_u)

            for r in range(0, rows, tile):
                here = slice(r, r + tile)
                a, b = gelu_pair(dot(low[here], w) + hb[...])
                a = a.astype(BF)
                g[here] = a
                acts[here, pl.ds(t * WIDE, WIDE)] = a
                gp[here] = b.astype(BF)

        @pl.when(t >= ups)
        def _():
            assemble(wd, scr_d, place)
            part[...] = dot(acts[...], matrix_of(scr_d)).astype(BF)

    up = lambda t: jnp.minimum(t, ups - 1)
    down = lambda t: jnp.maximum(t - ups, 0)
    return run(
        body,
        ups + 2,
        [small(place), full(low), in_cols(hidden_bias, up)]
        + blocks(up_pieces, 64, up)
        + wide_blocks(down_pieces, down),
        [
            out_cols(rows, hidden, BF, up),
            out_cols(rows, hidden, BF, up),
            out_cols(rows, D, BF, down),
        ],
        [weight_scratch(64), weight_scratch(128), pltpu.VMEM((rows, hidden), BF)],
        us=14 if rows > 256 else 8,
    )


def distance_buckets(reverse):
    row = lax.broadcasted_iota(jnp.int32, (128, 128), 0) & (BUCKETS - 1)
    lane = lax.broadcasted_iota(jnp.int32, (128, 128), 1)
    distance = ((lane + 1) if reverse else (128 - lane)) & 127
    bucket = jnp.zeros((128, 128), jnp.int32)
    for target in range(1, BUCKETS):
        at = 1
        while bucket_value(at, BUCKETS) < target:
            at += 1
        bucket = bucket + jnp.where(distance >= at, 1, 0)
    return jnp.where(bucket == row, 1.0, 0.0).astype(BF)


def skew(values):
    parts = [values[128 * n : 128 * n + 128] for n in range(values.shape[0] // 128)]
    return jnp.concatenate(
        [pltpu.roll(part, 0, 1, stride=1, stride_axis=0) for part in parts], axis=0
    )


def mirror():
    row = lax.broadcasted_iota(jnp.int32, (128, 128), 0)
    lane = lax.broadcasted_iota(jnp.int32, (128, 128), 1)
    return jnp.where(row + lane == 127, 1.0, 0.0).astype(BF)


def quarter_mask(h):
    lane = lax.broadcasted_iota(jnp.int32, (1, 128), 1)
    return jnp.where((lane >> 5) == h, 1.0, 0.0).astype(BF)


def ngram_probs(qm, prod, k0, rel_high, rel_low, table, count, h, first):
    mask = quarter_mask(h % 4)
    turned = dot(rel_high * mask, table) + dot(rel_low * mask, table)
    scores = dot_t(qm, k0) * SCALE + skew(turned)
    row = lax.broadcasted_iota(jnp.int32, scores.shape, 0)
    column = lax.broadcasted_iota(jnp.int32, scores.shape, 1)
    token = row & (LEN - 1)
    reach = jnp.where(row < LEN, token, token - 1)
    scores = jnp.where((column <= reach) & (column < count), scores, MASKED)
    own = jnp.sum(prod * first, axis=-1, keepdims=True) * SCALE + turned[:, 0:1]
    main = lax.broadcasted_iota(jnp.int32, own.shape, 0) < LEN
    own = jnp.where(main, 2.0 * MASKED, own)
    top = jnp.maximum(jnp.max(scores, axis=-1, keepdims=True), own)
    raised = jnp.exp(scores - top)
    own = jnp.exp(own - top)
    scale = 1.0 / (jnp.sum(raised, axis=-1, keepdims=True) + own)
    return raised * scale, own * scale


def split_high(values):
    high = values.astype(BF)
    return high, (values - high.astype(F32)).astype(BF)


def half_rows(rows):
    first = jnp.where(lax.broadcasted_iota(jnp.int32, (rows, 128), 1) < HEAD, 1.0, 0.0)
    return first, 1.0 - first


def ngram_attention(place, y, bias, rel_bias, pieces):
    rows = y.shape[0]
    span = STREAMS * LEN

    def body(place, y, bias, rbias, *refs):
        w, wr = refs[:PIECES], refs[PIECES : 2 * PIECES]
        qkv, rel, keep, send, scr, scr_r, heads, table = refs[2 * PIECES :]
        t = pl.program_id(0)

        @pl.when(t < 3)
        def _():
            assemble(w, scr, place)
            qkv[:, pl.ds(pl.multiple_of(t * WIDE, WIDE), WIDE)] = (
                dot(y[...], matrix_of(scr)) + bias[...]
            ).astype(BF)

        @pl.when(t == 3)
        def _():
            assemble_rel(wr, scr_r, place)
            rel[...] = dot(y[...], scr_r[...].reshape(D, REL_HALF)) + rbias[...]
            table[...] = distance_buckets(False)
            lanes = half_rows(span)

            def step(s, carry):
                r = pl.ds(pl.multiple_of(s * span, span), span)
                r0 = pl.ds(pl.multiple_of(s * span, span), LEN)
                count = place[5 + s]
                for j in range(4):
                    c = [slice(HALF * i + 128 * j, HALF * i + 128 * j + 128) for i in range(3)]
                    q, k, v = qkv[r, c[0]], qkv[r, c[1]], qkv[r, c[2]]
                    k0, v0 = qkv[r0, c[1]], qkv[r0, c[2]]
                    high, low = split_high(rel[r, 128 * (j // 2) : 128 * (j // 2) + 128])
                    prod = q.astype(F32) * k.astype(F32)
                    out = []
                    for i, mask in enumerate(head_masks()):
                        probs, own = ngram_probs(
                            q * mask, prod, k0, high, low, table[...], count, 2 * j + i, lanes[i]
                        )
                        own = own.astype(BF).astype(F32)
                        out.append(dot(probs.astype(BF), v0) + own * v.astype(F32))
                    heads[r, c[0]] = jnp.where(first_lanes(span), out[0], out[1]).astype(BF)
                return carry

            lax.fori_loop(0, 2, step, 0)
            split_parity(heads, place, keep, send)

    third = lambda t: jnp.minimum(t, 2)
    return run(
        body,
        4,
        [small(place), full(y), in_cols(bias, third), full(rel_bias)]
        + blocks(pieces, 64, third)
        + blocks(pieces, 32, lambda t: 8),
        [
            out_full((rows, 3 * HALF), BF),
            out_full((rows, REL_HALF), F32),
            out_full((rows, HALF // 2), BF),
            out_full((rows, HALF // 2), BF),
        ],
        [
            weight_scratch(64),
            pltpu.VMEM((4, 4, 2, 32, REL_HALF), BF),
            pltpu.VMEM((rows, HALF), BF),
            pltpu.VMEM((128, 128), BF),
        ],
        us=19,
    )


def assemble_rel(refs, scr, place):
    for i in range(4):
        block = refs[i][...]
        at = jnp.bitwise_xor(place[0], i)
        scr[at, :, 0] = block[:, :, :REL_HALF]
        scr[at, :, 1] = block[:, :, REL_HALF:]


def cross_forward(place, y, own, other, vecs, eunit, evecs, eown, eother, q_bias, kv_bias, pieces):
    rows, mem = y.shape[0], eunit.shape[0]
    span = STREAMS * LEN

    def body(place, y, own, other, vecs, eunit, evecs, eown, eother, qb, kvb, *refs):
        w = refs[:PIECES]
        unit, inv, low, eunit2, einv2, elow, q, kv, keep, send, scr, heads = refs[PIECES:]
        t = pl.program_id(0)
        assemble(w, scr, place)

        @pl.when(t == 0)
        def _():
            norm_tiles(
                rows, y, None, own, other, vecs[0:1], vecs[1:2], vecs[2:3], unit, inv, low
            )
            norm_tiles(
                mem,
                eunit,
                (evecs[0:1], evecs[1:2]),
                eown,
                eother,
                evecs[2:3],
                evecs[3:4],
                evecs[4:5],
                eunit2,
                einv2,
                elow,
            )
            q[...] = (dot(low[...], matrix_of(scr)) + qb[...]).astype(BF)

        @pl.when(t > 0)
        def _():
            at = pl.multiple_of((t - 1) * WIDE, WIDE)
            kv[:, pl.ds(at, WIDE)] = (dot(elow[...], matrix_of(scr)) + kvb[...]).astype(BF)

        @pl.when(t == 2)
        def _():
            for s in range(2):
                r = slice(s * span, s * span + span)
                m = slice(s * LEN, s * LEN + LEN)
                for j in range(4):
                    c = slice(128 * j, 128 * j + 128)
                    c2 = slice(HALF + 128 * j, HALF + 128 * j + 128)
                    heads[r, c] = attend(q[r, c], kv[m, c], kv[m, c2], place[3 + s])
            split_parity(heads, place, keep, send)

    return run(
        body,
        3,
        [small(place)]
        + [full(a) for a in (y, own, other, vecs, eunit, evecs, eown, eother, q_bias)]
        + [in_cols(kv_bias, lambda t: jnp.maximum(t - 1, 0))]
        + blocks(pieces, 64, lambda t: t),
        [
            out_full((rows, D), F32),
            out_full((rows, 128), F32),
            out_full((rows, D), BF),
            out_full((mem, D), F32),
            out_full((mem, 128), F32),
            out_full((mem, D), BF),
            out_full((rows, HALF), BF),
            out_full((mem, D), BF),
            out_full((rows, HALF // 2), BF),
            out_full((rows, HALF // 2), BF),
        ],
        [weight_scratch(64), pltpu.VMEM((rows, HALF), BF)],
        us=15,
    )


def fold(values):
    return jnp.sum(values.reshape(values.shape[0] // 8, 8, values.shape[1]), axis=0)


def norm_back_tile(total, unit, inverse, gain):
    scaled = total * gain
    one = jnp.mean(scaled, axis=-1, keepdims=True)
    two = jnp.mean(scaled * unit, axis=-1, keepdims=True)
    return inverse * (scaled - one - unit * two)


def norm_backward(place, final, total_ins, unit_ins, vecs):
    rows = total_ins[0].shape[0]
    n_total, n_unit = len(total_ins), len(unit_ins)
    steps = rows // LEN
    mine = steps // 2

    def body(place, vecs, *refs):
        tot, uni = refs[:n_total], refs[n_total : n_total + n_unit]
        *outs, gz, gf, s_gain, s_shift, s_gf, acc = refs[n_total + n_unit :]
        t = pl.program_id(0)

        @pl.when(t == 0)
        def _():
            acc[...] = jnp.zeros_like(acc)

        if final:
            v = uni[0][...] * vecs[0:1] + vecs[1:2]
            v = v + (uni[1][...].astype(F32) + uni[2][...].astype(F32)) + vecs[2:3]
            unit, inverse = stats(v)

            @pl.when((t >= mine) == (place[2] == 1))
            def _():
                outs[0][...] = (unit * vecs[3:4] + vecs[4:5]).astype(BF)

        else:
            unit, inverse = uni[0][...], uni[1][:, 0:1]
        total = tot[0][...].astype(F32)
        if n_total > 1:
            total = total + (tot[1][...].astype(F32) + tot[2][...].astype(F32))
        acc[0:8] += fold(total * unit)
        acc[8:16] += fold(total)
        back = norm_back_tile(total, unit, inverse, vecs[3:4])
        gz[...] = back
        low = back.astype(BF)
        gf[...] = low
        acc[16:24] += fold(low.astype(F32))

        @pl.when(t == steps - 1)
        def _():
            s_gain[...] = jnp.sum(acc[0:8], axis=0, keepdims=True)
            s_shift[...] = jnp.sum(acc[8:16], axis=0, keepdims=True)
            s_gf[...] = jnp.sum(acc[16:24], axis=0, keepdims=True)

    def tiles(array):
        skip = (array.shape[0] - rows) // LEN
        return array, pl.BlockSpec((LEN, array.shape[1]), lambda t: (t + skip, 0))

    def out(dtype):
        return jax.ShapeDtypeStruct((rows, D), dtype), pl.BlockSpec((LEN, D), lambda t: (t, 0))

    def own_tile(t, place):
        return (jnp.clip(t - mine * place[2], 0, mine - 1), 0)

    outs = [out(F32), out(BF)] + [out_full((1, D), F32)] * 3
    specs = [s for a, s in outs]
    shapes = [a for a, s in outs]
    ins = [full(vecs)] + [tiles(a) for a in total_ins + unit_ins]

    def with_place(spec):
        index = spec.index_map
        return pl.BlockSpec(
            spec.block_shape, lambda t, place: index(t), pipeline_mode=spec.pipeline_mode
        )

    specs = [with_place(s) for s in specs]
    if final:
        shapes = [jax.ShapeDtypeStruct((rows // 2, D), BF)] + shapes
        specs = [pl.BlockSpec((LEN, D), own_tile)] + specs
    return pl.pallas_call(
        body,
        grid_spec=pltpu.PrefetchScalarGridSpec(
            num_scalar_prefetch=1,
            grid=(steps,),
            in_specs=[with_place(s) for a, s in ins],
            out_specs=specs,
            scratch_shapes=[pltpu.VMEM((24, D), F32)],
        ),
        out_shape=shapes,
        compiler_params=pltpu.CompilerParams(vmem_limit_bytes=BUDGET),
        cost_estimate=pl.CostEstimate(
            flops=int(5 * FLOP_RATE), bytes_accessed=int(5 * HBM_RATE), transcendentals=0
        ),
    )(place, *[a for a, s in ins])


def ffn_back(place, gf, gp, up_pieces, down_pieces):
    rows, hidden = gp.shape
    ups = hidden // WIDE

    def body(place, gf, gp, *refs):
        wu, wd = refs[:PIECES], refs[PIECES : 2 * PIECES]
        gu, part, s_gu, scr_u, scr_d, all_u, scr_all_u = refs[2 * PIECES :]
        t = pl.program_id(0)

        @pl.when(t < 2)
        def _():
            assemble(wd, scr_d.at[t], place)

        @pl.when(t >= 2)
        def _():
            b = t - 2
            assemble(wu, scr_u, place)
            scr_all_u[:, pl.ds(pl.multiple_of(b * WIDE, WIDE), WIDE)] = matrix_of(scr_u)
            w0 = scr_d[0, b].reshape(WIDE, WIDE)
            w1 = scr_d[1, b].reshape(WIDE, WIDE)
            back = dot_t(gf[:, :WIDE], w0) + dot_t(gf[:, WIDE:], w1)
            low = (back * gp[...].astype(F32)).astype(BF)
            gu[...] = low
            all_u[:, pl.ds(pl.multiple_of(b * WIDE, WIDE), WIDE)] = low
            s_gu[...] = jnp.sum(fold(low.astype(F32)), axis=0, keepdims=True)

        @pl.when(t == ups + 1)
        def _():
            part[...] = dot_t(all_u[...], scr_all_u[...]).astype(BF)

    up = lambda t: jnp.maximum(t - 2, 0)
    down = lambda t: jnp.minimum(t, 1)
    return run(
        body,
        ups + 2,
        [small(place), full(gf), in_cols(gp, up)]
        + blocks(up_pieces, 64, up)
        + wide_blocks(down_pieces, down),
        [
            out_cols(rows, hidden, BF, up),
            out_full((rows, D), BF),
            out_cols(1, hidden, F32, up),
        ],
        [
            weight_scratch(64),
            pltpu.VMEM((2, 4, 4, 128, WIDE), BF),
            pltpu.VMEM((rows, hidden), BF),
            pltpu.VMEM((D, hidden), BF),
        ],
        us=14 if rows > 256 else 8,
    )


def branch_back(place, resid, own, other, unit, inv, gain, pieces):
    rows = resid.shape[0]

    def body(place, resid, own, other, unit, inv, gain, *refs):
        w = refs[:PIECES]
        gz, gx, keep, send, s_gain, s_shift, s_gx, scr, total_out, acc = refs[PIECES:]
        t = pl.program_id(0)
        assemble(w, scr, place)

        @pl.when(t == 0)
        def _():
            acc[...] = jnp.zeros_like(acc)

            def step(r):
                here = pl.ds(r, LEN)
                total = resid[here] + (own[here].astype(F32) + other[here].astype(F32))
                acc[0:8] += fold(total * unit[here])
                acc[8:16] += fold(total)
                back = norm_back_tile(total, unit[here], inv[here, 0:1], gain[...])
                gz[here] = back
                low = back.astype(BF)
                gx[here] = low
                acc[16:24] += fold(low.astype(F32))

            each_tile(rows, LEN, step)
            s_gain[...] = jnp.sum(acc[0:8], axis=0, keepdims=True)
            s_shift[...] = jnp.sum(acc[8:16], axis=0, keepdims=True)
            s_gx[...] = jnp.sum(acc[16:24], axis=0, keepdims=True)
            total_out[...] = dot_t(gx[:, :WIDE], matrix_of(scr))

        @pl.when(t == 1)
        def _():
            total_out[...] += dot_t(gx[:, WIDE:], matrix_of(scr))
            core = place[2]
            quarter = HALF // 2
            keep[...] = total_out[:, pl.ds(pl.multiple_of(quarter * core, 128), quarter)].astype(BF)
            send[...] = total_out[
                :, pl.ds(pl.multiple_of(quarter * (1 - core), 128), quarter)
            ].astype(BF)

    return run(
        body,
        2,
        [small(place)]
        + [full(a) for a in (resid, own, other, unit, inv, gain)]
        + blocks(pieces, 32, lambda t: 6 + t),
        [
            out_full((rows, D), F32),
            out_full((rows, D), BF),
            out_full((rows, HALF // 2), BF),
            out_full((rows, HALF // 2), BF),
            out_full((1, D), F32),
            out_full((1, D), F32),
            out_full((1, D), F32),
        ],
        [weight_scratch(32), pltpu.VMEM((rows, HALF), F32), pltpu.VMEM((24, D), F32)],
        us=10 if rows > 256 else 5,
    )


def column_sums(out, values):
    out[...] = jnp.sum(fold(values.astype(F32)), axis=0, keepdims=True)


def cross_back(place, q, kv, keep, got, pieces):
    rows, mem = q.shape[0], kv.shape[0]
    span = STREAMS * LEN

    def body(place, q, kv, keep, got, *refs):
        w = refs[:PIECES]
        gq, gkv, part, s_gq, s_gkv, scr, g, acc = refs[PIECES:]
        t = pl.program_id(0)
        assemble(w, scr, place)

        @pl.when(t == 0)
        def _():
            join_parity(keep, got, place, g)
            for s in range(2):
                r = slice(s * span, s * span + span)
                m = slice(s * LEN, s * LEN + LEN)
                for j in range(4):
                    c = slice(128 * j, 128 * j + 128)
                    c2 = slice(HALF + 128 * j, HALF + 128 * j + 128)
                    gq[r, c], gkv[m, c], gkv[m, c2] = attend_back(
                        q[r, c], kv[m, c], kv[m, c2], g[r, c], place[3 + s]
                    )
            column_sums(s_gq, gq[...])
            column_sums(s_gkv, gkv[...])
            part[:rows] = dot_t(gq[...], matrix_of(scr)).astype(BF)

        @pl.when(t == 1)
        def _():
            acc[...] = dot_t(gkv[:, :HALF], matrix_of(scr))

        @pl.when(t == 2)
        def _():
            part[rows:] = (acc[...] + dot_t(gkv[:, HALF:], matrix_of(scr))).astype(BF)

    return run(
        body,
        3,
        [small(place), full(q), full(kv), full(keep), full(got)]
        + blocks(pieces, 64, lambda t: t),
        [
            out_full((rows, HALF), BF),
            out_full((mem, D), BF),
            out_full((rows + mem, D), BF),
            out_full((1, HALF), F32),
            out_full((1, D), F32),
        ],
        [weight_scratch(64), pltpu.VMEM((rows, HALF), BF), pltpu.VMEM((mem, D), F32)],
        us=14,
    )


def input_grads(place, gz, parts, keep, send):
    rows = gz.shape[0] // 2
    core = place[2]
    here = pl.ds(pl.multiple_of(rows * core, LEN), rows)
    there = pl.ds(pl.multiple_of(rows * (1 - core), LEN), rows)
    total = gz[here]
    for g, w in parts:
        total = total + dot_t(g[here], w)
    keep[...] = total
    total = 0.0
    for g, w in parts:
        total = total + dot_t(g[there], w)
    send[...] = total.astype(BF)


def enc_attention_back(place, qkv, keep, got, gz, pieces):
    rows = qkv.shape[0]

    def body(place, qkv, keep, got, gz, *refs):
        w = refs[:PIECES]
        gqkv, out, send, sums, scr, g, win = refs[PIECES:]
        t = pl.program_id(0)
        assemble(w, scr, place)
        win[:, pl.ds(pl.multiple_of(t * WIDE, WIDE), WIDE)] = matrix_of(scr)

        @pl.when(t == 0)
        def _():
            join_parity(keep, got, place, g)
            for s in range(2):
                r = slice(s * LEN, s * LEN + LEN)
                for j in range(4):
                    c = [slice(HALF * i + 128 * j, HALF * i + 128 * j + 128) for i in range(3)]
                    gqkv[r, c[0]], gqkv[r, c[1]], gqkv[r, c[2]] = attend_back(
                        qkv[r, c[0]], qkv[r, c[1]], qkv[r, c[2]], g[r, c[0]], place[3 + s]
                    )
            column_sums(sums, gqkv[...])

        @pl.when(t == 2)
        def _():
            input_grads(place, gz, [(gqkv, win[...])], out, send)

    return run(
        body,
        3,
        [small(place), full(qkv), full(keep), full(got), full(gz)]
        + blocks(pieces, 64, lambda t: t),
        [
            out_full((rows, 3 * HALF), BF),
            out_full((rows // 2, D), F32),
            out_full((rows // 2, D), BF),
            out_full((1, 3 * HALF), F32),
        ],
        [weight_scratch(64), pltpu.VMEM((rows, HALF), BF), pltpu.VMEM((D, 3 * HALF), BF)],
        us=13,
    )


def ngram_back_kernel(place, qkv, rel, keep, got, gz, pieces):
    rows = qkv.shape[0]
    span = STREAMS * LEN

    def body(place, qkv, rel, keep, got, gz, *refs):
        w, wr = refs[:PIECES], refs[PIECES : 2 * PIECES]
        gqkv, grel, out, send, sums, s_rel, scr, scr_r, g, win, *tables = refs[2 * PIECES :]
        table, table_back, flip = tables
        t = pl.program_id(0)

        @pl.when(t < 3)
        def _():
            assemble(w, scr, place)
            win[:, pl.ds(pl.multiple_of(t * WIDE, WIDE), WIDE)] = matrix_of(scr)

        @pl.when(t == 0)
        def _():
            join_parity(keep, got, place, g)
            table[...] = distance_buckets(False)
            table_back[...] = distance_buckets(True)
            flip[...] = mirror()
            lanes = half_rows(span)

            def step(s, carry):
                r = pl.ds(pl.multiple_of(s * span, span), span)
                r0 = pl.ds(pl.multiple_of(s * span, span), LEN)
                r1 = pl.ds(pl.multiple_of(s * span + LEN, LEN), span - LEN)
                count = place[5 + s]
                for j in range(4):
                    c = [slice(HALF * i + 128 * j, HALF * i + 128 * j + 128) for i in range(3)]
                    q, k, v = qkv[r, c[0]], qkv[r, c[1]], qkv[r, c[2]]
                    k0, v0 = qkv[r0, c[1]], qkv[r0, c[2]]
                    go = g[r, c[0]]
                    high, low = split_high(rel[r, 128 * (j // 2) : 128 * (j // 2) + 128])
                    prod = q.astype(F32) * k.astype(F32)
                    prod_g = go.astype(F32) * v.astype(F32)
                    gq, gk0, gv0, p_own, d_own, turned = [], 0.0, 0.0, [], [], []
                    for i, mask in enumerate(head_masks()):
                        qm, gm = q * mask, go * mask
                        h = 2 * j + i
                        probs, own = ngram_probs(
                            qm, prod, k0, high, low, table[...], count, h, lanes[i]
                        )
                        gp = dot_t(gm, v0)
                        g_own = jnp.sum(prod_g * lanes[i], axis=-1, keepdims=True)
                        inner = jnp.sum(probs * gp, axis=-1, keepdims=True) + own * g_own
                        ds = (probs * (gp - inner)).astype(BF)
                        ds_own = (own * (g_own - inner)).astype(BF).astype(F32)
                        gq.append(dot(ds, k0))
                        gk0 = gk0 + dot_g(ds, qm)
                        gv0 = gv0 + dot_g(probs.astype(BF), gm)
                        p_own.append(own.astype(BF).astype(F32))
                        d_own.append(ds_own)
                        back = skew(dot(ds, flip[...]))
                        lane = lax.broadcasted_iota(jnp.int32, back.shape, 1)
                        main = lax.broadcasted_iota(jnp.int32, back.shape, 0) < LEN
                        back = jnp.where((lane == 127) & jnp.logical_not(main), ds_own, back)
                        grads = dot_t(back.astype(BF), table_back[...])
                        turned.append(grads * quarter_mask(h % 4).astype(F32))
                    first = first_lanes(span)
                    d_own = jnp.where(first, d_own[0], d_own[1])
                    p_own = jnp.where(first, p_own[0], p_own[1])
                    gqf = jnp.where(first, gq[0], gq[1]) + d_own * k.astype(F32)
                    gqkv[r, c[0]] = (gqf * SCALE).astype(BF)
                    gkn = d_own * q.astype(F32) * SCALE
                    gvn = p_own * go.astype(F32)
                    gqkv[r0, c[1]] = (gk0 * SCALE).astype(BF)
                    gqkv[r0, c[2]] = gv0.astype(BF)
                    gqkv[r1, c[1]] = gkn[LEN:].astype(BF)
                    gqkv[r1, c[2]] = gvn[LEN:].astype(BF)
                    both = turned[0] + turned[1]
                    at = slice(128 * (j // 2), 128 * (j // 2) + 128)
                    if j % 2 == 0:
                        held = both
                    else:
                        grel[r, at] = (held + both).astype(BF)
                return carry

            lax.fori_loop(0, 2, step, 0)
            column_sums(sums, gqkv[...])
            column_sums(s_rel, grel[...])

        @pl.when(t == 3)
        def _():
            assemble_rel(wr, scr_r, place)
            wrel = scr_r[...].reshape(D, REL_HALF)
            input_grads(place, gz, [(gqkv, win[...]), (grel, wrel)], out, send)

    third = lambda t: jnp.minimum(t, 2)
    return run(
        body,
        4,
        [small(place), full(qkv), full(rel), full(keep), full(got), full(gz)]
        + blocks(pieces, 64, third)
        + blocks(pieces, 32, lambda t: 8),
        [
            out_full((rows, 3 * HALF), BF),
            out_full((rows, REL_HALF), BF),
            out_full((rows // 2, D), F32),
            out_full((rows // 2, D), BF),
            out_full((1, 3 * HALF), F32),
            out_full((1, REL_HALF), F32),
        ],
        [
            weight_scratch(64),
            pltpu.VMEM((4, 4, 2, 32, REL_HALF), BF),
            pltpu.VMEM((rows, HALF), BF),
            pltpu.VMEM((D, 3 * HALF), BF),
        ]
        + [pltpu.VMEM((128, 128), BF)] * 3,
        us=29,
    )


def grad_chunk(place, arrays, terms, total_rows, width=WIDE):
    n = len(arrays)

    def body(place, *refs):
        ins, outs, scr = refs[:n], refs[n : n + 4], refs[n + 4]
        t = pl.program_id(0)
        dp, core = place[0], place[2]

        def spread(value, at, rows, lanes=slice(0, WIDE)):
            v = value.astype(BF).reshape(4, 4, rows, WIDE)
            scr[:, :, :rows] = v
            for i in range(4):
                outs[i][:, at : at + rows, lanes] = scr[jnp.bitwise_xor(dp, i), :, :rows]

        for index, (kind, at, x, g, col) in enumerate(terms):

            @pl.when(t == index)
            def _(kind=kind, at=at, x=x, g=g, col=col):
                if kind == "whole":
                    spread(ins[x][...], at, ins[x].shape[0] // 16)
                    return
                if kind == "heads":
                    right = ins[g][:, col : col + WIDE]
                    mine, theirs = ins[x][...], ins[x + 1][...]
                    keep, got = dot_g(mine, right), dot_g(theirs, right)
                    quarter = (2, 4, 32, WIDE)
                    scr[pl.ds(2 * core, 2), :, :32] = keep.astype(BF).reshape(quarter)
                    scr[pl.ds(2 - 2 * core, 2), :, :32] = got.astype(BF).reshape(quarter)
                    spread(scr[:, :, :32], at, 32)
                    return
                if kind == "rel":
                    v = dot_g(ins[x][...], ins[g][...]).astype(BF).reshape(16, 2, 32, REL_HALF)
                    spread(jnp.concatenate([v[:, 0], v[:, 1]], axis=-1), at, 32)
                    return
                value = dot_g(ins[x][...], ins[g][:, col : col + WIDE])
                lanes = slice(col, col + WIDE) if kind == "rows" else slice(0, WIDE)
                spread(value, at, value.shape[0] // 16, lanes)

    return run(
        body,
        len(terms),
        [small(place)] + [full(a) for a in arrays],
        [out_full((4, total_rows, width), BF)] * 4,
        [weight_scratch(128)],
        us=10,
    )


def vec_chunk(place, pieces):
    def body(place, *refs):
        assemble(refs[:PIECES], refs[PIECES], place)

    return run(
        body,
        1,
        [small(place)] + blocks(pieces, 16, lambda t: 18),
        [out_full((4, 4, 16, WIDE), BF)],
        us=2,
    )[0]


class Order:

    def __init__(self, place):
        self.place = place
        self.last = None

    def after(self, *values):
        if self.last is not None:
            values = (self.last,) + values
        self.place = tie(self.place, *values)
        self.last = None

    def run(self, kernel, *args):
        if self.last is not None:
            self.place = tie(self.place, self.last)
        out = kernel(self.place, *args)
        self.last = out[0] if isinstance(out, (list, tuple)) else out
        return out

    def matmul(self, left, right):
        if self.last is not None:
            right = tie(right, self.last)
        self.last = dot_g(left, right).astype(BF)
        return self.last

    def add(self, first, *others, dtype=BF):
        if self.last is not None:
            first = tie(first, self.last)
        self.last = sum((v.astype(F32) for v in others), first.astype(F32)).astype(dtype)
        return self.last


class Links:

    def __init__(self, lay, before):
        self.lay = lay
        self.gathered = []
        self.first = []
        self.before = before
        self.second = []
        self.far = 2
        self.groups = [list(range(core, lay.nf, 2)) for core in range(2)]

    def turn(self):
        self.far = 3 - self.far
        return self.far

    def gather(self, buf, direct=False):
        far = 3 if direct else self.turn()
        if len(self.gathered) >= 2:
            buf = tie(buf, self.gathered[-2])
        own = lax.all_gather(buf, "fsdp", axis=0, axis_index_groups=self.groups)
        self.gathered.append(own)
        ready = tie(own, *(self.first[-1] if self.first else self.before))
        if len(self.second) >= 3:
            ready = tie(ready, self.second[-3])
        x, y = self.lay.flip_dp(ready, 1), self.lay.flip_dp(ready, 2)
        self.first.append((x, y))
        if direct:
            d = self.lay.flip_dp(ready, 3)
        else:
            d = self.lay.flip_dp(x, 2) if far == 2 else self.lay.flip_dp(y, 1)
        self.second.append(d)
        return [own, x, y, d]

    def scatter_whole(self, value):
        lay = self.lay
        groups = [
            [dp * lay.nf + fs for dp in range(lay.ndp) for fs in range(core, lay.nf, 2)]
            for core in range(2)
        ]
        return lax.psum_scatter(
            value, ("dp", "fsdp"), scatter_dimension=0, tiled=True, axis_index_groups=groups
        ).astype(F32)

    def scatter(self, order, parts, direct=False):
        own, x, y, d = parts
        if direct:
            moved = [self.lay.flip_dp(part, i + 1) for i, part in enumerate((x, y, d))]
            yield
            yield
            total = order.add(own, *moved)
        else:
            far = self.turn()
            d = self.lay.flip_dp(d, far)
            if far == 2:
                y = self.lay.flip_dp(y, 2)
                yield
                x = self.lay.flip_dp(order.add(x, d), 1)
            else:
                x = self.lay.flip_dp(x, 1)
                yield
                y = self.lay.flip_dp(order.add(y, d), 2)
            yield
            total = order.add(own, x, y)
        yield lax.psum_scatter(
            total, "fsdp", scatter_dimension=0, axis_index_groups=self.groups
        ).astype(F32)


def shards_fast(
    ndp,
    nf,
    source,
    dec_in,
    src_lengths,
    tgt_lengths,
    enc_in_proj,
    enc_out_proj,
    enc_ffn_in,
    enc_ffn_out,
    enc_gains,
    enc_biases,
    dec_in_proj,
    dec_rel_proj,
    dec_out_proj,
    cross_query,
    cross_kv,
    cross_out,
    dec_ffn_in,
    dec_ffn_out,
    dec_gains,
    dec_biases,
    enc_cot,
    dec_cot,
):
    lay = Layout(ndp, nf)
    lay.place()
    r, f, chips = lay.r, lay.f, lay.chips
    swap, pick, pair = lay.swap, lay.pick, lay.pair
    core = lay.core
    dec_rows = STREAMS * LEN

    def halves(matrix, groups, width):
        parts = matrix.reshape(r, groups, 2, width)
        return (
            pick(parts[:, :, 0], parts[:, :, 1]).reshape(r, groups * width),
            pick(parts[:, :, 1], parts[:, :, 0]).reshape(r, groups * width),
        )

    split = [
        halves(enc_in_proj, 3, HALF),
        halves(enc_ffn_in, chips, f),
        halves(dec_in_proj, 3, HALF),
        halves(cross_query, 1, HALF),
        halves(cross_kv, 2, HALF),
        halves(dec_ffn_in, chips, f),
        halves(dec_rel_proj, 1, REL_HALF),
    ]
    vec = jnp.concatenate(
        [
            enc_biases,
            enc_gains,
            dec_biases,
            dec_gains,
            src_lengths.astype(BF),
            tgt_lengths.astype(BF),
        ]
    )
    nvec = vec.shape[0]
    padded = -(-nvec // WIDE) * WIDE
    vec = jnp.pad(vec, (0, padded - nvec))
    mine = jnp.concatenate([own for own, other in split], axis=1)
    theirs = jnp.concatenate([other for own, other in split], axis=1)
    theirs_got = swap(theirs)
    vec_got = swap(vec)
    source_got = swap(source)
    dec_own = dec_in.transpose(1, 0, 2).reshape(dec_rows, D)
    dec_got = swap(dec_own)
    dcot_own = dec_cot.transpose(1, 0, 2).reshape(dec_rows, D)
    dcot_got = swap(dcot_own)
    ecot_got = swap(enc_cot)
    links = Links(lay, (theirs_got, vec_got, source_got, dec_got, dcot_got, ecot_got))
    w = {"dec_down": links.gather(dec_ffn_out), "enc_down": links.gather(enc_ffn_out)}

    def column_blocks(start, count):
        return [
            pair(
                mine[:, start + WIDE * i : start + WIDE * i + WIDE],
                theirs_got[:, start + WIDE * i : start + WIDE * i + WIDE],
                0,
            )
            for i in range(count)
        ]

    def row_blocks(matrix):
        return [matrix[:, :WIDE], matrix[:, WIDE:]]

    rel_start = mine.shape[1] - REL_HALF
    rel_block = pair(mine[:, rel_start:], theirs_got[:, rel_start:], 1)
    vec_pair = pair(vec[None], vec_got[None], 0)
    vec_used = 2 * padded // WIDE
    vec_block = jnp.pad(vec_pair.reshape(vec_used, WIDE), ((0, 16 - vec_used), (0, 0)))
    at = [0, 3 * WIDE, 7 * WIDE, 10 * WIDE, 11 * WIDE, 13 * WIDE]
    chunk_parts = {
        "enc": column_blocks(at[0], 3) + row_blocks(enc_out_proj),
        "enc_up": column_blocks(at[1], 4),
        "dec": column_blocks(at[2], 3) + row_blocks(dec_out_proj) + [rel_block, vec_block],
        "cross": column_blocks(at[3], 1) + column_blocks(at[4], 2) + row_blocks(cross_out),
        "dec_up": column_blocks(at[5], 4),
    }
    for name in ("dec", "enc", "enc_up", "cross", "dec_up"):
        w[name] = links.gather(jnp.concatenate(chunk_parts[name], axis=0))

    lens = vec_pair[:, nvec - 2 : nvec].T.reshape(-1).astype(F32).astype(jnp.int32)
    place = jnp.concatenate(
        [jnp.stack([lay.dp, lay.z, core]).astype(jnp.int32), lens, jnp.zeros((1,), jnp.int32)]
    )

    order = Order(place)
    vec_all = order.run(vec_chunk, w["dec"]).reshape(chips, 16, WIDE)[:, :vec_used]
    vec_all = vec_all.reshape(lay.devices, padded).astype(F32)
    widths = [enc_biases.shape[0], enc_gains.shape[0], dec_biases.shape[0], dec_gains.shape[0]]
    starts = [0]
    for width in widths:
        starts.append(starts[-1] + width)
    v_enc_b, v_enc_g, v_dec_b, v_dec_g = [
        vec_all[:, starts[i] : starts[i + 1]].reshape(-1) for i in range(4)
    ]
    eb, eg_rows = v_enc_b.reshape(-1, D), v_enc_g.reshape(2, D)
    dg_rows = v_dec_g.reshape(3, D)
    d_split = 2 * D + HEADS * BUCKETS
    db = v_dec_b[d_split:].reshape(-1, D)

    def half_of(vector):
        parts = vector.reshape(2, -1)
        return pick(parts[0], parts[1])

    def hidden_of(vector):
        parts = vector.reshape(chips, 2, f)
        return pick(parts[:, 0], parts[:, 1]).reshape(1, -1)

    zero_half = jnp.zeros((HALF,), F32)

    def qkv_bias(q, v):
        return jnp.concatenate([half_of(q), zero_half, half_of(v)])[None]

    def rows_of(*vectors):
        return jnp.stack(vectors)

    x = pair(source, source_got, 0)
    y = pair(dec_own, dec_got, 0)
    dcot = pair(dcot_own, dcot_got, 0)
    ecot = pair(enc_cot, ecot_got, 0)
    order.after(x, y, dcot, ecot)
    order.after(links.gathered[5], *links.first[3], links.second[1])
    dqkv, rel, da_keep, da_send = order.run(
        ngram_attention,
        y,
        qkv_bias(v_dec_b[:D], v_dec_b[D : 2 * D]),
        half_of(v_dec_b[2 * D : d_split])[None],
        w["dec"],
    )
    da_got = swap(da_send)
    order.after(links.gathered[6], *links.first[4])
    eqkv, ea_keep, ea_send = order.run(enc_attention, x, qkv_bias(eb[0], eb[1]), w["enc"])
    ea_got = swap(ea_send)
    order.after(*links.first[5])
    p3 = order.run(out_projection, da_keep, da_got, w["dec"])
    p3_got = swap(p3)
    p1 = order.run(out_projection, ea_keep, ea_got, w["enc"])
    p1_got = swap(p1)
    eunit1, einv1, eh1_low = order.run(
        norm_forward,
        x,
        False,
        p1,
        p1_got,
        rows_of(eb[2], eb[2], eb[2], eg_rows[0], eb[8]),
    )
    order.after(links.second[5], *links.first[6])
    eg, egp, p2 = order.run(
        ffn_forward, eh1_low, hidden_of(eb[3:7]), w["enc_up"], w["enc_down"]
    )
    p2_got = swap(p2)
    order.after(links.second[6])
    dunit1, dinv1, dh1_low, eunit2, einv2, enc_low, cq, ckv, ca_keep, ca_send = order.run(
        cross_forward,
        y,
        p3,
        p3_got,
        rows_of(db[0], dg_rows[0], db[9]),
        eunit1,
        rows_of(eg_rows[0], eb[8], eb[7], eg_rows[1], eb[9]),
        p2,
        p2_got,
        half_of(db[1])[None],
        jnp.concatenate([zero_half, half_of(db[2])])[None],
        w["cross"],
    )
    ca_got = swap(ca_send)
    p4 = order.run(out_projection, ca_keep, ca_got, w["cross"])
    p4_got = swap(p4)
    dunit2, dinv2, dh2_low = order.run(
        norm_forward,
        dunit1,
        True,
        p4,
        p4_got,
        rows_of(dg_rows[0], db[9], db[3], dg_rows[1], db[10]),
    )
    dg, dgp, p5 = order.run(
        ffn_forward, dh2_low, hidden_of(db[4:8]), w["dec_up"], w["dec_down"]
    )
    p5_got = swap(p5)

    up_terms = [("plain", 64 * b, 0, 1, WIDE * b) for b in range(4)]
    down_terms = [("rows", 0, 0, 1, WIDE * h) for h in range(2)]

    def grads(*args):
        scatter = links.scatter(order, order.run(grad_chunk, *args))
        next(scatter)
        return scatter

    dec_out, gz3, gf, s_gain3, s_shift3, s_gf = order.run(
        norm_backward,
        True,
        [dcot],
        [dunit2, p5, p5_got],
        rows_of(dg_rows[1], db[10], db[8], dg_rows[2], db[11]),
    )
    r_dd = grads([dg, gf], down_terms, 128, D)
    gu, p6, s_gu = order.run(ffn_back, gf, dgp, w["dec_up"], w["dec_down"])
    p6_got = swap(p6)
    r_du = grads([dh2_low, gu], up_terms, 256)
    gz2, gx, gca_keep, gca_send, s_gain2, s_shift2, s_gx = order.run(
        branch_back, gz3, p6, p6_got, dunit2, dinv2, dg_rows[1:2], w["cross"]
    )
    gca_got = swap(gca_send)
    gcq, gckv, p7, s_gcq, s_gckv = order.run(
        cross_back, cq, ckv, gca_keep, gca_got, w["cross"]
    )
    p7_got = swap(p7)
    next(r_dd)
    next(r_du)
    r_cross = grads(
        [dh1_low, gcq, enc_low, gckv, ca_keep, ca_got, gx],
        [
            ("plain", 0, 0, 1, 0),
            ("plain", 64, 2, 3, 0),
            ("plain", 128, 2, 3, WIDE),
            ("heads", 192, 4, 6, 0),
            ("heads", 224, 4, 6, WIDE),
        ],
        256,
    )
    gz1, go, gda_keep, gda_send, s_gain1, s_shift1, s_go = order.run(
        branch_back, gz2, p7, p7_got, dunit1, dinv1, dg_rows[0:1], w["dec"]
    )
    gda_got = swap(gda_send)
    gz2e, gfe, e_gain2, e_shift2, s_gfe = order.run(
        norm_backward, False, [ecot, p7, p7_got], [eunit2, einv2], rows_of(*([eg_rows[1]] * 5))
    )
    gue, p9, s_gue = order.run(ffn_back, gfe, egp, w["enc_up"], w["enc_down"])
    p9_got = swap(p9)
    r_ed = grads([eg, gfe], down_terms, 128, D)
    r_eu = grads([eh1_low, gue], up_terms, 256)
    total_dd = next(r_dd)
    next(r_cross)
    total_du = next(r_du)
    gz1e, goe, gea_keep, gea_send, e_gain1, e_shift1, s_goe = order.run(
        branch_back, gz2e, p9, p9_got, eunit1, einv1, eg_rows[0:1], w["enc"]
    )
    gea_got = swap(gea_send)
    gqkv, grel, p8, p8_send, s_gqkv, s_grel = order.run(
        ngram_back_kernel, dqkv, rel, gda_keep, gda_got, gz1, w["dec"]
    )
    p8_got = swap(p8_send)
    next(r_ed)
    next(r_eu)
    total_cross = next(r_cross)
    geqkv, p10, p10_send, s_geqkv = order.run(
        enc_attention_back, eqkv, gea_keep, gea_got, gz1e, w["enc"]
    )
    p10_got = swap(p10_send)
    g_dec_in = order.add(p8, p8_got, dtype=F32)
    r_dec = grads(
        [y, gqkv, da_keep, da_got, go, grel],
        [("plain", 64 * b, 0, 1, WIDE * b) for b in range(3)]
        + [("heads", 192, 2, 4, 0), ("heads", 224, 2, 4, WIDE), ("rel", 256, 0, 5, 0)],
        288,
    )
    g_source = order.add(p10, p10_got, dtype=F32)
    total_ed = next(r_ed)
    total_eu = next(r_eu)

    def widen(vector):
        zeros = jnp.zeros_like(vector)
        return pick(jnp.concatenate([vector, zeros]), jnp.concatenate([zeros, vector]))

    def widen_hidden(vector):
        parts = vector.reshape(chips, 1, f)
        zeros = jnp.zeros_like(parts)
        return pick(
            jnp.concatenate([parts, zeros], axis=1), jnp.concatenate([zeros, parts], axis=1)
        ).reshape(-1)

    def owned(*vectors):
        return jnp.concatenate(vectors).reshape(lay.devices, -1)

    vec_grads = jnp.concatenate(
        [
            owned(
                widen(s_geqkv[0, :HALF]),
                widen(s_geqkv[0, 2 * HALF :]),
                0.5 * s_goe[0],
                widen_hidden(s_gue),
                0.5 * s_gfe[0],
                0.5 * e_shift1[0],
                0.5 * e_shift2[0],
            ),
            owned(0.5 * e_gain1[0], 0.5 * e_gain2[0]),
            owned(
                widen(s_gqkv[0, :HALF]),
                widen(s_gqkv[0, 2 * HALF :]),
                widen(s_grel[0]),
                0.5 * s_go[0],
                widen(s_gcq[0]),
                widen(s_gckv[0, HALF:]),
                0.5 * s_gx[0],
                widen_hidden(s_gu),
                0.5 * s_gf[0],
                0.5 * s_shift1[0],
                0.5 * s_shift2[0],
                0.5 * s_shift3[0],
            ),
            owned(0.5 * s_gain1[0], 0.5 * s_gain2[0], 0.5 * s_gain3[0]),
        ],
        axis=1,
    ).astype(BF)
    vec_width = vec_grads.shape[1]
    vec_grads = jnp.pad(vec_grads, ((0, 0), (0, padded - vec_width)))
    vec_grads = vec_grads.reshape(chips, vec_used, WIDE)
    vec_grads = jnp.pad(vec_grads, ((0, 0), (0, 16 - vec_used), (0, 0))).reshape(chips * 16, WIDE)
    r_enc = grads(
        [x, geqkv, ea_keep, ea_got, goe, vec_grads],
        [("plain", 64 * b, 0, 1, WIDE * b) for b in range(3)]
        + [("heads", 192, 2, 4, 0), ("heads", 224, 2, 4, WIDE), ("whole", 256, 5, 5, 0)],
        272,
    )
    next(r_dec)
    next(r_enc)
    total2 = next(r_dec)
    total0 = next(r_enc)

    def split_rows(total, sizes):
        at = 0
        result = []
        for size in sizes:
            result.append(total[at : at + size])
            at += size
        return result

    def own_rows_of(total, count):
        rows = total.reshape(count, 2, r, WIDE)
        keep = pick(rows[:, 0], rows[:, 1])
        got = swap(pick(rows[:, 1], rows[:, 0]))
        return pair(keep[:, None], got[:, None], 1)

    def in_rows(rows):
        return rows.transpose(2, 0, 1, 3).reshape(r, -1)

    def up_rows(rows):
        per = WIDE // f
        return rows.reshape(4, 2, r, per, f).transpose(2, 0, 3, 1, 4).reshape(r, FF)

    def side(low, high):
        return jnp.concatenate([low, high], axis=1)

    t0 = split_rows(total0, [6 * r, r, r, 16])
    o_enc_in, o_enc_out = in_rows(own_rows_of(t0[0], 3)), side(t0[1], t0[2])
    vec_sum = t0[3][:vec_used].reshape(2, padded)
    vec_sum = pick(vec_sum[0], vec_sum[1]) + swap(pick(vec_sum[1], vec_sum[0]))
    o_vec = [vec_sum[starts[i] : starts[i + 1]] for i in range(4)]
    o_enc_up = up_rows(own_rows_of(total_eu, 4))
    o_enc_down = total_ed
    t2 = split_rows(total2, [6 * r, r, r, r])
    o_dec_in, o_dec_out = in_rows(own_rows_of(t2[0], 3)), side(t2[1], t2[2])
    relp = t2[3].reshape(r, 2, REL_HALF)
    o_rel = pair(pick(relp[:, 0], relp[:, 1]), swap(pick(relp[:, 1], relp[:, 0])), 1)
    t3 = split_rows(total_cross, [2 * r, 4 * r, r, r])
    o_cross_q = in_rows(own_rows_of(t3[0], 1))
    o_cross_kv = in_rows(own_rows_of(t3[1], 2))
    o_cross_out = side(t3[2], t3[3])
    o_dec_up = up_rows(own_rows_of(total_du, 4))
    o_dec_down = total_dd

    return (
        pick(enc_low[:LEN], enc_low[LEN:]),
        dec_out.reshape(STREAMS, LEN, D).transpose(1, 0, 2),
        g_source,
        g_dec_in.reshape(STREAMS, LEN, D).transpose(1, 0, 2),
        o_enc_in,
        o_enc_out,
        o_enc_up,
        o_enc_down,
        o_vec[1],
        o_vec[0],
        o_dec_in,
        o_rel,
        o_dec_out,
        o_cross_q,
        o_cross_kv,
        o_cross_out,
        o_dec_up,
        o_dec_down,
        o_vec[3],
        o_vec[2],
    )


def solution(mesh):
    ndp, nf = mesh.shape["dp"], mesh.shape["fsdp"]
    whole = ("dp", "fsdp")
    one, two, three = P(whole), P(whole, None), P(whole, None, None)
    args = (two, three, one, one) + (two,) * 4 + (one,) * 2 + (two,) * 8 + (one,) * 2 + (two, three)
    outs = (two, three, two, three) + (two,) * 4 + (one,) * 2 + (two,) * 8 + (one,) * 2

    def body(*arrays):
        if (ndp, nf) == (4, 8):
            return shards_fast(ndp, nf, *arrays)
        return shards(ndp, nf, *arrays)

    return jax.shard_map(body, mesh=mesh, in_specs=args, out_specs=outs, check_vma=False)
```
